32 devices in a mesh: replica: 8 (over y, x, core), shard: 4 (over z).
Axes of the slice: x: 2, y: 2, z: 4, core: 2. Of those that a mesh axis runs over, the one named last changes fastest.
Arguments:
- frames: bfloat16 [16, 1536, 1536], P('replica', 'shard'), may hold values from -6 to 6
- text_states: bfloat16 [16, 64, 1536], P('replica'), may hold values from -6 to 6
- text_mask: int32 [16, 64], P('replica'), may hold values from 0 to 1, as said below
- clip_lengths: int32 [16], P('replica'), may hold values from 384 to 1536, as said below
- slot_used: int32 [16], P('replica'), may hold values from 0 to 1, as said below
- teacher: bfloat16 [16, 1536, 1536], P('replica', 'shard'), may hold values from -16 to 16
- self_norm_gain: bfloat16 [1536], P('shard'), may hold values from 0.5 to 1.5
- self_norm_bias: bfloat16 [1536], P('shard'), may hold values from -1.1953125 to 1.1953125
- self_query_weight: bfloat16 [1536, 1536], P('shard'), may hold values from -0.15625 to 0.15625
- self_key_weight: bfloat16 [1536, 1536], P('shard'), may hold values from -0.15625 to 0.15625
- self_value_weight: bfloat16 [1536, 1536], P('shard'), may hold values from -0.15625 to 0.15625
- self_output_weight: bfloat16 [1536, 1536], P('shard'), may hold values from -1.25 to 1.25
- cross_norm_gain: bfloat16 [1536], P('shard'), may hold values from 0.5 to 1.5
- cross_norm_bias: bfloat16 [1536], P('shard'), may hold values from -1.1953125 to 1.1953125
- cross_query_weight: bfloat16 [1536, 1536], P('shard'), may hold values from -0.15625 to 0.15625
- cross_key_weight: bfloat16 [1536, 1536], P('shard'), may hold values from -0.15625 to 0.15625
- cross_value_weight: bfloat16 [1536, 1536], P('shard'), may hold values from -0.15625 to 0.15625
- cross_output_weight: bfloat16 [1536, 1536], P('shard'), may hold values from -0.625 to 0.625
- feed_norm_gain: bfloat16 [1536], P('shard'), may hold values from 0.5 to 1.5
- feed_norm_bias: bfloat16 [1536], P('shard'), may hold values from -1.1953125 to 1.1953125
- feed_up_weight: bfloat16 [1536, 6144], P('shard'), may hold values from -0.15625 to 0.15625
- feed_down_weight: bfloat16 [6144, 1536], P('shard'), may hold values from -0.078125 to 0.078125
Outputs:
- output: bfloat16 [16, 1536, 1536], P('replica', 'shard')
- loss: float32 [], replicated
- frames_grad: float32 [16, 1536, 1536], P('replica', 'shard')
- text_grad: float32 [16, 64, 1536], P('replica')
- self_norm_gain_grad: float32 [1536], P('shard')
- self_norm_bias_grad: float32 [1536], P('shard')
- self_query_weight_grad: float32 [1536, 1536], P('shard')
- self_key_weight_grad: float32 [1536, 1536], P('shard')
- self_value_weight_grad: float32 [1536, 1536], P('shard')
- self_output_weight_grad: float32 [1536, 1536], P('shard')
- cross_norm_gain_grad: float32 [1536], P('shard')
- cross_norm_bias_grad: float32 [1536], P('shard')
- cross_query_weight_grad: float32 [1536, 1536], P('shard')
- cross_key_weight_grad: float32 [1536, 1536], P('shard')
- cross_value_weight_grad: float32 [1536, 1536], P('shard')
- cross_output_weight_grad: float32 [1536, 1536], P('shard')
- feed_norm_gain_grad: float32 [1536], P('shard')
- feed_norm_bias_grad: float32 [1536], P('shard')
- feed_up_weight_grad: float32 [1536, 6144], P('shard')
- feed_down_weight_grad: float32 [6144, 1536], P('shard')
The draws below stay inside these ranges and needn't reach their ends.
Inputs may be any that keep to these rules, and one draw needn't show every extreme that they name: `clip_lengths`: the first slot of every replica holds more than 1152 frames, slot 0 exactly 1536. `slot_used`: the first of the 2 slots of every replica is used. `text_mask`: each row is ones followed by zeros, with 8 or more ones; row 0 is all ones.
All inputs are finite; a program needn't handle non-finite values.
Results may differ from the reference program's by a relative error of at most 0.015.
Values may be sent and summed in bfloat16 or wider, within the bound.
No kernel may reach another device: no remote copies, remote signals or barrier semaphores. Data moves between devices by JAX's collectives and lax.ppermute only.
A program may use at most 512 MiB of HBM per device.

```python
import jax
import jax.numpy as jnp
from jax import lax

D = 1536
HEADS = 24
HEAD_DIM = 64
FF = 6144
CLIP = 1536
TEXT = 64
FR = 384
SLOTS = 16
GRAD_SCALE = 18874368


def draw_clip_lengths(key, part):
    key = jax.random.fold_in(key, 11)
    first_key, second_key, coin_key = jax.random.split(key, 3)
    first = jax.random.randint(first_key, (SLOTS // 2,), CLIP - FR // 2, CLIP + 1)
    first = first.at[0].set(CLIP)
    second = jax.random.randint(second_key, (SLOTS // 2,), CLIP // 4, CLIP + 1)
    coin = jax.random.randint(coin_key, (SLOTS // 2,), 0, 2)
    second = jnp.where(coin > 0, CLIP, second)
    return jnp.stack([first, second], axis=1).reshape(SLOTS).astype(jnp.int32)


def draw_slot_used(key, part):
    key = jax.random.fold_in(key, 12)
    second = (jax.random.randint(key, (SLOTS // 2,), 0, 8) < 3).astype(jnp.int32)
    first = jnp.ones((SLOTS // 2,), jnp.int32)
    return jnp.stack([first, second], axis=1).reshape(SLOTS).astype(jnp.int32)


def draw_text_mask(key, part):
    key = jax.random.fold_in(key, 13)
    present = jax.random.randint(key, (SLOTS,), TEXT // 8, TEXT + 1)
    present = present.at[0].set(TEXT)
    places = jnp.arange(TEXT, dtype=jnp.int32)
    return (places[None, :] < present[:, None]).astype(jnp.int32)


def draw_teacher(key, part):
    key = jax.random.fold_in(key, 14)
    place = (jnp.arange(SLOTS, dtype=jnp.float32)[:, None] * CLIP + jnp.arange(CLIP, dtype=jnp.float32)[None, :]) / (SLOTS * CLIP)
    scale = 0.5 * 6.0 ** place
    values = jnp.clip(jax.random.normal(key, (SLOTS, CLIP, D), jnp.float32), -4.0, 4.0)
    return (values * scale[:, :, None]).astype(jnp.bfloat16)


def level_of(key, extent, cuts, least, top_value):
    level, own = 1.0, jax.random.fold_in(key, 6)
    for axis_at, shards_of in cuts:
        steps = jnp.exp(jax.random.uniform(jax.random.fold_in(own, axis_at), (shards_of,), jnp.float32, least / len(cuts), top_value / len(cuts)))
        level = level * jnp.repeat(steps, extent[axis_at] // shards_of).reshape([-1 if axis == axis_at else 1 for axis in range(len(extent))])
    return level


def gaussian(stream_key, dims, spread, most, cuts=(), kind=jnp.bfloat16):
    values = spread * jax.random.normal(stream_key, dims, jnp.float32)
    if cuts:
        values = values * level_of(stream_key, dims, cuts, -0.22, 0.18)
    return jnp.clip(values, -most, most).astype(kind)


def setup_inputs(seed: int = 0) -> dict:
    seeds = jax.random.split(jax.random.key(seed), 23)
    return {
        "frames": gaussian(seeds[0], (SLOTS, CLIP, D), 1.0, 6.0, ((0, 8), (1, 4))),
        "text_states": gaussian(seeds[1], (SLOTS, TEXT, D), 1.0, 6.0, ((0, 8),)),
        "text_mask": draw_text_mask(jax.random.fold_in(seeds[22], 71), 0),
        "clip_lengths": draw_clip_lengths(jax.random.fold_in(seeds[22], 71), 0),
        "slot_used": draw_slot_used(jax.random.fold_in(seeds[22], 71), 0),
        "teacher": draw_teacher(jax.random.fold_in(seeds[22], 71), 0),
        "self_norm_gain": jnp.clip(1.0 + 0.1 * jax.random.normal(seeds[6], (D,), jnp.float32), 0.5, 1.5).astype(jnp.bfloat16),
        "self_norm_bias": gaussian(seeds[7], (D,), 0.2, 1.1953125, ((0, 4),)),
        "self_query_weight": gaussian(seeds[8], (D, D), D ** -0.5, 0.15625, ((0, 4),)),
        "self_key_weight": gaussian(seeds[9], (D, D), D ** -0.5, 0.15625, ((0, 4),)),
        "self_value_weight": gaussian(seeds[10], (D, D), D ** -0.5, 0.15625, ((0, 4),)),
        "self_output_weight": gaussian(seeds[11], (D, D), (D // 64) ** -0.5, 1.25, ((0, 4),)),
        "cross_norm_gain": jnp.clip(1.0 + 0.1 * jax.random.normal(seeds[12], (D,), jnp.float32), 0.5, 1.5).astype(jnp.bfloat16),
        "cross_norm_bias": gaussian(seeds[13], (D,), 0.2, 1.1953125, ((0, 4),)),
        "cross_query_weight": gaussian(seeds[14], (D, D), D ** -0.5, 0.15625, ((0, 4),)),
        "cross_key_weight": gaussian(seeds[15], (D, D), D ** -0.5, 0.15625, ((0, 4),)),
        "cross_value_weight": gaussian(seeds[16], (D, D), D ** -0.5, 0.15625, ((0, 4),)),
        "cross_output_weight": gaussian(seeds[17], (D, D), (D // 16) ** -0.5, 0.625, ((0, 4),)),
        "feed_norm_gain": jnp.clip(1.0 + 0.1 * jax.random.normal(seeds[18], (D,), jnp.float32), 0.5, 1.5).astype(jnp.bfloat16),
        "feed_norm_bias": gaussian(seeds[19], (D,), 0.2, 1.1953125, ((0, 4),)),
        "feed_up_weight": gaussian(seeds[20], (D, FF), D ** -0.5, 0.15625, ((0, 4),)),
        "feed_down_weight": gaussian(seeds[21], (FF, D), FF ** -0.5, 0.078125, ((0, 4),)),
    }


epsilon = 1e-05
masked_score = -1e+30
highest = lax.Precision.HIGHEST

@jax.custom_vjp
def low(v):
    return lax.optimization_barrier(v.astype(jnp.bfloat16)).astype(jnp.float32)

@jax.custom_vjp
def low_back(v):
    return v

def low_keep(v):
    return (low(v), None)

def low_pass(kept, grad):
    return (grad,)

def back_keep(v):
    return (v, None)

def back_low(kept, grad):
    return (low(grad),)
low.defvjp(low_keep, low_pass)
low_back.defvjp(back_keep, back_low)

def layer_norm(values, gain, shift):
    center = values - lax.optimization_barrier(jnp.mean(values, axis=-1, keepdims=True))
    variance = lax.optimization_barrier(jnp.mean(center * center, axis=-1, keepdims=True))
    return center * lax.rsqrt(variance + epsilon) * gain + shift

def product(left, right):
    return jnp.dot(left, right, precision=highest)

def split_heads(values):
    return values.reshape(values.shape[0], HEADS, HEAD_DIM)

def attend(queries, keys, values, allowed):
    scale = HEAD_DIM ** (-0.5)
    raw = jnp.einsum('qhd,khd->hqk', split_heads(queries), split_heads(keys), precision=highest) * scale
    scores = low_back(jnp.where(allowed[None], raw, masked_score))
    peak = lax.optimization_barrier(jnp.max(scores, axis=-1, keepdims=True))
    weights = jnp.exp(scores - peak)
    probs = weights / lax.optimization_barrier(jnp.sum(weights, axis=-1, keepdims=True))
    mixed = jnp.einsum('hqk,khd->qhd', low(probs), split_heads(values), precision=highest)
    return low_back(low(mixed.reshape(mixed.shape[0], HEADS * HEAD_DIM)))

def decoder_layer(params, clip_frames, clip_text, mask_row, length):
    gain_attend, bias_attend, query_matrix, key_matrix, value_matrix, output_matrix, gain_cross, bias_cross, probe_matrix, lookup_matrix, content_matrix, merge_matrix, gain_feed, bias_feed, expand_matrix, reduce_matrix = params
    positions = jnp.arange(CLIP, dtype=jnp.int32)
    causal = (positions[None, :] <= positions[:, None]) & (positions[None, :] < length)
    hidden_one = low(layer_norm(clip_frames, gain_attend, bias_attend))
    queries = low_back(low(product(hidden_one, query_matrix)))
    keys = low_back(low(product(hidden_one, key_matrix)))
    values = low_back(low(product(hidden_one, value_matrix)))
    mixed_self = attend(queries, keys, values, causal)
    after_self = clip_frames + low_back(product(mixed_self, output_matrix))
    hidden_two = low(layer_norm(after_self, gain_cross, bias_cross))
    probes = low_back(low(product(hidden_two, probe_matrix)))
    lookups = low_back(low(product(clip_text, lookup_matrix)))
    contents = low_back(low(product(clip_text, content_matrix)))
    text_allowed = mask_row[None, :] > 0
    mixed_cross = attend(probes, lookups, contents, text_allowed)
    after_cross = after_self + low_back(product(mixed_cross, merge_matrix))
    hidden_three = low(layer_norm(after_cross, gain_feed, bias_feed))
    upward = low_back(product(hidden_three, expand_matrix))
    activated = low(jax.nn.gelu(upward, approximate=False))
    return after_cross + low_back(product(activated, reduce_matrix))

def reference(frames, text_states, text_mask, clip_lengths, slot_used, teacher, self_norm_gain, self_norm_bias, self_query_weight, self_key_weight, self_value_weight, self_output_weight, cross_norm_gain, cross_norm_bias, cross_query_weight, cross_key_weight, cross_value_weight, cross_output_weight, feed_norm_gain, feed_norm_bias, feed_up_weight, feed_down_weight):
    params = tuple((item.astype(jnp.float32) for item in (self_norm_gain, self_norm_bias, self_query_weight, self_key_weight, self_value_weight, self_output_weight, cross_norm_gain, cross_norm_bias, cross_query_weight, cross_key_weight, cross_value_weight, cross_output_weight, feed_norm_gain, feed_norm_bias, feed_up_weight, feed_down_weight)))
    frames_wide = frames.astype(jnp.float32)
    texts_wide = text_states.astype(jnp.float32)
    targets = teacher.astype(jnp.float32)
    positions = jnp.arange(CLIP, dtype=jnp.int32)
    valid = ((positions[None, :] < clip_lengths[:, None]) & (slot_used[:, None] > 0)).astype(jnp.float32)
    count = jnp.sum(valid)

    def objective(weights, clip_frames, clip_texts):

        def one_clip(operands):
            frames_one, text_one, mask_one, length_one, valid_one, target_one = operands
            result = decoder_layer(weights, frames_one, text_one, mask_one, length_one)
            errors = (result - target_one) * valid_one[:, None]
            return (result, jnp.sum(errors * errors))
        results, squares = lax.map(jax.checkpoint(one_clip), (clip_frames, clip_texts, text_mask, clip_lengths, valid, targets))
        total = jnp.sum(squares)
        return (GRAD_SCALE * total / (D * count), (results, total))
    scaled, pull, aux = jax.vjp(objective, params, frames_wide, texts_wide, has_aux=True)
    results, total = aux
    param_grads, frames_grad, text_grad = pull(jnp.ones_like(scaled))
    loss = total / (D * count)
    return (results.astype(jnp.bfloat16), loss, frames_grad, text_grad, param_grads[0], param_grads[1], param_grads[2], param_grads[3], param_grads[4], param_grads[5], param_grads[6], param_grads[7], param_grads[8], param_grads[9], param_grads[10], param_grads[11], param_grads[12], param_grads[13], param_grads[14], param_grads[15])
```

```python
import jax
import jax.numpy as jnp
from jax import lax
from jax.experimental import pallas as pl
from jax.experimental.pallas import tpu as pltpu
from jax.sharding import Mesh
from jax.sharding import PartitionSpec as P

HEADS = 24
HEAD_DIM = 64


epsilon = 1e-05
masked_score = -1e30


def layer_norm(values, gain, shift):
    center = values - jnp.mean(values, axis=-1, keepdims=True)
    variance = jnp.mean(center * center, axis=-1, keepdims=True)
    return center * lax.rsqrt(variance + epsilon) * gain + shift


def exact_gelu(values):
    return jax.nn.gelu(values, approximate=False)


def project(left, right):
    return jnp.dot(left, right, preferred_element_type=jnp.float32)


def outer_sum(left, right):
    return jnp.einsum("rd,re->de", left, right, preferred_element_type=jnp.float32)


def back_project(grads, matrix):
    return jnp.einsum("re,de->rd", grads, matrix, preferred_element_type=jnp.float32)


def split_heads(values):
    return values.reshape(values.shape[:-1] + (HEADS, HEAD_DIM))


def self_forward(operands):
    queries, keys_all, values_all, allowed = operands
    scale = HEAD_DIM ** (-0.5)
    scores = (
        jnp.einsum("qhd,khd->hqk", queries, keys_all, preferred_element_type=jnp.float32) * scale
    )
    scores = jnp.where(allowed[None], scores, masked_score)
    peak = jnp.max(scores, axis=-1, keepdims=True)
    weights = jnp.exp(scores - peak)
    totals = jnp.sum(weights, axis=-1, keepdims=True)
    probs = (weights / totals).astype(jnp.bfloat16)
    mixed = jnp.einsum("hqk,khd->qhd", probs, values_all, preferred_element_type=jnp.float32)
    return (mixed.astype(jnp.bfloat16), (peak + jnp.log(totals))[..., 0])


def self_backward(operands):
    queries, keys_all, values_all, allowed, log_totals, grad_mixed = operands
    scale = HEAD_DIM ** (-0.5)
    scores = (
        jnp.einsum("qhd,khd->hqk", queries, keys_all, preferred_element_type=jnp.float32) * scale
    )
    scores = jnp.where(allowed[None], scores, masked_score)
    probs = jnp.exp(scores - log_totals[..., None])
    grad_probs = jnp.einsum(
        "qhd,khd->hqk", grad_mixed, values_all, preferred_element_type=jnp.float32
    )
    grad_values = jnp.einsum(
        "hqk,qhd->khd", probs.astype(jnp.bfloat16), grad_mixed, preferred_element_type=jnp.float32
    )
    inner = jnp.sum(probs * grad_probs, axis=-1, keepdims=True)
    grad_scores = (probs * (grad_probs - inner)).astype(jnp.bfloat16)
    grad_queries = (
        jnp.einsum("hqk,khd->qhd", grad_scores, keys_all, preferred_element_type=jnp.float32)
        * scale
    ).astype(jnp.bfloat16)
    grad_keys = (
        jnp.einsum("hqk,qhd->khd", grad_scores, queries, preferred_element_type=jnp.float32) * scale
    )
    return (grad_queries, grad_keys, grad_values)


def general_body(
    frames,
    text_states,
    text_mask,
    clip_lengths,
    slot_used,
    teacher,
    self_norm_gain,
    self_norm_bias,
    self_query_weight,
    self_key_weight,
    self_value_weight,
    self_output_weight,
    cross_norm_gain,
    cross_norm_bias,
    cross_query_weight,
    cross_key_weight,
    cross_value_weight,
    cross_output_weight,
    feed_norm_gain,
    feed_norm_bias,
    feed_up_weight,
    feed_down_weight,
):
    gathered = (
        lax.all_gather(self_norm_gain, "shard", axis=0, tiled=True),
        lax.all_gather(self_norm_bias, "shard", axis=0, tiled=True),
        lax.all_gather(self_query_weight, "shard", axis=0, tiled=True),
        lax.all_gather(self_key_weight, "shard", axis=0, tiled=True),
        lax.all_gather(self_value_weight, "shard", axis=0, tiled=True),
        lax.all_gather(self_output_weight, "shard", axis=0, tiled=True),
        lax.all_gather(cross_norm_gain, "shard", axis=0, tiled=True),
        lax.all_gather(cross_norm_bias, "shard", axis=0, tiled=True),
        lax.all_gather(cross_query_weight, "shard", axis=0, tiled=True),
        lax.all_gather(cross_key_weight, "shard", axis=0, tiled=True),
        lax.all_gather(cross_value_weight, "shard", axis=0, tiled=True),
        lax.all_gather(cross_output_weight, "shard", axis=0, tiled=True),
        lax.all_gather(feed_norm_gain, "shard", axis=0, tiled=True),
        lax.all_gather(feed_norm_bias, "shard", axis=0, tiled=True),
        lax.all_gather(feed_up_weight, "shard", axis=0, tiled=True),
        lax.all_gather(feed_down_weight, "shard", axis=0, tiled=True),
    )
    (
        gain_attend,
        bias_attend,
        query_matrix,
        key_matrix,
        value_matrix,
        output_matrix,
        gain_cross,
        bias_cross,
        probe_matrix,
        lookup_matrix,
        content_matrix,
        merge_matrix,
        gain_feed,
        bias_feed,
        expand_matrix,
        reduce_matrix,
    ) = gathered
    slots = frames.shape[0]
    frame_count = frames.shape[1]
    width = frames.shape[2]
    text_len = text_states.shape[1]
    shards = lax.axis_size("shard")
    replicas = lax.axis_size("replica")
    clip_total = frame_count * shards
    row_count = slots * frame_count
    scale = HEAD_DIM ** (-0.5)
    shard_rank = lax.axis_index("shard")
    positions = shard_rank * frame_count + jnp.arange(frame_count, dtype=jnp.int32)
    key_positions = jnp.arange(clip_total, dtype=jnp.int32)
    allowed = (key_positions[None, None, :] <= positions[None, :, None]) & (
        key_positions[None, None, :] < clip_lengths[:, None, None]
    )
    valid_rows = ((positions[None, :] < clip_lengths[:, None]) & (slot_used[:, None] > 0)).astype(
        jnp.float32
    )
    text_allowed = text_mask > 0
    inputs = frames.astype(jnp.float32)
    normed_one, pull_one = jax.vjp(
        layer_norm, inputs, gain_attend.astype(jnp.float32), bias_attend.astype(jnp.float32)
    )
    hidden_one = normed_one.astype(jnp.bfloat16).reshape(row_count, width)
    queries = (
        project(hidden_one, query_matrix).astype(jnp.bfloat16).reshape(slots, frame_count, width)
    )
    keys_local = (
        project(hidden_one, key_matrix).astype(jnp.bfloat16).reshape(slots, frame_count, width)
    )
    values_local = (
        project(hidden_one, value_matrix).astype(jnp.bfloat16).reshape(slots, frame_count, width)
    )
    keys_all, values_all = (
        lax.all_gather(keys_local, "shard", axis=1, tiled=True),
        lax.all_gather(values_local, "shard", axis=1, tiled=True),
    )
    head_queries = split_heads(queries)
    head_keys = split_heads(keys_all)
    head_values = split_heads(values_all)
    mixed_self, log_totals = lax.map(self_forward, (head_queries, head_keys, head_values, allowed))
    mixed_rows = mixed_self.reshape(row_count, width)
    after_self = inputs + project(mixed_rows, output_matrix).reshape(slots, frame_count, width)
    normed_two, pull_two = jax.vjp(
        layer_norm, after_self, gain_cross.astype(jnp.float32), bias_cross.astype(jnp.float32)
    )
    hidden_two = normed_two.astype(jnp.bfloat16).reshape(row_count, width)
    probes = split_heads(
        project(hidden_two, probe_matrix).astype(jnp.bfloat16).reshape(slots, frame_count, width)
    )
    text_rows = text_states.reshape(slots * text_len, width)
    lookups = split_heads(
        project(text_rows, lookup_matrix).astype(jnp.bfloat16).reshape(slots, text_len, width)
    )
    contents = split_heads(
        project(text_rows, content_matrix).astype(jnp.bfloat16).reshape(slots, text_len, width)
    )
    cross_scores = (
        jnp.einsum("sqhd,skhd->shqk", probes, lookups, preferred_element_type=jnp.float32) * scale
    )
    cross_scores = jnp.where(text_allowed[:, None, None, :], cross_scores, masked_score)
    cross_peak = jnp.max(cross_scores, axis=-1, keepdims=True)
    cross_weights = jnp.exp(cross_scores - cross_peak)
    cross_probs = cross_weights / jnp.sum(cross_weights, axis=-1, keepdims=True)
    cross_probs_low = cross_probs.astype(jnp.bfloat16)
    cross_mixed = jnp.einsum(
        "shqk,skhd->sqhd", cross_probs_low, contents, preferred_element_type=jnp.float32
    )
    cross_mixed = cross_mixed.astype(jnp.bfloat16).reshape(row_count, width)
    after_cross = after_self + project(cross_mixed, merge_matrix).reshape(slots, frame_count, width)
    normed_three, pull_three = jax.vjp(
        layer_norm, after_cross, gain_feed.astype(jnp.float32), bias_feed.astype(jnp.float32)
    )
    hidden_three = normed_three.astype(jnp.bfloat16).reshape(row_count, width)
    upward = project(hidden_three, expand_matrix)
    activated, gelu_pull = jax.vjp(exact_gelu, upward)
    activated_low = activated.astype(jnp.bfloat16)
    result = after_cross + project(activated_low, reduce_matrix).reshape(slots, frame_count, width)
    output = result.astype(jnp.bfloat16)
    errors = (result - teacher.astype(jnp.float32)) * valid_rows[..., None]
    squares_total, count_total = lax.psum(
        (jnp.sum(errors * errors), jnp.sum(valid_rows)), ("replica", "shard")
    )
    loss = squares_total / (width * count_total)
    grad_result = errors * (slots * replicas * clip_total / count_total)
    grad_feed_low = grad_result.reshape(row_count, width).astype(jnp.bfloat16)
    grad_activated = back_project(grad_feed_low, reduce_matrix)
    grad_upward = gelu_pull(grad_activated)[0].astype(jnp.bfloat16)
    grad_hidden_three = back_project(grad_upward, expand_matrix).reshape(slots, frame_count, width)
    grad_cross_norm, gain_feed_part, bias_feed_part = pull_three(grad_hidden_three)
    grad_after_cross = grad_result + grad_cross_norm
    feed_owned = (
        lax.psum_scatter(
            outer_sum(hidden_three, grad_upward).astype(jnp.bfloat16),
            "shard",
            scatter_dimension=0,
            tiled=True,
        ).astype(jnp.float32),
        lax.psum_scatter(
            outer_sum(activated_low, grad_feed_low).astype(jnp.bfloat16),
            "shard",
            scatter_dimension=0,
            tiled=True,
        ).astype(jnp.float32),
        lax.psum_scatter(
            gain_feed_part.astype(jnp.bfloat16), "shard", scatter_dimension=0, tiled=True
        ).astype(jnp.float32),
        lax.psum_scatter(
            bias_feed_part.astype(jnp.bfloat16), "shard", scatter_dimension=0, tiled=True
        ).astype(jnp.float32),
    )
    grad_cross_low = grad_after_cross.reshape(row_count, width).astype(jnp.bfloat16)
    grad_cross_mixed = split_heads(
        back_project(grad_cross_low, merge_matrix)
        .astype(jnp.bfloat16)
        .reshape(slots, frame_count, width)
    )
    grad_cross_probs = jnp.einsum(
        "sqhd,skhd->shqk", grad_cross_mixed, contents, preferred_element_type=jnp.float32
    )
    content_grads = jnp.einsum(
        "shqk,sqhd->skhd", cross_probs_low, grad_cross_mixed, preferred_element_type=jnp.float32
    )
    cross_inner = jnp.sum(cross_probs * grad_cross_probs, axis=-1, keepdims=True)
    grad_cross_scores = (cross_probs * (grad_cross_probs - cross_inner)).astype(jnp.bfloat16)
    probe_grads = (
        jnp.einsum(
            "shqk,skhd->sqhd", grad_cross_scores, lookups, preferred_element_type=jnp.float32
        )
        * scale
    )
    probe_grads = probe_grads.astype(jnp.bfloat16).reshape(row_count, width)
    lookup_grads = (
        jnp.einsum("shqk,sqhd->skhd", grad_cross_scores, probes, preferred_element_type=jnp.float32)
        * scale
    )
    lookup_sum, content_sum = (
        lax.psum(lookup_grads.astype(jnp.bfloat16), "shard").astype(jnp.float32),
        lax.psum(content_grads.astype(jnp.bfloat16), "shard").astype(jnp.float32),
    )
    lookup_low = lookup_sum.astype(jnp.bfloat16).reshape(slots * text_len, width)
    content_low = content_sum.astype(jnp.bfloat16).reshape(slots * text_len, width)
    own_width = width // shards
    own_text = lax.dynamic_slice_in_dim(text_rows, shard_rank * own_width, own_width, 1)
    lookup_own = outer_sum(own_text, lookup_low)
    content_own = outer_sum(own_text, content_low)
    text_grad = (
        back_project(lookup_low, lookup_matrix) + back_project(content_low, content_matrix)
    ).reshape(slots, text_len, width)
    grad_hidden_two = back_project(probe_grads, probe_matrix).reshape(slots, frame_count, width)
    grad_self_norm, gain_cross_part, bias_cross_part = pull_two(grad_hidden_two)
    grad_after_self = grad_after_cross + grad_self_norm
    grad_self_low = grad_after_self.reshape(row_count, width).astype(jnp.bfloat16)
    grad_mixed = split_heads(
        back_project(grad_self_low, output_matrix)
        .astype(jnp.bfloat16)
        .reshape(slots, frame_count, width)
    )
    grad_queries, grad_keys, grad_values = lax.map(
        self_backward, (head_queries, head_keys, head_values, allowed, log_totals, grad_mixed)
    )
    key_sum, value_sum = (
        lax.psum_scatter(
            grad_keys.reshape(slots, clip_total, width).astype(jnp.bfloat16),
            "shard",
            scatter_dimension=1,
            tiled=True,
        ).astype(jnp.float32),
        lax.psum_scatter(
            grad_values.reshape(slots, clip_total, width).astype(jnp.bfloat16),
            "shard",
            scatter_dimension=1,
            tiled=True,
        ).astype(jnp.float32),
    )
    key_low = key_sum.astype(jnp.bfloat16).reshape(row_count, width)
    value_low = value_sum.astype(jnp.bfloat16).reshape(row_count, width)
    query_low = grad_queries.reshape(row_count, width)
    grad_hidden_one = (
        back_project(query_low, query_matrix)
        + back_project(key_low, key_matrix)
        + back_project(value_low, value_matrix)
    )
    grad_inputs, gain_attend_part, bias_attend_part = pull_one(
        grad_hidden_one.reshape(slots, frame_count, width)
    )
    frames_grad = grad_after_self + grad_inputs
    attend_owned = (
        lax.psum_scatter(
            outer_sum(hidden_one, query_low).astype(jnp.bfloat16),
            "shard",
            scatter_dimension=0,
            tiled=True,
        ).astype(jnp.float32),
        lax.psum_scatter(
            outer_sum(hidden_one, key_low).astype(jnp.bfloat16),
            "shard",
            scatter_dimension=0,
            tiled=True,
        ).astype(jnp.float32),
        lax.psum_scatter(
            outer_sum(hidden_one, value_low).astype(jnp.bfloat16),
            "shard",
            scatter_dimension=0,
            tiled=True,
        ).astype(jnp.float32),
        lax.psum_scatter(
            outer_sum(mixed_rows, grad_self_low).astype(jnp.bfloat16),
            "shard",
            scatter_dimension=0,
            tiled=True,
        ).astype(jnp.float32),
        lax.psum_scatter(
            outer_sum(hidden_two, probe_grads).astype(jnp.bfloat16),
            "shard",
            scatter_dimension=0,
            tiled=True,
        ).astype(jnp.float32),
        lax.psum_scatter(
            outer_sum(cross_mixed, grad_cross_low).astype(jnp.bfloat16),
            "shard",
            scatter_dimension=0,
            tiled=True,
        ).astype(jnp.float32),
        lax.psum_scatter(
            gain_attend_part.astype(jnp.bfloat16), "shard", scatter_dimension=0, tiled=True
        ).astype(jnp.float32),
        lax.psum_scatter(
            bias_attend_part.astype(jnp.bfloat16), "shard", scatter_dimension=0, tiled=True
        ).astype(jnp.float32),
        lax.psum_scatter(
            gain_cross_part.astype(jnp.bfloat16), "shard", scatter_dimension=0, tiled=True
        ).astype(jnp.float32),
        lax.psum_scatter(
            bias_cross_part.astype(jnp.bfloat16), "shard", scatter_dimension=0, tiled=True
        ).astype(jnp.float32),
    )
    summed = (
        lax.psum(attend_owned[6].astype(jnp.bfloat16), "replica").astype(jnp.float32),
        lax.psum(attend_owned[7].astype(jnp.bfloat16), "replica").astype(jnp.float32),
        lax.psum(attend_owned[0].astype(jnp.bfloat16), "replica").astype(jnp.float32),
        lax.psum(attend_owned[1].astype(jnp.bfloat16), "replica").astype(jnp.float32),
        lax.psum(attend_owned[2].astype(jnp.bfloat16), "replica").astype(jnp.float32),
        lax.psum(attend_owned[3].astype(jnp.bfloat16), "replica").astype(jnp.float32),
        lax.psum(attend_owned[8].astype(jnp.bfloat16), "replica").astype(jnp.float32),
        lax.psum(attend_owned[9].astype(jnp.bfloat16), "replica").astype(jnp.float32),
        lax.psum(attend_owned[4].astype(jnp.bfloat16), "replica").astype(jnp.float32),
        lax.psum(lookup_own.astype(jnp.bfloat16), "replica").astype(jnp.float32),
        lax.psum(content_own.astype(jnp.bfloat16), "replica").astype(jnp.float32),
        lax.psum(attend_owned[5].astype(jnp.bfloat16), "replica").astype(jnp.float32),
        lax.psum(feed_owned[2].astype(jnp.bfloat16), "replica").astype(jnp.float32),
        lax.psum(feed_owned[3].astype(jnp.bfloat16), "replica").astype(jnp.float32),
        lax.psum(feed_owned[0].astype(jnp.bfloat16), "replica").astype(jnp.float32),
        lax.psum(feed_owned[1].astype(jnp.bfloat16), "replica").astype(jnp.float32),
    )
    return (
        output,
        loss,
        frames_grad,
        text_grad,
        summed[0],
        summed[1],
        summed[2],
        summed[3],
        summed[4],
        summed[5],
        summed[6],
        summed[7],
        summed[8],
        summed[9],
        summed[10],
        summed[11],
        summed[12],
        summed[13],
        summed[14],
        summed[15],
    )


PAIR = 2 * HEAD_DIM
EVERY = ("shard", "y", "x", "core")
REPLICAS = ("core", "y", "x")
NT = (((1,), (1,)), ((), ()))
TN = (((0,), (0,)), ((), ()))
NN = (((1,), (0,)), ((), ()))


def dot(left, right, dims):
    return lax.dot_general(left, right, dims, preferred_element_type=jnp.float32)


def half_mask(side, value):
    lanes = lax.broadcasted_iota(jnp.int32, (1, PAIR), 1)
    inside = (lanes >= HEAD_DIM) if side else (lanes < HEAD_DIM)
    return jnp.where(inside, value, 0.0).astype(jnp.bfloat16)


def self_forward_kernel(place, q_ref, k_ref, v_ref, mixed_ref, lse_ref, acc_ref):
    block = q_ref.shape[0] // 2
    length = place[2]
    low = lax.broadcasted_iota(jnp.int32, (PAIR, 1), 0) < HEAD_DIM
    for part in range(2):
        first = place[part] * block
        rows = slice(part * block, (part + 1) * block)
        q = q_ref[rows, :]
        q_half = [q * half_mask(side, HEAD_DIM ** (-0.5)) for side in range(2)]
        limit = jnp.minimum(
            first + lax.broadcasted_iota(jnp.int32, (1, block), 1) + 1, length
        )
        acc_ref[...] = jnp.zeros_like(acc_ref)

        def step(j, peaks, q_half=q_half, limit=limit):
            at = pl.multiple_of(j * block, block)
            k = k_ref[pl.ds(at, block), :]
            v = v_ref[pl.ds(at, block), :]
            allowed = at + lax.broadcasted_iota(jnp.int32, (block, block), 0) < limit
            out = []
            for side in range(2):
                scores = jnp.where(allowed, dot(k, q_half[side], NT), masked_score)
                peak = jnp.maximum(peaks[side], jnp.max(scores, axis=0, keepdims=True))
                weights = jnp.exp(scores - peak).astype(jnp.bfloat16)
                v_ones = v * half_mask(side, 1.0) + half_mask(1 - side, 1.0)
                acc_ref[side] = acc_ref[side] * jnp.exp(peaks[side] - peak) + dot(
                    v_ones, weights, TN
                )
                out.append(peak)
            return tuple(out)

        peaks = lax.fori_loop(
            0, place[part] + 1, step, (jnp.full((1, block), masked_score, jnp.float32),) * 2
        )
        top, bottom = acc_ref[0], acc_ref[1]
        total = jnp.where(low, top[HEAD_DIM : HEAD_DIM + 1], bottom[0:1])
        mixed = jnp.where(low, top, bottom) / total
        mixed_ref[rows, :] = mixed.T.astype(jnp.bfloat16)
        lse_ref[0:1, rows] = peaks[0] + jnp.log(top[HEAD_DIM : HEAD_DIM + 1])
        lse_ref[1:2, rows] = peaks[1] + jnp.log(bottom[0:1])


def self_backward_kernel(
    place, q_ref, k_ref, v_ref, mixed_ref, grad_ref, lse_ref, dq_ref, dk_ref, dv_ref,
    dq_acc, dk_acc, dv_acc,
):
    block = q_ref.shape[0] // 2
    length = place[2]
    scale = HEAD_DIM ** (-0.5)
    dk_acc[...] = jnp.zeros_like(dk_acc)
    dv_acc[...] = jnp.zeros_like(dv_acc)
    for part in range(2):
        first = place[part] * block
        rows = slice(part * block, (part + 1) * block)
        q = q_ref[rows, :]
        grad = grad_ref[rows, :]
        q_half = [q * half_mask(side, scale) for side in range(2)]
        grad_half = [grad * half_mask(side, 1.0) for side in range(2)]
        product = (grad.astype(jnp.float32) * mixed_ref[rows, :].astype(jnp.float32)).T
        inner = [
            jnp.sum(product[side * HEAD_DIM : (side + 1) * HEAD_DIM], axis=0, keepdims=True)
            for side in range(2)
        ]
        lse = [lse_ref[side : side + 1, rows] for side in range(2)]
        limit = jnp.minimum(
            first + lax.broadcasted_iota(jnp.int32, (1, block), 1) + 1, length
        )
        dq_acc[...] = jnp.zeros_like(dq_acc)

        def step(
            j, carry, q_half=q_half, grad_half=grad_half, inner=inner, lse=lse, limit=limit
        ):
            at = pl.multiple_of(j * block, block)
            k = k_ref[pl.ds(at, block), :]
            v = v_ref[pl.ds(at, block), :]
            allowed = at + lax.broadcasted_iota(jnp.int32, (block, block), 0) < limit
            dq, dk, dv = 0.0, 0.0, 0.0
            for side in range(2):
                scores = jnp.where(allowed, dot(k, q_half[side], NT), masked_score)
                probs = jnp.exp(scores - lse[side])
                grad_probs = dot(v, grad_half[side], NT)
                grad_scores = (probs * (grad_probs - inner[side])).astype(jnp.bfloat16)
                dv += dot(probs.astype(jnp.bfloat16), grad_half[side], NN)
                dk += dot(grad_scores, q_half[side], NN)
                dq += dot(k * half_mask(side, scale), grad_scores, TN)
            dk_acc[pl.ds(at, block), :] += dk
            dv_acc[pl.ds(at, block), :] += dv
            dq_acc[...] += dq
            return carry

        lax.fori_loop(0, place[part] + 1, step, 0)
        dq_ref[rows, :] = dq_acc[...].T.astype(jnp.bfloat16)
    dk_ref[...] = dk_acc[...].astype(jnp.bfloat16)
    dv_ref[...] = dv_acc[...].astype(jnp.bfloat16)


def pair_block(rows):
    return pl.BlockSpec((rows, PAIR), lambda i, *_: (0, i))


def self_attend(place, queries, keys, values):
    rows, width = queries.shape
    clip = keys.shape[0]
    pairs = width // PAIR
    return pl.pallas_call(
        self_forward_kernel,
        out_shape=(
            jax.ShapeDtypeStruct((rows, width), jnp.bfloat16),
            jax.ShapeDtypeStruct((pairs * 8, rows), jnp.float32),
        ),
        grid_spec=pltpu.PrefetchScalarGridSpec(
            num_scalar_prefetch=1,
            grid=(pairs,),
            in_specs=[pair_block(rows), pair_block(clip), pair_block(clip)],
            out_specs=(pair_block(rows), pl.BlockSpec((8, rows), lambda i, *_: (i, 0))),
            scratch_shapes=[pltpu.VMEM((2, PAIR, rows // 2), jnp.float32)],
        ),
        compiler_params=pltpu.CompilerParams(vmem_limit_bytes=32 * 2**20),
        cost_estimate=pl.CostEstimate(
            flops=2 * 2 * rows * clip * width, bytes_accessed=8 * clip * width, transcendentals=0
        ),
        name="self_attend",
    )(place, queries, keys, values)


def self_attend_back(place, queries, keys, values, mixed, grads, lse):
    rows, width = queries.shape
    clip = keys.shape[0]
    pairs = width // PAIR
    return pl.pallas_call(
        self_backward_kernel,
        out_shape=(
            jax.ShapeDtypeStruct((rows, width), jnp.bfloat16),
            jax.ShapeDtypeStruct((clip, width), jnp.bfloat16),
            jax.ShapeDtypeStruct((clip, width), jnp.bfloat16),
        ),
        grid_spec=pltpu.PrefetchScalarGridSpec(
            num_scalar_prefetch=1,
            grid=(pairs,),
            in_specs=[
                pair_block(rows),
                pair_block(clip),
                pair_block(clip),
                pair_block(rows),
                pair_block(rows),
                pl.BlockSpec((8, rows), lambda i, *_: (i, 0)),
            ],
            out_specs=(pair_block(rows), pair_block(clip), pair_block(clip)),
            scratch_shapes=[
                pltpu.VMEM((PAIR, rows // 2), jnp.float32),
                pltpu.VMEM((clip, PAIR), jnp.float32),
                pltpu.VMEM((clip, PAIR), jnp.float32),
            ],
        ),
        compiler_params=pltpu.CompilerParams(vmem_limit_bytes=32 * 2**20),
        cost_estimate=pl.CostEstimate(
            flops=5 * 2 * rows * clip * width, bytes_accessed=16 * clip * width, transcendentals=0
        ),
        name="self_attend_back",
    )(place, queries, keys, values, mixed, grads, lse)


def both_heads(rows, value):
    return jnp.concatenate([rows * half_mask(side, value) for side in range(2)], axis=0)


def cross_probs_of(lookup_two, probes, present):
    text = present.shape[0]
    scores = dot(lookup_two, probes, NT)
    out = []
    for side in range(2):
        part = jnp.where(
            present > 0, scores[side * text : (side + 1) * text], masked_score
        )
        weights = jnp.exp(part - jnp.max(part, axis=0, keepdims=True))
        out.append(weights / jnp.sum(weights, axis=0, keepdims=True))
    return out


def cross_forward_kernel(probe_ref, lookup_ref, content_ref, present_ref, mixed_ref):
    probs = cross_probs_of(
        both_heads(lookup_ref[...], HEAD_DIM ** (-0.5)), probe_ref[...], present_ref[...]
    )
    probs = jnp.concatenate(probs, axis=0).astype(jnp.bfloat16)
    mixed_ref[...] = dot(probs, both_heads(content_ref[...], 1.0), TN).astype(jnp.bfloat16)


def cross_backward_kernel(
    probe_ref, lookup_ref, content_ref, present_ref, grad_ref, dp_ref, dl_ref, dc_ref
):
    text = present_ref.shape[0]
    scale = HEAD_DIM ** (-0.5)
    probes = probe_ref[...]
    grads = grad_ref[...]
    lookup_two = both_heads(lookup_ref[...], scale)
    probs = cross_probs_of(lookup_two, probes, present_ref[...])
    grad_probs = dot(both_heads(content_ref[...], 1.0), grads, NT)
    grad_scores = []
    for side in range(2):
        part = grad_probs[side * text : (side + 1) * text]
        inner = jnp.sum(probs[side] * part, axis=0, keepdims=True)
        grad_scores.append(probs[side] * (part - inner))
    grad_scores = jnp.concatenate(grad_scores, axis=0).astype(jnp.bfloat16)
    probs = jnp.concatenate(probs, axis=0).astype(jnp.bfloat16)
    low = lax.broadcasted_iota(jnp.int32, (1, PAIR), 1) < HEAD_DIM
    dp_ref[...] = dot(grad_scores, lookup_two, TN).astype(jnp.bfloat16)
    dl = dot(grad_scores, probes, NN) * scale
    dl_ref[...] = jnp.where(low, dl[:text], dl[text:]).astype(jnp.bfloat16)
    dc = dot(probs, grads, NN)
    dc_ref[...] = jnp.where(low, dc[:text], dc[text:]).astype(jnp.bfloat16)


def cross_attend(probes, lookups, contents, present):
    rows, width = probes.shape
    text = lookups.shape[0]
    return pl.pallas_call(
        cross_forward_kernel,
        out_shape=jax.ShapeDtypeStruct((rows, width), jnp.bfloat16),
        grid=(width // PAIR,),
        in_specs=[
            pair_block(rows),
            pair_block(text),
            pair_block(text),
            pl.BlockSpec((text, 1), lambda i: (0, 0)),
        ],
        out_specs=pair_block(rows),
        compiler_params=pltpu.CompilerParams(vmem_limit_bytes=32 * 2**20),
        cost_estimate=pl.CostEstimate(
            flops=8 * rows * text * width, bytes_accessed=4 * rows * width, transcendentals=0
        ),
        name="cross_attend",
    )(probes, lookups, contents, present)


def cross_attend_back(probes, lookups, contents, present, grads):
    rows, width = probes.shape
    text = lookups.shape[0]
    return pl.pallas_call(
        cross_backward_kernel,
        out_shape=(
            jax.ShapeDtypeStruct((rows, width), jnp.bfloat16),
            jax.ShapeDtypeStruct((text, width), jnp.bfloat16),
            jax.ShapeDtypeStruct((text, width), jnp.bfloat16),
        ),
        grid=(width // PAIR,),
        in_specs=[
            pair_block(rows),
            pair_block(text),
            pair_block(text),
            pl.BlockSpec((text, 1), lambda i: (0, 0)),
            pair_block(rows),
        ],
        out_specs=(pair_block(rows), pair_block(text), pair_block(text)),
        compiler_params=pltpu.CompilerParams(vmem_limit_bytes=32 * 2**20),
        cost_estimate=pl.CostEstimate(
            flops=20 * rows * text * width, bytes_accessed=6 * rows * width, transcendentals=0
        ),
        name="cross_attend_back",
    )(probes, lookups, contents, present, grads)


def unpack_kernel(in_ref, out_ref):
    pieces = in_ref[...]
    out_ref[...] = pieces.reshape(-1, pieces.shape[-1]).T.astype(jnp.float32)


def unpack(full, rows, place, out_shape, out_at, together):
    owners, _, features = full.shape
    tall = out_shape[0] // features
    wide = out_shape[1] // (together * rows)
    return pl.pallas_call(
        unpack_kernel,
        out_shape=jax.ShapeDtypeStruct(out_shape, jnp.float32),
        grid=(tall, wide),
        in_specs=[
            pl.BlockSpec((together, rows, features), lambda i, j: (j + out_at, place + i, 0))
        ],
        out_specs=pl.BlockSpec((features, together * rows), lambda i, j: (i, j)),
        compiler_params=pltpu.CompilerParams(vmem_limit_bytes=32 * 2**20),
        cost_estimate=pl.CostEstimate(
            flops=0, bytes_accessed=6 * out_shape[0] * out_shape[1], transcendentals=0
        ),
        name="unpack",
    )(full)


def after(value, *others):
    return lax.optimization_barrier((value, *others))[0]


def norm_parts(values):
    mean = jnp.mean(values, axis=-1, keepdims=True)
    center = values - mean
    return mean, lax.rsqrt(jnp.mean(center * center, axis=-1, keepdims=True) + epsilon)


def norm_back(grads, values, parts, gain):
    mean, inverse = parts
    unit = (values - mean) * inverse
    gain_grad = jnp.sum(grads * unit, axis=0)
    bias_grad = jnp.sum(grads, axis=0)
    scaled = grads * gain
    back = inverse * (
        scaled
        - jnp.mean(scaled, axis=-1, keepdims=True)
        - unit * jnp.mean(scaled * unit, axis=-1, keepdims=True)
    )
    return back, gain_grad, bias_grad


def clip_body(
    frames,
    text_states,
    text_mask,
    clip_lengths,
    slot_used,
    teacher,
    self_norm_gain,
    self_norm_bias,
    self_query_weight,
    self_key_weight,
    self_value_weight,
    self_output_weight,
    cross_norm_gain,
    cross_norm_bias,
    cross_query_weight,
    cross_key_weight,
    cross_value_weight,
    cross_output_weight,
    feed_norm_gain,
    feed_norm_bias,
    feed_up_weight,
    feed_down_weight,
):
    block, width = frames.shape[1:]
    text_len = text_states.shape[1]
    shards, replicas, outers = 4, 8, 4
    core = lax.axis_index("core")
    shard = lax.axis_index("shard")
    outer = 2 * lax.axis_index("y") + lax.axis_index("x")
    replica = 2 * outer + core
    clip = block * shards
    hidden_units = feed_up_weight.shape[1]

    holder = {0: 0, 1: 1, 2: 1, 3: 0}
    there = ([], [])
    for c in range(2):
        for s in range(4):
            for turn in range(2):
                slot = turn if s < 2 else 1 - turn
                there[turn].append((c * 4 + s, holder[s] * 4 + 2 * c + slot))
    back = tuple([(b, a) for a, b in pairs] for pairs in there)
    spot = ("core", "shard")
    swap = [(0, 1), (1, 0)]
    even = shard % 2 == 0
    lower = shard < 2
    first_core = core == 0

    def hop(values, distance):
        pairs = [(i, (i + distance) % shards) for i in range(shards)]
        return lax.ppermute(values, "shard", pairs)

    def to_chip(pair):
        one = lax.ppermute(jnp.where(lower, pair[0], pair[1]), spot, there[0])
        two = lax.ppermute(jnp.where(lower, pair[1], pair[0]), spot, there[1])
        return jnp.concatenate([jnp.where(even, one, two), jnp.where(even, two, one)], axis=0)

    def from_chip(values):
        early, late = values[:block], values[block:]
        one = lax.ppermute(jnp.where(even, early, late), spot, back[0])
        two = lax.ppermute(jnp.where(even, late, early), spot, back[1])
        return jnp.stack([jnp.where(lower, one, two), jnp.where(lower, two, one)])

    def share_of(weight):
        share = weight.shape[0] // replicas
        return lax.dynamic_slice_in_dim(weight, replica * share, share, 0)

    def whole(parts):
        return lax.all_gather(jnp.concatenate(parts, axis=1), EVERY, axis=0, tiled=True)

    share = block // replicas
    facts = jnp.concatenate(
        [(clip_lengths // 64)[:, None], (clip_lengths % 64)[:, None], slot_used[:, None], text_mask],
        axis=1,
    ).astype(jnp.bfloat16)
    rider = jnp.zeros((share, PAIR), jnp.bfloat16)
    for i, vector in enumerate(
        (
            self_norm_gain,
            self_norm_bias,
            cross_norm_gain,
            cross_norm_bias,
            feed_norm_gain,
            feed_norm_bias,
        )
    ):
        rider = rider.at[:, i].set(share_of(vector))
    rider = rider.at[:2, 8 : 8 + facts.shape[1]].set(facts)
    first = whole(
        [
            share_of(self_query_weight),
            share_of(self_key_weight),
            share_of(self_value_weight),
            rider,
        ]
    )
    x_low = to_chip(frames)
    teacher_low = to_chip(teacher)
    rest = whole(
        [share_of(self_output_weight), share_of(cross_query_weight), share_of(cross_output_weight)]
    )
    expand_matrix = whole([share_of(feed_up_weight)])

    quarter_rows = feed_down_weight.shape[0] // 4
    quarter = 2 * lax.axis_index("x") + core
    mine = lax.dynamic_slice_in_dim(feed_down_weight, quarter * quarter_rows, quarter_rows, 0)
    reduce_matrix = jnp.zeros((hidden_units, width), jnp.bfloat16)
    reduce_matrix = lax.dynamic_update_slice_in_dim(
        reduce_matrix, feed_down_weight, shard * 4 * quarter_rows, 0
    )
    for distance in (1, 2, 3):
        came = hop(mine, distance)
        across = lax.ppermute(came, "x", swap)
        owner = lax.rem(shard + shards - distance, shards)
        for values, which in (
            (came, quarter),
            (across, lax.rem(quarter + 2, 4)),
            (lax.ppermute(came, "core", swap), quarter + 1 - 2 * core),
            (lax.ppermute(across, "core", swap), lax.rem(quarter + 3 - 2 * core, 4)),
        ):
            reduce_matrix = lax.dynamic_update_slice_in_dim(
                reduce_matrix, values, (owner * 4 + which) * quarter_rows, 0
            )

    text_other = lax.ppermute(text_states, "core", swap)
    text_all = jnp.concatenate(
        [
            jnp.where(first_core, text_states, text_other),
            jnp.where(first_core, text_other, text_states),
        ],
        axis=0,
    ).reshape(4 * text_len, width)
    text_all = lax.dynamic_slice_in_dim(text_all, shard * block, block, 1)
    text_matrix = jnp.where(first_core, cross_key_weight, cross_value_weight)
    text_part = project(text_all, text_matrix).astype(jnp.bfloat16).reshape(4, text_len, width)
    text_half = lax.dynamic_index_in_dim(text_part, shard, 0, keepdims=False).astype(jnp.float32)
    for distance in (1, 2, 3):
        away = lax.dynamic_index_in_dim(
            text_part, lax.rem(shard + distance, shards), 0, keepdims=False
        )
        text_half += hop(away, distance).astype(jnp.float32)
    text_half = text_half.astype(jnp.bfloat16)
    text_swap = lax.ppermute(text_half, "core", swap)
    lookups = jnp.where(first_core, text_half, text_swap)
    contents = jnp.where(first_core, text_swap, text_half)

    qkv_matrix = first[:, : 3 * width]
    norms = first[:, 3 * width : 3 * width + 8].astype(jnp.float32).T
    facts = (
        first[: replicas * share, 3 * width + 8 : 3 * width + 11 + text_len]
        .reshape(replicas, share, 3 + text_len)[:, :2]
        .astype(jnp.int32)
        .reshape(2 * replicas, 3 + text_len)
    )
    lengths = facts[:, 0] * 64 + facts[:, 1]
    slot = outer * 4 + shard
    length = lengths[slot]
    used = facts[slot, 2]
    present = facts[slot, 3:].reshape(text_len, 1)
    count = jnp.sum(jnp.where(facts[:, 2] > 0, jnp.minimum(lengths, clip), 0)).astype(jnp.float32)
    places = jnp.stack([core, 3 - core, length]).astype(jnp.int32)
    positions = jnp.concatenate(
        [core * block + jnp.arange(block), (3 - core) * block + jnp.arange(block)]
    )
    valid_rows = ((positions < length) & (used > 0)).astype(jnp.float32)[:, None]
    output_matrix = rest[:, :width]
    probe_matrix = rest[:, width : 2 * width]
    merge_matrix = rest[:, 2 * width :]

    inputs = x_low.astype(jnp.float32)
    parts_one = norm_parts(inputs)
    hidden_one = ((inputs - parts_one[0]) * parts_one[1] * norms[0] + norms[1]).astype(
        jnp.bfloat16
    )
    kv = project(hidden_one, qkv_matrix[:, width:]).astype(jnp.bfloat16)
    kv_other = lax.ppermute(kv, "core", swap)
    queries = project(after(hidden_one, kv), qkv_matrix[:, :width]).astype(jnp.bfloat16)

    def in_order(mine, other):
        return jnp.concatenate(
            [
                jnp.where(first_core, mine[:block], other[:block]),
                jnp.where(first_core, other[:block], mine[:block]),
                jnp.where(first_core, other[block:], mine[block:]),
                jnp.where(first_core, mine[block:], other[block:]),
            ],
            axis=0,
        )

    keys = in_order(kv[:, :width], kv_other[:, :width])
    values = in_order(kv[:, width:], kv_other[:, width:])
    mixed_self, lse = self_attend(places, queries, keys, values)
    after_self = inputs + project(mixed_self, output_matrix)
    parts_two = norm_parts(after_self)
    hidden_two = ((after_self - parts_two[0]) * parts_two[1] * norms[2] + norms[3]).astype(
        jnp.bfloat16
    )
    probes = project(hidden_two, probe_matrix).astype(jnp.bfloat16)
    cross_mixed = cross_attend(probes, lookups, contents, present)
    after_cross = after_self + project(cross_mixed, merge_matrix)
    parts_three = norm_parts(after_cross)
    hidden_three = (
        (after_cross - parts_three[0]) * parts_three[1] * norms[4] + norms[5]
    ).astype(jnp.bfloat16)
    upward = project(hidden_three, expand_matrix)
    activated, gelu_pull = jax.vjp(exact_gelu, upward)
    activated_low = activated.astype(jnp.bfloat16)
    result = after_cross + project(activated_low, reduce_matrix)
    errors = (result - teacher_low.astype(jnp.float32)) * valid_rows
    squares = jnp.sum(errors * errors)
    grad_result = errors * (4 * outers * clip / count)
    grad_feed_low = grad_result.astype(jnp.bfloat16)

    def theirs_of(right, left):
        columns = right.shape[1] // 2
        part = lax.dynamic_slice_in_dim(right, (1 - core) * columns, columns, 1)
        return outer_sum(part, left).astype(jnp.bfloat16)

    def ours_of(right, left, theirs):
        columns = right.shape[1] // 2
        sent = lax.ppermute(theirs, "core", swap)
        part = lax.dynamic_slice_in_dim(right, core * columns, columns, 1)
        return (outer_sum(part, left) + sent.astype(jnp.float32)).astype(jnp.bfloat16)

    def over_outer(values):
        return lax.psum_scatter(values, ("y", "x"), scatter_dimension=0, tiled=True)

    def over_shard(values):
        columns = values.shape[1] // shards
        total = lax.dynamic_slice_in_dim(values, shard * columns, columns, 1).astype(jnp.float32)
        for distance in (1, 2, 3):
            away = lax.dynamic_slice_in_dim(
                values, lax.rem(shard + distance, shards) * columns, columns, 1
            )
            total += hop(away, distance).astype(jnp.float32)
        return total.astype(jnp.bfloat16)

    down_theirs = theirs_of(grad_feed_low, activated_low)
    grad_activated = back_project(after(grad_feed_low, down_theirs), reduce_matrix)
    grad_upward = gelu_pull(grad_activated)[0].astype(jnp.bfloat16)
    down_ours = ours_of(after(grad_feed_low, grad_upward), activated_low, down_theirs)
    down_sum = over_outer(down_ours)
    up_theirs = theirs_of(after(grad_upward, down_ours), hidden_three)
    grad_hidden_three = back_project(after(grad_upward, up_theirs), expand_matrix)
    up_ours = ours_of(after(grad_upward, grad_hidden_three), hidden_three, up_theirs)
    up_sum = over_outer(up_ours)
    output = from_chip(after(result.astype(jnp.bfloat16), up_ours))
    grad_norm, gain_feed, bias_feed = norm_back(
        after(grad_hidden_three, up_ours), after_cross, parts_three, norms[4]
    )
    grad_after_cross = grad_result + grad_norm
    grad_cross_low = grad_after_cross.astype(jnp.bfloat16)
    merge_theirs = theirs_of(grad_cross_low, cross_mixed)
    grad_cross_mixed = back_project(after(grad_cross_low, merge_theirs), merge_matrix).astype(
        jnp.bfloat16
    )
    probe_grads, lookup_grads, content_grads = cross_attend_back(
        probes, lookups, contents, present, grad_cross_mixed
    )
    text_mine = jnp.where(first_core, lookup_grads, content_grads)
    text_sent = lax.ppermute(
        jnp.where(first_core, content_grads, lookup_grads), "core", swap
    )
    text_mine = (text_mine.astype(jnp.float32) + text_sent.astype(jnp.float32)).astype(
        jnp.bfloat16
    )
    merge_ours = ours_of(after(grad_cross_low, probe_grads), cross_mixed, merge_theirs)
    probe_theirs = theirs_of(after(probe_grads, merge_ours), hidden_two)
    grad_hidden_two = back_project(after(probe_grads, probe_theirs), probe_matrix)
    text_four = jnp.zeros((4, text_len, width), jnp.bfloat16)
    text_four = lax.dynamic_update_index_in_dim(text_four, text_mine, shard, 0)
    for distance in (1, 2, 3):
        text_four = lax.dynamic_update_index_in_dim(
            text_four,
            hop(text_mine, distance),
            lax.rem(shard + shards - distance, shards),
            0,
        )
    text_four = text_four.reshape(4 * text_len, width)
    grad_norm, gain_cross, bias_cross = norm_back(
        grad_hidden_two, after_self, parts_two, norms[2]
    )
    grad_after_self = grad_after_cross + grad_norm
    grad_self_low = grad_after_self.astype(jnp.bfloat16)
    output_theirs = theirs_of(grad_self_low, mixed_self)
    grad_mixed = back_project(after(grad_self_low, output_theirs), output_matrix).astype(
        jnp.bfloat16
    )
    probe_ours = ours_of(after(probe_grads, grad_mixed), hidden_two, probe_theirs)
    text_weights = outer_sum(text_four, text_all).astype(jnp.bfloat16)
    text_back = back_project(text_four, text_matrix).astype(jnp.bfloat16)
    output_ours = ours_of(after(grad_self_low, probe_ours), mixed_self, output_theirs)
    text_rows = width // outers
    middle = jnp.concatenate(
        [
            values.reshape(outers, -1, width)
            for values in (
                output_ours,
                probe_ours,
                merge_ours,
                text_weights.reshape(outers, shards, text_rows // shards, block)
                .transpose(0, 2, 1, 3)
                .reshape(outers, text_rows // shards, width),
            )
        ],
        axis=1,
    )
    middle_rows = middle.shape[1]
    middle = middle.reshape(outers * middle_rows, width)
    middle_sum = over_outer(middle)
    text_split = text_rows // shards
    text_piece = (
        middle_sum[middle_rows - text_split :]
        .reshape(text_split, shards, block)
        .transpose(1, 0, 2)
        .reshape(text_rows, block)
    )
    grad_queries, grad_keys, grad_values = self_attend_back(
        places, queries, keys, values, mixed_self, after(grad_mixed, middle), lse
    )

    text_back = text_back.reshape(2, 2, text_len, block)
    text_kept = lax.dynamic_index_in_dim(text_back, core, 0, keepdims=False)
    text_gone = lax.dynamic_index_in_dim(text_back, 1 - core, 0, keepdims=False)
    text_own = text_kept.astype(jnp.float32) + lax.ppermute(text_gone, "core", swap).astype(
        jnp.float32
    )
    text_own = text_own.astype(jnp.bfloat16)
    text_grad = jnp.zeros(text_states.shape, jnp.float32)
    text_grad = lax.dynamic_update_slice_in_dim(
        text_grad, text_own.astype(jnp.float32), shard * block, 2
    )
    for distance in (1, 2, 3):
        text_grad = lax.dynamic_update_slice_in_dim(
            text_grad,
            hop(text_own, distance).astype(jnp.float32),
            lax.rem(shard + shards - distance, shards) * block,
            2,
        )

    def gather_sum(grads):
        quarters = [grads[i * block : (i + 1) * block] for i in range(4)]
        outside = jnp.concatenate([quarters[0], quarters[3]], axis=0)
        inside = jnp.concatenate([quarters[1], quarters[2]], axis=0)
        mine = jnp.where(first_core, outside, inside)
        other = lax.ppermute(jnp.where(first_core, inside, outside), "core", swap)
        return (mine.astype(jnp.float32) + other.astype(jnp.float32)).astype(jnp.bfloat16)

    qkv_grads = jnp.concatenate(
        [grad_queries, gather_sum(grad_keys), gather_sum(grad_values)], axis=1
    )
    qkv_theirs = theirs_of(qkv_grads, hidden_one)
    grad_hidden_one = back_project(after(qkv_grads, qkv_theirs), qkv_matrix)
    qkv_ours = ours_of(after(qkv_grads, grad_hidden_one), hidden_one, qkv_theirs)
    qkv_sum = over_outer(qkv_ours)
    grad_norm, gain_self, bias_self = norm_back(
        after(grad_hidden_one, qkv_ours), inputs, parts_one, norms[0]
    )
    frames_grad = from_chip((grad_after_self + grad_norm).astype(jnp.bfloat16)).astype(
        jnp.float32
    )

    small = jnp.stack(
        [
            gain_self,
            bias_self,
            gain_cross,
            bias_cross,
            gain_feed,
            bias_feed,
            jnp.full((width,), squares),
            jnp.zeros((width,), jnp.float32),
        ]
    )
    for axis, pairs in (
        ("core", swap),
        ("x", swap),
        ("y", swap),
        ("shard", [(0, 1), (1, 0), (2, 3), (3, 2)]),
        ("shard", [(0, 2), (2, 0), (1, 3), (3, 1)]),
    ):
        small += lax.ppermute(small, axis, pairs)
    loss = small[6, 0] / (width * count)
    small_own = lax.dynamic_slice_in_dim(small, shard * block, block, 1)

    down_piece = over_shard(down_sum)
    middle_piece = over_shard(middle_sum[: middle_rows - text_split])
    early = jnp.concatenate(
        [over_shard(up_sum)]
        + [down_piece[:, i * block : (i + 1) * block] for i in range(4)]
        + [text_piece, middle_piece],
        axis=0,
    )
    early = lax.all_gather(early, REPLICAS, axis=0)
    piece = width // replicas
    square = (block, width)
    up_grad = unpack(early, hidden_units // replicas, 0, (block, hidden_units), 0, 1)
    at = hidden_units // replicas // piece
    down_grad = unpack(early, piece, at, (4 * block, width), 0, 2)
    at += 4
    key_grad = unpack(early, text_rows, at * piece // text_rows, square, 0, 1)
    value_grad = unpack(early, text_rows, at * piece // text_rows, square, 4, 1)
    at += text_rows // piece
    output_grad = unpack(early, piece, at, square, 0, 2)
    probe_grad = unpack(early, piece, at + 1, square, 0, 2)
    merge_grad = unpack(early, piece, at + 2, square, 0, 2)
    late = lax.all_gather(over_shard(qkv_sum), REPLICAS, axis=0, tiled=True)
    late = late.reshape(3, width, block)
    qkv_grad = [late[i].T.astype(jnp.float32) for i in range(3)]
    return (
        output,
        loss,
        frames_grad,
        text_grad,
        small_own[0],
        small_own[1],
        qkv_grad[0],
        qkv_grad[1],
        qkv_grad[2],
        output_grad,
        small_own[2],
        small_own[3],
        probe_grad,
        key_grad,
        value_grad,
        merge_grad,
        small_own[4],
        small_own[5],
        up_grad,
        down_grad,
    )


def solution(mesh):
    by_chip = mesh.shape["shard"] == 4 and mesh.shape["replica"] == 8
    replica = ("y", "x", "core") if by_chip else "replica"
    row = P(replica)
    clip = P(replica, "shard", None)
    text = P(replica, None, None)
    vector = P("shard")
    matrix = P("shard", None)
    weights = (
        [vector, vector] + [matrix] * 4 + [vector, vector] + [matrix] * 4 + [vector, vector]
        + [matrix] * 2
    )
    if by_chip:
        mesh = Mesh(mesh.devices.reshape(2, 2, 2, 4), ("y", "x", "core", "shard"))
    return jax.shard_map(
        clip_body if by_chip else general_body,
        mesh=mesh,
        in_specs=(clip, text, P(replica, None), row, row, clip, *weights),
        out_specs=(clip, P(), clip, text, *weights),
        check_vma=False,
    )
```

```python
import jax
import jax.numpy as jnp
from jax import lax
from jax.experimental import pallas as pl
from jax.experimental.pallas import tpu as pltpu
from jax.sharding import Mesh
from jax.sharding import PartitionSpec as P

HEADS = 24
HEAD_DIM = 64


epsilon = 1e-05
masked_score = -1e30


def layer_norm(values, gain, shift):
    center = values - jnp.mean(values, axis=-1, keepdims=True)
    variance = jnp.mean(center * center, axis=-1, keepdims=True)
    return center * lax.rsqrt(variance + epsilon) * gain + shift


def exact_gelu(values):
    return jax.nn.gelu(values, approximate=False)


def project(left, right):
    return jnp.dot(left, right, preferred_element_type=jnp.float32)


def outer_sum(left, right):
    return jnp.einsum("rd,re->de", left, right, preferred_element_type=jnp.float32)


def back_project(grads, matrix):
    return jnp.einsum("re,de->rd", grads, matrix, preferred_element_type=jnp.float32)


def split_heads(values):
    return values.reshape(values.shape[:-1] + (HEADS, HEAD_DIM))


def self_forward(operands):
    queries, keys_all, values_all, allowed = operands
    scale = HEAD_DIM ** (-0.5)
    scores = (
        jnp.einsum("qhd,khd->hqk", queries, keys_all, preferred_element_type=jnp.float32) * scale
    )
    scores = jnp.where(allowed[None], scores, masked_score)
    peak = jnp.max(scores, axis=-1, keepdims=True)
    weights = jnp.exp(scores - peak)
    totals = jnp.sum(weights, axis=-1, keepdims=True)
    probs = (weights / totals).astype(jnp.bfloat16)
    mixed = jnp.einsum("hqk,khd->qhd", probs, values_all, preferred_element_type=jnp.float32)
    return (mixed.astype(jnp.bfloat16), (peak + jnp.log(totals))[..., 0])


def self_backward(operands):
    queries, keys_all, values_all, allowed, log_totals, grad_mixed = operands
    scale = HEAD_DIM ** (-0.5)
    scores = (
        jnp.einsum("qhd,khd->hqk", queries, keys_all, preferred_element_type=jnp.float32) * scale
    )
    scores = jnp.where(allowed[None], scores, masked_score)
    probs = jnp.exp(scores - log_totals[..., None])
    grad_probs = jnp.einsum(
        "qhd,khd->hqk", grad_mixed, values_all, preferred_element_type=jnp.float32
    )
    grad_values = jnp.einsum(
        "hqk,qhd->khd", probs.astype(jnp.bfloat16), grad_mixed, preferred_element_type=jnp.float32
    )
    inner = jnp.sum(probs * grad_probs, axis=-1, keepdims=True)
    grad_scores = (probs * (grad_probs - inner)).astype(jnp.bfloat16)
    grad_queries = (
        jnp.einsum("hqk,khd->qhd", grad_scores, keys_all, preferred_element_type=jnp.float32)
        * scale
    ).astype(jnp.bfloat16)
    grad_keys = (
        jnp.einsum("hqk,qhd->khd", grad_scores, queries, preferred_element_type=jnp.float32) * scale
    )
    return (grad_queries, grad_keys, grad_values)


def general_body(
    frames,
    text_states,
    text_mask,
    clip_lengths,
    slot_used,
    teacher,
    self_norm_gain,
    self_norm_bias,
    self_query_weight,
    self_key_weight,
    self_value_weight,
    self_output_weight,
    cross_norm_gain,
    cross_norm_bias,
    cross_query_weight,
    cross_key_weight,
    cross_value_weight,
    cross_output_weight,
    feed_norm_gain,
    feed_norm_bias,
    feed_up_weight,
    feed_down_weight,
):
    gathered = (
        lax.all_gather(self_norm_gain, "shard", axis=0, tiled=True),
        lax.all_gather(self_norm_bias, "shard", axis=0, tiled=True),
        lax.all_gather(self_query_weight, "shard", axis=0, tiled=True),
        lax.all_gather(self_key_weight, "shard", axis=0, tiled=True),
        lax.all_gather(self_value_weight, "shard", axis=0, tiled=True),
        lax.all_gather(self_output_weight, "shard", axis=0, tiled=True),
        lax.all_gather(cross_norm_gain, "shard", axis=0, tiled=True),
        lax.all_gather(cross_norm_bias, "shard", axis=0, tiled=True),
        lax.all_gather(cross_query_weight, "shard", axis=0, tiled=True),
        lax.all_gather(cross_key_weight, "shard", axis=0, tiled=True),
        lax.all_gather(cross_value_weight, "shard", axis=0, tiled=True),
        lax.all_gather(cross_output_weight, "shard", axis=0, tiled=True),
        lax.all_gather(feed_norm_gain, "shard", axis=0, tiled=True),
        lax.all_gather(feed_norm_bias, "shard", axis=0, tiled=True),
        lax.all_gather(feed_up_weight, "shard", axis=0, tiled=True),
        lax.all_gather(feed_down_weight, "shard", axis=0, tiled=True),
    )
    (
        gain_attend,
        bias_attend,
        query_matrix,
        key_matrix,
        value_matrix,
        output_matrix,
        gain_cross,
        bias_cross,
        probe_matrix,
        lookup_matrix,
        content_matrix,
        merge_matrix,
        gain_feed,
        bias_feed,
        expand_matrix,
        reduce_matrix,
    ) = gathered
    slots = frames.shape[0]
    frame_count = frames.shape[1]
    width = frames.shape[2]
    text_len = text_states.shape[1]
    shards = lax.axis_size("shard")
    replicas = lax.axis_size("replica")
    clip_total = frame_count * shards
    row_count = slots * frame_count
    scale = HEAD_DIM ** (-0.5)
    shard_rank = lax.axis_index("shard")
    positions = shard_rank * frame_count + jnp.arange(frame_count, dtype=jnp.int32)
    key_positions = jnp.arange(clip_total, dtype=jnp.int32)
    allowed = (key_positions[None, None, :] <= positions[None, :, None]) & (
        key_positions[None, None, :] < clip_lengths[:, None, None]
    )
    valid_rows = ((positions[None, :] < clip_lengths[:, None]) & (slot_used[:, None] > 0)).astype(
        jnp.float32
    )
    text_allowed = text_mask > 0
    inputs = frames.astype(jnp.float32)
    normed_one, pull_one = jax.vjp(
        layer_norm, inputs, gain_attend.astype(jnp.float32), bias_attend.astype(jnp.float32)
    )
    hidden_one = normed_one.astype(jnp.bfloat16).reshape(row_count, width)
    queries = (
        project(hidden_one, query_matrix).astype(jnp.bfloat16).reshape(slots, frame_count, width)
    )
    keys_local = (
        project(hidden_one, key_matrix).astype(jnp.bfloat16).reshape(slots, frame_count, width)
    )
    values_local = (
        project(hidden_one, value_matrix).astype(jnp.bfloat16).reshape(slots, frame_count, width)
    )
    keys_all, values_all = (
        lax.all_gather(keys_local, "shard", axis=1, tiled=True),
        lax.all_gather(values_local, "shard", axis=1, tiled=True),
    )
    head_queries = split_heads(queries)
    head_keys = split_heads(keys_all)
    head_values = split_heads(values_all)
    mixed_self, log_totals = lax.map(self_forward, (head_queries, head_keys, head_values, allowed))
    mixed_rows = mixed_self.reshape(row_count, width)
    after_self = inputs + project(mixed_rows, output_matrix).reshape(slots, frame_count, width)
    normed_two, pull_two = jax.vjp(
        layer_norm, after_self, gain_cross.astype(jnp.float32), bias_cross.astype(jnp.float32)
    )
    hidden_two = normed_two.astype(jnp.bfloat16).reshape(row_count, width)
    probes = split_heads(
        project(hidden_two, probe_matrix).astype(jnp.bfloat16).reshape(slots, frame_count, width)
    )
    text_rows = text_states.reshape(slots * text_len, width)
    lookups = split_heads(
        project(text_rows, lookup_matrix).astype(jnp.bfloat16).reshape(slots, text_len, width)
    )
    contents = split_heads(
        project(text_rows, content_matrix).astype(jnp.bfloat16).reshape(slots, text_len, width)
    )
    cross_scores = (
        jnp.einsum("sqhd,skhd->shqk", probes, lookups, preferred_element_type=jnp.float32) * scale
    )
    cross_scores = jnp.where(text_allowed[:, None, None, :], cross_scores, masked_score)
    cross_peak = jnp.max(cross_scores, axis=-1, keepdims=True)
    cross_weights = jnp.exp(cross_scores - cross_peak)
    cross_probs = cross_weights / jnp.sum(cross_weights, axis=-1, keepdims=True)
    cross_probs_low = cross_probs.astype(jnp.bfloat16)
    cross_mixed = jnp.einsum(
        "shqk,skhd->sqhd", cross_probs_low, contents, preferred_element_type=jnp.float32
    )
    cross_mixed = cross_mixed.astype(jnp.bfloat16).reshape(row_count, width)
    after_cross = after_self + project(cross_mixed, merge_matrix).reshape(slots, frame_count, width)
    normed_three, pull_three = jax.vjp(
        layer_norm, after_cross, gain_feed.astype(jnp.float32), bias_feed.astype(jnp.float32)
    )
    hidden_three = normed_three.astype(jnp.bfloat16).reshape(row_count, width)
    upward = project(hidden_three, expand_matrix)
    activated, gelu_pull = jax.vjp(exact_gelu, upward)
    activated_low = activated.astype(jnp.bfloat16)
    result = after_cross + project(activated_low, reduce_matrix).reshape(slots, frame_count, width)
    output = result.astype(jnp.bfloat16)
    errors = (result - teacher.astype(jnp.float32)) * valid_rows[..., None]
    squares_total, count_total = lax.psum(
        (jnp.sum(errors * errors), jnp.sum(valid_rows)), ("replica", "shard")
    )
    loss = squares_total / (width * count_total)
    grad_result = errors * (slots * replicas * clip_total / count_total)
    grad_feed_low = grad_result.reshape(row_count, width).astype(jnp.bfloat16)
    grad_activated = back_project(grad_feed_low, reduce_matrix)
    grad_upward = gelu_pull(grad_activated)[0].astype(jnp.bfloat16)
    grad_hidden_three = back_project(grad_upward, expand_matrix).reshape(slots, frame_count, width)
    grad_cross_norm, gain_feed_part, bias_feed_part = pull_three(grad_hidden_three)
    grad_after_cross = grad_result + grad_cross_norm
    feed_owned = (
        lax.psum_scatter(
            outer_sum(hidden_three, grad_upward).astype(jnp.bfloat16),
            "shard",
            scatter_dimension=0,
            tiled=True,
        ).astype(jnp.float32),
        lax.psum_scatter(
            outer_sum(activated_low, grad_feed_low).astype(jnp.bfloat16),
            "shard",
            scatter_dimension=0,
            tiled=True,
        ).astype(jnp.float32),
        lax.psum_scatter(
            gain_feed_part.astype(jnp.bfloat16), "shard", scatter_dimension=0, tiled=True
        ).astype(jnp.float32),
        lax.psum_scatter(
            bias_feed_part.astype(jnp.bfloat16), "shard", scatter_dimension=0, tiled=True
        ).astype(jnp.float32),
    )
    grad_cross_low = grad_after_cross.reshape(row_count, width).astype(jnp.bfloat16)
    grad_cross_mixed = split_heads(
        back_project(grad_cross_low, merge_matrix)
        .astype(jnp.bfloat16)
        .reshape(slots, frame_count, width)
    )
    grad_cross_probs = jnp.einsum(
        "sqhd,skhd->shqk", grad_cross_mixed, contents, preferred_element_type=jnp.float32
    )
    content_grads = jnp.einsum(
        "shqk,sqhd->skhd", cross_probs_low, grad_cross_mixed, preferred_element_type=jnp.float32
    )
    cross_inner = jnp.sum(cross_probs * grad_cross_probs, axis=-1, keepdims=True)
    grad_cross_scores = (cross_probs * (grad_cross_probs - cross_inner)).astype(jnp.bfloat16)
    probe_grads = (
        jnp.einsum(
            "shqk,skhd->sqhd", grad_cross_scores, lookups, preferred_element_type=jnp.float32
        )
        * scale
    )
    probe_grads = probe_grads.astype(jnp.bfloat16).reshape(row_count, width)
    lookup_grads = (
        jnp.einsum("shqk,sqhd->skhd", grad_cross_scores, probes, preferred_element_type=jnp.float32)
        * scale
    )
    lookup_sum, content_sum = (
        lax.psum(lookup_grads.astype(jnp.bfloat16), "shard").astype(jnp.float32),
        lax.psum(content_grads.astype(jnp.bfloat16), "shard").astype(jnp.float32),
    )
    lookup_low = lookup_sum.astype(jnp.bfloat16).reshape(slots * text_len, width)
    content_low = content_sum.astype(jnp.bfloat16).reshape(slots * text_len, width)
    own_width = width // shards
    own_text = lax.dynamic_slice_in_dim(text_rows, shard_rank * own_width, own_width, 1)
    lookup_own = outer_sum(own_text, lookup_low)
    content_own = outer_sum(own_text, content_low)
    text_grad = (
        back_project(lookup_low, lookup_matrix) + back_project(content_low, content_matrix)
    ).reshape(slots, text_len, width)
    grad_hidden_two = back_project(probe_grads, probe_matrix).reshape(slots, frame_count, width)
    grad_self_norm, gain_cross_part, bias_cross_part = pull_two(grad_hidden_two)
    grad_after_self = grad_after_cross + grad_self_norm
    grad_self_low = grad_after_self.reshape(row_count, width).astype(jnp.bfloat16)
    grad_mixed = split_heads(
        back_project(grad_self_low, output_matrix)
        .astype(jnp.bfloat16)
        .reshape(slots, frame_count, width)
    )
    grad_queries, grad_keys, grad_values = lax.map(
        self_backward, (head_queries, head_keys, head_values, allowed, log_totals, grad_mixed)
    )
    key_sum, value_sum = (
        lax.psum_scatter(
            grad_keys.reshape(slots, clip_total, width).astype(jnp.bfloat16),
            "shard",
            scatter_dimension=1,
            tiled=True,
        ).astype(jnp.float32),
        lax.psum_scatter(
            grad_values.reshape(slots, clip_total, width).astype(jnp.bfloat16),
            "shard",
            scatter_dimension=1,
            tiled=True,
        ).astype(jnp.float32),
    )
    key_low = key_sum.astype(jnp.bfloat16).reshape(row_count, width)
    value_low = value_sum.astype(jnp.bfloat16).reshape(row_count, width)
    query_low = grad_queries.reshape(row_count, width)
    grad_hidden_one = (
        back_project(query_low, query_matrix)
        + back_project(key_low, key_matrix)
        + back_project(value_low, value_matrix)
    )
    grad_inputs, gain_attend_part, bias_attend_part = pull_one(
        grad_hidden_one.reshape(slots, frame_count, width)
    )
    frames_grad = grad_after_self + grad_inputs
    attend_owned = (
        lax.psum_scatter(
            outer_sum(hidden_one, query_low).astype(jnp.bfloat16),
            "shard",
            scatter_dimension=0,
            tiled=True,
        ).astype(jnp.float32),
        lax.psum_scatter(
            outer_sum(hidden_one, key_low).astype(jnp.bfloat16),
            "shard",
            scatter_dimension=0,
            tiled=True,
        ).astype(jnp.float32),
        lax.psum_scatter(
            outer_sum(hidden_one, value_low).astype(jnp.bfloat16),
            "shard",
            scatter_dimension=0,
            tiled=True,
        ).astype(jnp.float32),
        lax.psum_scatter(
            outer_sum(mixed_rows, grad_self_low).astype(jnp.bfloat16),
            "shard",
            scatter_dimension=0,
            tiled=True,
        ).astype(jnp.float32),
        lax.psum_scatter(
            outer_sum(hidden_two, probe_grads).astype(jnp.bfloat16),
            "shard",
            scatter_dimension=0,
            tiled=True,
        ).astype(jnp.float32),
        lax.psum_scatter(
            outer_sum(cross_mixed, grad_cross_low).astype(jnp.bfloat16),
            "shard",
            scatter_dimension=0,
            tiled=True,
        ).astype(jnp.float32),
        lax.psum_scatter(
            gain_attend_part.astype(jnp.bfloat16), "shard", scatter_dimension=0, tiled=True
        ).astype(jnp.float32),
        lax.psum_scatter(
            bias_attend_part.astype(jnp.bfloat16), "shard", scatter_dimension=0, tiled=True
        ).astype(jnp.float32),
        lax.psum_scatter(
            gain_cross_part.astype(jnp.bfloat16), "shard", scatter_dimension=0, tiled=True
        ).astype(jnp.float32),
        lax.psum_scatter(
            bias_cross_part.astype(jnp.bfloat16), "shard", scatter_dimension=0, tiled=True
        ).astype(jnp.float32),
    )
    summed = (
        lax.psum(attend_owned[6].astype(jnp.bfloat16), "replica").astype(jnp.float32),
        lax.psum(attend_owned[7].astype(jnp.bfloat16), "replica").astype(jnp.float32),
        lax.psum(attend_owned[0].astype(jnp.bfloat16), "replica").astype(jnp.float32),
        lax.psum(attend_owned[1].astype(jnp.bfloat16), "replica").astype(jnp.float32),
        lax.psum(attend_owned[2].astype(jnp.bfloat16), "replica").astype(jnp.float32),
        lax.psum(attend_owned[3].astype(jnp.bfloat16), "replica").astype(jnp.float32),
        lax.psum(attend_owned[8].astype(jnp.bfloat16), "replica").astype(jnp.float32),
        lax.psum(attend_owned[9].astype(jnp.bfloat16), "replica").astype(jnp.float32),
        lax.psum(attend_owned[4].astype(jnp.bfloat16), "replica").astype(jnp.float32),
        lax.psum(lookup_own.astype(jnp.bfloat16), "replica").astype(jnp.float32),
        lax.psum(content_own.astype(jnp.bfloat16), "replica").astype(jnp.float32),
        lax.psum(attend_owned[5].astype(jnp.bfloat16), "replica").astype(jnp.float32),
        lax.psum(feed_owned[2].astype(jnp.bfloat16), "replica").astype(jnp.float32),
        lax.psum(feed_owned[3].astype(jnp.bfloat16), "replica").astype(jnp.float32),
        lax.psum(feed_owned[0].astype(jnp.bfloat16), "replica").astype(jnp.float32),
        lax.psum(feed_owned[1].astype(jnp.bfloat16), "replica").astype(jnp.float32),
    )
    return (
        output,
        loss,
        frames_grad,
        text_grad,
        summed[0],
        summed[1],
        summed[2],
        summed[3],
        summed[4],
        summed[5],
        summed[6],
        summed[7],
        summed[8],
        summed[9],
        summed[10],
        summed[11],
        summed[12],
        summed[13],
        summed[14],
        summed[15],
    )


PAIR = 2 * HEAD_DIM
EVERY = ("shard", "y", "x", "core")
REPLICAS = ("core", "y", "x")
NT = (((1,), (1,)), ((), ()))
TN = (((0,), (0,)), ((), ()))
NN = (((1,), (0,)), ((), ()))


def dot(left, right, dims):
    return lax.dot_general(left, right, dims, preferred_element_type=jnp.float32)


def half_mask(side, value):
    lanes = lax.broadcasted_iota(jnp.int32, (1, PAIR), 1)
    inside = (lanes >= HEAD_DIM) if side else (lanes < HEAD_DIM)
    return jnp.where(inside, value, 0.0).astype(jnp.bfloat16)


def self_forward_kernel(place, q_ref, k_ref, v_ref, mixed_ref, lse_ref, acc_ref):
    block = q_ref.shape[0] // 2
    length = place[2]
    low = lax.broadcasted_iota(jnp.int32, (PAIR, 1), 0) < HEAD_DIM
    for part in range(2):
        first = place[part] * block
        rows = slice(part * block, (part + 1) * block)
        q = q_ref[rows, :]
        q_half = [q * half_mask(side, HEAD_DIM ** (-0.5)) for side in range(2)]
        limit = jnp.minimum(
            first + lax.broadcasted_iota(jnp.int32, (1, block), 1) + 1, length
        )
        acc_ref[...] = jnp.zeros_like(acc_ref)

        def step(j, peaks, q_half=q_half, limit=limit):
            at = pl.multiple_of(j * block, block)
            k = k_ref[pl.ds(at, block), :]
            v = v_ref[pl.ds(at, block), :]
            allowed = at + lax.broadcasted_iota(jnp.int32, (block, block), 0) < limit
            out = []
            for side in range(2):
                scores = jnp.where(allowed, dot(k, q_half[side], NT), masked_score)
                peak = jnp.maximum(peaks[side], jnp.max(scores, axis=0, keepdims=True))
                weights = jnp.exp(scores - peak).astype(jnp.bfloat16)
                v_ones = v * half_mask(side, 1.0) + half_mask(1 - side, 1.0)
                acc_ref[side] = acc_ref[side] * jnp.exp(peaks[side] - peak) + dot(
                    v_ones, weights, TN
                )
                out.append(peak)
            return tuple(out)

        peaks = lax.fori_loop(
            0, place[part] + 1, step, (jnp.full((1, block), masked_score, jnp.float32),) * 2
        )
        top, bottom = acc_ref[0], acc_ref[1]
        total = jnp.where(low, top[HEAD_DIM : HEAD_DIM + 1], bottom[0:1])
        mixed = jnp.where(low, top, bottom) / total
        mixed_ref[rows, :] = mixed.T.astype(jnp.bfloat16)
        lse_ref[0:1, rows] = peaks[0] + jnp.log(top[HEAD_DIM : HEAD_DIM + 1])
        lse_ref[1:2, rows] = peaks[1] + jnp.log(bottom[0:1])


def self_backward_kernel(
    place, q_ref, k_ref, v_ref, mixed_ref, grad_ref, lse_ref, dq_ref, dk_ref, dv_ref,
    dq_acc, dk_acc, dv_acc,
):
    block = q_ref.shape[0] // 2
    length = place[2]
    scale = HEAD_DIM ** (-0.5)
    dk_acc[...] = jnp.zeros_like(dk_acc)
    dv_acc[...] = jnp.zeros_like(dv_acc)
    for part in range(2):
        first = place[part] * block
        rows = slice(part * block, (part + 1) * block)
        q = q_ref[rows, :]
        grad = grad_ref[rows, :]
        q_half = [q * half_mask(side, scale) for side in range(2)]
        grad_half = [grad * half_mask(side, 1.0) for side in range(2)]
        product = (grad.astype(jnp.float32) * mixed_ref[rows, :].astype(jnp.float32)).T
        inner = [
            jnp.sum(product[side * HEAD_DIM : (side + 1) * HEAD_DIM], axis=0, keepdims=True)
            for side in range(2)
        ]
        lse = [lse_ref[side : side + 1, rows] for side in range(2)]
        limit = jnp.minimum(
            first + lax.broadcasted_iota(jnp.int32, (1, block), 1) + 1, length
        )
        dq_acc[...] = jnp.zeros_like(dq_acc)

        def step(
            j, carry, q_half=q_half, grad_half=grad_half, inner=inner, lse=lse, limit=limit
        ):
            at = pl.multiple_of(j * block, block)
            k = k_ref[pl.ds(at, block), :]
            v = v_ref[pl.ds(at, block), :]
            allowed = at + lax.broadcasted_iota(jnp.int32, (block, block), 0) < limit
            dq, dk, dv = 0.0, 0.0, 0.0
            for side in range(2):
                scores = jnp.where(allowed, dot(k, q_half[side], NT), masked_score)
                probs = jnp.exp(scores - lse[side])
                grad_probs = dot(v, grad_half[side], NT)
                grad_scores = (probs * (grad_probs - inner[side])).astype(jnp.bfloat16)
                dv += dot(probs.astype(jnp.bfloat16), grad_half[side], NN)
                dk += dot(grad_scores, q_half[side], NN)
                dq += dot(k * half_mask(side, scale), grad_scores, TN)
            dk_acc[pl.ds(at, block), :] += dk
            dv_acc[pl.ds(at, block), :] += dv
            dq_acc[...] += dq
            return carry

        lax.fori_loop(0, place[part] + 1, step, 0)
        dq_ref[rows, :] = dq_acc[...].T.astype(jnp.bfloat16)
    dk_ref[...] = dk_acc[...].astype(jnp.bfloat16)
    dv_ref[...] = dv_acc[...].astype(jnp.bfloat16)


def pair_block(rows):
    return pl.BlockSpec((rows, PAIR), lambda i, *_: (0, i))


def self_attend(place, queries, keys, values):
    rows, width = queries.shape
    clip = keys.shape[0]
    pairs = width // PAIR
    return pl.pallas_call(
        self_forward_kernel,
        out_shape=(
            jax.ShapeDtypeStruct((rows, width), jnp.bfloat16),
            jax.ShapeDtypeStruct((pairs * 8, rows), jnp.float32),
        ),
        grid_spec=pltpu.PrefetchScalarGridSpec(
            num_scalar_prefetch=1,
            grid=(pairs,),
            in_specs=[pair_block(rows), pair_block(clip), pair_block(clip)],
            out_specs=(pair_block(rows), pl.BlockSpec((8, rows), lambda i, *_: (i, 0))),
            scratch_shapes=[pltpu.VMEM((2, PAIR, rows // 2), jnp.float32)],
        ),
        compiler_params=pltpu.CompilerParams(vmem_limit_bytes=32 * 2**20),
        cost_estimate=pl.CostEstimate(
            flops=2 * 2 * rows * clip * width, bytes_accessed=8 * clip * width, transcendentals=0
        ),
        name="self_attend",
    )(place, queries, keys, values)


def self_attend_back(place, queries, keys, values, mixed, grads, lse):
    rows, width = queries.shape
    clip = keys.shape[0]
    pairs = width // PAIR
    return pl.pallas_call(
        self_backward_kernel,
        out_shape=(
            jax.ShapeDtypeStruct((rows, width), jnp.bfloat16),
            jax.ShapeDtypeStruct((clip, width), jnp.bfloat16),
            jax.ShapeDtypeStruct((clip, width), jnp.bfloat16),
        ),
        grid_spec=pltpu.PrefetchScalarGridSpec(
            num_scalar_prefetch=1,
            grid=(pairs,),
            in_specs=[
                pair_block(rows),
                pair_block(clip),
                pair_block(clip),
                pair_block(rows),
                pair_block(rows),
                pl.BlockSpec((8, rows), lambda i, *_: (i, 0)),
            ],
            out_specs=(pair_block(rows), pair_block(clip), pair_block(clip)),
            scratch_shapes=[
                pltpu.VMEM((PAIR, rows // 2), jnp.float32),
                pltpu.VMEM((clip, PAIR), jnp.float32),
                pltpu.VMEM((clip, PAIR), jnp.float32),
            ],
        ),
        compiler_params=pltpu.CompilerParams(vmem_limit_bytes=32 * 2**20),
        cost_estimate=pl.CostEstimate(
            flops=5 * 2 * rows * clip * width, bytes_accessed=16 * clip * width, transcendentals=0
        ),
        name="self_attend_back",
    )(place, queries, keys, values, mixed, grads, lse)


def both_heads(rows, value):
    return jnp.concatenate([rows * half_mask(side, value) for side in range(2)], axis=0)


def cross_probs_of(lookup_two, probes, present):
    text = present.shape[0]
    scores = dot(lookup_two, probes, NT)
    out = []
    for side in range(2):
        part = jnp.where(
            present > 0, scores[side * text : (side + 1) * text], masked_score
        )
        weights = jnp.exp(part - jnp.max(part, axis=0, keepdims=True))
        out.append(weights / jnp.sum(weights, axis=0, keepdims=True))
    return out


def cross_forward_kernel(probe_ref, lookup_ref, content_ref, present_ref, mixed_ref):
    probs = cross_probs_of(
        both_heads(lookup_ref[...], HEAD_DIM ** (-0.5)), probe_ref[...], present_ref[...]
    )
    probs = jnp.concatenate(probs, axis=0).astype(jnp.bfloat16)
    mixed_ref[...] = dot(probs, both_heads(content_ref[...], 1.0), TN).astype(jnp.bfloat16)


def cross_backward_kernel(
    probe_ref, lookup_ref, content_ref, present_ref, grad_ref, dp_ref, dl_ref, dc_ref
):
    text = present_ref.shape[0]
    scale = HEAD_DIM ** (-0.5)
    probes = probe_ref[...]
    grads = grad_ref[...]
    lookup_two = both_heads(lookup_ref[...], scale)
    probs = cross_probs_of(lookup_two, probes, present_ref[...])
    grad_probs = dot(both_heads(content_ref[...], 1.0), grads, NT)
    grad_scores = []
    for side in range(2):
        part = grad_probs[side * text : (side + 1) * text]
        inner = jnp.sum(probs[side] * part, axis=0, keepdims=True)
        grad_scores.append(probs[side] * (part - inner))
    grad_scores = jnp.concatenate(grad_scores, axis=0).astype(jnp.bfloat16)
    probs = jnp.concatenate(probs, axis=0).astype(jnp.bfloat16)
    low = lax.broadcasted_iota(jnp.int32, (1, PAIR), 1) < HEAD_DIM
    dp_ref[...] = dot(grad_scores, lookup_two, TN).astype(jnp.bfloat16)
    dl = dot(grad_scores, probes, NN) * scale
    dl_ref[...] = jnp.where(low, dl[:text], dl[text:]).astype(jnp.bfloat16)
    dc = dot(probs, grads, NN)
    dc_ref[...] = jnp.where(low, dc[:text], dc[text:]).astype(jnp.bfloat16)


def cross_attend(probes, lookups, contents, present):
    rows, width = probes.shape
    text = lookups.shape[0]
    return pl.pallas_call(
        cross_forward_kernel,
        out_shape=jax.ShapeDtypeStruct((rows, width), jnp.bfloat16),
        grid=(width // PAIR,),
        in_specs=[
            pair_block(rows),
            pair_block(text),
            pair_block(text),
            pl.BlockSpec((text, 1), lambda i: (0, 0)),
        ],
        out_specs=pair_block(rows),
        compiler_params=pltpu.CompilerParams(vmem_limit_bytes=32 * 2**20),
        cost_estimate=pl.CostEstimate(
            flops=8 * rows * text * width, bytes_accessed=4 * rows * width, transcendentals=0
        ),
        name="cross_attend",
    )(probes, lookups, contents, present)


def cross_attend_back(probes, lookups, contents, present, grads):
    rows, width = probes.shape
    text = lookups.shape[0]
    return pl.pallas_call(
        cross_backward_kernel,
        out_shape=(
            jax.ShapeDtypeStruct((rows, width), jnp.bfloat16),
            jax.ShapeDtypeStruct((text, width), jnp.bfloat16),
            jax.ShapeDtypeStruct((text, width), jnp.bfloat16),
        ),
        grid=(width // PAIR,),
        in_specs=[
            pair_block(rows),
            pair_block(text),
            pair_block(text),
            pl.BlockSpec((text, 1), lambda i: (0, 0)),
            pair_block(rows),
        ],
        out_specs=(pair_block(rows), pair_block(text), pair_block(text)),
        compiler_params=pltpu.CompilerParams(vmem_limit_bytes=32 * 2**20),
        cost_estimate=pl.CostEstimate(
            flops=20 * rows * text * width, bytes_accessed=6 * rows * width, transcendentals=0
        ),
        name="cross_attend_back",
    )(probes, lookups, contents, present, grads)


def assemble_kernel(spot, own_ref, *refs):
    *pieces, out_ref, sems = refs
    shard, y, x, core = spot[0], spot[1], spot[2], spot[3]
    rows = own_ref.shape[0]
    share = rows // 8
    copies = [(own_ref, shard * rows, rows)]
    for flip in range(2):
        z_ref, x_ref, y_ref, first_ref, second_ref = pieces[5 * flip : 5 * flip + 5]
        c = core if flip == 0 else 1 - core
        split = first_ref.shape[0] // share
        for k in range(3):
            owner = lax.rem(shard + 3 - k, 4) * rows
            part = pl.ds(k * share, share)
            copies.append((z_ref.at[part], owner + (4 * y + 2 * x + c) * share, share))
            copies.append((x_ref.at[part], owner + (4 * y + 2 * (1 - x) + c) * share, share))
            copies.append((y_ref.at[part], owner + (4 * (1 - y) + 2 * x + c) * share, share))
            at = owner + (4 * (1 - y) + 2 * (1 - x) + c) * share
            if k < split:
                copies.append((first_ref.at[part], at, share))
            else:
                copies.append((second_ref.at[pl.ds((k - split) * share, share)], at, share))
    started = []
    for i, (source, at, size) in enumerate(copies):
        copy = pltpu.make_async_copy(
            source, out_ref.at[pl.ds(pl.multiple_of(at, 16), size)], sems.at[i]
        )
        copy.start()
        started.append(copy)
    for copy in started:
        copy.wait()


def assemble(spot, own, pieces):
    rows, columns = own.shape
    return pl.pallas_call(
        assemble_kernel,
        out_shape=jax.ShapeDtypeStruct((4 * rows, columns), own.dtype),
        in_specs=[pl.BlockSpec(memory_space=pltpu.SMEM)]
        + [pl.BlockSpec(memory_space=pl.ANY)] * (1 + len(pieces)),
        out_specs=pl.BlockSpec(memory_space=pl.ANY),
        scratch_shapes=[pltpu.SemaphoreType.DMA((25,))],
        compiler_params=pltpu.CompilerParams(vmem_limit_bytes=4 * 2**20),
        cost_estimate=pl.CostEstimate(
            flops=0, bytes_accessed=16 * rows * columns, transcendentals=0
        ),
        name="assemble",
    )(spot, own, *pieces)


def unpack_kernel(in_ref, out_ref):
    pieces = in_ref[...]
    out_ref[...] = pieces.reshape(-1, pieces.shape[-1]).T.astype(jnp.float32)


def unpack(full, rows, place, out_shape, out_at, together):
    owners, _, features = full.shape
    tall = out_shape[0] // features
    wide = out_shape[1] // (together * rows)
    return pl.pallas_call(
        unpack_kernel,
        out_shape=jax.ShapeDtypeStruct(out_shape, jnp.float32),
        grid=(tall, wide),
        in_specs=[
            pl.BlockSpec((together, rows, features), lambda i, j: (j + out_at, place + i, 0))
        ],
        out_specs=pl.BlockSpec((features, together * rows), lambda i, j: (i, j)),
        compiler_params=pltpu.CompilerParams(vmem_limit_bytes=32 * 2**20),
        cost_estimate=pl.CostEstimate(
            flops=0, bytes_accessed=6 * out_shape[0] * out_shape[1], transcendentals=0
        ),
        name="unpack",
    )(full)


def after(value, *others):
    return lax.optimization_barrier((value, *others))[0]


def norm_parts(values):
    mean = jnp.mean(values, axis=-1, keepdims=True)
    center = values - mean
    return mean, lax.rsqrt(jnp.mean(center * center, axis=-1, keepdims=True) + epsilon)


def norm_back(grads, values, parts, gain):
    mean, inverse = parts
    unit = (values - mean) * inverse
    gain_grad = jnp.sum(grads * unit, axis=0)
    bias_grad = jnp.sum(grads, axis=0)
    scaled = grads * gain
    back = inverse * (
        scaled
        - jnp.mean(scaled, axis=-1, keepdims=True)
        - unit * jnp.mean(scaled * unit, axis=-1, keepdims=True)
    )
    return back, gain_grad, bias_grad


def clip_body(
    frames,
    text_states,
    text_mask,
    clip_lengths,
    slot_used,
    teacher,
    self_norm_gain,
    self_norm_bias,
    self_query_weight,
    self_key_weight,
    self_value_weight,
    self_output_weight,
    cross_norm_gain,
    cross_norm_bias,
    cross_query_weight,
    cross_key_weight,
    cross_value_weight,
    cross_output_weight,
    feed_norm_gain,
    feed_norm_bias,
    feed_up_weight,
    feed_down_weight,
):
    block, width = frames.shape[1:]
    text_len = text_states.shape[1]
    shards, replicas, outers = 4, 8, 4
    core = lax.axis_index("core")
    shard = lax.axis_index("shard")
    outer = 2 * lax.axis_index("y") + lax.axis_index("x")
    replica = 2 * outer + core
    clip = block * shards
    hidden_units = feed_up_weight.shape[1]

    holder = {0: 0, 1: 1, 2: 1, 3: 0}
    there = ([], [])
    for c in range(2):
        for s in range(4):
            for turn in range(2):
                slot = turn if s < 2 else 1 - turn
                there[turn].append((c * 4 + s, holder[s] * 4 + 2 * c + slot))
    back = tuple([(b, a) for a, b in pairs] for pairs in there)
    spot = ("core", "shard")
    swap = [(0, 1), (1, 0)]
    even = shard % 2 == 0
    lower = shard < 2
    first_core = core == 0

    def hop(values, distance):
        pairs = [(i, (i + distance) % shards) for i in range(shards)]
        return lax.ppermute(values, "shard", pairs)

    def to_chip(pair):
        one = lax.ppermute(jnp.where(lower, pair[0], pair[1]), spot, there[0])
        two = lax.ppermute(jnp.where(lower, pair[1], pair[0]), spot, there[1])
        return jnp.concatenate([jnp.where(even, one, two), jnp.where(even, two, one)], axis=0)

    def from_chip(values):
        early, late = values[:block], values[block:]
        one = lax.ppermute(jnp.where(even, early, late), spot, back[0])
        two = lax.ppermute(jnp.where(even, late, early), spot, back[1])
        return jnp.stack([jnp.where(lower, one, two), jnp.where(lower, two, one)])

    def share_of(weight):
        share = weight.shape[0] // replicas
        return lax.dynamic_slice_in_dim(weight, replica * share, share, 0)

    def whole(parts):
        return lax.all_gather(jnp.concatenate(parts, axis=1), EVERY, axis=0, tiled=True)

    share = block // replicas
    facts = jnp.concatenate(
        [(clip_lengths // 64)[:, None], (clip_lengths % 64)[:, None], slot_used[:, None], text_mask],
        axis=1,
    ).astype(jnp.bfloat16)
    rider = jnp.zeros((share, PAIR), jnp.bfloat16)
    for i, vector in enumerate(
        (
            self_norm_gain,
            self_norm_bias,
            cross_norm_gain,
            cross_norm_bias,
            feed_norm_gain,
            feed_norm_bias,
        )
    ):
        rider = rider.at[:, i].set(share_of(vector))
    rider = rider.at[:2, 8 : 8 + facts.shape[1]].set(facts)
    first = whole(
        [
            share_of(self_query_weight),
            share_of(self_key_weight),
            share_of(self_value_weight),
            rider,
        ]
    )
    x_low = to_chip(frames)
    rest = whole(
        [share_of(self_output_weight), share_of(cross_query_weight), share_of(cross_output_weight)]
    )

    def along_line(mine):
        return jnp.concatenate([hop(mine, distance) for distance in (1, 2, 3)], axis=0)

    def over_sides(line):
        return [line, lax.ppermute(line, "x", swap), lax.ppermute(line, "y", swap)]

    def over_corner(pieces, split):
        _, over_x, over_y = pieces
        return pieces + [
            lax.ppermute(over_x[:split], "y", swap),
            lax.ppermute(over_y[split:], "x", swap),
        ]

    def over_core(pieces):
        return pieces + [lax.ppermute(values, "core", swap) for values in pieces]

    seat = jnp.stack([shard, lax.axis_index("y"), lax.axis_index("x"), core]).astype(jnp.int32)
    expand_share = share_of(feed_up_weight)
    reduce_share = share_of(feed_down_weight)
    expand_pieces = over_sides(along_line(after(expand_share, x_low)))
    reduce_line = along_line(after(reduce_share, expand_pieces[0]))

    text_other = lax.ppermute(text_states, "core", swap)
    text_all = jnp.concatenate(
        [
            jnp.where(first_core, text_states, text_other),
            jnp.where(first_core, text_other, text_states),
        ],
        axis=0,
    ).reshape(4 * text_len, width)
    text_all = lax.dynamic_slice_in_dim(text_all, shard * block, block, 1)
    text_matrix = jnp.where(first_core, cross_key_weight, cross_value_weight)
    text_part = project(text_all, text_matrix).astype(jnp.bfloat16).reshape(4, text_len, width)
    text_half = lax.dynamic_index_in_dim(text_part, shard, 0, keepdims=False).astype(jnp.float32)
    for distance in (1, 2, 3):
        away = lax.dynamic_index_in_dim(
            text_part, lax.rem(shard + distance, shards), 0, keepdims=False
        )
        text_half += hop(away, distance).astype(jnp.float32)
    text_half = text_half.astype(jnp.bfloat16)
    text_swap = lax.ppermute(text_half, "core", swap)
    lookups = jnp.where(first_core, text_half, text_swap)
    contents = jnp.where(first_core, text_swap, text_half)

    qkv_matrix = first[:, : 3 * width]
    norms = first[:, 3 * width : 3 * width + 8].astype(jnp.float32).T
    facts = (
        first[: replicas * share, 3 * width + 8 : 3 * width + 11 + text_len]
        .reshape(replicas, share, 3 + text_len)[:, :2]
        .astype(jnp.int32)
        .reshape(2 * replicas, 3 + text_len)
    )
    lengths = facts[:, 0] * 64 + facts[:, 1]
    slot = outer * 4 + shard
    length = lengths[slot]
    used = facts[slot, 2]
    present = facts[slot, 3:].reshape(text_len, 1)
    count = jnp.sum(jnp.where(facts[:, 2] > 0, jnp.minimum(lengths, clip), 0)).astype(jnp.float32)
    places = jnp.stack([core, 3 - core, length]).astype(jnp.int32)
    positions = jnp.concatenate(
        [core * block + jnp.arange(block), (3 - core) * block + jnp.arange(block)]
    )
    valid_rows = ((positions < length) & (used > 0)).astype(jnp.float32)[:, None]
    output_matrix = rest[:, :width]
    probe_matrix = rest[:, width : 2 * width]
    merge_matrix = rest[:, 2 * width :]

    inputs = x_low.astype(jnp.float32)
    parts_one = norm_parts(inputs)
    hidden_one = ((inputs - parts_one[0]) * parts_one[1] * norms[0] + norms[1]).astype(
        jnp.bfloat16
    )
    kv = project(after(hidden_one, expand_pieces[0]), qkv_matrix[:, width:]).astype(jnp.bfloat16)
    kv_other = lax.ppermute(kv, "core", swap)
    queries = project(after(hidden_one, kv, *expand_pieces), qkv_matrix[:, :width])
    queries = after(queries.astype(jnp.bfloat16), reduce_line)
    expand_pieces = over_corner(
        list(lax.optimization_barrier((*expand_pieces, queries))[:3]), expand_share.shape[0]
    )
    reduce_pieces = over_sides(after(reduce_line, queries))

    def in_order(mine, other):
        return jnp.concatenate(
            [
                jnp.where(first_core, mine[:block], other[:block]),
                jnp.where(first_core, other[:block], mine[:block]),
                jnp.where(first_core, other[block:], mine[block:]),
                jnp.where(first_core, mine[block:], other[block:]),
            ],
            axis=0,
        )

    keys = in_order(kv[:, :width], kv_other[:, :width])
    values = in_order(kv[:, width:], kv_other[:, width:])
    mixed_self, lse = self_attend(places, queries, keys, values)
    expand_pieces = over_core(list(lax.optimization_barrier((*expand_pieces, mixed_self))[:5]))
    reduce_pieces = over_corner(
        list(lax.optimization_barrier((*reduce_pieces, mixed_self))[:3]),
        2 * reduce_share.shape[0],
    )
    teacher_low = to_chip(after(teacher, mixed_self))
    after_self = inputs + project(mixed_self, output_matrix)
    parts_two = norm_parts(after_self)
    hidden_two = ((after_self - parts_two[0]) * parts_two[1] * norms[2] + norms[3]).astype(
        jnp.bfloat16
    )
    probes = project(hidden_two, probe_matrix).astype(jnp.bfloat16)
    reduce_pieces = over_core(list(lax.optimization_barrier((*reduce_pieces, probes))[:5]))
    cross_mixed = cross_attend(probes, lookups, contents, present)
    after_cross = after_self + project(cross_mixed, merge_matrix)
    parts_three = norm_parts(after_cross)
    hidden_three = (
        (after_cross - parts_three[0]) * parts_three[1] * norms[4] + norms[5]
    ).astype(jnp.bfloat16)
    expand_matrix = assemble(seat, feed_up_weight, expand_pieces)
    upward = project(hidden_three, expand_matrix)
    activated, gelu_pull = jax.vjp(exact_gelu, upward)
    activated_low = activated.astype(jnp.bfloat16)
    reduce_matrix = assemble(seat, feed_down_weight, reduce_pieces)
    result = after_cross + project(activated_low, reduce_matrix)
    errors = (result - teacher_low.astype(jnp.float32)) * valid_rows
    squares = jnp.sum(errors * errors)
    grad_result = errors * (4 * outers * clip / count)
    grad_feed_low = grad_result.astype(jnp.bfloat16)

    def theirs_of(right, left):
        columns = right.shape[1] // 2
        part = lax.dynamic_slice_in_dim(right, (1 - core) * columns, columns, 1)
        return outer_sum(part, left).astype(jnp.bfloat16)

    def ours_of(right, left, theirs):
        columns = right.shape[1] // 2
        sent = lax.ppermute(theirs, "core", swap)
        part = lax.dynamic_slice_in_dim(right, core * columns, columns, 1)
        return (outer_sum(part, left) + sent.astype(jnp.float32)).astype(jnp.bfloat16)

    def over_outer(values):
        return lax.psum_scatter(values, ("y", "x"), scatter_dimension=0, tiled=True)

    def over_shard(values):
        columns = values.shape[1] // shards
        total = lax.dynamic_slice_in_dim(values, shard * columns, columns, 1).astype(jnp.float32)
        for distance in (1, 2, 3):
            away = lax.dynamic_slice_in_dim(
                values, lax.rem(shard + distance, shards) * columns, columns, 1
            )
            total += hop(away, distance).astype(jnp.float32)
        return total.astype(jnp.bfloat16)

    down_theirs = theirs_of(grad_feed_low, activated_low)
    grad_activated = back_project(after(grad_feed_low, down_theirs), reduce_matrix)
    grad_upward = gelu_pull(grad_activated)[0].astype(jnp.bfloat16)
    down_ours = ours_of(after(grad_feed_low, grad_upward), activated_low, down_theirs)
    down_sum = over_outer(down_ours)
    up_theirs = theirs_of(after(grad_upward, down_ours), hidden_three)
    grad_hidden_three = back_project(after(grad_upward, up_theirs), expand_matrix)
    up_ours = ours_of(after(grad_upward, grad_hidden_three), hidden_three, up_theirs)
    output = from_chip(after(result.astype(jnp.bfloat16), up_ours))
    grad_norm, gain_feed, bias_feed = norm_back(
        after(grad_hidden_three, up_ours), after_cross, parts_three, norms[4]
    )
    grad_after_cross = grad_result + grad_norm
    grad_cross_low = grad_after_cross.astype(jnp.bfloat16)
    merge_theirs = theirs_of(grad_cross_low, cross_mixed)
    grad_cross_mixed = back_project(after(grad_cross_low, merge_theirs), merge_matrix).astype(
        jnp.bfloat16
    )
    probe_grads, lookup_grads, content_grads = cross_attend_back(
        probes, lookups, contents, present, grad_cross_mixed
    )
    up_sum = over_outer(after(up_ours, down_sum, probe_grads))
    text_mine = jnp.where(first_core, lookup_grads, content_grads)
    text_sent = lax.ppermute(
        jnp.where(first_core, content_grads, lookup_grads), "core", swap
    )
    text_mine = (text_mine.astype(jnp.float32) + text_sent.astype(jnp.float32)).astype(
        jnp.bfloat16
    )
    merge_ours = ours_of(after(grad_cross_low, probe_grads), cross_mixed, merge_theirs)
    probe_theirs = theirs_of(after(probe_grads, merge_ours), hidden_two)
    grad_hidden_two = back_project(after(probe_grads, probe_theirs), probe_matrix)
    text_four = jnp.zeros((4, text_len, width), jnp.bfloat16)
    text_four = lax.dynamic_update_index_in_dim(text_four, text_mine, shard, 0)
    for distance in (1, 2, 3):
        text_four = lax.dynamic_update_index_in_dim(
            text_four,
            hop(text_mine, distance),
            lax.rem(shard + shards - distance, shards),
            0,
        )
    text_four = text_four.reshape(4 * text_len, width)
    grad_norm, gain_cross, bias_cross = norm_back(
        grad_hidden_two, after_self, parts_two, norms[2]
    )
    grad_after_self = grad_after_cross + grad_norm
    grad_self_low = grad_after_self.astype(jnp.bfloat16)
    output_theirs = theirs_of(grad_self_low, mixed_self)
    grad_mixed = back_project(after(grad_self_low, output_theirs), output_matrix).astype(
        jnp.bfloat16
    )
    probe_ours = ours_of(after(probe_grads, grad_mixed), hidden_two, probe_theirs)
    text_weights = outer_sum(text_four, text_all).astype(jnp.bfloat16)
    text_back = back_project(text_four, text_matrix).astype(jnp.bfloat16)
    output_ours = ours_of(after(grad_self_low, probe_ours), mixed_self, output_theirs)
    text_rows = width // outers
    middle = jnp.concatenate(
        [
            values.reshape(outers, -1, width)
            for values in (
                output_ours,
                probe_ours,
                merge_ours,
                text_weights.reshape(outers, shards, text_rows // shards, block)
                .transpose(0, 2, 1, 3)
                .reshape(outers, text_rows // shards, width),
            )
        ],
        axis=1,
    )
    middle_rows = middle.shape[1]
    middle = middle.reshape(outers * middle_rows, width)
    middle_sum = over_outer(after(middle, up_sum))
    text_split = text_rows // shards
    text_piece = (
        middle_sum[middle_rows - text_split :]
        .reshape(text_split, shards, block)
        .transpose(1, 0, 2)
        .reshape(text_rows, block)
    )
    grad_queries, grad_keys, grad_values = self_attend_back(
        places, queries, keys, values, mixed_self, after(grad_mixed, middle), lse
    )

    text_back = text_back.reshape(2, 2, text_len, block)
    text_kept = lax.dynamic_index_in_dim(text_back, core, 0, keepdims=False)
    text_gone = lax.dynamic_index_in_dim(text_back, 1 - core, 0, keepdims=False)
    text_own = text_kept.astype(jnp.float32) + lax.ppermute(text_gone, "core", swap).astype(
        jnp.float32
    )
    text_own = text_own.astype(jnp.bfloat16)
    text_grad = jnp.zeros(text_states.shape, jnp.float32)
    text_grad = lax.dynamic_update_slice_in_dim(
        text_grad, text_own.astype(jnp.float32), shard * block, 2
    )
    for distance in (1, 2, 3):
        text_grad = lax.dynamic_update_slice_in_dim(
            text_grad,
            hop(text_own, distance).astype(jnp.float32),
            lax.rem(shard + shards - distance, shards) * block,
            2,
        )

    def gather_sum(grads):
        quarters = [grads[i * block : (i + 1) * block] for i in range(4)]
        outside = jnp.concatenate([quarters[0], quarters[3]], axis=0)
        inside = jnp.concatenate([quarters[1], quarters[2]], axis=0)
        mine = jnp.where(first_core, outside, inside)
        other = lax.ppermute(jnp.where(first_core, inside, outside), "core", swap)
        return (mine.astype(jnp.float32) + other.astype(jnp.float32)).astype(jnp.bfloat16)

    qkv_grads = jnp.concatenate(
        [grad_queries, gather_sum(grad_keys), gather_sum(grad_values)], axis=1
    )
    qkv_theirs = theirs_of(qkv_grads, hidden_one)
    grad_hidden_one = back_project(after(qkv_grads, qkv_theirs), qkv_matrix)
    qkv_ours = ours_of(after(qkv_grads, grad_hidden_one), hidden_one, qkv_theirs)
    qkv_sum = over_outer(after(qkv_ours, middle_sum))
    grad_norm, gain_self, bias_self = norm_back(
        after(grad_hidden_one, qkv_ours), inputs, parts_one, norms[0]
    )
    frames_grad = from_chip((grad_after_self + grad_norm).astype(jnp.bfloat16)).astype(
        jnp.float32
    )

    small = jnp.stack(
        [
            gain_self,
            bias_self,
            gain_cross,
            bias_cross,
            gain_feed,
            bias_feed,
            jnp.full((width,), squares),
            jnp.zeros((width,), jnp.float32),
        ]
    )
    for axis, pairs in (
        ("core", swap),
        ("x", swap),
        ("y", swap),
        ("shard", [(0, 1), (1, 0), (2, 3), (3, 2)]),
        ("shard", [(0, 2), (2, 0), (1, 3), (3, 1)]),
    ):
        small += lax.ppermute(small, axis, pairs)
    loss = small[6, 0] / (width * count)
    small_own = lax.dynamic_slice_in_dim(small, shard * block, block, 1)

    down_piece = over_shard(down_sum)
    middle_piece = over_shard(middle_sum[: middle_rows - text_split])
    early = jnp.concatenate(
        [over_shard(up_sum)]
        + [down_piece[:, i * block : (i + 1) * block] for i in range(4)]
        + [text_piece, middle_piece],
        axis=0,
    )
    early = lax.all_gather(after(early, qkv_sum), REPLICAS, axis=0)
    piece = width // replicas
    square = (block, width)
    up_grad = unpack(early, hidden_units // replicas, 0, (block, hidden_units), 0, 1)
    at = hidden_units // replicas // piece
    down_grad = unpack(early, piece, at, (4 * block, width), 0, 2)
    at += 4
    key_grad = unpack(early, text_rows, at * piece // text_rows, square, 0, 1)
    value_grad = unpack(early, text_rows, at * piece // text_rows, square, 4, 1)
    at += text_rows // piece
    output_grad = unpack(early, piece, at, square, 0, 2)
    probe_grad = unpack(early, piece, at + 1, square, 0, 2)
    merge_grad = unpack(early, piece, at + 2, square, 0, 2)
    late = lax.all_gather(after(over_shard(qkv_sum), early), REPLICAS, axis=0, tiled=True)
    late = late.reshape(3, width, block)
    qkv_grad = [late[i].T.astype(jnp.float32) for i in range(3)]
    return (
        output,
        loss,
        frames_grad,
        text_grad,
        small_own[0],
        small_own[1],
        qkv_grad[0],
        qkv_grad[1],
        qkv_grad[2],
        output_grad,
        small_own[2],
        small_own[3],
        probe_grad,
        key_grad,
        value_grad,
        merge_grad,
        small_own[4],
        small_own[5],
        up_grad,
        down_grad,
    )


def solution(mesh):
    by_chip = mesh.shape["shard"] == 4 and mesh.shape["replica"] == 8
    replica = ("y", "x", "core") if by_chip else "replica"
    row = P(replica)
    clip = P(replica, "shard", None)
    text = P(replica, None, None)
    vector = P("shard")
    matrix = P("shard", None)
    weights = (
        [vector, vector] + [matrix] * 4 + [vector, vector] + [matrix] * 4 + [vector, vector]
        + [matrix] * 2
    )
    if by_chip:
        mesh = Mesh(mesh.devices.reshape(2, 2, 2, 4), ("y", "x", "core", "shard"))
    return jax.shard_map(
        clip_body if by_chip else general_body,
        mesh=mesh,
        in_specs=(clip, text, P(replica, None), row, row, clip, *weights),
        out_specs=(clip, P(), clip, text, *weights),
        check_vma=False,
    )
```

```python
import jax
import jax.numpy as jnp
from jax import lax
from jax.experimental import pallas as pl
from jax.experimental.pallas import tpu as pltpu
from jax.sharding import Mesh
from jax.sharding import PartitionSpec as P

HEADS = 24
HEAD_DIM = 64


epsilon = 1e-05
masked_score = -1e30


def layer_norm(values, gain, shift):
    center = values - jnp.mean(values, axis=-1, keepdims=True)
    variance = jnp.mean(center * center, axis=-1, keepdims=True)
    return center * lax.rsqrt(variance + epsilon) * gain + shift


def exact_gelu(values):
    return jax.nn.gelu(values, approximate=False)


def project(left, right):
    return jnp.dot(left, right, preferred_element_type=jnp.float32)


def outer_sum(left, right):
    return jnp.einsum("rd,re->de", left, right, preferred_element_type=jnp.float32)


def back_project(grads, matrix):
    return jnp.einsum("re,de->rd", grads, matrix, preferred_element_type=jnp.float32)


def split_heads(values):
    return values.reshape(values.shape[:-1] + (HEADS, HEAD_DIM))


def self_forward(operands):
    queries, keys_all, values_all, allowed = operands
    scale = HEAD_DIM ** (-0.5)
    scores = (
        jnp.einsum("qhd,khd->hqk", queries, keys_all, preferred_element_type=jnp.float32) * scale
    )
    scores = jnp.where(allowed[None], scores, masked_score)
    peak = jnp.max(scores, axis=-1, keepdims=True)
    weights = jnp.exp(scores - peak)
    totals = jnp.sum(weights, axis=-1, keepdims=True)
    probs = (weights / totals).astype(jnp.bfloat16)
    mixed = jnp.einsum("hqk,khd->qhd", probs, values_all, preferred_element_type=jnp.float32)
    return (mixed.astype(jnp.bfloat16), (peak + jnp.log(totals))[..., 0])


def self_backward(operands):
    queries, keys_all, values_all, allowed, log_totals, grad_mixed = operands
    scale = HEAD_DIM ** (-0.5)
    scores = (
        jnp.einsum("qhd,khd->hqk", queries, keys_all, preferred_element_type=jnp.float32) * scale
    )
    scores = jnp.where(allowed[None], scores, masked_score)
    probs = jnp.exp(scores - log_totals[..., None])
    grad_probs = jnp.einsum(
        "qhd,khd->hqk", grad_mixed, values_all, preferred_element_type=jnp.float32
    )
    grad_values = jnp.einsum(
        "hqk,qhd->khd", probs.astype(jnp.bfloat16), grad_mixed, preferred_element_type=jnp.float32
    )
    inner = jnp.sum(probs * grad_probs, axis=-1, keepdims=True)
    grad_scores = (probs * (grad_probs - inner)).astype(jnp.bfloat16)
    grad_queries = (
        jnp.einsum("hqk,khd->qhd", grad_scores, keys_all, preferred_element_type=jnp.float32)
        * scale
    ).astype(jnp.bfloat16)
    grad_keys = (
        jnp.einsum("hqk,qhd->khd", grad_scores, queries, preferred_element_type=jnp.float32) * scale
    )
    return (grad_queries, grad_keys, grad_values)


def general_body(
    frames,
    text_states,
    text_mask,
    clip_lengths,
    slot_used,
    teacher,
    self_norm_gain,
    self_norm_bias,
    self_query_weight,
    self_key_weight,
    self_value_weight,
    self_output_weight,
    cross_norm_gain,
    cross_norm_bias,
    cross_query_weight,
    cross_key_weight,
    cross_value_weight,
    cross_output_weight,
    feed_norm_gain,
    feed_norm_bias,
    feed_up_weight,
    feed_down_weight,
):
    gathered = (
        lax.all_gather(self_norm_gain, "shard", axis=0, tiled=True),
        lax.all_gather(self_norm_bias, "shard", axis=0, tiled=True),
        lax.all_gather(self_query_weight, "shard", axis=0, tiled=True),
        lax.all_gather(self_key_weight, "shard", axis=0, tiled=True),
        lax.all_gather(self_value_weight, "shard", axis=0, tiled=True),
        lax.all_gather(self_output_weight, "shard", axis=0, tiled=True),
        lax.all_gather(cross_norm_gain, "shard", axis=0, tiled=True),
        lax.all_gather(cross_norm_bias, "shard", axis=0, tiled=True),
        lax.all_gather(cross_query_weight, "shard", axis=0, tiled=True),
        lax.all_gather(cross_key_weight, "shard", axis=0, tiled=True),
        lax.all_gather(cross_value_weight, "shard", axis=0, tiled=True),
        lax.all_gather(cross_output_weight, "shard", axis=0, tiled=True),
        lax.all_gather(feed_norm_gain, "shard", axis=0, tiled=True),
        lax.all_gather(feed_norm_bias, "shard", axis=0, tiled=True),
        lax.all_gather(feed_up_weight, "shard", axis=0, tiled=True),
        lax.all_gather(feed_down_weight, "shard", axis=0, tiled=True),
    )
    (
        gain_attend,
        bias_attend,
        query_matrix,
        key_matrix,
        value_matrix,
        output_matrix,
        gain_cross,
        bias_cross,
        probe_matrix,
        lookup_matrix,
        content_matrix,
        merge_matrix,
        gain_feed,
        bias_feed,
        expand_matrix,
        reduce_matrix,
    ) = gathered
    slots = frames.shape[0]
    frame_count = frames.shape[1]
    width = frames.shape[2]
    text_len = text_states.shape[1]
    shards = lax.axis_size("shard")
    replicas = lax.axis_size("replica")
    clip_total = frame_count * shards
    row_count = slots * frame_count
    scale = HEAD_DIM ** (-0.5)
    shard_rank = lax.axis_index("shard")
    positions = shard_rank * frame_count + jnp.arange(frame_count, dtype=jnp.int32)
    key_positions = jnp.arange(clip_total, dtype=jnp.int32)
    allowed = (key_positions[None, None, :] <= positions[None, :, None]) & (
        key_positions[None, None, :] < clip_lengths[:, None, None]
    )
    valid_rows = ((positions[None, :] < clip_lengths[:, None]) & (slot_used[:, None] > 0)).astype(
        jnp.float32
    )
    text_allowed = text_mask > 0
    inputs = frames.astype(jnp.float32)
    normed_one, pull_one = jax.vjp(
        layer_norm, inputs, gain_attend.astype(jnp.float32), bias_attend.astype(jnp.float32)
    )
    hidden_one = normed_one.astype(jnp.bfloat16).reshape(row_count, width)
    queries = (
        project(hidden_one, query_matrix).astype(jnp.bfloat16).reshape(slots, frame_count, width)
    )
    keys_local = (
        project(hidden_one, key_matrix).astype(jnp.bfloat16).reshape(slots, frame_count, width)
    )
    values_local = (
        project(hidden_one, value_matrix).astype(jnp.bfloat16).reshape(slots, frame_count, width)
    )
    keys_all, values_all = (
        lax.all_gather(keys_local, "shard", axis=1, tiled=True),
        lax.all_gather(values_local, "shard", axis=1, tiled=True),
    )
    head_queries = split_heads(queries)
    head_keys = split_heads(keys_all)
    head_values = split_heads(values_all)
    mixed_self, log_totals = lax.map(self_forward, (head_queries, head_keys, head_values, allowed))
    mixed_rows = mixed_self.reshape(row_count, width)
    after_self = inputs + project(mixed_rows, output_matrix).reshape(slots, frame_count, width)
    normed_two, pull_two = jax.vjp(
        layer_norm, after_self, gain_cross.astype(jnp.float32), bias_cross.astype(jnp.float32)
    )
    hidden_two = normed_two.astype(jnp.bfloat16).reshape(row_count, width)
    probes = split_heads(
        project(hidden_two, probe_matrix).astype(jnp.bfloat16).reshape(slots, frame_count, width)
    )
    text_rows = text_states.reshape(slots * text_len, width)
    lookups = split_heads(
        project(text_rows, lookup_matrix).astype(jnp.bfloat16).reshape(slots, text_len, width)
    )
    contents = split_heads(
        project(text_rows, content_matrix).astype(jnp.bfloat16).reshape(slots, text_len, width)
    )
    cross_scores = (
        jnp.einsum("sqhd,skhd->shqk", probes, lookups, preferred_element_type=jnp.float32) * scale
    )
    cross_scores = jnp.where(text_allowed[:, None, None, :], cross_scores, masked_score)
    cross_peak = jnp.max(cross_scores, axis=-1, keepdims=True)
    cross_weights = jnp.exp(cross_scores - cross_peak)
    cross_probs = cross_weights / jnp.sum(cross_weights, axis=-1, keepdims=True)
    cross_probs_low = cross_probs.astype(jnp.bfloat16)
    cross_mixed = jnp.einsum(
        "shqk,skhd->sqhd", cross_probs_low, contents, preferred_element_type=jnp.float32
    )
    cross_mixed = cross_mixed.astype(jnp.bfloat16).reshape(row_count, width)
    after_cross = after_self + project(cross_mixed, merge_matrix).reshape(slots, frame_count, width)
    normed_three, pull_three = jax.vjp(
        layer_norm, after_cross, gain_feed.astype(jnp.float32), bias_feed.astype(jnp.float32)
    )
    hidden_three = normed_three.astype(jnp.bfloat16).reshape(row_count, width)
    upward = project(hidden_three, expand_matrix)
    activated, gelu_pull = jax.vjp(exact_gelu, upward)
    activated_low = activated.astype(jnp.bfloat16)
    result = after_cross + project(activated_low, reduce_matrix).reshape(slots, frame_count, width)
    output = result.astype(jnp.bfloat16)
    errors = (result - teacher.astype(jnp.float32)) * valid_rows[..., None]
    squares_total, count_total = lax.psum(
        (jnp.sum(errors * errors), jnp.sum(valid_rows)), ("replica", "shard")
    )
    loss = squares_total / (width * count_total)
    grad_result = errors * (slots * replicas * clip_total / count_total)
    grad_feed_low = grad_result.reshape(row_count, width).astype(jnp.bfloat16)
    grad_activated = back_project(grad_feed_low, reduce_matrix)
    grad_upward = gelu_pull(grad_activated)[0].astype(jnp.bfloat16)
    grad_hidden_three = back_project(grad_upward, expand_matrix).reshape(slots, frame_count, width)
    grad_cross_norm, gain_feed_part, bias_feed_part = pull_three(grad_hidden_three)
    grad_after_cross = grad_result + grad_cross_norm
    feed_owned = (
        lax.psum_scatter(
            outer_sum(hidden_three, grad_upward).astype(jnp.bfloat16),
            "shard",
            scatter_dimension=0,
            tiled=True,
        ).astype(jnp.float32),
        lax.psum_scatter(
            outer_sum(activated_low, grad_feed_low).astype(jnp.bfloat16),
            "shard",
            scatter_dimension=0,
            tiled=True,
        ).astype(jnp.float32),
        lax.psum_scatter(
            gain_feed_part.astype(jnp.bfloat16), "shard", scatter_dimension=0, tiled=True
        ).astype(jnp.float32),
        lax.psum_scatter(
            bias_feed_part.astype(jnp.bfloat16), "shard", scatter_dimension=0, tiled=True
        ).astype(jnp.float32),
    )
    grad_cross_low = grad_after_cross.reshape(row_count, width).astype(jnp.bfloat16)
    grad_cross_mixed = split_heads(
        back_project(grad_cross_low, merge_matrix)
        .astype(jnp.bfloat16)
        .reshape(slots, frame_count, width)
    )
    grad_cross_probs = jnp.einsum(
        "sqhd,skhd->shqk", grad_cross_mixed, contents, preferred_element_type=jnp.float32
    )
    content_grads = jnp.einsum(
        "shqk,sqhd->skhd", cross_probs_low, grad_cross_mixed, preferred_element_type=jnp.float32
    )
    cross_inner = jnp.sum(cross_probs * grad_cross_probs, axis=-1, keepdims=True)
    grad_cross_scores = (cross_probs * (grad_cross_probs - cross_inner)).astype(jnp.bfloat16)
    probe_grads = (
        jnp.einsum(
            "shqk,skhd->sqhd", grad_cross_scores, lookups, preferred_element_type=jnp.float32
        )
        * scale
    )
    probe_grads = probe_grads.astype(jnp.bfloat16).reshape(row_count, width)
    lookup_grads = (
        jnp.einsum("shqk,sqhd->skhd", grad_cross_scores, probes, preferred_element_type=jnp.float32)
        * scale
    )
    lookup_sum, content_sum = (
        lax.psum(lookup_grads.astype(jnp.bfloat16), "shard").astype(jnp.float32),
        lax.psum(content_grads.astype(jnp.bfloat16), "shard").astype(jnp.float32),
    )
    lookup_low = lookup_sum.astype(jnp.bfloat16).reshape(slots * text_len, width)
    content_low = content_sum.astype(jnp.bfloat16).reshape(slots * text_len, width)
    own_width = width // shards
    own_text = lax.dynamic_slice_in_dim(text_rows, shard_rank * own_width, own_width, 1)
    lookup_own = outer_sum(own_text, lookup_low)
    content_own = outer_sum(own_text, content_low)
    text_grad = (
        back_project(lookup_low, lookup_matrix) + back_project(content_low, content_matrix)
    ).reshape(slots, text_len, width)
    grad_hidden_two = back_project(probe_grads, probe_matrix).reshape(slots, frame_count, width)
    grad_self_norm, gain_cross_part, bias_cross_part = pull_two(grad_hidden_two)
    grad_after_self = grad_after_cross + grad_self_norm
    grad_self_low = grad_after_self.reshape(row_count, width).astype(jnp.bfloat16)
    grad_mixed = split_heads(
        back_project(grad_self_low, output_matrix)
        .astype(jnp.bfloat16)
        .reshape(slots, frame_count, width)
    )
    grad_queries, grad_keys, grad_values = lax.map(
        self_backward, (head_queries, head_keys, head_values, allowed, log_totals, grad_mixed)
    )
    key_sum, value_sum = (
        lax.psum_scatter(
            grad_keys.reshape(slots, clip_total, width).astype(jnp.bfloat16),
            "shard",
            scatter_dimension=1,
            tiled=True,
        ).astype(jnp.float32),
        lax.psum_scatter(
            grad_values.reshape(slots, clip_total, width).astype(jnp.bfloat16),
            "shard",
            scatter_dimension=1,
            tiled=True,
        ).astype(jnp.float32),
    )
    key_low = key_sum.astype(jnp.bfloat16).reshape(row_count, width)
    value_low = value_sum.astype(jnp.bfloat16).reshape(row_count, width)
    query_low = grad_queries.reshape(row_count, width)
    grad_hidden_one = (
        back_project(query_low, query_matrix)
        + back_project(key_low, key_matrix)
        + back_project(value_low, value_matrix)
    )
    grad_inputs, gain_attend_part, bias_attend_part = pull_one(
        grad_hidden_one.reshape(slots, frame_count, width)
    )
    frames_grad = grad_after_self + grad_inputs
    attend_owned = (
        lax.psum_scatter(
            outer_sum(hidden_one, query_low).astype(jnp.bfloat16),
            "shard",
            scatter_dimension=0,
            tiled=True,
        ).astype(jnp.float32),
        lax.psum_scatter(
            outer_sum(hidden_one, key_low).astype(jnp.bfloat16),
            "shard",
            scatter_dimension=0,
            tiled=True,
        ).astype(jnp.float32),
        lax.psum_scatter(
            outer_sum(hidden_one, value_low).astype(jnp.bfloat16),
            "shard",
            scatter_dimension=0,
            tiled=True,
        ).astype(jnp.float32),
        lax.psum_scatter(
            outer_sum(mixed_rows, grad_self_low).astype(jnp.bfloat16),
            "shard",
            scatter_dimension=0,
            tiled=True,
        ).astype(jnp.float32),
        lax.psum_scatter(
            outer_sum(hidden_two, probe_grads).astype(jnp.bfloat16),
            "shard",
            scatter_dimension=0,
            tiled=True,
        ).astype(jnp.float32),
        lax.psum_scatter(
            outer_sum(cross_mixed, grad_cross_low).astype(jnp.bfloat16),
            "shard",
            scatter_dimension=0,
            tiled=True,
        ).astype(jnp.float32),
        lax.psum_scatter(
            gain_attend_part.astype(jnp.bfloat16), "shard", scatter_dimension=0, tiled=True
        ).astype(jnp.float32),
        lax.psum_scatter(
            bias_attend_part.astype(jnp.bfloat16), "shard", scatter_dimension=0, tiled=True
        ).astype(jnp.float32),
        lax.psum_scatter(
            gain_cross_part.astype(jnp.bfloat16), "shard", scatter_dimension=0, tiled=True
        ).astype(jnp.float32),
        lax.psum_scatter(
            bias_cross_part.astype(jnp.bfloat16), "shard", scatter_dimension=0, tiled=True
        ).astype(jnp.float32),
    )
    summed = (
        lax.psum(attend_owned[6].astype(jnp.bfloat16), "replica").astype(jnp.float32),
        lax.psum(attend_owned[7].astype(jnp.bfloat16), "replica").astype(jnp.float32),
        lax.psum(attend_owned[0].astype(jnp.bfloat16), "replica").astype(jnp.float32),
        lax.psum(attend_owned[1].astype(jnp.bfloat16), "replica").astype(jnp.float32),
        lax.psum(attend_owned[2].astype(jnp.bfloat16), "replica").astype(jnp.float32),
        lax.psum(attend_owned[3].astype(jnp.bfloat16), "replica").astype(jnp.float32),
        lax.psum(attend_owned[8].astype(jnp.bfloat16), "replica").astype(jnp.float32),
        lax.psum(attend_owned[9].astype(jnp.bfloat16), "replica").astype(jnp.float32),
        lax.psum(attend_owned[4].astype(jnp.bfloat16), "replica").astype(jnp.float32),
        lax.psum(lookup_own.astype(jnp.bfloat16), "replica").astype(jnp.float32),
        lax.psum(content_own.astype(jnp.bfloat16), "replica").astype(jnp.float32),
        lax.psum(attend_owned[5].astype(jnp.bfloat16), "replica").astype(jnp.float32),
        lax.psum(feed_owned[2].astype(jnp.bfloat16), "replica").astype(jnp.float32),
        lax.psum(feed_owned[3].astype(jnp.bfloat16), "replica").astype(jnp.float32),
        lax.psum(feed_owned[0].astype(jnp.bfloat16), "replica").astype(jnp.float32),
        lax.psum(feed_owned[1].astype(jnp.bfloat16), "replica").astype(jnp.float32),
    )
    return (
        output,
        loss,
        frames_grad,
        text_grad,
        summed[0],
        summed[1],
        summed[2],
        summed[3],
        summed[4],
        summed[5],
        summed[6],
        summed[7],
        summed[8],
        summed[9],
        summed[10],
        summed[11],
        summed[12],
        summed[13],
        summed[14],
        summed[15],
    )


PAIR = 2 * HEAD_DIM
EVERY = ("shard", "y", "x", "core")
REPLICAS = ("core", "y", "x")
NT = (((1,), (1,)), ((), ()))
TN = (((0,), (0,)), ((), ()))
NN = (((1,), (0,)), ((), ()))


def dot(left, right, dims):
    return lax.dot_general(left, right, dims, preferred_element_type=jnp.float32)


def half_mask(side, value):
    lanes = lax.broadcasted_iota(jnp.int32, (1, PAIR), 1)
    inside = (lanes >= HEAD_DIM) if side else (lanes < HEAD_DIM)
    return jnp.where(inside, value, 0.0).astype(jnp.bfloat16)


def self_forward_kernel(place, q_ref, k_ref, v_ref, mixed_ref, lse_ref, acc_ref):
    block = q_ref.shape[0] // 2
    length = place[2]
    low = lax.broadcasted_iota(jnp.int32, (PAIR, 1), 0) < HEAD_DIM
    for part in range(2):
        first = place[part] * block
        rows = slice(part * block, (part + 1) * block)
        q = q_ref[rows, :]
        q_half = [q * half_mask(side, HEAD_DIM ** (-0.5)) for side in range(2)]
        limit = jnp.minimum(
            first + lax.broadcasted_iota(jnp.int32, (1, block), 1) + 1, length
        )
        acc_ref[...] = jnp.zeros_like(acc_ref)

        def step(j, peaks, q_half=q_half, limit=limit):
            at = pl.multiple_of(j * block, block)
            k = k_ref[pl.ds(at, block), :]
            v = v_ref[pl.ds(at, block), :]
            allowed = at + lax.broadcasted_iota(jnp.int32, (block, block), 0) < limit
            out = []
            for side in range(2):
                scores = jnp.where(allowed, dot(k, q_half[side], NT), masked_score)
                peak = jnp.maximum(peaks[side], jnp.max(scores, axis=0, keepdims=True))
                weights = jnp.exp(scores - peak).astype(jnp.bfloat16)
                v_ones = v * half_mask(side, 1.0) + half_mask(1 - side, 1.0)
                acc_ref[side] = acc_ref[side] * jnp.exp(peaks[side] - peak) + dot(
                    v_ones, weights, TN
                )
                out.append(peak)
            return tuple(out)

        peaks = lax.fori_loop(
            0, place[part] + 1, step, (jnp.full((1, block), masked_score, jnp.float32),) * 2
        )
        top, bottom = acc_ref[0], acc_ref[1]
        total = jnp.where(low, top[HEAD_DIM : HEAD_DIM + 1], bottom[0:1])
        mixed = jnp.where(low, top, bottom) / total
        mixed_ref[rows, :] = mixed.T.astype(jnp.bfloat16)
        lse_ref[0:1, rows] = peaks[0] + jnp.log(top[HEAD_DIM : HEAD_DIM + 1])
        lse_ref[1:2, rows] = peaks[1] + jnp.log(bottom[0:1])


def self_backward_kernel(
    place, q_ref, k_ref, v_ref, mixed_ref, grad_ref, lse_ref, dq_ref, dk_ref, dv_ref,
    dq_acc, dk_acc, dv_acc,
):
    block = q_ref.shape[0] // 2
    length = place[2]
    scale = HEAD_DIM ** (-0.5)
    dk_acc[...] = jnp.zeros_like(dk_acc)
    dv_acc[...] = jnp.zeros_like(dv_acc)
    for part in range(2):
        first = place[part] * block
        rows = slice(part * block, (part + 1) * block)
        q = q_ref[rows, :]
        grad = grad_ref[rows, :]
        q_half = [q * half_mask(side, scale) for side in range(2)]
        grad_half = [grad * half_mask(side, 1.0) for side in range(2)]
        product = (grad.astype(jnp.float32) * mixed_ref[rows, :].astype(jnp.float32)).T
        inner = [
            jnp.sum(product[side * HEAD_DIM : (side + 1) * HEAD_DIM], axis=0, keepdims=True)
            for side in range(2)
        ]
        lse = [lse_ref[side : side + 1, rows] for side in range(2)]
        limit = jnp.minimum(
            first + lax.broadcasted_iota(jnp.int32, (1, block), 1) + 1, length
        )
        dq_acc[...] = jnp.zeros_like(dq_acc)

        def step(
            j, carry, q_half=q_half, grad_half=grad_half, inner=inner, lse=lse, limit=limit
        ):
            at = pl.multiple_of(j * block, block)
            k = k_ref[pl.ds(at, block), :]
            v = v_ref[pl.ds(at, block), :]
            allowed = at + lax.broadcasted_iota(jnp.int32, (block, block), 0) < limit
            dq, dk, dv = 0.0, 0.0, 0.0
            for side in range(2):
                scores = jnp.where(allowed, dot(k, q_half[side], NT), masked_score)
                probs = jnp.exp(scores - lse[side])
                grad_probs = dot(v, grad_half[side], NT)
                grad_scores = (probs * (grad_probs - inner[side])).astype(jnp.bfloat16)
                dv += dot(probs.astype(jnp.bfloat16), grad_half[side], NN)
                dk += dot(grad_scores, q_half[side], NN)
                dq += dot(k * half_mask(side, scale), grad_scores, TN)
            dk_acc[pl.ds(at, block), :] += dk
            dv_acc[pl.ds(at, block), :] += dv
            dq_acc[...] += dq
            return carry

        lax.fori_loop(0, place[part] + 1, step, 0)
        dq_ref[rows, :] = dq_acc[...].T.astype(jnp.bfloat16)
    dk_ref[...] = dk_acc[...].astype(jnp.bfloat16)
    dv_ref[...] = dv_acc[...].astype(jnp.bfloat16)


def pair_block(rows):
    return pl.BlockSpec((rows, PAIR), lambda i, *_: (0, i))


def self_attend(place, queries, keys, values):
    rows, width = queries.shape
    clip = keys.shape[0]
    pairs = width // PAIR
    return pl.pallas_call(
        self_forward_kernel,
        out_shape=(
            jax.ShapeDtypeStruct((rows, width), jnp.bfloat16),
            jax.ShapeDtypeStruct((pairs * 8, rows), jnp.float32),
        ),
        grid_spec=pltpu.PrefetchScalarGridSpec(
            num_scalar_prefetch=1,
            grid=(pairs,),
            in_specs=[pair_block(rows), pair_block(clip), pair_block(clip)],
            out_specs=(pair_block(rows), pl.BlockSpec((8, rows), lambda i, *_: (i, 0))),
            scratch_shapes=[pltpu.VMEM((2, PAIR, rows // 2), jnp.float32)],
        ),
        compiler_params=pltpu.CompilerParams(vmem_limit_bytes=32 * 2**20),
        cost_estimate=pl.CostEstimate(
            flops=2 * 2 * rows * clip * width, bytes_accessed=8 * clip * width, transcendentals=0
        ),
        name="self_attend",
    )(place, queries, keys, values)


def self_attend_back(place, queries, keys, values, mixed, grads, lse):
    rows, width = queries.shape
    clip = keys.shape[0]
    pairs = width // PAIR
    return pl.pallas_call(
        self_backward_kernel,
        out_shape=(
            jax.ShapeDtypeStruct((rows, width), jnp.bfloat16),
            jax.ShapeDtypeStruct((clip, width), jnp.bfloat16),
            jax.ShapeDtypeStruct((clip, width), jnp.bfloat16),
        ),
        grid_spec=pltpu.PrefetchScalarGridSpec(
            num_scalar_prefetch=1,
            grid=(pairs,),
            in_specs=[
                pair_block(rows),
                pair_block(clip),
                pair_block(clip),
                pair_block(rows),
                pair_block(rows),
                pl.BlockSpec((8, rows), lambda i, *_: (i, 0)),
            ],
            out_specs=(pair_block(rows), pair_block(clip), pair_block(clip)),
            scratch_shapes=[
                pltpu.VMEM((PAIR, rows // 2), jnp.float32),
                pltpu.VMEM((clip, PAIR), jnp.float32),
                pltpu.VMEM((clip, PAIR), jnp.float32),
            ],
        ),
        compiler_params=pltpu.CompilerParams(vmem_limit_bytes=32 * 2**20),
        cost_estimate=pl.CostEstimate(
            flops=5 * 2 * rows * clip * width, bytes_accessed=16 * clip * width, transcendentals=0
        ),
        name="self_attend_back",
    )(place, queries, keys, values, mixed, grads, lse)


def both_heads(rows, value):
    return jnp.concatenate([rows * half_mask(side, value) for side in range(2)], axis=0)


def cross_probs_of(lookup_two, probes, present):
    text = present.shape[0]
    scores = dot(lookup_two, probes, NT)
    out = []
    for side in range(2):
        part = jnp.where(
            present > 0, scores[side * text : (side + 1) * text], masked_score
        )
        weights = jnp.exp(part - jnp.max(part, axis=0, keepdims=True))
        out.append(weights / jnp.sum(weights, axis=0, keepdims=True))
    return out


def cross_forward_kernel(probe_ref, lookup_ref, content_ref, present_ref, mixed_ref):
    probs = cross_probs_of(
        both_heads(lookup_ref[...], HEAD_DIM ** (-0.5)), probe_ref[...], present_ref[...]
    )
    probs = jnp.concatenate(probs, axis=0).astype(jnp.bfloat16)
    mixed_ref[...] = dot(probs, both_heads(content_ref[...], 1.0), TN).astype(jnp.bfloat16)


def cross_backward_kernel(
    probe_ref, lookup_ref, content_ref, present_ref, grad_ref, dp_ref, dl_ref, dc_ref
):
    text = present_ref.shape[0]
    scale = HEAD_DIM ** (-0.5)
    probes = probe_ref[...]
    grads = grad_ref[...]
    lookup_two = both_heads(lookup_ref[...], scale)
    probs = cross_probs_of(lookup_two, probes, present_ref[...])
    grad_probs = dot(both_heads(content_ref[...], 1.0), grads, NT)
    grad_scores = []
    for side in range(2):
        part = grad_probs[side * text : (side + 1) * text]
        inner = jnp.sum(probs[side] * part, axis=0, keepdims=True)
        grad_scores.append(probs[side] * (part - inner))
    grad_scores = jnp.concatenate(grad_scores, axis=0).astype(jnp.bfloat16)
    probs = jnp.concatenate(probs, axis=0).astype(jnp.bfloat16)
    low = lax.broadcasted_iota(jnp.int32, (1, PAIR), 1) < HEAD_DIM
    dp_ref[...] = dot(grad_scores, lookup_two, TN).astype(jnp.bfloat16)
    dl = dot(grad_scores, probes, NN) * scale
    dl_ref[...] = jnp.where(low, dl[:text], dl[text:]).astype(jnp.bfloat16)
    dc = dot(probs, grads, NN)
    dc_ref[...] = jnp.where(low, dc[:text], dc[text:]).astype(jnp.bfloat16)


def cross_attend(probes, lookups, contents, present):
    rows, width = probes.shape
    text = lookups.shape[0]
    return pl.pallas_call(
        cross_forward_kernel,
        out_shape=jax.ShapeDtypeStruct((rows, width), jnp.bfloat16),
        grid=(width // PAIR,),
        in_specs=[
            pair_block(rows),
            pair_block(text),
            pair_block(text),
            pl.BlockSpec((text, 1), lambda i: (0, 0)),
        ],
        out_specs=pair_block(rows),
        compiler_params=pltpu.CompilerParams(vmem_limit_bytes=32 * 2**20),
        cost_estimate=pl.CostEstimate(
            flops=8 * rows * text * width, bytes_accessed=4 * rows * width, transcendentals=0
        ),
        name="cross_attend",
    )(probes, lookups, contents, present)


def cross_attend_back(probes, lookups, contents, present, grads):
    rows, width = probes.shape
    text = lookups.shape[0]
    return pl.pallas_call(
        cross_backward_kernel,
        out_shape=(
            jax.ShapeDtypeStruct((rows, width), jnp.bfloat16),
            jax.ShapeDtypeStruct((text, width), jnp.bfloat16),
            jax.ShapeDtypeStruct((text, width), jnp.bfloat16),
        ),
        grid=(width // PAIR,),
        in_specs=[
            pair_block(rows),
            pair_block(text),
            pair_block(text),
            pl.BlockSpec((text, 1), lambda i: (0, 0)),
            pair_block(rows),
        ],
        out_specs=(pair_block(rows), pair_block(text), pair_block(text)),
        compiler_params=pltpu.CompilerParams(vmem_limit_bytes=32 * 2**20),
        cost_estimate=pl.CostEstimate(
            flops=20 * rows * text * width, bytes_accessed=6 * rows * width, transcendentals=0
        ),
        name="cross_attend_back",
    )(probes, lookups, contents, present, grads)


def assemble_kernel(spot, own_ref, *refs):
    *pieces, out_ref, sems = refs
    shard, y, x, core = spot[0], spot[1], spot[2], spot[3]
    rows = own_ref.shape[0]
    share = rows // 8
    copies = [(own_ref, shard * rows, rows)]
    for flip in range(2):
        z_ref, x_ref, y_ref, first_ref, second_ref = pieces[5 * flip : 5 * flip + 5]
        c = core if flip == 0 else 1 - core
        split = first_ref.shape[0] // share
        for k in range(3):
            owner = lax.rem(shard + 3 - k, 4) * rows
            part = pl.ds(k * share, share)
            copies.append((z_ref.at[part], owner + (4 * y + 2 * x + c) * share, share))
            copies.append((x_ref.at[part], owner + (4 * y + 2 * (1 - x) + c) * share, share))
            copies.append((y_ref.at[part], owner + (4 * (1 - y) + 2 * x + c) * share, share))
            at = owner + (4 * (1 - y) + 2 * (1 - x) + c) * share
            if k < split:
                copies.append((first_ref.at[part], at, share))
            else:
                copies.append((second_ref.at[pl.ds((k - split) * share, share)], at, share))
    started = []
    for i, (source, at, size) in enumerate(copies):
        copy = pltpu.make_async_copy(
            source, out_ref.at[pl.ds(pl.multiple_of(at, 16), size)], sems.at[i]
        )
        copy.start()
        started.append(copy)
    for copy in started:
        copy.wait()


def assemble(spot, own, pieces):
    rows, columns = own.shape
    return pl.pallas_call(
        assemble_kernel,
        out_shape=jax.ShapeDtypeStruct((4 * rows, columns), own.dtype),
        in_specs=[pl.BlockSpec(memory_space=pltpu.SMEM)]
        + [pl.BlockSpec(memory_space=pl.ANY)] * (1 + len(pieces)),
        out_specs=pl.BlockSpec(memory_space=pl.ANY),
        scratch_shapes=[pltpu.SemaphoreType.DMA((25,))],
        compiler_params=pltpu.CompilerParams(vmem_limit_bytes=4 * 2**20),
        cost_estimate=pl.CostEstimate(
            flops=0, bytes_accessed=16 * rows * columns, transcendentals=0
        ),
        name="assemble",
    )(spot, own, *pieces)


def unpack_kernel(in_ref, out_ref):
    pieces = in_ref[...]
    out_ref[...] = pieces.reshape(-1, pieces.shape[-1]).T.astype(jnp.float32)


def unpack(full, rows, place, out_shape, out_at, together):
    owners, _, features = full.shape
    tall = out_shape[0] // features
    wide = out_shape[1] // (together * rows)
    return pl.pallas_call(
        unpack_kernel,
        out_shape=jax.ShapeDtypeStruct(out_shape, jnp.float32),
        grid=(tall, wide),
        in_specs=[
            pl.BlockSpec((together, rows, features), lambda i, j: (j + out_at, place + i, 0))
        ],
        out_specs=pl.BlockSpec((features, together * rows), lambda i, j: (i, j)),
        compiler_params=pltpu.CompilerParams(vmem_limit_bytes=32 * 2**20),
        cost_estimate=pl.CostEstimate(
            flops=0, bytes_accessed=6 * out_shape[0] * out_shape[1], transcendentals=0
        ),
        name="unpack",
    )(full)


def after(value, *others):
    return lax.optimization_barrier((value, *others))[0]


def norm_parts(values):
    mean = jnp.mean(values, axis=-1, keepdims=True)
    center = values - mean
    return mean, lax.rsqrt(jnp.mean(center * center, axis=-1, keepdims=True) + epsilon)


def norm_back(grads, values, parts, gain):
    mean, inverse = parts
    unit = (values - mean) * inverse
    gain_grad = jnp.sum(grads * unit, axis=0)
    bias_grad = jnp.sum(grads, axis=0)
    scaled = grads * gain
    back = inverse * (
        scaled
        - jnp.mean(scaled, axis=-1, keepdims=True)
        - unit * jnp.mean(scaled * unit, axis=-1, keepdims=True)
    )
    return back, gain_grad, bias_grad


def clip_body(
    frames,
    text_states,
    text_mask,
    clip_lengths,
    slot_used,
    teacher,
    self_norm_gain,
    self_norm_bias,
    self_query_weight,
    self_key_weight,
    self_value_weight,
    self_output_weight,
    cross_norm_gain,
    cross_norm_bias,
    cross_query_weight,
    cross_key_weight,
    cross_value_weight,
    cross_output_weight,
    feed_norm_gain,
    feed_norm_bias,
    feed_up_weight,
    feed_down_weight,
):
    block, width = frames.shape[1:]
    text_len = text_states.shape[1]
    shards, replicas, outers = 4, 8, 4
    core = lax.axis_index("core")
    shard = lax.axis_index("shard")
    outer = 2 * lax.axis_index("y") + lax.axis_index("x")
    replica = 2 * outer + core
    clip = block * shards
    hidden_units = feed_up_weight.shape[1]

    holder = {0: 0, 1: 1, 2: 1, 3: 0}
    there = ([], [])
    for c in range(2):
        for s in range(4):
            for turn in range(2):
                slot = turn if s < 2 else 1 - turn
                there[turn].append((c * 4 + s, holder[s] * 4 + 2 * c + slot))
    back = tuple([(b, a) for a, b in pairs] for pairs in there)
    spot = ("core", "shard")
    swap = [(0, 1), (1, 0)]
    even = shard % 2 == 0
    lower = shard < 2
    first_core = core == 0

    def hop(values, distance):
        pairs = [(i, (i + distance) % shards) for i in range(shards)]
        return lax.ppermute(values, "shard", pairs)

    def to_chip(pair):
        one = lax.ppermute(jnp.where(lower, pair[0], pair[1]), spot, there[0])
        two = lax.ppermute(jnp.where(lower, pair[1], pair[0]), spot, there[1])
        return one, two

    def by_time(one, two):
        return jnp.concatenate([jnp.where(even, one, two), jnp.where(even, two, one)], axis=0)

    def from_chip(values):
        early, late = values[:block], values[block:]
        one = lax.ppermute(jnp.where(even, early, late), spot, back[0])
        two = lax.ppermute(jnp.where(even, late, early), spot, back[1])
        return jnp.stack([jnp.where(lower, one, two), jnp.where(lower, two, one)])

    def share_of(weight):
        share = weight.shape[0] // replicas
        return lax.dynamic_slice_in_dim(weight, replica * share, share, 0)

    def from_shards(mine, hops=None):
        hops = hops or [hop(mine, distance) for distance in (1, 2, 3)]
        out = jnp.zeros((shards,) + mine.shape, mine.dtype)
        out = lax.dynamic_update_index_in_dim(out, mine, shard, 0)
        for distance in (1, 2, 3):
            owner = lax.rem(shard + shards - distance, shards)
            out = lax.dynamic_update_index_in_dim(out, hops[distance - 1], owner, 0)
        return out

    def from_replicas(line):
        full = lax.all_gather(line, ("y", "x", "core"), axis=1, tiled=True)
        return full.reshape(-1, line.shape[-1])

    def over_sides(line):
        return [line, lax.ppermute(line, "x", swap), lax.ppermute(line, "y", swap)]

    def over_corner(pieces, split):
        _, over_x, over_y = pieces
        return pieces + [
            lax.ppermute(over_x[:split], "y", swap),
            lax.ppermute(over_y[split:], "x", swap),
        ]

    def over_core(pieces):
        return pieces + [lax.ppermute(values, "core", swap) for values in pieces]

    qkv_line = from_shards(
        jnp.concatenate(
            [share_of(self_query_weight), share_of(self_key_weight), share_of(self_value_weight)],
            axis=1,
        )
    )
    rest_own = jnp.concatenate([self_output_weight, cross_query_weight, cross_output_weight], axis=1)
    rest_share = share_of(rest_own)
    rest_mine = after(rest_share, qkv_line)
    rest_line = jnp.concatenate([hop(rest_mine, distance) for distance in (1, 2, 3)], axis=0)
    norms = from_shards(
        jnp.stack(
            [
                self_norm_gain,
                self_norm_bias,
                cross_norm_gain,
                cross_norm_bias,
                feed_norm_gain,
                feed_norm_bias,
            ]
        )
    )
    norms = norms.transpose(1, 0, 2).reshape(6, width).astype(jnp.float32)
    came = to_chip(after(frames, rest_line))
    x_low = by_time(*came)
    expand_line = from_shards(after(share_of(feed_up_weight), *came))
    qkv_matrix = from_replicas(qkv_line)
    expand_matrix = from_replicas(expand_line)
    seat = jnp.stack([shard, lax.axis_index("y"), lax.axis_index("x"), core]).astype(jnp.int32)

    text_other = lax.ppermute(text_states, "core", swap)
    text_all = jnp.concatenate(
        [
            jnp.where(first_core, text_states, text_other),
            jnp.where(first_core, text_other, text_states),
        ],
        axis=0,
    ).reshape(4 * text_len, width)
    text_all = lax.dynamic_slice_in_dim(text_all, shard * block, block, 1)
    text_matrix = jnp.where(first_core, cross_key_weight, cross_value_weight)
    text_part = project(text_all, text_matrix).astype(jnp.bfloat16).reshape(4, text_len, width)
    text_half = lax.dynamic_index_in_dim(text_part, shard, 0, keepdims=False).astype(jnp.float32)
    for distance in (1, 2, 3):
        away = lax.dynamic_index_in_dim(
            text_part, lax.rem(shard + distance, shards), 0, keepdims=False
        )
        text_half += hop(away, distance).astype(jnp.float32)
    text_half = text_half.astype(jnp.bfloat16)
    text_swap = lax.ppermute(text_half, "core", swap)
    lookups = jnp.where(first_core, text_half, text_swap)
    contents = jnp.where(first_core, text_swap, text_half)

    facts = jnp.concatenate([clip_lengths[:, None], slot_used[:, None], text_mask], axis=1)
    facts_other = lax.ppermute(facts, "core", swap)
    fact = lax.dynamic_index_in_dim(
        jnp.where(shard // 2 == core, facts, facts_other), shard % 2, 0, keepdims=False
    )
    length, used = fact[0], fact[1]
    present = fact[2:].reshape(text_len, 1)
    both = jnp.stack([facts, facts_other])
    count = jnp.sum(
        jnp.where(both[:, :, 1] > 0, jnp.minimum(both[:, :, 0], clip), 0).astype(jnp.float32)
    )
    count = jnp.full((8, 128), count)
    for axis in ("x", "y"):
        count += lax.ppermute(count, axis, swap)
    count = count[0, 0]
    places = jnp.stack([core, 3 - core, length]).astype(jnp.int32)
    positions = jnp.concatenate(
        [core * block + jnp.arange(block), (3 - core) * block + jnp.arange(block)]
    )
    valid_rows = ((positions < length) & (used > 0)).astype(jnp.float32)[:, None]
    inputs = x_low.astype(jnp.float32)
    parts_one = norm_parts(inputs)
    hidden_one = ((inputs - parts_one[0]) * parts_one[1] * norms[0] + norms[1]).astype(
        jnp.bfloat16
    )
    kv = project(hidden_one, qkv_matrix[:, width:]).astype(jnp.bfloat16)
    kv_other = lax.ppermute(kv, "core", swap)
    rest_pieces = over_sides(after(rest_line, qkv_matrix))
    queries = project(after(hidden_one, kv), qkv_matrix[:, :width]).astype(jnp.bfloat16)
    def in_order(mine, other):
        return jnp.concatenate(
            [
                jnp.where(first_core, mine[:block], other[:block]),
                jnp.where(first_core, other[:block], mine[:block]),
                jnp.where(first_core, other[block:], mine[block:]),
                jnp.where(first_core, mine[block:], other[block:]),
            ],
            axis=0,
        )

    keys = in_order(kv[:, :width], kv_other[:, :width])
    values = in_order(kv[:, width:], kv_other[:, width:])
    rest_pieces = over_corner(
        list(lax.optimization_barrier((*rest_pieces, values))[:3]), 2 * rest_share.shape[0]
    )
    reduce_share = after(share_of(feed_down_weight), expand_line, keys)
    reduce_hops = [hop(reduce_share, distance) for distance in (1, 2, 3)]
    mixed_self, lse = self_attend(
        after(places, expand_line, text_part, *rest_pieces), queries, keys, values
    )
    rest_pieces = over_core(list(lax.optimization_barrier((*rest_pieces, mixed_self))[:5]))
    rest = assemble(seat, rest_own, rest_pieces)
    reduce_line = from_shards(
        reduce_share, list(lax.optimization_barrier((*reduce_hops, mixed_self))[:3])
    )
    reduce_matrix = from_replicas(reduce_line)
    output_matrix = rest[:, :width]
    probe_matrix = rest[:, width : 2 * width]
    merge_matrix = rest[:, 2 * width :]
    after_self = inputs + project(mixed_self, output_matrix)
    parts_two = norm_parts(after_self)
    hidden_two = ((after_self - parts_two[0]) * parts_two[1] * norms[2] + norms[3]).astype(
        jnp.bfloat16
    )
    probes = project(hidden_two, probe_matrix).astype(jnp.bfloat16)
    teacher_low = by_time(*to_chip(after(teacher, reduce_line, probes)))
    cross_mixed = cross_attend(probes, lookups, contents, present)
    after_cross = after_self + project(cross_mixed, merge_matrix)
    parts_three = norm_parts(after_cross)
    hidden_three = (
        (after_cross - parts_three[0]) * parts_three[1] * norms[4] + norms[5]
    ).astype(jnp.bfloat16)
    upward = project(hidden_three, expand_matrix)
    activated, gelu_pull = jax.vjp(exact_gelu, upward)
    activated_low = activated.astype(jnp.bfloat16)
    result = after_cross + project(activated_low, reduce_matrix)
    errors = (result - teacher_low.astype(jnp.float32)) * valid_rows
    squares = jnp.sum(errors * errors)
    grad_result = errors * (4 * outers * clip / count)
    grad_feed_low = grad_result.astype(jnp.bfloat16)

    def theirs_of(right, left):
        columns = right.shape[1] // 2
        part = lax.dynamic_slice_in_dim(right, (1 - core) * columns, columns, 1)
        return outer_sum(part, left).astype(jnp.bfloat16)

    def ours_of(right, left, theirs):
        columns = right.shape[1] // 2
        sent = lax.ppermute(theirs, "core", swap)
        part = lax.dynamic_slice_in_dim(right, core * columns, columns, 1)
        return (outer_sum(part, left) + sent.astype(jnp.float32)).astype(jnp.bfloat16)

    def over_outer(values):
        return lax.psum_scatter(values, ("y", "x"), scatter_dimension=0, tiled=True)

    def over_shard(values):
        columns = values.shape[1] // shards
        total = lax.dynamic_slice_in_dim(values, shard * columns, columns, 1).astype(jnp.float32)
        for distance in (1, 2, 3):
            away = lax.dynamic_slice_in_dim(
                values, lax.rem(shard + distance, shards) * columns, columns, 1
            )
            total += hop(away, distance).astype(jnp.float32)
        return total.astype(jnp.bfloat16)

    down_theirs = theirs_of(grad_feed_low, activated_low)
    grad_activated = back_project(after(grad_feed_low, down_theirs), reduce_matrix)
    grad_upward = gelu_pull(grad_activated)[0].astype(jnp.bfloat16)
    down_ours = ours_of(after(grad_feed_low, grad_upward), activated_low, down_theirs)
    down_sum = over_outer(down_ours)
    up_theirs = theirs_of(after(grad_upward, down_ours), hidden_three)
    grad_hidden_three = back_project(after(grad_upward, up_theirs), expand_matrix)
    up_ours = ours_of(after(grad_upward, grad_hidden_three), hidden_three, up_theirs)
    output = from_chip(after(result.astype(jnp.bfloat16), up_ours))
    grad_norm, gain_feed, bias_feed = norm_back(
        after(grad_hidden_three, up_ours), after_cross, parts_three, norms[4]
    )
    grad_after_cross = grad_result + grad_norm
    grad_cross_low = grad_after_cross.astype(jnp.bfloat16)
    merge_theirs = theirs_of(grad_cross_low, cross_mixed)
    grad_cross_mixed = back_project(after(grad_cross_low, merge_theirs), merge_matrix).astype(
        jnp.bfloat16
    )
    probe_grads, lookup_grads, content_grads = cross_attend_back(
        probes, lookups, contents, present, grad_cross_mixed
    )
    up_sum = over_outer(up_ours)
    down_piece = over_shard(down_sum)
    text_mine = jnp.where(first_core, lookup_grads, content_grads)
    text_sent = lax.ppermute(
        jnp.where(first_core, content_grads, lookup_grads), "core", swap
    )
    text_mine = (text_mine.astype(jnp.float32) + text_sent.astype(jnp.float32)).astype(
        jnp.bfloat16
    )
    merge_ours = ours_of(after(grad_cross_low, probe_grads), cross_mixed, merge_theirs)
    probe_theirs = theirs_of(after(probe_grads, merge_ours), hidden_two)
    grad_hidden_two = back_project(after(probe_grads, probe_theirs), probe_matrix)
    text_four = jnp.zeros((4, text_len, width), jnp.bfloat16)
    text_four = lax.dynamic_update_index_in_dim(text_four, text_mine, shard, 0)
    for distance in (1, 2, 3):
        text_four = lax.dynamic_update_index_in_dim(
            text_four,
            hop(text_mine, distance),
            lax.rem(shard + shards - distance, shards),
            0,
        )
    text_four = text_four.reshape(4 * text_len, width)
    grad_norm, gain_cross, bias_cross = norm_back(
        grad_hidden_two, after_self, parts_two, norms[2]
    )
    grad_after_self = grad_after_cross + grad_norm
    grad_self_low = grad_after_self.astype(jnp.bfloat16)
    output_theirs = theirs_of(grad_self_low, mixed_self)
    grad_mixed = back_project(after(grad_self_low, output_theirs), output_matrix).astype(
        jnp.bfloat16
    )
    probe_ours = ours_of(after(probe_grads, grad_mixed), hidden_two, probe_theirs)
    text_weights = outer_sum(text_four, text_all).astype(jnp.bfloat16)
    text_back = back_project(text_four, text_matrix).astype(jnp.bfloat16)
    output_ours = ours_of(after(grad_self_low, probe_ours), mixed_self, output_theirs)
    text_rows = width // outers
    middle = jnp.concatenate(
        [
            values.reshape(outers, -1, width)
            for values in (
                output_ours,
                probe_ours,
                merge_ours,
                text_weights.reshape(outers, shards, text_rows // shards, block)
                .transpose(0, 2, 1, 3)
                .reshape(outers, text_rows // shards, width),
            )
        ],
        axis=1,
    )
    middle_rows = middle.shape[1]
    middle = middle.reshape(outers * middle_rows, width)
    middle_sum = over_outer(middle)
    text_split = text_rows // shards
    text_piece = (
        middle_sum[middle_rows - text_split :]
        .reshape(text_split, shards, block)
        .transpose(1, 0, 2)
        .reshape(text_rows, block)
    )
    grad_queries, grad_keys, grad_values = self_attend_back(
        places, queries, keys, values, mixed_self, after(grad_mixed, middle, down_piece, output), lse
    )
    up_piece = over_shard(after(up_sum, down_piece, grad_queries))

    text_back = text_back.reshape(2, 2, text_len, block)
    text_kept = lax.dynamic_index_in_dim(text_back, core, 0, keepdims=False)
    text_gone = lax.dynamic_index_in_dim(text_back, 1 - core, 0, keepdims=False)
    text_own = text_kept.astype(jnp.float32) + lax.ppermute(text_gone, "core", swap).astype(
        jnp.float32
    )
    text_own = text_own.astype(jnp.bfloat16)
    text_grad = jnp.zeros(text_states.shape, jnp.float32)
    text_grad = lax.dynamic_update_slice_in_dim(
        text_grad, text_own.astype(jnp.float32), shard * block, 2
    )
    for distance in (1, 2, 3):
        text_grad = lax.dynamic_update_slice_in_dim(
            text_grad,
            hop(text_own, distance).astype(jnp.float32),
            lax.rem(shard + shards - distance, shards) * block,
            2,
        )

    def gather_sum(grads):
        quarters = [grads[i * block : (i + 1) * block] for i in range(4)]
        outside = jnp.concatenate([quarters[0], quarters[3]], axis=0)
        inside = jnp.concatenate([quarters[1], quarters[2]], axis=0)
        mine = jnp.where(first_core, outside, inside)
        other = lax.ppermute(jnp.where(first_core, inside, outside), "core", swap)
        return (mine.astype(jnp.float32) + other.astype(jnp.float32)).astype(jnp.bfloat16)

    qkv_grads = jnp.concatenate(
        [grad_queries, gather_sum(grad_keys), gather_sum(grad_values)], axis=1
    )
    qkv_theirs = theirs_of(after(qkv_grads, text_grad), hidden_one)
    grad_hidden_one = back_project(after(qkv_grads, qkv_theirs), qkv_matrix)
    qkv_ours = ours_of(after(qkv_grads, grad_hidden_one, up_piece), hidden_one, qkv_theirs)
    qkv_sum = over_outer(qkv_ours)
    grad_norm, gain_self, bias_self = norm_back(
        after(grad_hidden_one, qkv_ours), inputs, parts_one, norms[0]
    )
    frames_grad = from_chip((grad_after_self + grad_norm).astype(jnp.bfloat16)).astype(
        jnp.float32
    )

    small = jnp.stack(
        [
            gain_self,
            bias_self,
            gain_cross,
            bias_cross,
            gain_feed,
            bias_feed,
            jnp.full((width,), squares),
            jnp.zeros((width,), jnp.float32),
        ]
    )
    for axis, pairs in (
        ("core", swap),
        ("x", swap),
        ("y", swap),
        ("shard", [(0, 1), (1, 0), (2, 3), (3, 2)]),
        ("shard", [(0, 2), (2, 0), (1, 3), (3, 1)]),
    ):
        small += lax.ppermute(small, axis, pairs)
    loss = small[6, 0] / (width * count)
    small_own = lax.dynamic_slice_in_dim(small, shard * block, block, 1)

    middle_sum = after(middle_sum, up_piece, frames_grad)
    middle_piece = over_shard(middle_sum[: middle_rows - text_split])
    early = jnp.concatenate(
        [up_piece]
        + [down_piece[:, i * block : (i + 1) * block] for i in range(4)]
        + [text_piece, middle_piece],
        axis=0,
    )
    early = lax.all_gather(early, REPLICAS, axis=0)
    piece = width // replicas
    square = (block, width)
    up_grad = unpack(early, hidden_units // replicas, 0, (block, hidden_units), 0, 1)
    at = hidden_units // replicas // piece
    down_grad = unpack(early, piece, at, (4 * block, width), 0, 2)
    at += 4
    key_grad = unpack(early, text_rows, at * piece // text_rows, square, 0, 1)
    value_grad = unpack(early, text_rows, at * piece // text_rows, square, 4, 1)
    at += text_rows // piece
    output_grad = unpack(early, piece, at, square, 0, 2)
    probe_grad = unpack(early, piece, at + 1, square, 0, 2)
    merge_grad = unpack(early, piece, at + 2, square, 0, 2)
    late = over_shard(after(qkv_sum, middle_piece))
    late = lax.all_gather(after(late, small, early), REPLICAS, axis=0, tiled=True)
    late = late.reshape(3, width, block)
    qkv_grad = [late[i].T.astype(jnp.float32) for i in range(3)]
    return (
        output,
        loss,
        frames_grad,
        text_grad,
        small_own[0],
        small_own[1],
        qkv_grad[0],
        qkv_grad[1],
        qkv_grad[2],
        output_grad,
        small_own[2],
        small_own[3],
        probe_grad,
        key_grad,
        value_grad,
        merge_grad,
        small_own[4],
        small_own[5],
        up_grad,
        down_grad,
    )


def solution(mesh):
    by_chip = mesh.shape["shard"] == 4 and mesh.shape["replica"] == 8
    replica = ("y", "x", "core") if by_chip else "replica"
    row = P(replica)
    clip = P(replica, "shard", None)
    text = P(replica, None, None)
    vector = P("shard")
    matrix = P("shard", None)
    weights = (
        [vector, vector] + [matrix] * 4 + [vector, vector] + [matrix] * 4 + [vector, vector]
        + [matrix] * 2
    )
    if by_chip:
        mesh = Mesh(mesh.devices.reshape(2, 2, 2, 4), ("y", "x", "core", "shard"))
    return jax.shard_map(
        clip_body if by_chip else general_body,
        mesh=mesh,
        in_specs=(clip, text, P(replica, None), row, row, clip, *weights),
        out_specs=(clip, P(), clip, text, *weights),
        check_vma=False,
    )
```

```python
import jax
import jax.numpy as jnp
from jax import lax
from jax.experimental import pallas as pl
from jax.experimental.pallas import tpu as pltpu
from jax.sharding import Mesh
from jax.sharding import PartitionSpec as P

HEADS = 24
HEAD_DIM = 64


epsilon = 1e-05
masked_score = -1e30


def layer_norm(values, gain, shift):
    center = values - jnp.mean(values, axis=-1, keepdims=True)
    variance = jnp.mean(center * center, axis=-1, keepdims=True)
    return center * lax.rsqrt(variance + epsilon) * gain + shift


def exact_gelu(values):
    return jax.nn.gelu(values, approximate=False)


def project(left, right):
    return jnp.dot(left, right, preferred_element_type=jnp.float32)


def outer_sum(left, right):
    return jnp.einsum("rd,re->de", left, right, preferred_element_type=jnp.float32)


def back_project(grads, matrix):
    return jnp.einsum("re,de->rd", grads, matrix, preferred_element_type=jnp.float32)


def split_heads(values):
    return values.reshape(values.shape[:-1] + (HEADS, HEAD_DIM))


def self_forward(operands):
    queries, keys_all, values_all, allowed = operands
    scale = HEAD_DIM ** (-0.5)
    scores = (
        jnp.einsum("qhd,khd->hqk", queries, keys_all, preferred_element_type=jnp.float32) * scale
    )
    scores = jnp.where(allowed[None], scores, masked_score)
    peak = jnp.max(scores, axis=-1, keepdims=True)
    weights = jnp.exp(scores - peak)
    totals = jnp.sum(weights, axis=-1, keepdims=True)
    probs = (weights / totals).astype(jnp.bfloat16)
    mixed = jnp.einsum("hqk,khd->qhd", probs, values_all, preferred_element_type=jnp.float32)
    return (mixed.astype(jnp.bfloat16), (peak + jnp.log(totals))[..., 0])


def self_backward(operands):
    queries, keys_all, values_all, allowed, log_totals, grad_mixed = operands
    scale = HEAD_DIM ** (-0.5)
    scores = (
        jnp.einsum("qhd,khd->hqk", queries, keys_all, preferred_element_type=jnp.float32) * scale
    )
    scores = jnp.where(allowed[None], scores, masked_score)
    probs = jnp.exp(scores - log_totals[..., None])
    grad_probs = jnp.einsum(
        "qhd,khd->hqk", grad_mixed, values_all, preferred_element_type=jnp.float32
    )
    grad_values = jnp.einsum(
        "hqk,qhd->khd", probs.astype(jnp.bfloat16), grad_mixed, preferred_element_type=jnp.float32
    )
    inner = jnp.sum(probs * grad_probs, axis=-1, keepdims=True)
    grad_scores = (probs * (grad_probs - inner)).astype(jnp.bfloat16)
    grad_queries = (
        jnp.einsum("hqk,khd->qhd", grad_scores, keys_all, preferred_element_type=jnp.float32)
        * scale
    ).astype(jnp.bfloat16)
    grad_keys = (
        jnp.einsum("hqk,qhd->khd", grad_scores, queries, preferred_element_type=jnp.float32) * scale
    )
    return (grad_queries, grad_keys, grad_values)


def general_body(
    frames,
    text_states,
    text_mask,
    clip_lengths,
    slot_used,
    teacher,
    self_norm_gain,
    self_norm_bias,
    self_query_weight,
    self_key_weight,
    self_value_weight,
    self_output_weight,
    cross_norm_gain,
    cross_norm_bias,
    cross_query_weight,
    cross_key_weight,
    cross_value_weight,
    cross_output_weight,
    feed_norm_gain,
    feed_norm_bias,
    feed_up_weight,
    feed_down_weight,
):
    gathered = (
        lax.all_gather(self_norm_gain, "shard", axis=0, tiled=True),
        lax.all_gather(self_norm_bias, "shard", axis=0, tiled=True),
        lax.all_gather(self_query_weight, "shard", axis=0, tiled=True),
        lax.all_gather(self_key_weight, "shard", axis=0, tiled=True),
        lax.all_gather(self_value_weight, "shard", axis=0, tiled=True),
        lax.all_gather(self_output_weight, "shard", axis=0, tiled=True),
        lax.all_gather(cross_norm_gain, "shard", axis=0, tiled=True),
        lax.all_gather(cross_norm_bias, "shard", axis=0, tiled=True),
        lax.all_gather(cross_query_weight, "shard", axis=0, tiled=True),
        lax.all_gather(cross_key_weight, "shard", axis=0, tiled=True),
        lax.all_gather(cross_value_weight, "shard", axis=0, tiled=True),
        lax.all_gather(cross_output_weight, "shard", axis=0, tiled=True),
        lax.all_gather(feed_norm_gain, "shard", axis=0, tiled=True),
        lax.all_gather(feed_norm_bias, "shard", axis=0, tiled=True),
        lax.all_gather(feed_up_weight, "shard", axis=0, tiled=True),
        lax.all_gather(feed_down_weight, "shard", axis=0, tiled=True),
    )
    (
        gain_attend,
        bias_attend,
        query_matrix,
        key_matrix,
        value_matrix,
        output_matrix,
        gain_cross,
        bias_cross,
        probe_matrix,
        lookup_matrix,
        content_matrix,
        merge_matrix,
        gain_feed,
        bias_feed,
        expand_matrix,
        reduce_matrix,
    ) = gathered
    slots = frames.shape[0]
    frame_count = frames.shape[1]
    width = frames.shape[2]
    text_len = text_states.shape[1]
    shards = lax.axis_size("shard")
    replicas = lax.axis_size("replica")
    clip_total = frame_count * shards
    row_count = slots * frame_count
    scale = HEAD_DIM ** (-0.5)
    shard_rank = lax.axis_index("shard")
    positions = shard_rank * frame_count + jnp.arange(frame_count, dtype=jnp.int32)
    key_positions = jnp.arange(clip_total, dtype=jnp.int32)
    allowed = (key_positions[None, None, :] <= positions[None, :, None]) & (
        key_positions[None, None, :] < clip_lengths[:, None, None]
    )
    valid_rows = ((positions[None, :] < clip_lengths[:, None]) & (slot_used[:, None] > 0)).astype(
        jnp.float32
    )
    text_allowed = text_mask > 0
    inputs = frames.astype(jnp.float32)
    normed_one, pull_one = jax.vjp(
        layer_norm, inputs, gain_attend.astype(jnp.float32), bias_attend.astype(jnp.float32)
    )
    hidden_one = normed_one.astype(jnp.bfloat16).reshape(row_count, width)
    queries = (
        project(hidden_one, query_matrix).astype(jnp.bfloat16).reshape(slots, frame_count, width)
    )
    keys_local = (
        project(hidden_one, key_matrix).astype(jnp.bfloat16).reshape(slots, frame_count, width)
    )
    values_local = (
        project(hidden_one, value_matrix).astype(jnp.bfloat16).reshape(slots, frame_count, width)
    )
    keys_all, values_all = (
        lax.all_gather(keys_local, "shard", axis=1, tiled=True),
        lax.all_gather(values_local, "shard", axis=1, tiled=True),
    )
    head_queries = split_heads(queries)
    head_keys = split_heads(keys_all)
    head_values = split_heads(values_all)
    mixed_self, log_totals = lax.map(self_forward, (head_queries, head_keys, head_values, allowed))
    mixed_rows = mixed_self.reshape(row_count, width)
    after_self = inputs + project(mixed_rows, output_matrix).reshape(slots, frame_count, width)
    normed_two, pull_two = jax.vjp(
        layer_norm, after_self, gain_cross.astype(jnp.float32), bias_cross.astype(jnp.float32)
    )
    hidden_two = normed_two.astype(jnp.bfloat16).reshape(row_count, width)
    probes = split_heads(
        project(hidden_two, probe_matrix).astype(jnp.bfloat16).reshape(slots, frame_count, width)
    )
    text_rows = text_states.reshape(slots * text_len, width)
    lookups = split_heads(
        project(text_rows, lookup_matrix).astype(jnp.bfloat16).reshape(slots, text_len, width)
    )
    contents = split_heads(
        project(text_rows, content_matrix).astype(jnp.bfloat16).reshape(slots, text_len, width)
    )
    cross_scores = (
        jnp.einsum("sqhd,skhd->shqk", probes, lookups, preferred_element_type=jnp.float32) * scale
    )
    cross_scores = jnp.where(text_allowed[:, None, None, :], cross_scores, masked_score)
    cross_peak = jnp.max(cross_scores, axis=-1, keepdims=True)
    cross_weights = jnp.exp(cross_scores - cross_peak)
    cross_probs = cross_weights / jnp.sum(cross_weights, axis=-1, keepdims=True)
    cross_probs_low = cross_probs.astype(jnp.bfloat16)
    cross_mixed = jnp.einsum(
        "shqk,skhd->sqhd", cross_probs_low, contents, preferred_element_type=jnp.float32
    )
    cross_mixed = cross_mixed.astype(jnp.bfloat16).reshape(row_count, width)
    after_cross = after_self + project(cross_mixed, merge_matrix).reshape(slots, frame_count, width)
    normed_three, pull_three = jax.vjp(
        layer_norm, after_cross, gain_feed.astype(jnp.float32), bias_feed.astype(jnp.float32)
    )
    hidden_three = normed_three.astype(jnp.bfloat16).reshape(row_count, width)
    upward = project(hidden_three, expand_matrix)
    activated, gelu_pull = jax.vjp(exact_gelu, upward)
    activated_low = activated.astype(jnp.bfloat16)
    result = after_cross + project(activated_low, reduce_matrix).reshape(slots, frame_count, width)
    output = result.astype(jnp.bfloat16)
    errors = (result - teacher.astype(jnp.float32)) * valid_rows[..., None]
    squares_total, count_total = lax.psum(
        (jnp.sum(errors * errors), jnp.sum(valid_rows)), ("replica", "shard")
    )
    loss = squares_total / (width * count_total)
    grad_result = errors * (slots * replicas * clip_total / count_total)
    grad_feed_low = grad_result.reshape(row_count, width).astype(jnp.bfloat16)
    grad_activated = back_project(grad_feed_low, reduce_matrix)
    grad_upward = gelu_pull(grad_activated)[0].astype(jnp.bfloat16)
    grad_hidden_three = back_project(grad_upward, expand_matrix).reshape(slots, frame_count, width)
    grad_cross_norm, gain_feed_part, bias_feed_part = pull_three(grad_hidden_three)
    grad_after_cross = grad_result + grad_cross_norm
    feed_owned = (
        lax.psum_scatter(
            outer_sum(hidden_three, grad_upward).astype(jnp.bfloat16),
            "shard",
            scatter_dimension=0,
            tiled=True,
        ).astype(jnp.float32),
        lax.psum_scatter(
            outer_sum(activated_low, grad_feed_low).astype(jnp.bfloat16),
            "shard",
            scatter_dimension=0,
            tiled=True,
        ).astype(jnp.float32),
        lax.psum_scatter(
            gain_feed_part.astype(jnp.bfloat16), "shard", scatter_dimension=0, tiled=True
        ).astype(jnp.float32),
        lax.psum_scatter(
            bias_feed_part.astype(jnp.bfloat16), "shard", scatter_dimension=0, tiled=True
        ).astype(jnp.float32),
    )
    grad_cross_low = grad_after_cross.reshape(row_count, width).astype(jnp.bfloat16)
    grad_cross_mixed = split_heads(
        back_project(grad_cross_low, merge_matrix)
        .astype(jnp.bfloat16)
        .reshape(slots, frame_count, width)
    )
    grad_cross_probs = jnp.einsum(
        "sqhd,skhd->shqk", grad_cross_mixed, contents, preferred_element_type=jnp.float32
    )
    content_grads = jnp.einsum(
        "shqk,sqhd->skhd", cross_probs_low, grad_cross_mixed, preferred_element_type=jnp.float32
    )
    cross_inner = jnp.sum(cross_probs * grad_cross_probs, axis=-1, keepdims=True)
    grad_cross_scores = (cross_probs * (grad_cross_probs - cross_inner)).astype(jnp.bfloat16)
    probe_grads = (
        jnp.einsum(
            "shqk,skhd->sqhd", grad_cross_scores, lookups, preferred_element_type=jnp.float32
        )
        * scale
    )
    probe_grads = probe_grads.astype(jnp.bfloat16).reshape(row_count, width)
    lookup_grads = (
        jnp.einsum("shqk,sqhd->skhd", grad_cross_scores, probes, preferred_element_type=jnp.float32)
        * scale
    )
    lookup_sum, content_sum = (
        lax.psum(lookup_grads.astype(jnp.bfloat16), "shard").astype(jnp.float32),
        lax.psum(content_grads.astype(jnp.bfloat16), "shard").astype(jnp.float32),
    )
    lookup_low = lookup_sum.astype(jnp.bfloat16).reshape(slots * text_len, width)
    content_low = content_sum.astype(jnp.bfloat16).reshape(slots * text_len, width)
    own_width = width // shards
    own_text = lax.dynamic_slice_in_dim(text_rows, shard_rank * own_width, own_width, 1)
    lookup_own = outer_sum(own_text, lookup_low)
    content_own = outer_sum(own_text, content_low)
    text_grad = (
        back_project(lookup_low, lookup_matrix) + back_project(content_low, content_matrix)
    ).reshape(slots, text_len, width)
    grad_hidden_two = back_project(probe_grads, probe_matrix).reshape(slots, frame_count, width)
    grad_self_norm, gain_cross_part, bias_cross_part = pull_two(grad_hidden_two)
    grad_after_self = grad_after_cross + grad_self_norm
    grad_self_low = grad_after_self.reshape(row_count, width).astype(jnp.bfloat16)
    grad_mixed = split_heads(
        back_project(grad_self_low, output_matrix)
        .astype(jnp.bfloat16)
        .reshape(slots, frame_count, width)
    )
    grad_queries, grad_keys, grad_values = lax.map(
        self_backward, (head_queries, head_keys, head_values, allowed, log_totals, grad_mixed)
    )
    key_sum, value_sum = (
        lax.psum_scatter(
            grad_keys.reshape(slots, clip_total, width).astype(jnp.bfloat16),
            "shard",
            scatter_dimension=1,
            tiled=True,
        ).astype(jnp.float32),
        lax.psum_scatter(
            grad_values.reshape(slots, clip_total, width).astype(jnp.bfloat16),
            "shard",
            scatter_dimension=1,
            tiled=True,
        ).astype(jnp.float32),
    )
    key_low = key_sum.astype(jnp.bfloat16).reshape(row_count, width)
    value_low = value_sum.astype(jnp.bfloat16).reshape(row_count, width)
    query_low = grad_queries.reshape(row_count, width)
    grad_hidden_one = (
        back_project(query_low, query_matrix)
        + back_project(key_low, key_matrix)
        + back_project(value_low, value_matrix)
    )
    grad_inputs, gain_attend_part, bias_attend_part = pull_one(
        grad_hidden_one.reshape(slots, frame_count, width)
    )
    frames_grad = grad_after_self + grad_inputs
    attend_owned = (
        lax.psum_scatter(
            outer_sum(hidden_one, query_low).astype(jnp.bfloat16),
            "shard",
            scatter_dimension=0,
            tiled=True,
        ).astype(jnp.float32),
        lax.psum_scatter(
            outer_sum(hidden_one, key_low).astype(jnp.bfloat16),
            "shard",
            scatter_dimension=0,
            tiled=True,
        ).astype(jnp.float32),
        lax.psum_scatter(
            outer_sum(hidden_one, value_low).astype(jnp.bfloat16),
            "shard",
            scatter_dimension=0,
            tiled=True,
        ).astype(jnp.float32),
        lax.psum_scatter(
            outer_sum(mixed_rows, grad_self_low).astype(jnp.bfloat16),
            "shard",
            scatter_dimension=0,
            tiled=True,
        ).astype(jnp.float32),
        lax.psum_scatter(
            outer_sum(hidden_two, probe_grads).astype(jnp.bfloat16),
            "shard",
            scatter_dimension=0,
            tiled=True,
        ).astype(jnp.float32),
        lax.psum_scatter(
            outer_sum(cross_mixed, grad_cross_low).astype(jnp.bfloat16),
            "shard",
            scatter_dimension=0,
            tiled=True,
        ).astype(jnp.float32),
        lax.psum_scatter(
            gain_attend_part.astype(jnp.bfloat16), "shard", scatter_dimension=0, tiled=True
        ).astype(jnp.float32),
        lax.psum_scatter(
            bias_attend_part.astype(jnp.bfloat16), "shard", scatter_dimension=0, tiled=True
        ).astype(jnp.float32),
        lax.psum_scatter(
            gain_cross_part.astype(jnp.bfloat16), "shard", scatter_dimension=0, tiled=True
        ).astype(jnp.float32),
        lax.psum_scatter(
            bias_cross_part.astype(jnp.bfloat16), "shard", scatter_dimension=0, tiled=True
        ).astype(jnp.float32),
    )
    summed = (
        lax.psum(attend_owned[6].astype(jnp.bfloat16), "replica").astype(jnp.float32),
        lax.psum(attend_owned[7].astype(jnp.bfloat16), "replica").astype(jnp.float32),
        lax.psum(attend_owned[0].astype(jnp.bfloat16), "replica").astype(jnp.float32),
        lax.psum(attend_owned[1].astype(jnp.bfloat16), "replica").astype(jnp.float32),
        lax.psum(attend_owned[2].astype(jnp.bfloat16), "replica").astype(jnp.float32),
        lax.psum(attend_owned[3].astype(jnp.bfloat16), "replica").astype(jnp.float32),
        lax.psum(attend_owned[8].astype(jnp.bfloat16), "replica").astype(jnp.float32),
        lax.psum(attend_owned[9].astype(jnp.bfloat16), "replica").astype(jnp.float32),
        lax.psum(attend_owned[4].astype(jnp.bfloat16), "replica").astype(jnp.float32),
        lax.psum(lookup_own.astype(jnp.bfloat16), "replica").astype(jnp.float32),
        lax.psum(content_own.astype(jnp.bfloat16), "replica").astype(jnp.float32),
        lax.psum(attend_owned[5].astype(jnp.bfloat16), "replica").astype(jnp.float32),
        lax.psum(feed_owned[2].astype(jnp.bfloat16), "replica").astype(jnp.float32),
        lax.psum(feed_owned[3].astype(jnp.bfloat16), "replica").astype(jnp.float32),
        lax.psum(feed_owned[0].astype(jnp.bfloat16), "replica").astype(jnp.float32),
        lax.psum(feed_owned[1].astype(jnp.bfloat16), "replica").astype(jnp.float32),
    )
    return (
        output,
        loss,
        frames_grad,
        text_grad,
        summed[0],
        summed[1],
        summed[2],
        summed[3],
        summed[4],
        summed[5],
        summed[6],
        summed[7],
        summed[8],
        summed[9],
        summed[10],
        summed[11],
        summed[12],
        summed[13],
        summed[14],
        summed[15],
    )


PAIR = 2 * HEAD_DIM
EVERY = ("shard", "y", "x", "core")
REPLICAS = ("core", "y", "x")
NT = (((1,), (1,)), ((), ()))
TN = (((0,), (0,)), ((), ()))
NN = (((1,), (0,)), ((), ()))


def dot(left, right, dims):
    return lax.dot_general(left, right, dims, preferred_element_type=jnp.float32)


def half_mask(side, value):
    lanes = lax.broadcasted_iota(jnp.int32, (1, PAIR), 1)
    inside = (lanes >= HEAD_DIM) if side else (lanes < HEAD_DIM)
    return jnp.where(inside, value, 0.0).astype(jnp.bfloat16)


def fill_clip(place, own_ref, other_ref, all_ref):
    block = own_ref.shape[0] // 2
    for part in range(2):
        rows = slice(part * block, (part + 1) * block)
        for at, ref in ((place[part], own_ref), (place[3 + part], other_ref)):
            all_ref[pl.ds(pl.multiple_of(at * block, block), block), :] = ref[rows, :]


def self_forward_kernel(
    place, q_ref, own_k, own_v, other_k, other_v, mixed_ref, lse_ref, k_ref, v_ref, acc_ref
):
    fill_clip(place, own_k, other_k, k_ref)
    fill_clip(place, own_v, other_v, v_ref)
    block = q_ref.shape[0] // 2
    length = place[2]
    low = lax.broadcasted_iota(jnp.int32, (PAIR, 1), 0) < HEAD_DIM
    for part in range(2):
        first = place[part] * block
        rows = slice(part * block, (part + 1) * block)
        q = q_ref[rows, :]
        q_half = [q * half_mask(side, HEAD_DIM ** (-0.5)) for side in range(2)]
        limit = jnp.minimum(
            first + lax.broadcasted_iota(jnp.int32, (1, block), 1) + 1, length
        )
        acc_ref[...] = jnp.zeros_like(acc_ref)

        def step(j, peaks, q_half=q_half, limit=limit):
            at = pl.multiple_of(j * block, block)
            k = k_ref[pl.ds(at, block), :]
            v = v_ref[pl.ds(at, block), :]
            allowed = at + lax.broadcasted_iota(jnp.int32, (block, block), 0) < limit
            out = []
            for side in range(2):
                scores = jnp.where(allowed, dot(k, q_half[side], NT), masked_score)
                peak = jnp.maximum(peaks[side], jnp.max(scores, axis=0, keepdims=True))
                weights = jnp.exp(scores - peak).astype(jnp.bfloat16)
                v_ones = v * half_mask(side, 1.0) + half_mask(1 - side, 1.0)
                acc_ref[side] = acc_ref[side] * jnp.exp(peaks[side] - peak) + dot(
                    v_ones, weights, TN
                )
                out.append(peak)
            return tuple(out)

        peaks = lax.fori_loop(
            0, place[part] + 1, step, (jnp.full((1, block), masked_score, jnp.float32),) * 2
        )
        top, bottom = acc_ref[0], acc_ref[1]
        total = jnp.where(low, top[HEAD_DIM : HEAD_DIM + 1], bottom[0:1])
        mixed = jnp.where(low, top, bottom) / total
        mixed_ref[rows, :] = mixed.T.astype(jnp.bfloat16)
        lse_ref[0:1, rows] = peaks[0] + jnp.log(top[HEAD_DIM : HEAD_DIM + 1])
        lse_ref[1:2, rows] = peaks[1] + jnp.log(bottom[0:1])


def self_backward_kernel(
    place, q_ref, own_k, own_v, other_k, other_v, mixed_ref, grad_ref, lse_ref,
    dq_ref, own_dk, own_dv, other_dk, other_dv, k_ref, v_ref, dq_acc, dk_acc, dv_acc,
):
    fill_clip(place, own_k, other_k, k_ref)
    fill_clip(place, own_v, other_v, v_ref)
    block = q_ref.shape[0] // 2
    length = place[2]
    scale = HEAD_DIM ** (-0.5)
    dk_acc[...] = jnp.zeros_like(dk_acc)
    dv_acc[...] = jnp.zeros_like(dv_acc)
    for part in range(2):
        first = place[part] * block
        rows = slice(part * block, (part + 1) * block)
        q = q_ref[rows, :]
        grad = grad_ref[rows, :]
        q_half = [q * half_mask(side, scale) for side in range(2)]
        grad_half = [grad * half_mask(side, 1.0) for side in range(2)]
        product = (grad.astype(jnp.float32) * mixed_ref[rows, :].astype(jnp.float32)).T
        inner = [
            jnp.sum(product[side * HEAD_DIM : (side + 1) * HEAD_DIM], axis=0, keepdims=True)
            for side in range(2)
        ]
        lse = [lse_ref[side : side + 1, rows] for side in range(2)]
        limit = jnp.minimum(
            first + lax.broadcasted_iota(jnp.int32, (1, block), 1) + 1, length
        )
        dq_acc[...] = jnp.zeros_like(dq_acc)

        def step(
            j, carry, q_half=q_half, grad_half=grad_half, inner=inner, lse=lse, limit=limit
        ):
            at = pl.multiple_of(j * block, block)
            k = k_ref[pl.ds(at, block), :]
            v = v_ref[pl.ds(at, block), :]
            allowed = at + lax.broadcasted_iota(jnp.int32, (block, block), 0) < limit
            dq, dk, dv = 0.0, 0.0, 0.0
            for side in range(2):
                scores = jnp.where(allowed, dot(k, q_half[side], NT), masked_score)
                probs = jnp.exp(scores - lse[side])
                grad_probs = dot(v, grad_half[side], NT)
                grad_scores = (probs * (grad_probs - inner[side])).astype(jnp.bfloat16)
                dv += dot(probs.astype(jnp.bfloat16), grad_half[side], NN)
                dk += dot(grad_scores, q_half[side], NN)
                dq += dot(k * half_mask(side, scale), grad_scores, TN)
            dk_acc[pl.ds(at, block), :] += dk
            dv_acc[pl.ds(at, block), :] += dv
            dq_acc[...] += dq
            return carry

        lax.fori_loop(0, place[part] + 1, step, 0)
        dq_ref[rows, :] = dq_acc[...].T.astype(jnp.bfloat16)
    for part in range(2):
        rows = slice(part * block, (part + 1) * block)
        own = pl.ds(pl.multiple_of(place[part] * block, block), block)
        other = pl.ds(pl.multiple_of(place[3 + part] * block, block), block)
        own_dk[rows, :] = dk_acc[own, :].astype(jnp.bfloat16)
        own_dv[rows, :] = dv_acc[own, :].astype(jnp.bfloat16)
        other_dk[rows, :] = dk_acc[other, :].astype(jnp.bfloat16)
        other_dv[rows, :] = dv_acc[other, :].astype(jnp.bfloat16)


def pair_block(rows):
    return pl.BlockSpec((rows, PAIR), lambda i, *_: (0, i))


def value_block(rows, pairs):
    return pl.BlockSpec((rows, PAIR), lambda i, *_: (0, pairs + i))


def self_attend(place, queries, own, other):
    rows, width = queries.shape
    clip = 2 * rows
    pairs = width // PAIR
    return pl.pallas_call(
        self_forward_kernel,
        out_shape=(
            jax.ShapeDtypeStruct((rows, width), jnp.bfloat16),
            jax.ShapeDtypeStruct((pairs * 8, rows), jnp.float32),
        ),
        grid_spec=pltpu.PrefetchScalarGridSpec(
            num_scalar_prefetch=1,
            grid=(pairs,),
            in_specs=[pair_block(rows)] + [pair_block(rows), value_block(rows, pairs)] * 2,
            out_specs=(pair_block(rows), pl.BlockSpec((8, rows), lambda i, *_: (i, 0))),
            scratch_shapes=[
                pltpu.VMEM((clip, PAIR), jnp.bfloat16),
                pltpu.VMEM((clip, PAIR), jnp.bfloat16),
                pltpu.VMEM((2, PAIR, rows // 2), jnp.float32),
            ],
        ),
        compiler_params=pltpu.CompilerParams(vmem_limit_bytes=32 * 2**20),
        cost_estimate=pl.CostEstimate(
            flops=2 * 2 * rows * clip * width, bytes_accessed=8 * clip * width, transcendentals=0
        ),
        name="self_attend",
    )(place, queries, own, own, other, other)


def self_attend_back(place, queries, own, other, mixed, grads, lse):
    rows, width = queries.shape
    clip = 2 * rows
    pairs = width // PAIR
    return pl.pallas_call(
        self_backward_kernel,
        out_shape=(jax.ShapeDtypeStruct((rows, width), jnp.bfloat16),) * 5,
        grid_spec=pltpu.PrefetchScalarGridSpec(
            num_scalar_prefetch=1,
            grid=(pairs,),
            in_specs=[pair_block(rows)]
            + [pair_block(rows), value_block(rows, pairs)] * 2
            + [
                pair_block(rows),
                pair_block(rows),
                pl.BlockSpec((8, rows), lambda i, *_: (i, 0)),
            ],
            out_specs=(pair_block(rows),) * 5,
            scratch_shapes=[
                pltpu.VMEM((clip, PAIR), jnp.bfloat16),
                pltpu.VMEM((clip, PAIR), jnp.bfloat16),
                pltpu.VMEM((PAIR, rows // 2), jnp.float32),
                pltpu.VMEM((clip, PAIR), jnp.float32),
                pltpu.VMEM((clip, PAIR), jnp.float32),
            ],
        ),
        compiler_params=pltpu.CompilerParams(vmem_limit_bytes=32 * 2**20),
        cost_estimate=pl.CostEstimate(
            flops=5 * 2 * rows * clip * width, bytes_accessed=16 * clip * width, transcendentals=0
        ),
        name="self_attend_back",
    )(place, queries, own, own, other, other, mixed, grads, lse)


def both_heads(rows, value):
    return jnp.concatenate([rows * half_mask(side, value) for side in range(2)], axis=0)


def cross_probs_of(lookup_two, probes, present):
    text = present.shape[0]
    scores = dot(lookup_two, probes, NT)
    out = []
    for side in range(2):
        part = jnp.where(
            present > 0, scores[side * text : (side + 1) * text], masked_score
        )
        weights = jnp.exp(part - jnp.max(part, axis=0, keepdims=True))
        out.append(weights / jnp.sum(weights, axis=0, keepdims=True))
    return out


def cross_forward_kernel(probe_ref, lookup_ref, content_ref, present_ref, mixed_ref):
    probs = cross_probs_of(
        both_heads(lookup_ref[...], HEAD_DIM ** (-0.5)), probe_ref[...], present_ref[...]
    )
    probs = jnp.concatenate(probs, axis=0).astype(jnp.bfloat16)
    mixed_ref[...] = dot(probs, both_heads(content_ref[...], 1.0), TN).astype(jnp.bfloat16)


def cross_backward_kernel(
    probe_ref, lookup_ref, content_ref, present_ref, grad_ref, dp_ref, dl_ref, dc_ref
):
    text = present_ref.shape[0]
    scale = HEAD_DIM ** (-0.5)
    probes = probe_ref[...]
    grads = grad_ref[...]
    lookup_two = both_heads(lookup_ref[...], scale)
    probs = cross_probs_of(lookup_two, probes, present_ref[...])
    grad_probs = dot(both_heads(content_ref[...], 1.0), grads, NT)
    grad_scores = []
    for side in range(2):
        part = grad_probs[side * text : (side + 1) * text]
        inner = jnp.sum(probs[side] * part, axis=0, keepdims=True)
        grad_scores.append(probs[side] * (part - inner))
    grad_scores = jnp.concatenate(grad_scores, axis=0).astype(jnp.bfloat16)
    probs = jnp.concatenate(probs, axis=0).astype(jnp.bfloat16)
    low = lax.broadcasted_iota(jnp.int32, (1, PAIR), 1) < HEAD_DIM
    dp_ref[...] = dot(grad_scores, lookup_two, TN).astype(jnp.bfloat16)
    dl = dot(grad_scores, probes, NN) * scale
    dl_ref[...] = jnp.where(low, dl[:text], dl[text:]).astype(jnp.bfloat16)
    dc = dot(probs, grads, NN)
    dc_ref[...] = jnp.where(low, dc[:text], dc[text:]).astype(jnp.bfloat16)


def cross_attend(probes, lookups, contents, present):
    rows, width = probes.shape
    text = lookups.shape[0]
    return pl.pallas_call(
        cross_forward_kernel,
        out_shape=jax.ShapeDtypeStruct((rows, width), jnp.bfloat16),
        grid=(width // PAIR,),
        in_specs=[
            pair_block(rows),
            pair_block(text),
            pair_block(text),
            pl.BlockSpec((text, 1), lambda i: (0, 0)),
        ],
        out_specs=pair_block(rows),
        compiler_params=pltpu.CompilerParams(vmem_limit_bytes=32 * 2**20),
        cost_estimate=pl.CostEstimate(
            flops=8 * rows * text * width, bytes_accessed=4 * rows * width, transcendentals=0
        ),
        name="cross_attend",
    )(probes, lookups, contents, present)


def cross_attend_back(probes, lookups, contents, present, grads):
    rows, width = probes.shape
    text = lookups.shape[0]
    return pl.pallas_call(
        cross_backward_kernel,
        out_shape=(
            jax.ShapeDtypeStruct((rows, width), jnp.bfloat16),
            jax.ShapeDtypeStruct((text, width), jnp.bfloat16),
            jax.ShapeDtypeStruct((text, width), jnp.bfloat16),
        ),
        grid=(width // PAIR,),
        in_specs=[
            pair_block(rows),
            pair_block(text),
            pair_block(text),
            pl.BlockSpec((text, 1), lambda i: (0, 0)),
            pair_block(rows),
        ],
        out_specs=(pair_block(rows), pair_block(text), pair_block(text)),
        compiler_params=pltpu.CompilerParams(vmem_limit_bytes=32 * 2**20),
        cost_estimate=pl.CostEstimate(
            flops=20 * rows * text * width, bytes_accessed=6 * rows * width, transcendentals=0
        ),
        name="cross_attend_back",
    )(probes, lookups, contents, present, grads)


def unpack_kernel(in_ref, out_ref):
    pieces = in_ref[...]
    out_ref[...] = pieces.reshape(-1, pieces.shape[-1]).T.astype(jnp.float32)


def unpack(full, rows, place, out_shape, out_at, together):
    owners, _, features = full.shape
    tall = out_shape[0] // features
    wide = out_shape[1] // (together * rows)
    return pl.pallas_call(
        unpack_kernel,
        out_shape=jax.ShapeDtypeStruct(out_shape, jnp.float32),
        grid=(tall, wide),
        in_specs=[
            pl.BlockSpec((together, rows, features), lambda i, j: (j + out_at, place + i, 0))
        ],
        out_specs=pl.BlockSpec((features, together * rows), lambda i, j: (i, j)),
        compiler_params=pltpu.CompilerParams(vmem_limit_bytes=32 * 2**20),
        cost_estimate=pl.CostEstimate(
            flops=0, bytes_accessed=6 * out_shape[0] * out_shape[1], transcendentals=0
        ),
        name="unpack",
    )(full)


def held(values, *others):
    return list(lax.optimization_barrier((*values, *others))[: len(values)])


def after(value, *others):
    return lax.optimization_barrier((value, *others))[0]


def norm_parts(values):
    mean = jnp.mean(values, axis=-1, keepdims=True)
    center = values - mean
    return mean, lax.rsqrt(jnp.mean(center * center, axis=-1, keepdims=True) + epsilon)


def norm_back(grads, values, parts, gain):
    mean, inverse = parts
    unit = (values - mean) * inverse
    gain_grad = jnp.sum(grads * unit, axis=0)
    bias_grad = jnp.sum(grads, axis=0)
    scaled = grads * gain
    back = inverse * (
        scaled
        - jnp.mean(scaled, axis=-1, keepdims=True)
        - unit * jnp.mean(scaled * unit, axis=-1, keepdims=True)
    )
    return back, gain_grad, bias_grad


def clip_body(
    frames,
    text_states,
    text_mask,
    clip_lengths,
    slot_used,
    teacher,
    self_norm_gain,
    self_norm_bias,
    self_query_weight,
    self_key_weight,
    self_value_weight,
    self_output_weight,
    cross_norm_gain,
    cross_norm_bias,
    cross_query_weight,
    cross_key_weight,
    cross_value_weight,
    cross_output_weight,
    feed_norm_gain,
    feed_norm_bias,
    feed_up_weight,
    feed_down_weight,
):
    block, width = frames.shape[1:]
    text_len = text_states.shape[1]
    shards, replicas, outers = 4, 8, 4
    core = lax.axis_index("core")
    shard = lax.axis_index("shard")
    outer = 2 * lax.axis_index("y") + lax.axis_index("x")
    replica = 2 * outer + core
    clip = block * shards
    hidden_units = feed_up_weight.shape[1]

    holder = {0: 0, 1: 1, 2: 1, 3: 0}
    there = ([], [])
    for c in range(2):
        for s in range(4):
            for turn in range(2):
                slot = turn if s < 2 else 1 - turn
                there[turn].append((c * 4 + s, holder[s] * 4 + 2 * c + slot))
    back = tuple([(b, a) for a, b in pairs] for pairs in there)
    spot = ("core", "shard")
    swap = [(0, 1), (1, 0)]
    even = shard % 2 == 0
    lower = shard < 2
    first_core = core == 0

    def hop(values, distance):
        pairs = [(i, (i + distance) % shards) for i in range(shards)]
        return lax.ppermute(values, "shard", pairs)

    def hops(values):
        return [hop(values, distance) for distance in (1, 2, 3)]

    def line_up(mine, came):
        out = jnp.zeros((shards,) + mine.shape, mine.dtype)
        out = lax.dynamic_update_index_in_dim(out, mine, shard, 0)
        for distance, values in zip((1, 2, 3), came):
            owner = lax.rem(shard + shards - distance, shards)
            out = lax.dynamic_update_index_in_dim(out, values, owner, 0)
        return out

    def to_chip(pair):
        one = lax.ppermute(jnp.where(lower, pair[0], pair[1]), spot, there[0])
        two = lax.ppermute(jnp.where(lower, pair[1], pair[0]), spot, there[1])
        return one, two

    def by_time(one, two):
        return jnp.concatenate([jnp.where(even, one, two), jnp.where(even, two, one)], axis=0)

    def from_chip(values):
        early, late = values[:block], values[block:]
        one = lax.ppermute(jnp.where(even, early, late), spot, back[0])
        two = lax.ppermute(jnp.where(even, late, early), spot, back[1])
        return one, two

    def by_slot(one, two):
        return jnp.stack([jnp.where(lower, one, two), jnp.where(lower, two, one)])

    def share_of(weight):
        share = weight.shape[0] // replicas
        return lax.dynamic_slice_in_dim(weight, replica * share, share, 0)

    def from_replicas(line):
        full = lax.all_gather(line, ("y", "x", "core"), axis=1, tiled=True)
        return full.reshape(-1, line.shape[-1])

    qkv_share = jnp.concatenate(
        [share_of(self_query_weight), share_of(self_key_weight), share_of(self_value_weight)],
        axis=1,
    )
    vectors = jnp.concatenate(
        [
            self_norm_gain,
            self_norm_bias,
            cross_norm_gain,
            cross_norm_bias,
            feed_norm_gain,
            feed_norm_bias,
        ]
    )
    vectors = jnp.pad(vectors[None, :], ((0, 15), (0, 3 * width - 6 * block)))
    qkv_mine = jnp.concatenate([qkv_share, vectors], axis=0)
    qkv_came = hops(qkv_mine)
    share = qkv_share.shape[0]
    qkv_line = line_up(qkv_share, [values[:share] for values in qkv_came])
    qkv_matrix = from_replicas(qkv_line)
    norms = line_up(qkv_mine[share], [values[share] for values in qkv_came])
    norms = norms[:, : 6 * block].reshape(shards, 6, block).transpose(1, 0, 2)
    norms = norms.reshape(6, width).astype(jnp.float32)

    came = to_chip(after(frames, *qkv_came))
    x_low = by_time(*came)
    rest_share = jnp.concatenate(
        [share_of(self_output_weight), share_of(cross_query_weight), share_of(cross_output_weight)],
        axis=1,
    )
    rest_came = hops(after(rest_share, *came))
    rest = from_replicas(line_up(rest_share, rest_came))
    output_matrix = rest[:, :width]
    probe_matrix = rest[:, width : 2 * width]
    merge_matrix = rest[:, 2 * width :]
    expand_share = share_of(feed_up_weight)
    expand_came = hops(after(expand_share, *rest_came))

    facts = jnp.concatenate(
        [(clip_lengths // 64)[:, None], (clip_lengths % 64)[:, None], slot_used[:, None], text_mask],
        axis=1,
    ).astype(jnp.bfloat16)
    facts = jnp.pad(facts[:, None, :], ((0, 0), (0, 15), (0, width - facts.shape[1])))
    text_sent = lax.ppermute(jnp.concatenate([text_states, facts], axis=1), "core", swap)
    text_other = text_sent[:, :text_len]
    both = jnp.stack([facts[:, 0], text_sent[:, text_len]])[:, :, : 3 + text_len].astype(jnp.int32)
    lengths = 64 * both[:, :, 0] + both[:, :, 1]
    fact = lax.dynamic_index_in_dim(
        jnp.where(shard // 2 == core, both[0], both[1]), shard % 2, 0, keepdims=False
    )
    length, used = 64 * fact[0] + fact[1], fact[2]
    present = fact[3:].reshape(text_len, 1)
    count = jnp.sum(
        jnp.where(both[:, :, 2] > 0, jnp.minimum(lengths, clip), 0).astype(jnp.float32)
    )
    count = jnp.full((8, 128), count)
    for axis in ("x", "y"):
        count += lax.ppermute(count, axis, swap)
    count = count[0, 0]
    text_all = jnp.concatenate(
        [
            jnp.where(first_core, text_states, text_other),
            jnp.where(first_core, text_other, text_states),
        ],
        axis=0,
    ).reshape(4 * text_len, width)
    text_all = lax.dynamic_slice_in_dim(text_all, shard * block, block, 1)
    text_matrix = jnp.where(first_core, cross_key_weight, cross_value_weight)
    text_part = project(text_all, text_matrix).astype(jnp.bfloat16).reshape(4, text_len, width)
    text_came = [
        hop(
            lax.dynamic_index_in_dim(
                text_part, lax.rem(shard + distance, shards), 0, keepdims=False
            ),
            distance,
        )
        for distance in (1, 2, 3)
    ]

    places = jnp.stack([core, 3 - core, length, 1 - core, 2 + core]).astype(jnp.int32)
    positions = jnp.concatenate(
        [core * block + jnp.arange(block), (3 - core) * block + jnp.arange(block)]
    )
    valid_rows = ((positions < length) & (used > 0)).astype(jnp.float32)[:, None]
    inputs = x_low.astype(jnp.float32)
    parts_one = norm_parts(inputs)
    hidden_one = ((inputs - parts_one[0]) * parts_one[1] * norms[0] + norms[1]).astype(
        jnp.bfloat16
    )
    kv = project(hidden_one, qkv_matrix[:, width:]).astype(jnp.bfloat16)
    kv_other = lax.ppermute(kv, "core", swap)
    queries = project(after(hidden_one, kv), qkv_matrix[:, :width]).astype(jnp.bfloat16)
    expand_line = line_up(expand_share, held(expand_came, queries, kv_other))
    expand_matrix = from_replicas(expand_line)
    reduce_share = share_of(feed_down_weight)
    reduce_came = hops(after(reduce_share, *expand_came))
    mixed_self, lse = self_attend(after(places, expand_line, text_part), queries, kv, kv_other)
    reduce_matrix = from_replicas(line_up(reduce_share, held(reduce_came, mixed_self)))
    text_came = held(text_came, mixed_self)
    text_half = lax.dynamic_index_in_dim(text_part, shard, 0, keepdims=False).astype(jnp.float32)
    for values in text_came:
        text_half += values.astype(jnp.float32)
    text_half = text_half.astype(jnp.bfloat16)
    text_swap = lax.ppermute(text_half, "core", swap)
    lookups = jnp.where(first_core, text_half, text_swap)
    contents = jnp.where(first_core, text_swap, text_half)
    after_self = inputs + project(mixed_self, output_matrix)
    parts_two = norm_parts(after_self)
    hidden_two = ((after_self - parts_two[0]) * parts_two[1] * norms[2] + norms[3]).astype(
        jnp.bfloat16
    )
    probes = project(hidden_two, probe_matrix).astype(jnp.bfloat16)
    teacher_low = by_time(*to_chip(after(teacher, *reduce_came, probes)))
    cross_mixed = cross_attend(probes, lookups, contents, after(present, count))
    after_cross = after_self + project(cross_mixed, merge_matrix)
    parts_three = norm_parts(after_cross)
    hidden_three = (
        (after_cross - parts_three[0]) * parts_three[1] * norms[4] + norms[5]
    ).astype(jnp.bfloat16)
    upward = project(hidden_three, expand_matrix)
    activated, gelu_pull = jax.vjp(exact_gelu, upward)
    activated_low = activated.astype(jnp.bfloat16)
    result = after_cross + project(activated_low, reduce_matrix)
    errors = (result - teacher_low.astype(jnp.float32)) * valid_rows
    squares = jnp.sum(errors * errors)
    grad_result = errors * (4 * outers * clip / count)
    grad_feed_low = grad_result.astype(jnp.bfloat16)

    def theirs_of(right, left):
        columns = right.shape[1] // 2
        part = lax.dynamic_slice_in_dim(right, (1 - core) * columns, columns, 1)
        return outer_sum(part, left).astype(jnp.bfloat16)

    def ours_of(right, left, theirs):
        columns = right.shape[1] // 2
        sent = lax.ppermute(theirs, "core", swap)
        part = lax.dynamic_slice_in_dim(right, core * columns, columns, 1)
        return (outer_sum(part, left) + sent.astype(jnp.float32)).astype(jnp.bfloat16)

    def over_outer(values):
        return lax.psum_scatter(values, ("y", "x"), scatter_dimension=0, tiled=True)

    def shard_hops(values):
        columns = values.shape[1] // shards
        return [
            hop(
                lax.dynamic_slice_in_dim(
                    values, lax.rem(shard + distance, shards) * columns, columns, 1
                ),
                distance,
            )
            for distance in (1, 2, 3)
        ]

    def over_shard(values, came):
        columns = values.shape[1] // shards
        total = lax.dynamic_slice_in_dim(values, shard * columns, columns, 1).astype(jnp.float32)
        for part in came:
            total += part.astype(jnp.float32)
        return total.astype(jnp.bfloat16)

    down_theirs = theirs_of(grad_feed_low, activated_low)
    grad_activated = back_project(after(grad_feed_low, down_theirs), reduce_matrix)
    grad_upward = gelu_pull(grad_activated)[0].astype(jnp.bfloat16)
    down_ours = ours_of(after(grad_feed_low, grad_upward), activated_low, down_theirs)
    down_sum = over_outer(down_ours)
    up_theirs = theirs_of(after(grad_upward, down_ours), hidden_three)
    grad_hidden_three = back_project(after(grad_upward, up_theirs), expand_matrix)
    up_ours = ours_of(after(grad_upward, grad_hidden_three), hidden_three, up_theirs)
    grad_norm, gain_feed, bias_feed = norm_back(
        after(grad_hidden_three, up_ours), after_cross, parts_three, norms[4]
    )
    grad_after_cross = grad_result + grad_norm
    grad_cross_low = grad_after_cross.astype(jnp.bfloat16)
    merge_theirs = theirs_of(grad_cross_low, cross_mixed)
    grad_cross_mixed = back_project(after(grad_cross_low, merge_theirs), merge_matrix).astype(
        jnp.bfloat16
    )
    probe_grads, lookup_grads, content_grads = cross_attend_back(
        probes, lookups, contents, present, grad_cross_mixed
    )
    up_sum = over_outer(up_ours)
    text_mine = jnp.where(first_core, lookup_grads, content_grads)
    text_sent = lax.ppermute(
        jnp.where(first_core, content_grads, lookup_grads), "core", swap
    )
    text_mine = (text_mine.astype(jnp.float32) + text_sent.astype(jnp.float32)).astype(
        jnp.bfloat16
    )
    merge_ours = ours_of(after(grad_cross_low, probe_grads), cross_mixed, merge_theirs)
    probe_theirs = theirs_of(after(probe_grads, merge_ours), hidden_two)
    grad_hidden_two = back_project(after(probe_grads, probe_theirs), probe_matrix)
    text_four = line_up(text_mine, hops(text_mine)).reshape(4 * text_len, width)
    grad_norm, gain_cross, bias_cross = norm_back(
        grad_hidden_two, after_self, parts_two, norms[2]
    )
    grad_after_self = grad_after_cross + grad_norm
    grad_self_low = grad_after_self.astype(jnp.bfloat16)
    output_theirs = theirs_of(grad_self_low, mixed_self)
    grad_mixed = back_project(after(grad_self_low, output_theirs), output_matrix).astype(
        jnp.bfloat16
    )
    probe_ours = ours_of(after(probe_grads, grad_mixed), hidden_two, probe_theirs)
    text_weights = outer_sum(text_four, text_all).astype(jnp.bfloat16)
    text_back = back_project(text_four, text_matrix).astype(jnp.bfloat16)
    output_ours = ours_of(after(grad_self_low, probe_ours), mixed_self, output_theirs)
    text_rows = width // outers
    middle = jnp.concatenate(
        [
            values.reshape(outers, -1, width)
            for values in (
                output_ours,
                probe_ours,
                merge_ours,
                text_weights.reshape(outers, shards, text_rows // shards, block)
                .transpose(0, 2, 1, 3)
                .reshape(outers, text_rows // shards, width),
            )
        ],
        axis=1,
    )
    middle_rows = middle.shape[1]
    middle = middle.reshape(outers * middle_rows, width)
    middle_sum = over_outer(middle)
    text_split = text_rows // shards
    text_piece = (
        middle_sum[middle_rows - text_split :]
        .reshape(text_split, shards, block)
        .transpose(1, 0, 2)
        .reshape(text_rows, block)
    )
    text_back = text_back.reshape(2, 2, text_len, block)
    text_kept = lax.dynamic_index_in_dim(text_back, core, 0, keepdims=False)
    text_gone = lax.dynamic_index_in_dim(text_back, 1 - core, 0, keepdims=False)
    text_own = text_kept.astype(jnp.float32) + lax.ppermute(text_gone, "core", swap).astype(
        jnp.float32
    )
    text_own = text_own.astype(jnp.bfloat16)
    down_came = shard_hops(down_sum)
    output_came = from_chip(after(result.astype(jnp.bfloat16), middle))
    grad_queries, own_keys, own_values, other_keys, other_values = self_attend_back(
        places, queries, kv, kv_other, mixed_self, after(grad_mixed, middle, text_own), lse
    )
    down_came = held(down_came, grad_queries)
    output_came = held(output_came, grad_queries)
    other_keys, other_values = held([other_keys, other_values], *down_came, *output_came)
    own_keys += lax.ppermute(other_keys, "core", swap)
    own_values += lax.ppermute(other_values, "core", swap)
    down_piece = over_shard(down_sum, down_came)
    output = by_slot(*output_came)
    up_came = shard_hops(after(up_sum, down_piece))
    text_came = hops(after(text_own, grad_queries))

    qkv_grads = jnp.concatenate([grad_queries, own_keys, own_values], axis=1)
    qkv_theirs = theirs_of(qkv_grads, hidden_one)
    grad_hidden_one = back_project(after(qkv_grads, qkv_theirs), qkv_matrix)
    qkv_ours = ours_of(
        after(qkv_grads, grad_hidden_one, *up_came, *text_came), hidden_one, qkv_theirs
    )
    up_piece = over_shard(up_sum, up_came)
    text_grad = line_up(text_own, text_came).astype(jnp.float32)
    text_grad = text_grad.transpose(1, 2, 0, 3).reshape(text_states.shape)
    qkv_sum = over_outer(qkv_ours)
    grad_norm, gain_self, bias_self = norm_back(
        after(grad_hidden_one, qkv_ours), inputs, parts_one, norms[0]
    )
    frames_came = from_chip((grad_after_self + grad_norm).astype(jnp.bfloat16))
    frames_grad = by_slot(*frames_came).astype(jnp.float32)

    small = jnp.stack(
        [
            gain_self,
            bias_self,
            gain_cross,
            bias_cross,
            gain_feed,
            bias_feed,
            jnp.full((width,), squares),
            jnp.zeros((width,), jnp.float32),
        ]
    )
    for axis, pairs in (
        ("core", swap),
        ("x", swap),
        ("y", swap),
        ("shard", [(0, 1), (1, 0), (2, 3), (3, 2)]),
        ("shard", [(0, 2), (2, 0), (1, 3), (3, 1)]),
    ):
        small += lax.ppermute(small, axis, pairs)
    loss = small[6, 0] / (width * count)
    small_own = lax.dynamic_slice_in_dim(small, shard * block, block, 1)

    middle_sum = after(middle_sum, up_piece, *frames_came)
    middle_kept = middle_sum[: middle_rows - text_split]
    middle_piece = over_shard(middle_kept, shard_hops(middle_kept))
    early = jnp.concatenate(
        [up_piece]
        + [down_piece[:, i * block : (i + 1) * block] for i in range(4)]
        + [text_piece, middle_piece],
        axis=0,
    )
    early = lax.all_gather(early, REPLICAS, axis=0)
    piece = width // replicas
    square = (block, width)
    up_grad = unpack(early, hidden_units // replicas, 0, (block, hidden_units), 0, 1)
    at = hidden_units // replicas // piece
    down_grad = unpack(early, piece, at, (4 * block, width), 0, 2)
    at += 4
    key_grad = unpack(early, text_rows, at * piece // text_rows, square, 0, 1)
    value_grad = unpack(early, text_rows, at * piece // text_rows, square, 4, 1)
    at += text_rows // piece
    output_grad = unpack(early, piece, at, square, 0, 2)
    probe_grad = unpack(early, piece, at + 1, square, 0, 2)
    merge_grad = unpack(early, piece, at + 2, square, 0, 2)
    qkv_sum = after(qkv_sum, middle_piece, small)
    late = over_shard(qkv_sum, shard_hops(qkv_sum))
    late = lax.all_gather(after(late, early), REPLICAS, axis=0, tiled=True)
    late = late.reshape(3, width, block)
    qkv_grad = [late[i].T.astype(jnp.float32) for i in range(3)]
    return (
        output,
        loss,
        frames_grad,
        text_grad,
        small_own[0],
        small_own[1],
        qkv_grad[0],
        qkv_grad[1],
        qkv_grad[2],
        output_grad,
        small_own[2],
        small_own[3],
        probe_grad,
        key_grad,
        value_grad,
        merge_grad,
        small_own[4],
        small_own[5],
        up_grad,
        down_grad,
    )


def solution(mesh):
    by_chip = mesh.shape["shard"] == 4 and mesh.shape["replica"] == 8
    replica = ("y", "x", "core") if by_chip else "replica"
    row = P(replica)
    clip = P(replica, "shard", None)
    text = P(replica, None, None)
    vector = P("shard")
    matrix = P("shard", None)
    weights = (
        [vector, vector] + [matrix] * 4 + [vector, vector] + [matrix] * 4 + [vector, vector]
        + [matrix] * 2
    )
    if by_chip:
        mesh = Mesh(mesh.devices.reshape(2, 2, 2, 4), ("y", "x", "core", "shard"))
    return jax.shard_map(
        clip_body if by_chip else general_body,
        mesh=mesh,
        in_specs=(clip, text, P(replica, None), row, row, clip, *weights),
        out_specs=(clip, P(), clip, text, *weights),
        check_vma=False,
    )
```

```python
import jax
import jax.numpy as jnp
from jax import lax
from jax.experimental import pallas as pl
from jax.experimental.pallas import tpu as pltpu
from jax.sharding import Mesh
from jax.sharding import PartitionSpec as P

HEADS = 24
HEAD_DIM = 64


epsilon = 1e-05
masked_score = -1e30


def layer_norm(values, gain, shift):
    center = values - jnp.mean(values, axis=-1, keepdims=True)
    variance = jnp.mean(center * center, axis=-1, keepdims=True)
    return center * lax.rsqrt(variance + epsilon) * gain + shift


def exact_gelu(values):
    return jax.nn.gelu(values, approximate=False)


def project(left, right):
    return jnp.dot(left, right, preferred_element_type=jnp.float32)


def outer_sum(left, right):
    return jnp.einsum("rd,re->de", left, right, preferred_element_type=jnp.float32)


def back_project(grads, matrix):
    return jnp.einsum("re,de->rd", grads, matrix, preferred_element_type=jnp.float32)


def split_heads(values):
    return values.reshape(values.shape[:-1] + (HEADS, HEAD_DIM))


def self_forward(operands):
    queries, keys_all, values_all, allowed = operands
    scale = HEAD_DIM ** (-0.5)
    scores = (
        jnp.einsum("qhd,khd->hqk", queries, keys_all, preferred_element_type=jnp.float32) * scale
    )
    scores = jnp.where(allowed[None], scores, masked_score)
    peak = jnp.max(scores, axis=-1, keepdims=True)
    weights = jnp.exp(scores - peak)
    totals = jnp.sum(weights, axis=-1, keepdims=True)
    probs = (weights / totals).astype(jnp.bfloat16)
    mixed = jnp.einsum("hqk,khd->qhd", probs, values_all, preferred_element_type=jnp.float32)
    return (mixed.astype(jnp.bfloat16), (peak + jnp.log(totals))[..., 0])


def self_backward(operands):
    queries, keys_all, values_all, allowed, log_totals, grad_mixed = operands
    scale = HEAD_DIM ** (-0.5)
    scores = (
        jnp.einsum("qhd,khd->hqk", queries, keys_all, preferred_element_type=jnp.float32) * scale
    )
    scores = jnp.where(allowed[None], scores, masked_score)
    probs = jnp.exp(scores - log_totals[..., None])
    grad_probs = jnp.einsum(
        "qhd,khd->hqk", grad_mixed, values_all, preferred_element_type=jnp.float32
    )
    grad_values = jnp.einsum(
        "hqk,qhd->khd", probs.astype(jnp.bfloat16), grad_mixed, preferred_element_type=jnp.float32
    )
    inner = jnp.sum(probs * grad_probs, axis=-1, keepdims=True)
    grad_scores = (probs * (grad_probs - inner)).astype(jnp.bfloat16)
    grad_queries = (
        jnp.einsum("hqk,khd->qhd", grad_scores, keys_all, preferred_element_type=jnp.float32)
        * scale
    ).astype(jnp.bfloat16)
    grad_keys = (
        jnp.einsum("hqk,qhd->khd", grad_scores, queries, preferred_element_type=jnp.float32) * scale
    )
    return (grad_queries, grad_keys, grad_values)


def general_body(
    frames,
    text_states,
    text_mask,
    clip_lengths,
    slot_used,
    teacher,
    self_norm_gain,
    self_norm_bias,
    self_query_weight,
    self_key_weight,
    self_value_weight,
    self_output_weight,
    cross_norm_gain,
    cross_norm_bias,
    cross_query_weight,
    cross_key_weight,
    cross_value_weight,
    cross_output_weight,
    feed_norm_gain,
    feed_norm_bias,
    feed_up_weight,
    feed_down_weight,
):
    gathered = (
        lax.all_gather(self_norm_gain, "shard", axis=0, tiled=True),
        lax.all_gather(self_norm_bias, "shard", axis=0, tiled=True),
        lax.all_gather(self_query_weight, "shard", axis=0, tiled=True),
        lax.all_gather(self_key_weight, "shard", axis=0, tiled=True),
        lax.all_gather(self_value_weight, "shard", axis=0, tiled=True),
        lax.all_gather(self_output_weight, "shard", axis=0, tiled=True),
        lax.all_gather(cross_norm_gain, "shard", axis=0, tiled=True),
        lax.all_gather(cross_norm_bias, "shard", axis=0, tiled=True),
        lax.all_gather(cross_query_weight, "shard", axis=0, tiled=True),
        lax.all_gather(cross_key_weight, "shard", axis=0, tiled=True),
        lax.all_gather(cross_value_weight, "shard", axis=0, tiled=True),
        lax.all_gather(cross_output_weight, "shard", axis=0, tiled=True),
        lax.all_gather(feed_norm_gain, "shard", axis=0, tiled=True),
        lax.all_gather(feed_norm_bias, "shard", axis=0, tiled=True),
        lax.all_gather(feed_up_weight, "shard", axis=0, tiled=True),
        lax.all_gather(feed_down_weight, "shard", axis=0, tiled=True),
    )
    (
        gain_attend,
        bias_attend,
        query_matrix,
        key_matrix,
        value_matrix,
        output_matrix,
        gain_cross,
        bias_cross,
        probe_matrix,
        lookup_matrix,
        content_matrix,
        merge_matrix,
        gain_feed,
        bias_feed,
        expand_matrix,
        reduce_matrix,
    ) = gathered
    slots = frames.shape[0]
    frame_count = frames.shape[1]
    width = frames.shape[2]
    text_len = text_states.shape[1]
    shards = lax.axis_size("shard")
    replicas = lax.axis_size("replica")
    clip_total = frame_count * shards
    row_count = slots * frame_count
    scale = HEAD_DIM ** (-0.5)
    shard_rank = lax.axis_index("shard")
    positions = shard_rank * frame_count + jnp.arange(frame_count, dtype=jnp.int32)
    key_positions = jnp.arange(clip_total, dtype=jnp.int32)
    allowed = (key_positions[None, None, :] <= positions[None, :, None]) & (
        key_positions[None, None, :] < clip_lengths[:, None, None]
    )
    valid_rows = ((positions[None, :] < clip_lengths[:, None]) & (slot_used[:, None] > 0)).astype(
        jnp.float32
    )
    text_allowed = text_mask > 0
    inputs = frames.astype(jnp.float32)
    normed_one, pull_one = jax.vjp(
        layer_norm, inputs, gain_attend.astype(jnp.float32), bias_attend.astype(jnp.float32)
    )
    hidden_one = normed_one.astype(jnp.bfloat16).reshape(row_count, width)
    queries = (
        project(hidden_one, query_matrix).astype(jnp.bfloat16).reshape(slots, frame_count, width)
    )
    keys_local = (
        project(hidden_one, key_matrix).astype(jnp.bfloat16).reshape(slots, frame_count, width)
    )
    values_local = (
        project(hidden_one, value_matrix).astype(jnp.bfloat16).reshape(slots, frame_count, width)
    )
    keys_all, values_all = (
        lax.all_gather(keys_local, "shard", axis=1, tiled=True),
        lax.all_gather(values_local, "shard", axis=1, tiled=True),
    )
    head_queries = split_heads(queries)
    head_keys = split_heads(keys_all)
    head_values = split_heads(values_all)
    mixed_self, log_totals = lax.map(self_forward, (head_queries, head_keys, head_values, allowed))
    mixed_rows = mixed_self.reshape(row_count, width)
    after_self = inputs + project(mixed_rows, output_matrix).reshape(slots, frame_count, width)
    normed_two, pull_two = jax.vjp(
        layer_norm, after_self, gain_cross.astype(jnp.float32), bias_cross.astype(jnp.float32)
    )
    hidden_two = normed_two.astype(jnp.bfloat16).reshape(row_count, width)
    probes = split_heads(
        project(hidden_two, probe_matrix).astype(jnp.bfloat16).reshape(slots, frame_count, width)
    )
    text_rows = text_states.reshape(slots * text_len, width)
    lookups = split_heads(
        project(text_rows, lookup_matrix).astype(jnp.bfloat16).reshape(slots, text_len, width)
    )
    contents = split_heads(
        project(text_rows, content_matrix).astype(jnp.bfloat16).reshape(slots, text_len, width)
    )
    cross_scores = (
        jnp.einsum("sqhd,skhd->shqk", probes, lookups, preferred_element_type=jnp.float32) * scale
    )
    cross_scores = jnp.where(text_allowed[:, None, None, :], cross_scores, masked_score)
    cross_peak = jnp.max(cross_scores, axis=-1, keepdims=True)
    cross_weights = jnp.exp(cross_scores - cross_peak)
    cross_probs = cross_weights / jnp.sum(cross_weights, axis=-1, keepdims=True)
    cross_probs_low = cross_probs.astype(jnp.bfloat16)
    cross_mixed = jnp.einsum(
        "shqk,skhd->sqhd", cross_probs_low, contents, preferred_element_type=jnp.float32
    )
    cross_mixed = cross_mixed.astype(jnp.bfloat16).reshape(row_count, width)
    after_cross = after_self + project(cross_mixed, merge_matrix).reshape(slots, frame_count, width)
    normed_three, pull_three = jax.vjp(
        layer_norm, after_cross, gain_feed.astype(jnp.float32), bias_feed.astype(jnp.float32)
    )
    hidden_three = normed_three.astype(jnp.bfloat16).reshape(row_count, width)
    upward = project(hidden_three, expand_matrix)
    activated, gelu_pull = jax.vjp(exact_gelu, upward)
    activated_low = activated.astype(jnp.bfloat16)
    result = after_cross + project(activated_low, reduce_matrix).reshape(slots, frame_count, width)
    output = result.astype(jnp.bfloat16)
    errors = (result - teacher.astype(jnp.float32)) * valid_rows[..., None]
    squares_total, count_total = lax.psum(
        (jnp.sum(errors * errors), jnp.sum(valid_rows)), ("replica", "shard")
    )
    loss = squares_total / (width * count_total)
    grad_result = errors * (slots * replicas * clip_total / count_total)
    grad_feed_low = grad_result.reshape(row_count, width).astype(jnp.bfloat16)
    grad_activated = back_project(grad_feed_low, reduce_matrix)
    grad_upward = gelu_pull(grad_activated)[0].astype(jnp.bfloat16)
    grad_hidden_three = back_project(grad_upward, expand_matrix).reshape(slots, frame_count, width)
    grad_cross_norm, gain_feed_part, bias_feed_part = pull_three(grad_hidden_three)
    grad_after_cross = grad_result + grad_cross_norm
    feed_owned = (
        lax.psum_scatter(
            outer_sum(hidden_three, grad_upward).astype(jnp.bfloat16),
            "shard",
            scatter_dimension=0,
            tiled=True,
        ).astype(jnp.float32),
        lax.psum_scatter(
            outer_sum(activated_low, grad_feed_low).astype(jnp.bfloat16),
            "shard",
            scatter_dimension=0,
            tiled=True,
        ).astype(jnp.float32),
        lax.psum_scatter(
            gain_feed_part.astype(jnp.bfloat16), "shard", scatter_dimension=0, tiled=True
        ).astype(jnp.float32),
        lax.psum_scatter(
            bias_feed_part.astype(jnp.bfloat16), "shard", scatter_dimension=0, tiled=True
        ).astype(jnp.float32),
    )
    grad_cross_low = grad_after_cross.reshape(row_count, width).astype(jnp.bfloat16)
    grad_cross_mixed = split_heads(
        back_project(grad_cross_low, merge_matrix)
        .astype(jnp.bfloat16)
        .reshape(slots, frame_count, width)
    )
    grad_cross_probs = jnp.einsum(
        "sqhd,skhd->shqk", grad_cross_mixed, contents, preferred_element_type=jnp.float32
    )
    content_grads = jnp.einsum(
        "shqk,sqhd->skhd", cross_probs_low, grad_cross_mixed, preferred_element_type=jnp.float32
    )
    cross_inner = jnp.sum(cross_probs * grad_cross_probs, axis=-1, keepdims=True)
    grad_cross_scores = (cross_probs * (grad_cross_probs - cross_inner)).astype(jnp.bfloat16)
    probe_grads = (
        jnp.einsum(
            "shqk,skhd->sqhd", grad_cross_scores, lookups, preferred_element_type=jnp.float32
        )
        * scale
    )
    probe_grads = probe_grads.astype(jnp.bfloat16).reshape(row_count, width)
    lookup_grads = (
        jnp.einsum("shqk,sqhd->skhd", grad_cross_scores, probes, preferred_element_type=jnp.float32)
        * scale
    )
    lookup_sum, content_sum = (
        lax.psum(lookup_grads.astype(jnp.bfloat16), "shard").astype(jnp.float32),
        lax.psum(content_grads.astype(jnp.bfloat16), "shard").astype(jnp.float32),
    )
    lookup_low = lookup_sum.astype(jnp.bfloat16).reshape(slots * text_len, width)
    content_low = content_sum.astype(jnp.bfloat16).reshape(slots * text_len, width)
    own_width = width // shards
    own_text = lax.dynamic_slice_in_dim(text_rows, shard_rank * own_width, own_width, 1)
    lookup_own = outer_sum(own_text, lookup_low)
    content_own = outer_sum(own_text, content_low)
    text_grad = (
        back_project(lookup_low, lookup_matrix) + back_project(content_low, content_matrix)
    ).reshape(slots, text_len, width)
    grad_hidden_two = back_project(probe_grads, probe_matrix).reshape(slots, frame_count, width)
    grad_self_norm, gain_cross_part, bias_cross_part = pull_two(grad_hidden_two)
    grad_after_self = grad_after_cross + grad_self_norm
    grad_self_low = grad_after_self.reshape(row_count, width).astype(jnp.bfloat16)
    grad_mixed = split_heads(
        back_project(grad_self_low, output_matrix)
        .astype(jnp.bfloat16)
        .reshape(slots, frame_count, width)
    )
    grad_queries, grad_keys, grad_values = lax.map(
        self_backward, (head_queries, head_keys, head_values, allowed, log_totals, grad_mixed)
    )
    key_sum, value_sum = (
        lax.psum_scatter(
            grad_keys.reshape(slots, clip_total, width).astype(jnp.bfloat16),
            "shard",
            scatter_dimension=1,
            tiled=True,
        ).astype(jnp.float32),
        lax.psum_scatter(
            grad_values.reshape(slots, clip_total, width).astype(jnp.bfloat16),
            "shard",
            scatter_dimension=1,
            tiled=True,
        ).astype(jnp.float32),
    )
    key_low = key_sum.astype(jnp.bfloat16).reshape(row_count, width)
    value_low = value_sum.astype(jnp.bfloat16).reshape(row_count, width)
    query_low = grad_queries.reshape(row_count, width)
    grad_hidden_one = (
        back_project(query_low, query_matrix)
        + back_project(key_low, key_matrix)
        + back_project(value_low, value_matrix)
    )
    grad_inputs, gain_attend_part, bias_attend_part = pull_one(
        grad_hidden_one.reshape(slots, frame_count, width)
    )
    frames_grad = grad_after_self + grad_inputs
    attend_owned = (
        lax.psum_scatter(
            outer_sum(hidden_one, query_low).astype(jnp.bfloat16),
            "shard",
            scatter_dimension=0,
            tiled=True,
        ).astype(jnp.float32),
        lax.psum_scatter(
            outer_sum(hidden_one, key_low).astype(jnp.bfloat16),
            "shard",
            scatter_dimension=0,
            tiled=True,
        ).astype(jnp.float32),
        lax.psum_scatter(
            outer_sum(hidden_one, value_low).astype(jnp.bfloat16),
            "shard",
            scatter_dimension=0,
            tiled=True,
        ).astype(jnp.float32),
        lax.psum_scatter(
            outer_sum(mixed_rows, grad_self_low).astype(jnp.bfloat16),
            "shard",
            scatter_dimension=0,
            tiled=True,
        ).astype(jnp.float32),
        lax.psum_scatter(
            outer_sum(hidden_two, probe_grads).astype(jnp.bfloat16),
            "shard",
            scatter_dimension=0,
            tiled=True,
        ).astype(jnp.float32),
        lax.psum_scatter(
            outer_sum(cross_mixed, grad_cross_low).astype(jnp.bfloat16),
            "shard",
            scatter_dimension=0,
            tiled=True,
        ).astype(jnp.float32),
        lax.psum_scatter(
            gain_attend_part.astype(jnp.bfloat16), "shard", scatter_dimension=0, tiled=True
        ).astype(jnp.float32),
        lax.psum_scatter(
            bias_attend_part.astype(jnp.bfloat16), "shard", scatter_dimension=0, tiled=True
        ).astype(jnp.float32),
        lax.psum_scatter(
            gain_cross_part.astype(jnp.bfloat16), "shard", scatter_dimension=0, tiled=True
        ).astype(jnp.float32),
        lax.psum_scatter(
            bias_cross_part.astype(jnp.bfloat16), "shard", scatter_dimension=0, tiled=True
        ).astype(jnp.float32),
    )
    summed = (
        lax.psum(attend_owned[6].astype(jnp.bfloat16), "replica").astype(jnp.float32),
        lax.psum(attend_owned[7].astype(jnp.bfloat16), "replica").astype(jnp.float32),
        lax.psum(attend_owned[0].astype(jnp.bfloat16), "replica").astype(jnp.float32),
        lax.psum(attend_owned[1].astype(jnp.bfloat16), "replica").astype(jnp.float32),
        lax.psum(attend_owned[2].astype(jnp.bfloat16), "replica").astype(jnp.float32),
        lax.psum(attend_owned[3].astype(jnp.bfloat16), "replica").astype(jnp.float32),
        lax.psum(attend_owned[8].astype(jnp.bfloat16), "replica").astype(jnp.float32),
        lax.psum(attend_owned[9].astype(jnp.bfloat16), "replica").astype(jnp.float32),
        lax.psum(attend_owned[4].astype(jnp.bfloat16), "replica").astype(jnp.float32),
        lax.psum(lookup_own.astype(jnp.bfloat16), "replica").astype(jnp.float32),
        lax.psum(content_own.astype(jnp.bfloat16), "replica").astype(jnp.float32),
        lax.psum(attend_owned[5].astype(jnp.bfloat16), "replica").astype(jnp.float32),
        lax.psum(feed_owned[2].astype(jnp.bfloat16), "replica").astype(jnp.float32),
        lax.psum(feed_owned[3].astype(jnp.bfloat16), "replica").astype(jnp.float32),
        lax.psum(feed_owned[0].astype(jnp.bfloat16), "replica").astype(jnp.float32),
        lax.psum(feed_owned[1].astype(jnp.bfloat16), "replica").astype(jnp.float32),
    )
    return (
        output,
        loss,
        frames_grad,
        text_grad,
        summed[0],
        summed[1],
        summed[2],
        summed[3],
        summed[4],
        summed[5],
        summed[6],
        summed[7],
        summed[8],
        summed[9],
        summed[10],
        summed[11],
        summed[12],
        summed[13],
        summed[14],
        summed[15],
    )


PAIR = 2 * HEAD_DIM
EVERY = ("shard", "y", "x", "core")
REPLICAS = ("core", "y", "x")
NT = (((1,), (1,)), ((), ()))
TN = (((0,), (0,)), ((), ()))
NN = (((1,), (0,)), ((), ()))


def dot(left, right, dims):
    return lax.dot_general(left, right, dims, preferred_element_type=jnp.float32)


def half_mask(side, value):
    lanes = lax.broadcasted_iota(jnp.int32, (1, PAIR), 1)
    inside = (lanes >= HEAD_DIM) if side else (lanes < HEAD_DIM)
    return jnp.where(inside, value, 0.0).astype(jnp.bfloat16)


def fill_clip(place, own_ref, other_ref, all_ref):
    block = own_ref.shape[0] // 2
    for part in range(2):
        rows = slice(part * block, (part + 1) * block)
        for at, ref in ((place[part], own_ref), (place[3 + part], other_ref)):
            all_ref[pl.ds(pl.multiple_of(at * block, block), block), :] = ref[rows, :]


def self_forward_kernel(
    place, q_ref, own_k, own_v, other_k, other_v, mixed_ref, lse_ref, k_ref, v_ref, acc_ref
):
    fill_clip(place, own_k, other_k, k_ref)
    fill_clip(place, own_v, other_v, v_ref)
    block = q_ref.shape[0] // 2
    length = place[2]
    low = lax.broadcasted_iota(jnp.int32, (PAIR, 1), 0) < HEAD_DIM
    for part in range(2):
        first = place[part] * block
        rows = slice(part * block, (part + 1) * block)
        q = q_ref[rows, :]
        q_half = [q * half_mask(side, HEAD_DIM ** (-0.5)) for side in range(2)]
        limit = jnp.minimum(
            first + lax.broadcasted_iota(jnp.int32, (1, block), 1) + 1, length
        )
        acc_ref[...] = jnp.zeros_like(acc_ref)

        def step(j, peaks, q_half=q_half, limit=limit):
            at = pl.multiple_of(j * block, block)
            k = k_ref[pl.ds(at, block), :]
            v = v_ref[pl.ds(at, block), :]
            allowed = at + lax.broadcasted_iota(jnp.int32, (block, block), 0) < limit
            out = []
            for side in range(2):
                scores = jnp.where(allowed, dot(k, q_half[side], NT), masked_score)
                peak = jnp.maximum(peaks[side], jnp.max(scores, axis=0, keepdims=True))
                weights = jnp.exp(scores - peak).astype(jnp.bfloat16)
                v_ones = v * half_mask(side, 1.0) + half_mask(1 - side, 1.0)
                acc_ref[side] = acc_ref[side] * jnp.exp(peaks[side] - peak) + dot(
                    v_ones, weights, TN
                )
                out.append(peak)
            return tuple(out)

        peaks = lax.fori_loop(
            0, place[part] + 1, step, (jnp.full((1, block), masked_score, jnp.float32),) * 2
        )
        top, bottom = acc_ref[0], acc_ref[1]
        total = jnp.where(low, top[HEAD_DIM : HEAD_DIM + 1], bottom[0:1])
        mixed = jnp.where(low, top, bottom) / total
        mixed_ref[rows, :] = mixed.T.astype(jnp.bfloat16)
        lse_ref[0:1, rows] = peaks[0] + jnp.log(top[HEAD_DIM : HEAD_DIM + 1])
        lse_ref[1:2, rows] = peaks[1] + jnp.log(bottom[0:1])


def self_backward_kernel(
    place, q_ref, own_k, own_v, other_k, other_v, mixed_ref, grad_ref, lse_ref,
    dq_ref, own_dk, own_dv, other_dk, other_dv, k_ref, v_ref, dq_acc, dk_acc, dv_acc,
):
    fill_clip(place, own_k, other_k, k_ref)
    fill_clip(place, own_v, other_v, v_ref)
    block = q_ref.shape[0] // 2
    length = place[2]
    scale = HEAD_DIM ** (-0.5)
    dk_acc[...] = jnp.zeros_like(dk_acc)
    dv_acc[...] = jnp.zeros_like(dv_acc)
    for part in range(2):
        first = place[part] * block
        rows = slice(part * block, (part + 1) * block)
        q = q_ref[rows, :]
        grad = grad_ref[rows, :]
        q_half = [q * half_mask(side, scale) for side in range(2)]
        grad_half = [grad * half_mask(side, 1.0) for side in range(2)]
        product = (grad.astype(jnp.float32) * mixed_ref[rows, :].astype(jnp.float32)).T
        inner = [
            jnp.sum(product[side * HEAD_DIM : (side + 1) * HEAD_DIM], axis=0, keepdims=True)
            for side in range(2)
        ]
        lse = [lse_ref[side : side + 1, rows] for side in range(2)]
        limit = jnp.minimum(
            first + lax.broadcasted_iota(jnp.int32, (1, block), 1) + 1, length
        )
        dq_acc[...] = jnp.zeros_like(dq_acc)

        def step(
            j, carry, q_half=q_half, grad_half=grad_half, inner=inner, lse=lse, limit=limit
        ):
            at = pl.multiple_of(j * block, block)
            k = k_ref[pl.ds(at, block), :]
            v = v_ref[pl.ds(at, block), :]
            allowed = at + lax.broadcasted_iota(jnp.int32, (block, block), 0) < limit
            dq, dk, dv = 0.0, 0.0, 0.0
            for side in range(2):
                scores = jnp.where(allowed, dot(k, q_half[side], NT), masked_score)
                probs = jnp.exp(scores - lse[side])
                grad_probs = dot(v, grad_half[side], NT)
                grad_scores = (probs * (grad_probs - inner[side])).astype(jnp.bfloat16)
                dv += dot(probs.astype(jnp.bfloat16), grad_half[side], NN)
                dk += dot(grad_scores, q_half[side], NN)
                dq += dot(k * half_mask(side, scale), grad_scores, TN)
            dk_acc[pl.ds(at, block), :] += dk
            dv_acc[pl.ds(at, block), :] += dv
            dq_acc[...] += dq
            return carry

        lax.fori_loop(0, place[part] + 1, step, 0)
        dq_ref[rows, :] = dq_acc[...].T.astype(jnp.bfloat16)
    for part in range(2):
        rows = slice(part * block, (part + 1) * block)
        own = pl.ds(pl.multiple_of(place[part] * block, block), block)
        other = pl.ds(pl.multiple_of(place[3 + part] * block, block), block)
        own_dk[rows, :] = dk_acc[own, :].astype(jnp.bfloat16)
        own_dv[rows, :] = dv_acc[own, :].astype(jnp.bfloat16)
        other_dk[rows, :] = dk_acc[other, :].astype(jnp.bfloat16)
        other_dv[rows, :] = dv_acc[other, :].astype(jnp.bfloat16)


def pair_block(rows):
    return pl.BlockSpec((rows, PAIR), lambda i, *_: (0, i))


def value_block(rows, pairs):
    return pl.BlockSpec((rows, PAIR), lambda i, *_: (0, pairs + i))


def self_attend(place, queries, own, other):
    rows, width = queries.shape
    clip = 2 * rows
    pairs = width // PAIR
    return pl.pallas_call(
        self_forward_kernel,
        out_shape=(
            jax.ShapeDtypeStruct((rows, width), jnp.bfloat16),
            jax.ShapeDtypeStruct((pairs * 8, rows), jnp.float32),
        ),
        grid_spec=pltpu.PrefetchScalarGridSpec(
            num_scalar_prefetch=1,
            grid=(pairs,),
            in_specs=[pair_block(rows)] + [pair_block(rows), value_block(rows, pairs)] * 2,
            out_specs=(pair_block(rows), pl.BlockSpec((8, rows), lambda i, *_: (i, 0))),
            scratch_shapes=[
                pltpu.VMEM((clip, PAIR), jnp.bfloat16),
                pltpu.VMEM((clip, PAIR), jnp.bfloat16),
                pltpu.VMEM((2, PAIR, rows // 2), jnp.float32),
            ],
        ),
        compiler_params=pltpu.CompilerParams(vmem_limit_bytes=32 * 2**20),
        cost_estimate=pl.CostEstimate(
            flops=2 * 2 * rows * clip * width, bytes_accessed=8 * clip * width, transcendentals=0
        ),
        name="self_attend",
    )(place, queries, own, own, other, other)


def self_attend_back(place, queries, own, other, mixed, grads, lse):
    rows, width = queries.shape
    clip = 2 * rows
    pairs = width // PAIR
    return pl.pallas_call(
        self_backward_kernel,
        out_shape=(jax.ShapeDtypeStruct((rows, width), jnp.bfloat16),) * 5,
        grid_spec=pltpu.PrefetchScalarGridSpec(
            num_scalar_prefetch=1,
            grid=(pairs,),
            in_specs=[pair_block(rows)]
            + [pair_block(rows), value_block(rows, pairs)] * 2
            + [
                pair_block(rows),
                pair_block(rows),
                pl.BlockSpec((8, rows), lambda i, *_: (i, 0)),
            ],
            out_specs=(pair_block(rows),) * 5,
            scratch_shapes=[
                pltpu.VMEM((clip, PAIR), jnp.bfloat16),
                pltpu.VMEM((clip, PAIR), jnp.bfloat16),
                pltpu.VMEM((PAIR, rows // 2), jnp.float32),
                pltpu.VMEM((clip, PAIR), jnp.float32),
                pltpu.VMEM((clip, PAIR), jnp.float32),
            ],
        ),
        compiler_params=pltpu.CompilerParams(vmem_limit_bytes=32 * 2**20),
        cost_estimate=pl.CostEstimate(
            flops=5 * 2 * rows * clip * width, bytes_accessed=16 * clip * width, transcendentals=0
        ),
        name="self_attend_back",
    )(place, queries, own, own, other, other, mixed, grads, lse)


def both_heads(rows, value):
    return jnp.concatenate([rows * half_mask(side, value) for side in range(2)], axis=0)


def cross_probs_of(lookup_two, probes, present):
    text = present.shape[0]
    scores = dot(lookup_two, probes, NT)
    out = []
    for side in range(2):
        part = jnp.where(
            present > 0, scores[side * text : (side + 1) * text], masked_score
        )
        weights = jnp.exp(part - jnp.max(part, axis=0, keepdims=True))
        out.append(weights / jnp.sum(weights, axis=0, keepdims=True))
    return out


def cross_forward_kernel(probe_ref, lookup_ref, content_ref, present_ref, mixed_ref):
    probs = cross_probs_of(
        both_heads(lookup_ref[...], HEAD_DIM ** (-0.5)), probe_ref[...], present_ref[...]
    )
    probs = jnp.concatenate(probs, axis=0).astype(jnp.bfloat16)
    mixed_ref[...] = dot(probs, both_heads(content_ref[...], 1.0), TN).astype(jnp.bfloat16)


def cross_backward_kernel(
    probe_ref, lookup_ref, content_ref, present_ref, grad_ref, dp_ref, dl_ref, dc_ref
):
    text = present_ref.shape[0]
    scale = HEAD_DIM ** (-0.5)
    probes = probe_ref[...]
    grads = grad_ref[...]
    lookup_two = both_heads(lookup_ref[...], scale)
    probs = cross_probs_of(lookup_two, probes, present_ref[...])
    grad_probs = dot(both_heads(content_ref[...], 1.0), grads, NT)
    grad_scores = []
    for side in range(2):
        part = grad_probs[side * text : (side + 1) * text]
        inner = jnp.sum(probs[side] * part, axis=0, keepdims=True)
        grad_scores.append(probs[side] * (part - inner))
    grad_scores = jnp.concatenate(grad_scores, axis=0).astype(jnp.bfloat16)
    probs = jnp.concatenate(probs, axis=0).astype(jnp.bfloat16)
    low = lax.broadcasted_iota(jnp.int32, (1, PAIR), 1) < HEAD_DIM
    dp_ref[...] = dot(grad_scores, lookup_two, TN).astype(jnp.bfloat16)
    dl = dot(grad_scores, probes, NN) * scale
    dl_ref[...] = jnp.where(low, dl[:text], dl[text:]).astype(jnp.bfloat16)
    dc = dot(probs, grads, NN)
    dc_ref[...] = jnp.where(low, dc[:text], dc[text:]).astype(jnp.bfloat16)


def cross_attend(probes, lookups, contents, present):
    rows, width = probes.shape
    text = lookups.shape[0]
    return pl.pallas_call(
        cross_forward_kernel,
        out_shape=jax.ShapeDtypeStruct((rows, width), jnp.bfloat16),
        grid=(width // PAIR,),
        in_specs=[
            pair_block(rows),
            pair_block(text),
            pair_block(text),
            pl.BlockSpec((text, 1), lambda i: (0, 0)),
        ],
        out_specs=pair_block(rows),
        compiler_params=pltpu.CompilerParams(vmem_limit_bytes=32 * 2**20),
        cost_estimate=pl.CostEstimate(
            flops=8 * rows * text * width, bytes_accessed=4 * rows * width, transcendentals=0
        ),
        name="cross_attend",
    )(probes, lookups, contents, present)


def cross_attend_back(probes, lookups, contents, present, grads):
    rows, width = probes.shape
    text = lookups.shape[0]
    return pl.pallas_call(
        cross_backward_kernel,
        out_shape=(
            jax.ShapeDtypeStruct((rows, width), jnp.bfloat16),
            jax.ShapeDtypeStruct((text, width), jnp.bfloat16),
            jax.ShapeDtypeStruct((text, width), jnp.bfloat16),
        ),
        grid=(width // PAIR,),
        in_specs=[
            pair_block(rows),
            pair_block(text),
            pair_block(text),
            pl.BlockSpec((text, 1), lambda i: (0, 0)),
            pair_block(rows),
        ],
        out_specs=(pair_block(rows), pair_block(text), pair_block(text)),
        compiler_params=pltpu.CompilerParams(vmem_limit_bytes=32 * 2**20),
        cost_estimate=pl.CostEstimate(
            flops=20 * rows * text * width, bytes_accessed=6 * rows * width, transcendentals=0
        ),
        name="cross_attend_back",
    )(probes, lookups, contents, present, grads)


def unpack_kernel(in_ref, out_ref):
    pieces = in_ref[...]
    out_ref[...] = pieces.reshape(-1, pieces.shape[-1]).T.astype(jnp.float32)


def unpack(full, rows, place, out_shape, out_at, together):
    owners, _, features = full.shape
    tall = out_shape[0] // features
    wide = out_shape[1] // (together * rows)
    return pl.pallas_call(
        unpack_kernel,
        out_shape=jax.ShapeDtypeStruct(out_shape, jnp.float32),
        grid=(tall, wide),
        in_specs=[
            pl.BlockSpec((together, rows, features), lambda i, j: (j + out_at, place + i, 0))
        ],
        out_specs=pl.BlockSpec((features, together * rows), lambda i, j: (i, j)),
        compiler_params=pltpu.CompilerParams(vmem_limit_bytes=32 * 2**20),
        cost_estimate=pl.CostEstimate(
            flops=0, bytes_accessed=6 * out_shape[0] * out_shape[1], transcendentals=0
        ),
        name="unpack",
    )(full)


def held(values, *others):
    return list(lax.optimization_barrier((*values, *others))[: len(values)])


def after(value, *others):
    return lax.optimization_barrier((value, *others))[0]


def norm_parts(values):
    mean = jnp.mean(values, axis=-1, keepdims=True)
    center = values - mean
    return mean, lax.rsqrt(jnp.mean(center * center, axis=-1, keepdims=True) + epsilon)


def norm_back(grads, values, parts, gain):
    mean, inverse = parts
    unit = (values - mean) * inverse
    gain_grad = jnp.sum(grads * unit, axis=0)
    bias_grad = jnp.sum(grads, axis=0)
    scaled = grads * gain
    back = inverse * (
        scaled
        - jnp.mean(scaled, axis=-1, keepdims=True)
        - unit * jnp.mean(scaled * unit, axis=-1, keepdims=True)
    )
    return back, gain_grad, bias_grad


def clip_body(
    frames,
    text_states,
    text_mask,
    clip_lengths,
    slot_used,
    teacher,
    self_norm_gain,
    self_norm_bias,
    self_query_weight,
    self_key_weight,
    self_value_weight,
    self_output_weight,
    cross_norm_gain,
    cross_norm_bias,
    cross_query_weight,
    cross_key_weight,
    cross_value_weight,
    cross_output_weight,
    feed_norm_gain,
    feed_norm_bias,
    feed_up_weight,
    feed_down_weight,
):
    block, width = frames.shape[1:]
    text_len = text_states.shape[1]
    shards, replicas, outers = 4, 8, 4
    core = lax.axis_index("core")
    shard = lax.axis_index("shard")
    outer = 2 * lax.axis_index("y") + lax.axis_index("x")
    replica = 2 * outer + core
    clip = block * shards
    hidden_units = feed_up_weight.shape[1]

    holder = {0: 0, 1: 1, 2: 1, 3: 0}
    there = ([], [])
    for c in range(2):
        for s in range(4):
            for turn in range(2):
                slot = turn if s < 2 else 1 - turn
                there[turn].append((c * 4 + s, holder[s] * 4 + 2 * c + slot))
    back = tuple([(b, a) for a, b in pairs] for pairs in there)
    spot = ("core", "shard")
    swap = [(0, 1), (1, 0)]
    even = shard % 2 == 0
    lower = shard < 2
    first_core = core == 0

    def hop(values, distance):
        pairs = [(i, (i + distance) % shards) for i in range(shards)]
        return lax.ppermute(values, "shard", pairs)

    def hops(values):
        return [hop(values, distance) for distance in (1, 2, 3)]

    def line_up(mine, came):
        out = jnp.zeros((shards,) + mine.shape, mine.dtype)
        out = lax.dynamic_update_index_in_dim(out, mine, shard, 0)
        for distance, values in zip((1, 2, 3), came):
            owner = lax.rem(shard + shards - distance, shards)
            out = lax.dynamic_update_index_in_dim(out, values, owner, 0)
        return out

    def to_chip(pair):
        one = lax.ppermute(jnp.where(lower, pair[0], pair[1]), spot, there[0])
        two = lax.ppermute(jnp.where(lower, pair[1], pair[0]), spot, there[1])
        return one, two

    def by_time(one, two):
        return jnp.concatenate([jnp.where(even, one, two), jnp.where(even, two, one)], axis=0)

    def from_chip(values):
        early, late = values[:block], values[block:]
        one = lax.ppermute(jnp.where(even, early, late), spot, back[0])
        two = lax.ppermute(jnp.where(even, late, early), spot, back[1])
        return one, two

    def by_slot(one, two):
        return jnp.stack([jnp.where(lower, one, two), jnp.where(lower, two, one)])

    def share_of(weight):
        share = weight.shape[0] // replicas
        return lax.dynamic_slice_in_dim(weight, replica * share, share, 0)

    def from_replicas(line):
        full = lax.all_gather(line, ("y", "x", "core"), axis=1, tiled=True)
        return full.reshape(-1, line.shape[-1])

    qkv_share = jnp.concatenate(
        [share_of(self_query_weight), share_of(self_key_weight), share_of(self_value_weight)],
        axis=1,
    )
    vectors = jnp.concatenate(
        [
            self_norm_gain,
            self_norm_bias,
            cross_norm_gain,
            cross_norm_bias,
            feed_norm_gain,
            feed_norm_bias,
        ]
    )
    vectors = jnp.pad(vectors[None, :], ((0, 15), (0, 3 * width - 6 * block)))
    qkv_matrix = lax.all_gather(qkv_share, EVERY, axis=0, tiled=True)
    came = to_chip(frames)
    x_low = by_time(*came)
    rest_share = jnp.concatenate(
        [share_of(self_output_weight), share_of(cross_query_weight), share_of(cross_output_weight)],
        axis=1,
    )
    share = rest_share.shape[0]
    rest_mine = jnp.concatenate([rest_share, vectors], axis=0)
    rest_came = hops(after(rest_mine, *came))
    rest = from_replicas(line_up(rest_share, [values[:share] for values in rest_came]))
    norms = line_up(vectors[0], [values[share] for values in rest_came])
    norms = norms[:, : 6 * block].reshape(shards, 6, block).transpose(1, 0, 2)
    norms = norms.reshape(6, width).astype(jnp.float32)
    output_matrix = rest[:, :width]
    probe_matrix = rest[:, width : 2 * width]
    merge_matrix = rest[:, 2 * width :]
    expand_share = share_of(feed_up_weight)
    expand_came = hops(after(expand_share, *rest_came))

    facts = jnp.concatenate(
        [(clip_lengths // 64)[:, None], (clip_lengths % 64)[:, None], slot_used[:, None], text_mask],
        axis=1,
    ).astype(jnp.bfloat16)
    facts = jnp.pad(facts[:, None, :], ((0, 0), (0, 15), (0, width - facts.shape[1])))
    text_sent = lax.ppermute(jnp.concatenate([text_states, facts], axis=1), "core", swap)
    text_other = text_sent[:, :text_len]
    both = jnp.stack([facts[:, 0], text_sent[:, text_len]])[:, :, : 3 + text_len].astype(jnp.int32)
    lengths = 64 * both[:, :, 0] + both[:, :, 1]
    fact = lax.dynamic_index_in_dim(
        jnp.where(shard // 2 == core, both[0], both[1]), shard % 2, 0, keepdims=False
    )
    length, used = 64 * fact[0] + fact[1], fact[2]
    present = fact[3:].reshape(text_len, 1)
    count = jnp.sum(
        jnp.where(both[:, :, 2] > 0, jnp.minimum(lengths, clip), 0).astype(jnp.float32)
    )
    count = jnp.full((8, 128), count)
    for axis in ("x", "y"):
        count += lax.ppermute(count, axis, swap)
    count = count[0, 0]
    text_all = jnp.concatenate(
        [
            jnp.where(first_core, text_states, text_other),
            jnp.where(first_core, text_other, text_states),
        ],
        axis=0,
    ).reshape(4 * text_len, width)
    text_all = lax.dynamic_slice_in_dim(text_all, shard * block, block, 1)
    text_matrix = jnp.where(first_core, cross_key_weight, cross_value_weight)
    text_part = project(text_all, text_matrix).astype(jnp.bfloat16).reshape(4, text_len, width)
    text_came = [
        hop(
            lax.dynamic_index_in_dim(
                after(text_part, *rest_came), lax.rem(shard + distance, shards), 0, keepdims=False
            ),
            distance,
        )
        for distance in (1, 2, 3)
    ]

    text_half = lax.dynamic_index_in_dim(text_part, shard, 0, keepdims=False).astype(jnp.float32)
    for values in text_came:
        text_half += values.astype(jnp.float32)
    text_half = text_half.astype(jnp.bfloat16)
    text_swap = lax.ppermute(text_half, "core", swap)
    lookups = jnp.where(first_core, text_half, text_swap)
    contents = jnp.where(first_core, text_swap, text_half)
    places = jnp.stack([core, 3 - core, length, 1 - core, 2 + core]).astype(jnp.int32)
    positions = jnp.concatenate(
        [core * block + jnp.arange(block), (3 - core) * block + jnp.arange(block)]
    )
    valid_rows = ((positions < length) & (used > 0)).astype(jnp.float32)[:, None]
    inputs = x_low.astype(jnp.float32)
    parts_one = norm_parts(inputs)
    hidden_one = ((inputs - parts_one[0]) * parts_one[1] * norms[0] + norms[1]).astype(
        jnp.bfloat16
    )
    kv = project(after(hidden_one, lookups, contents, count), qkv_matrix[:, width:]).astype(jnp.bfloat16)
    kv_other = lax.ppermute(kv, "core", swap)
    queries = project(after(hidden_one, kv), qkv_matrix[:, :width]).astype(jnp.bfloat16)
    mixed_self, lse = self_attend(places, queries, kv, kv_other)
    expand_came = held(expand_came, mixed_self)
    expand_matrix = from_replicas(line_up(expand_share, expand_came))
    reduce_share = share_of(feed_down_weight)
    reduce_came = hops(after(reduce_share, *expand_came))
    after_self = inputs + project(mixed_self, output_matrix)
    parts_two = norm_parts(after_self)
    hidden_two = ((after_self - parts_two[0]) * parts_two[1] * norms[2] + norms[3]).astype(
        jnp.bfloat16
    )
    probes = project(hidden_two, probe_matrix).astype(jnp.bfloat16)
    reduce_matrix = from_replicas(line_up(reduce_share, held(reduce_came, probes)))
    teacher_low = by_time(*to_chip(after(teacher, *reduce_came, probes)))
    cross_mixed = cross_attend(probes, lookups, contents, present)
    after_cross = after_self + project(cross_mixed, merge_matrix)
    parts_three = norm_parts(after_cross)
    hidden_three = (
        (after_cross - parts_three[0]) * parts_three[1] * norms[4] + norms[5]
    ).astype(jnp.bfloat16)
    upward = project(hidden_three, expand_matrix)
    activated, gelu_pull = jax.vjp(exact_gelu, upward)
    activated_low = activated.astype(jnp.bfloat16)
    result = after_cross + project(activated_low, reduce_matrix)
    errors = (result - teacher_low.astype(jnp.float32)) * valid_rows
    squares = jnp.sum(errors * errors)
    grad_result = errors * (4 * outers * clip / count)
    grad_feed_low = grad_result.astype(jnp.bfloat16)

    def theirs_of(right, left):
        columns = right.shape[1] // 2
        part = lax.dynamic_slice_in_dim(right, (1 - core) * columns, columns, 1)
        return outer_sum(part, left).astype(jnp.bfloat16)

    def ours_of(right, left, theirs):
        columns = right.shape[1] // 2
        sent = lax.ppermute(theirs, "core", swap)
        part = lax.dynamic_slice_in_dim(right, core * columns, columns, 1)
        return (outer_sum(part, left) + sent.astype(jnp.float32)).astype(jnp.bfloat16)

    def over_outer(values):
        return lax.psum_scatter(values, ("y", "x"), scatter_dimension=0, tiled=True)

    def shard_hops(values):
        columns = values.shape[1] // shards
        return [
            hop(
                lax.dynamic_slice_in_dim(
                    values, lax.rem(shard + distance, shards) * columns, columns, 1
                ),
                distance,
            )
            for distance in (1, 2, 3)
        ]

    def over_shard(values, came):
        columns = values.shape[1] // shards
        total = lax.dynamic_slice_in_dim(values, shard * columns, columns, 1).astype(jnp.float32)
        for part in came:
            total += part.astype(jnp.float32)
        return total.astype(jnp.bfloat16)

    down_theirs = theirs_of(grad_feed_low, activated_low)
    grad_activated = back_project(after(grad_feed_low, down_theirs), reduce_matrix)
    grad_upward = gelu_pull(grad_activated)[0].astype(jnp.bfloat16)
    down_ours = ours_of(after(grad_feed_low, grad_upward), activated_low, down_theirs)
    down_sum = over_outer(down_ours)
    up_theirs = theirs_of(after(grad_upward, down_ours), hidden_three)
    grad_hidden_three = back_project(after(grad_upward, up_theirs), expand_matrix)
    up_ours = ours_of(after(grad_upward, grad_hidden_three), hidden_three, up_theirs)
    grad_norm, gain_feed, bias_feed = norm_back(
        after(grad_hidden_three, up_ours), after_cross, parts_three, norms[4]
    )
    grad_after_cross = grad_result + grad_norm
    grad_cross_low = grad_after_cross.astype(jnp.bfloat16)
    merge_theirs = theirs_of(grad_cross_low, cross_mixed)
    grad_cross_mixed = back_project(after(grad_cross_low, merge_theirs), merge_matrix).astype(
        jnp.bfloat16
    )
    probe_grads, lookup_grads, content_grads = cross_attend_back(
        probes, lookups, contents, present, grad_cross_mixed
    )
    up_sum = over_outer(up_ours)
    text_mine = jnp.where(first_core, lookup_grads, content_grads)
    text_sent = lax.ppermute(
        jnp.where(first_core, content_grads, lookup_grads), "core", swap
    )
    text_mine = (text_mine.astype(jnp.float32) + text_sent.astype(jnp.float32)).astype(
        jnp.bfloat16
    )
    merge_ours = ours_of(after(grad_cross_low, probe_grads), cross_mixed, merge_theirs)
    probe_theirs = theirs_of(after(probe_grads, merge_ours), hidden_two)
    grad_hidden_two = back_project(after(probe_grads, probe_theirs), probe_matrix)
    text_four = line_up(text_mine, hops(text_mine)).reshape(4 * text_len, width)
    grad_norm, gain_cross, bias_cross = norm_back(
        grad_hidden_two, after_self, parts_two, norms[2]
    )
    grad_after_self = grad_after_cross + grad_norm
    grad_self_low = grad_after_self.astype(jnp.bfloat16)
    output_theirs = theirs_of(grad_self_low, mixed_self)
    grad_mixed = back_project(after(grad_self_low, output_theirs), output_matrix).astype(
        jnp.bfloat16
    )
    probe_ours = ours_of(after(probe_grads, grad_mixed), hidden_two, probe_theirs)
    text_weights = outer_sum(text_four, text_all).astype(jnp.bfloat16)
    text_back = back_project(text_four, text_matrix).astype(jnp.bfloat16)
    output_ours = ours_of(after(grad_self_low, probe_ours), mixed_self, output_theirs)
    text_rows = width // outers
    middle = jnp.concatenate(
        [
            values.reshape(outers, -1, width)
            for values in (
                output_ours,
                probe_ours,
                merge_ours,
                text_weights.reshape(outers, shards, text_rows // shards, block)
                .transpose(0, 2, 1, 3)
                .reshape(outers, text_rows // shards, width),
            )
        ],
        axis=1,
    )
    middle_rows = middle.shape[1]
    middle = middle.reshape(outers * middle_rows, width)
    middle_sum = over_outer(middle)
    text_split = text_rows // shards
    text_piece = (
        middle_sum[middle_rows - text_split :]
        .reshape(text_split, shards, block)
        .transpose(1, 0, 2)
        .reshape(text_rows, block)
    )
    text_back = text_back.reshape(2, 2, text_len, block)
    text_kept = lax.dynamic_index_in_dim(text_back, core, 0, keepdims=False)
    text_gone = lax.dynamic_index_in_dim(text_back, 1 - core, 0, keepdims=False)
    text_own = text_kept.astype(jnp.float32) + lax.ppermute(text_gone, "core", swap).astype(
        jnp.float32
    )
    text_own = text_own.astype(jnp.bfloat16)
    down_came = shard_hops(down_sum)
    output_came = from_chip(after(result.astype(jnp.bfloat16), middle))
    grad_queries, own_keys, own_values, other_keys, other_values = self_attend_back(
        places, queries, kv, kv_other, mixed_self, after(grad_mixed, middle, text_own), lse
    )
    down_came = held(down_came, grad_queries)
    output_came = held(output_came, grad_queries)
    other_keys, other_values = held([other_keys, other_values], *down_came, *output_came)
    own_keys += lax.ppermute(other_keys, "core", swap)
    own_values += lax.ppermute(other_values, "core", swap)
    down_piece = over_shard(down_sum, down_came)
    output = by_slot(*output_came)
    up_came = shard_hops(after(up_sum, down_piece))
    text_came = hops(after(text_own, grad_queries))

    qkv_grads = jnp.concatenate([grad_queries, own_keys, own_values], axis=1)
    qkv_theirs = theirs_of(qkv_grads, hidden_one)
    grad_hidden_one = back_project(after(qkv_grads, qkv_theirs), qkv_matrix)
    qkv_ours = ours_of(after(qkv_grads, grad_hidden_one), hidden_one, qkv_theirs)
    up_piece = over_shard(up_sum, up_came)
    text_grad = line_up(text_own, text_came).astype(jnp.float32)
    text_grad = text_grad.transpose(1, 2, 0, 3).reshape(text_states.shape)
    qkv_sum = over_outer(qkv_ours)
    grad_norm, gain_self, bias_self = norm_back(
        after(grad_hidden_one, qkv_ours, *up_came, *text_came), inputs, parts_one, norms[0]
    )
    frames_came = from_chip((grad_after_self + grad_norm).astype(jnp.bfloat16))
    frames_grad = by_slot(*frames_came).astype(jnp.float32)

    small = jnp.stack(
        [
            gain_self,
            bias_self,
            gain_cross,
            bias_cross,
            gain_feed,
            bias_feed,
            jnp.full((width,), squares),
            jnp.zeros((width,), jnp.float32),
        ]
    )
    for axis, pairs in (
        ("core", swap),
        ("x", swap),
        ("y", swap),
        ("shard", [(0, 1), (1, 0), (2, 3), (3, 2)]),
        ("shard", [(0, 2), (2, 0), (1, 3), (3, 1)]),
    ):
        small += lax.ppermute(small, axis, pairs)
    loss = small[6, 0] / (width * count)
    small_own = lax.dynamic_slice_in_dim(small, shard * block, block, 1)

    middle_sum = after(middle_sum, up_piece, *frames_came)
    middle_kept = middle_sum[: middle_rows - text_split]
    middle_piece = over_shard(middle_kept, shard_hops(middle_kept))
    early = jnp.concatenate(
        [up_piece]
        + [down_piece[:, i * block : (i + 1) * block] for i in range(4)]
        + [text_piece, middle_piece],
        axis=0,
    )
    early = lax.all_gather(after(early, text_grad), REPLICAS, axis=0)
    piece = width // replicas
    square = (block, width)
    up_grad = unpack(early, hidden_units // replicas, 0, (block, hidden_units), 0, 1)
    at = hidden_units // replicas // piece
    down_grad = unpack(early, piece, at, (4 * block, width), 0, 2)
    at += 4
    key_grad = unpack(early, text_rows, at * piece // text_rows, square, 0, 1)
    value_grad = unpack(early, text_rows, at * piece // text_rows, square, 4, 1)
    at += text_rows // piece
    output_grad = unpack(early, piece, at, square, 0, 2)
    probe_grad = unpack(early, piece, at + 1, square, 0, 2)
    merge_grad = unpack(early, piece, at + 2, square, 0, 2)
    qkv_sum = after(qkv_sum, middle_piece, small)
    late = over_shard(qkv_sum, shard_hops(qkv_sum))
    late = lax.all_gather(after(late, early), REPLICAS, axis=0, tiled=True)
    late = late.reshape(-1, block, block)
    qkv_grad = [unpack(late, block, 0, square, 2 * i, 2) for i in range(3)]
    return (
        output,
        loss,
        frames_grad,
        text_grad,
        small_own[0],
        small_own[1],
        qkv_grad[0],
        qkv_grad[1],
        qkv_grad[2],
        output_grad,
        small_own[2],
        small_own[3],
        probe_grad,
        key_grad,
        value_grad,
        merge_grad,
        small_own[4],
        small_own[5],
        up_grad,
        down_grad,
    )


def solution(mesh):
    by_chip = mesh.shape["shard"] == 4 and mesh.shape["replica"] == 8
    replica = ("y", "x", "core") if by_chip else "replica"
    row = P(replica)
    clip = P(replica, "shard", None)
    text = P(replica, None, None)
    vector = P("shard")
    matrix = P("shard", None)
    weights = (
        [vector, vector] + [matrix] * 4 + [vector, vector] + [matrix] * 4 + [vector, vector]
        + [matrix] * 2
    )
    if by_chip:
        mesh = Mesh(mesh.devices.reshape(2, 2, 2, 4), ("y", "x", "core", "shard"))
    return jax.shard_map(
        clip_body if by_chip else general_body,
        mesh=mesh,
        in_specs=(clip, text, P(replica, None), row, row, clip, *weights),
        out_specs=(clip, P(), clip, text, *weights),
        check_vma=False,
    )
```

```python
import jax
import jax.numpy as jnp
from jax import lax
from jax.experimental import pallas as pl
from jax.experimental.pallas import tpu as pltpu
from jax.sharding import Mesh
from jax.sharding import PartitionSpec as P

HEADS = 24
HEAD_DIM = 64


epsilon = 1e-05
masked_score = -1e30


def layer_norm(values, gain, shift):
    center = values - jnp.mean(values, axis=-1, keepdims=True)
    variance = jnp.mean(center * center, axis=-1, keepdims=True)
    return center * lax.rsqrt(variance + epsilon) * gain + shift


def exact_gelu(values):
    return jax.nn.gelu(values, approximate=False)


def project(left, right):
    return jnp.dot(left, right, preferred_element_type=jnp.float32)


def outer_sum(left, right):
    return jnp.einsum("rd,re->de", left, right, preferred_element_type=jnp.float32)


def back_project(grads, matrix):
    return jnp.einsum("re,de->rd", grads, matrix, preferred_element_type=jnp.float32)


def split_heads(values):
    return values.reshape(values.shape[:-1] + (HEADS, HEAD_DIM))


def self_forward(operands):
    queries, keys_all, values_all, allowed = operands
    scale = HEAD_DIM ** (-0.5)
    scores = (
        jnp.einsum("qhd,khd->hqk", queries, keys_all, preferred_element_type=jnp.float32) * scale
    )
    scores = jnp.where(allowed[None], scores, masked_score)
    peak = jnp.max(scores, axis=-1, keepdims=True)
    weights = jnp.exp(scores - peak)
    totals = jnp.sum(weights, axis=-1, keepdims=True)
    probs = (weights / totals).astype(jnp.bfloat16)
    mixed = jnp.einsum("hqk,khd->qhd", probs, values_all, preferred_element_type=jnp.float32)
    return (mixed.astype(jnp.bfloat16), (peak + jnp.log(totals))[..., 0])


def self_backward(operands):
    queries, keys_all, values_all, allowed, log_totals, grad_mixed = operands
    scale = HEAD_DIM ** (-0.5)
    scores = (
        jnp.einsum("qhd,khd->hqk", queries, keys_all, preferred_element_type=jnp.float32) * scale
    )
    scores = jnp.where(allowed[None], scores, masked_score)
    probs = jnp.exp(scores - log_totals[..., None])
    grad_probs = jnp.einsum(
        "qhd,khd->hqk", grad_mixed, values_all, preferred_element_type=jnp.float32
    )
    grad_values = jnp.einsum(
        "hqk,qhd->khd", probs.astype(jnp.bfloat16), grad_mixed, preferred_element_type=jnp.float32
    )
    inner = jnp.sum(probs * grad_probs, axis=-1, keepdims=True)
    grad_scores = (probs * (grad_probs - inner)).astype(jnp.bfloat16)
    grad_queries = (
        jnp.einsum("hqk,khd->qhd", grad_scores, keys_all, preferred_element_type=jnp.float32)
        * scale
    ).astype(jnp.bfloat16)
    grad_keys = (
        jnp.einsum("hqk,qhd->khd", grad_scores, queries, preferred_element_type=jnp.float32) * scale
    )
    return (grad_queries, grad_keys, grad_values)


def general_body(
    frames,
    text_states,
    text_mask,
    clip_lengths,
    slot_used,
    teacher,
    self_norm_gain,
    self_norm_bias,
    self_query_weight,
    self_key_weight,
    self_value_weight,
    self_output_weight,
    cross_norm_gain,
    cross_norm_bias,
    cross_query_weight,
    cross_key_weight,
    cross_value_weight,
    cross_output_weight,
    feed_norm_gain,
    feed_norm_bias,
    feed_up_weight,
    feed_down_weight,
):
    gathered = (
        lax.all_gather(self_norm_gain, "shard", axis=0, tiled=True),
        lax.all_gather(self_norm_bias, "shard", axis=0, tiled=True),
        lax.all_gather(self_query_weight, "shard", axis=0, tiled=True),
        lax.all_gather(self_key_weight, "shard", axis=0, tiled=True),
        lax.all_gather(self_value_weight, "shard", axis=0, tiled=True),
        lax.all_gather(self_output_weight, "shard", axis=0, tiled=True),
        lax.all_gather(cross_norm_gain, "shard", axis=0, tiled=True),
        lax.all_gather(cross_norm_bias, "shard", axis=0, tiled=True),
        lax.all_gather(cross_query_weight, "shard", axis=0, tiled=True),
        lax.all_gather(cross_key_weight, "shard", axis=0, tiled=True),
        lax.all_gather(cross_value_weight, "shard", axis=0, tiled=True),
        lax.all_gather(cross_output_weight, "shard", axis=0, tiled=True),
        lax.all_gather(feed_norm_gain, "shard", axis=0, tiled=True),
        lax.all_gather(feed_norm_bias, "shard", axis=0, tiled=True),
        lax.all_gather(feed_up_weight, "shard", axis=0, tiled=True),
        lax.all_gather(feed_down_weight, "shard", axis=0, tiled=True),
    )
    (
        gain_attend,
        bias_attend,
        query_matrix,
        key_matrix,
        value_matrix,
        output_matrix,
        gain_cross,
        bias_cross,
        probe_matrix,
        lookup_matrix,
        content_matrix,
        merge_matrix,
        gain_feed,
        bias_feed,
        expand_matrix,
        reduce_matrix,
    ) = gathered
    slots = frames.shape[0]
    frame_count = frames.shape[1]
    width = frames.shape[2]
    text_len = text_states.shape[1]
    shards = lax.axis_size("shard")
    replicas = lax.axis_size("replica")
    clip_total = frame_count * shards
    row_count = slots * frame_count
    scale = HEAD_DIM ** (-0.5)
    shard_rank = lax.axis_index("shard")
    positions = shard_rank * frame_count + jnp.arange(frame_count, dtype=jnp.int32)
    key_positions = jnp.arange(clip_total, dtype=jnp.int32)
    allowed = (key_positions[None, None, :] <= positions[None, :, None]) & (
        key_positions[None, None, :] < clip_lengths[:, None, None]
    )
    valid_rows = ((positions[None, :] < clip_lengths[:, None]) & (slot_used[:, None] > 0)).astype(
        jnp.float32
    )
    text_allowed = text_mask > 0
    inputs = frames.astype(jnp.float32)
    normed_one, pull_one = jax.vjp(
        layer_norm, inputs, gain_attend.astype(jnp.float32), bias_attend.astype(jnp.float32)
    )
    hidden_one = normed_one.astype(jnp.bfloat16).reshape(row_count, width)
    queries = (
        project(hidden_one, query_matrix).astype(jnp.bfloat16).reshape(slots, frame_count, width)
    )
    keys_local = (
        project(hidden_one, key_matrix).astype(jnp.bfloat16).reshape(slots, frame_count, width)
    )
    values_local = (
        project(hidden_one, value_matrix).astype(jnp.bfloat16).reshape(slots, frame_count, width)
    )
    keys_all, values_all = (
        lax.all_gather(keys_local, "shard", axis=1, tiled=True),
        lax.all_gather(values_local, "shard", axis=1, tiled=True),
    )
    head_queries = split_heads(queries)
    head_keys = split_heads(keys_all)
    head_values = split_heads(values_all)
    mixed_self, log_totals = lax.map(self_forward, (head_queries, head_keys, head_values, allowed))
    mixed_rows = mixed_self.reshape(row_count, width)
    after_self = inputs + project(mixed_rows, output_matrix).reshape(slots, frame_count, width)
    normed_two, pull_two = jax.vjp(
        layer_norm, after_self, gain_cross.astype(jnp.float32), bias_cross.astype(jnp.float32)
    )
    hidden_two = normed_two.astype(jnp.bfloat16).reshape(row_count, width)
    probes = split_heads(
        project(hidden_two, probe_matrix).astype(jnp.bfloat16).reshape(slots, frame_count, width)
    )
    text_rows = text_states.reshape(slots * text_len, width)
    lookups = split_heads(
        project(text_rows, lookup_matrix).astype(jnp.bfloat16).reshape(slots, text_len, width)
    )
    contents = split_heads(
        project(text_rows, content_matrix).astype(jnp.bfloat16).reshape(slots, text_len, width)
    )
    cross_scores = (
        jnp.einsum("sqhd,skhd->shqk", probes, lookups, preferred_element_type=jnp.float32) * scale
    )
    cross_scores = jnp.where(text_allowed[:, None, None, :], cross_scores, masked_score)
    cross_peak = jnp.max(cross_scores, axis=-1, keepdims=True)
    cross_weights = jnp.exp(cross_scores - cross_peak)
    cross_probs = cross_weights / jnp.sum(cross_weights, axis=-1, keepdims=True)
    cross_probs_low = cross_probs.astype(jnp.bfloat16)
    cross_mixed = jnp.einsum(
        "shqk,skhd->sqhd", cross_probs_low, contents, preferred_element_type=jnp.float32
    )
    cross_mixed = cross_mixed.astype(jnp.bfloat16).reshape(row_count, width)
    after_cross = after_self + project(cross_mixed, merge_matrix).reshape(slots, frame_count, width)
    normed_three, pull_three = jax.vjp(
        layer_norm, after_cross, gain_feed.astype(jnp.float32), bias_feed.astype(jnp.float32)
    )
    hidden_three = normed_three.astype(jnp.bfloat16).reshape(row_count, width)
    upward = project(hidden_three, expand_matrix)
    activated, gelu_pull = jax.vjp(exact_gelu, upward)
    activated_low = activated.astype(jnp.bfloat16)
    result = after_cross + project(activated_low, reduce_matrix).reshape(slots, frame_count, width)
    output = result.astype(jnp.bfloat16)
    errors = (result - teacher.astype(jnp.float32)) * valid_rows[..., None]
    squares_total, count_total = lax.psum(
        (jnp.sum(errors * errors), jnp.sum(valid_rows)), ("replica", "shard")
    )
    loss = squares_total / (width * count_total)
    grad_result = errors * (slots * replicas * clip_total / count_total)
    grad_feed_low = grad_result.reshape(row_count, width).astype(jnp.bfloat16)
    grad_activated = back_project(grad_feed_low, reduce_matrix)
    grad_upward = gelu_pull(grad_activated)[0].astype(jnp.bfloat16)
    grad_hidden_three = back_project(grad_upward, expand_matrix).reshape(slots, frame_count, width)
    grad_cross_norm, gain_feed_part, bias_feed_part = pull_three(grad_hidden_three)
    grad_after_cross = grad_result + grad_cross_norm
    feed_owned = (
        lax.psum_scatter(
            outer_sum(hidden_three, grad_upward).astype(jnp.bfloat16),
            "shard",
            scatter_dimension=0,
            tiled=True,
        ).astype(jnp.float32),
        lax.psum_scatter(
            outer_sum(activated_low, grad_feed_low).astype(jnp.bfloat16),
            "shard",
            scatter_dimension=0,
            tiled=True,
        ).astype(jnp.float32),
        lax.psum_scatter(
            gain_feed_part.astype(jnp.bfloat16), "shard", scatter_dimension=0, tiled=True
        ).astype(jnp.float32),
        lax.psum_scatter(
            bias_feed_part.astype(jnp.bfloat16), "shard", scatter_dimension=0, tiled=True
        ).astype(jnp.float32),
    )
    grad_cross_low = grad_after_cross.reshape(row_count, width).astype(jnp.bfloat16)
    grad_cross_mixed = split_heads(
        back_project(grad_cross_low, merge_matrix)
        .astype(jnp.bfloat16)
        .reshape(slots, frame_count, width)
    )
    grad_cross_probs = jnp.einsum(
        "sqhd,skhd->shqk", grad_cross_mixed, contents, preferred_element_type=jnp.float32
    )
    content_grads = jnp.einsum(
        "shqk,sqhd->skhd", cross_probs_low, grad_cross_mixed, preferred_element_type=jnp.float32
    )
    cross_inner = jnp.sum(cross_probs * grad_cross_probs, axis=-1, keepdims=True)
    grad_cross_scores = (cross_probs * (grad_cross_probs - cross_inner)).astype(jnp.bfloat16)
    probe_grads = (
        jnp.einsum(
            "shqk,skhd->sqhd", grad_cross_scores, lookups, preferred_element_type=jnp.float32
        )
        * scale
    )
    probe_grads = probe_grads.astype(jnp.bfloat16).reshape(row_count, width)
    lookup_grads = (
        jnp.einsum("shqk,sqhd->skhd", grad_cross_scores, probes, preferred_element_type=jnp.float32)
        * scale
    )
    lookup_sum, content_sum = (
        lax.psum(lookup_grads.astype(jnp.bfloat16), "shard").astype(jnp.float32),
        lax.psum(content_grads.astype(jnp.bfloat16), "shard").astype(jnp.float32),
    )
    lookup_low = lookup_sum.astype(jnp.bfloat16).reshape(slots * text_len, width)
    content_low = content_sum.astype(jnp.bfloat16).reshape(slots * text_len, width)
    own_width = width // shards
    own_text = lax.dynamic_slice_in_dim(text_rows, shard_rank * own_width, own_width, 1)
    lookup_own = outer_sum(own_text, lookup_low)
    content_own = outer_sum(own_text, content_low)
    text_grad = (
        back_project(lookup_low, lookup_matrix) + back_project(content_low, content_matrix)
    ).reshape(slots, text_len, width)
    grad_hidden_two = back_project(probe_grads, probe_matrix).reshape(slots, frame_count, width)
    grad_self_norm, gain_cross_part, bias_cross_part = pull_two(grad_hidden_two)
    grad_after_self = grad_after_cross + grad_self_norm
    grad_self_low = grad_after_self.reshape(row_count, width).astype(jnp.bfloat16)
    grad_mixed = split_heads(
        back_project(grad_self_low, output_matrix)
        .astype(jnp.bfloat16)
        .reshape(slots, frame_count, width)
    )
    grad_queries, grad_keys, grad_values = lax.map(
        self_backward, (head_queries, head_keys, head_values, allowed, log_totals, grad_mixed)
    )
    key_sum, value_sum = (
        lax.psum_scatter(
            grad_keys.reshape(slots, clip_total, width).astype(jnp.bfloat16),
            "shard",
            scatter_dimension=1,
            tiled=True,
        ).astype(jnp.float32),
        lax.psum_scatter(
            grad_values.reshape(slots, clip_total, width).astype(jnp.bfloat16),
            "shard",
            scatter_dimension=1,
            tiled=True,
        ).astype(jnp.float32),
    )
    key_low = key_sum.astype(jnp.bfloat16).reshape(row_count, width)
    value_low = value_sum.astype(jnp.bfloat16).reshape(row_count, width)
    query_low = grad_queries.reshape(row_count, width)
    grad_hidden_one = (
        back_project(query_low, query_matrix)
        + back_project(key_low, key_matrix)
        + back_project(value_low, value_matrix)
    )
    grad_inputs, gain_attend_part, bias_attend_part = pull_one(
        grad_hidden_one.reshape(slots, frame_count, width)
    )
    frames_grad = grad_after_self + grad_inputs
    attend_owned = (
        lax.psum_scatter(
            outer_sum(hidden_one, query_low).astype(jnp.bfloat16),
            "shard",
            scatter_dimension=0,
            tiled=True,
        ).astype(jnp.float32),
        lax.psum_scatter(
            outer_sum(hidden_one, key_low).astype(jnp.bfloat16),
            "shard",
            scatter_dimension=0,
            tiled=True,
        ).astype(jnp.float32),
        lax.psum_scatter(
            outer_sum(hidden_one, value_low).astype(jnp.bfloat16),
            "shard",
            scatter_dimension=0,
            tiled=True,
        ).astype(jnp.float32),
        lax.psum_scatter(
            outer_sum(mixed_rows, grad_self_low).astype(jnp.bfloat16),
            "shard",
            scatter_dimension=0,
            tiled=True,
        ).astype(jnp.float32),
        lax.psum_scatter(
            outer_sum(hidden_two, probe_grads).astype(jnp.bfloat16),
            "shard",
            scatter_dimension=0,
            tiled=True,
        ).astype(jnp.float32),
        lax.psum_scatter(
            outer_sum(cross_mixed, grad_cross_low).astype(jnp.bfloat16),
            "shard",
            scatter_dimension=0,
            tiled=True,
        ).astype(jnp.float32),
        lax.psum_scatter(
            gain_attend_part.astype(jnp.bfloat16), "shard", scatter_dimension=0, tiled=True
        ).astype(jnp.float32),
        lax.psum_scatter(
            bias_attend_part.astype(jnp.bfloat16), "shard", scatter_dimension=0, tiled=True
        ).astype(jnp.float32),
        lax.psum_scatter(
            gain_cross_part.astype(jnp.bfloat16), "shard", scatter_dimension=0, tiled=True
        ).astype(jnp.float32),
        lax.psum_scatter(
            bias_cross_part.astype(jnp.bfloat16), "shard", scatter_dimension=0, tiled=True
        ).astype(jnp.float32),
    )
    summed = (
        lax.psum(attend_owned[6].astype(jnp.bfloat16), "replica").astype(jnp.float32),
        lax.psum(attend_owned[7].astype(jnp.bfloat16), "replica").astype(jnp.float32),
        lax.psum(attend_owned[0].astype(jnp.bfloat16), "replica").astype(jnp.float32),
        lax.psum(attend_owned[1].astype(jnp.bfloat16), "replica").astype(jnp.float32),
        lax.psum(attend_owned[2].astype(jnp.bfloat16), "replica").astype(jnp.float32),
        lax.psum(attend_owned[3].astype(jnp.bfloat16), "replica").astype(jnp.float32),
        lax.psum(attend_owned[8].astype(jnp.bfloat16), "replica").astype(jnp.float32),
        lax.psum(attend_owned[9].astype(jnp.bfloat16), "replica").astype(jnp.float32),
        lax.psum(attend_owned[4].astype(jnp.bfloat16), "replica").astype(jnp.float32),
        lax.psum(lookup_own.astype(jnp.bfloat16), "replica").astype(jnp.float32),
        lax.psum(content_own.astype(jnp.bfloat16), "replica").astype(jnp.float32),
        lax.psum(attend_owned[5].astype(jnp.bfloat16), "replica").astype(jnp.float32),
        lax.psum(feed_owned[2].astype(jnp.bfloat16), "replica").astype(jnp.float32),
        lax.psum(feed_owned[3].astype(jnp.bfloat16), "replica").astype(jnp.float32),
        lax.psum(feed_owned[0].astype(jnp.bfloat16), "replica").astype(jnp.float32),
        lax.psum(feed_owned[1].astype(jnp.bfloat16), "replica").astype(jnp.float32),
    )
    return (
        output,
        loss,
        frames_grad,
        text_grad,
        summed[0],
        summed[1],
        summed[2],
        summed[3],
        summed[4],
        summed[5],
        summed[6],
        summed[7],
        summed[8],
        summed[9],
        summed[10],
        summed[11],
        summed[12],
        summed[13],
        summed[14],
        summed[15],
    )


PAIR = 2 * HEAD_DIM
EVERY = ("shard", "y", "x", "core")
REPLICAS = ("core", "y", "x")
NT = (((1,), (1,)), ((), ()))
TN = (((0,), (0,)), ((), ()))
NN = (((1,), (0,)), ((), ()))


def dot(left, right, dims):
    return lax.dot_general(left, right, dims, preferred_element_type=jnp.float32)


def half_mask(side, value):
    lanes = lax.broadcasted_iota(jnp.int32, (1, PAIR), 1)
    inside = (lanes >= HEAD_DIM) if side else (lanes < HEAD_DIM)
    return jnp.where(inside, value, 0.0).astype(jnp.bfloat16)


def fill_clip(place, own_ref, other_ref, all_ref):
    block = own_ref.shape[0] // 2
    for part in range(2):
        rows = slice(part * block, (part + 1) * block)
        for at, ref in ((place[part], own_ref), (place[3 + part], other_ref)):
            all_ref[pl.ds(pl.multiple_of(at * block, block), block), :] = ref[rows, :]


def self_forward_kernel(
    place, q_ref, own_k, own_v, other_k, other_v, mixed_ref, lse_ref, k_ref, v_ref, acc_ref
):
    fill_clip(place, own_k, other_k, k_ref)
    fill_clip(place, own_v, other_v, v_ref)
    block = q_ref.shape[0] // 2
    length = place[2]
    low = lax.broadcasted_iota(jnp.int32, (PAIR, 1), 0) < HEAD_DIM
    for part in range(2):
        first = place[part] * block
        rows = slice(part * block, (part + 1) * block)
        q = q_ref[rows, :]
        q_half = [q * half_mask(side, HEAD_DIM ** (-0.5)) for side in range(2)]
        limit = jnp.minimum(
            first + lax.broadcasted_iota(jnp.int32, (1, block), 1) + 1, length
        )
        acc_ref[...] = jnp.zeros_like(acc_ref)

        def step(j, peaks, q_half=q_half, limit=limit):
            at = pl.multiple_of(j * block, block)
            k = k_ref[pl.ds(at, block), :]
            v = v_ref[pl.ds(at, block), :]
            allowed = at + lax.broadcasted_iota(jnp.int32, (block, block), 0) < limit
            out = []
            for side in range(2):
                scores = jnp.where(allowed, dot(k, q_half[side], NT), masked_score)
                peak = jnp.maximum(peaks[side], jnp.max(scores, axis=0, keepdims=True))
                weights = jnp.exp(scores - peak).astype(jnp.bfloat16)
                v_ones = v * half_mask(side, 1.0) + half_mask(1 - side, 1.0)
                acc_ref[side] = acc_ref[side] * jnp.exp(peaks[side] - peak) + dot(
                    v_ones, weights, TN
                )
                out.append(peak)
            return tuple(out)

        peaks = lax.fori_loop(
            0, place[part] + 1, step, (jnp.full((1, block), masked_score, jnp.float32),) * 2
        )
        top, bottom = acc_ref[0], acc_ref[1]
        total = jnp.where(low, top[HEAD_DIM : HEAD_DIM + 1], bottom[0:1])
        mixed = jnp.where(low, top, bottom) / total
        mixed_ref[rows, :] = mixed.T.astype(jnp.bfloat16)
        lse_ref[0:1, rows] = peaks[0] + jnp.log(top[HEAD_DIM : HEAD_DIM + 1])
        lse_ref[1:2, rows] = peaks[1] + jnp.log(bottom[0:1])


def self_backward_kernel(
    place, q_ref, own_k, own_v, other_k, other_v, mixed_ref, grad_ref, lse_ref,
    dq_ref, own_dk, own_dv, other_dk, other_dv, k_ref, v_ref, dq_acc, dk_acc, dv_acc,
):
    fill_clip(place, own_k, other_k, k_ref)
    fill_clip(place, own_v, other_v, v_ref)
    block = q_ref.shape[0] // 2
    length = place[2]
    scale = HEAD_DIM ** (-0.5)
    dk_acc[...] = jnp.zeros_like(dk_acc)
    dv_acc[...] = jnp.zeros_like(dv_acc)
    for part in range(2):
        first = place[part] * block
        rows = slice(part * block, (part + 1) * block)
        q = q_ref[rows, :]
        grad = grad_ref[rows, :]
        q_half = [q * half_mask(side, scale) for side in range(2)]
        grad_half = [grad * half_mask(side, 1.0) for side in range(2)]
        product = (grad.astype(jnp.float32) * mixed_ref[rows, :].astype(jnp.float32)).T
        inner = [
            jnp.sum(product[side * HEAD_DIM : (side + 1) * HEAD_DIM], axis=0, keepdims=True)
            for side in range(2)
        ]
        lse = [lse_ref[side : side + 1, rows] for side in range(2)]
        limit = jnp.minimum(
            first + lax.broadcasted_iota(jnp.int32, (1, block), 1) + 1, length
        )
        dq_acc[...] = jnp.zeros_like(dq_acc)

        def step(
            j, carry, q_half=q_half, grad_half=grad_half, inner=inner, lse=lse, limit=limit
        ):
            at = pl.multiple_of(j * block, block)
            k = k_ref[pl.ds(at, block), :]
            v = v_ref[pl.ds(at, block), :]
            allowed = at + lax.broadcasted_iota(jnp.int32, (block, block), 0) < limit
            dq, dk, dv = 0.0, 0.0, 0.0
            for side in range(2):
                scores = jnp.where(allowed, dot(k, q_half[side], NT), masked_score)
                probs = jnp.exp(scores - lse[side])
                grad_probs = dot(v, grad_half[side], NT)
                grad_scores = (probs * (grad_probs - inner[side])).astype(jnp.bfloat16)
                dv += dot(probs.astype(jnp.bfloat16), grad_half[side], NN)
                dk += dot(grad_scores, q_half[side], NN)
                dq += dot(k * half_mask(side, scale), grad_scores, TN)
            dk_acc[pl.ds(at, block), :] += dk
            dv_acc[pl.ds(at, block), :] += dv
            dq_acc[...] += dq
            return carry

        lax.fori_loop(0, place[part] + 1, step, 0)
        dq_ref[rows, :] = dq_acc[...].T.astype(jnp.bfloat16)
    for part in range(2):
        rows = slice(part * block, (part + 1) * block)
        own = pl.ds(pl.multiple_of(place[part] * block, block), block)
        other = pl.ds(pl.multiple_of(place[3 + part] * block, block), block)
        own_dk[rows, :] = dk_acc[own, :].astype(jnp.bfloat16)
        own_dv[rows, :] = dv_acc[own, :].astype(jnp.bfloat16)
        other_dk[rows, :] = dk_acc[other, :].astype(jnp.bfloat16)
        other_dv[rows, :] = dv_acc[other, :].astype(jnp.bfloat16)


def pair_block(rows):
    return pl.BlockSpec((rows, PAIR), lambda i, *_: (0, i))


def value_block(rows, pairs):
    return pl.BlockSpec((rows, PAIR), lambda i, *_: (0, pairs + i))


def self_attend(place, queries, own, other):
    rows, width = queries.shape
    clip = 2 * rows
    pairs = width // PAIR
    return pl.pallas_call(
        self_forward_kernel,
        out_shape=(
            jax.ShapeDtypeStruct((rows, width), jnp.bfloat16),
            jax.ShapeDtypeStruct((pairs * 8, rows), jnp.float32),
        ),
        grid_spec=pltpu.PrefetchScalarGridSpec(
            num_scalar_prefetch=1,
            grid=(pairs,),
            in_specs=[pair_block(rows)] + [pair_block(rows), value_block(rows, pairs)] * 2,
            out_specs=(pair_block(rows), pl.BlockSpec((8, rows), lambda i, *_: (i, 0))),
            scratch_shapes=[
                pltpu.VMEM((clip, PAIR), jnp.bfloat16),
                pltpu.VMEM((clip, PAIR), jnp.bfloat16),
                pltpu.VMEM((2, PAIR, rows // 2), jnp.float32),
            ],
        ),
        compiler_params=pltpu.CompilerParams(vmem_limit_bytes=32 * 2**20),
        cost_estimate=pl.CostEstimate(
            flops=2 * 2 * rows * clip * width, bytes_accessed=8 * clip * width, transcendentals=0
        ),
        name="self_attend",
    )(place, queries, own, own, other, other)


def self_attend_back(place, queries, own, other, mixed, grads, lse):
    rows, width = queries.shape
    clip = 2 * rows
    pairs = width // PAIR
    return pl.pallas_call(
        self_backward_kernel,
        out_shape=(jax.ShapeDtypeStruct((rows, width), jnp.bfloat16),) * 5,
        grid_spec=pltpu.PrefetchScalarGridSpec(
            num_scalar_prefetch=1,
            grid=(pairs,),
            in_specs=[pair_block(rows)]
            + [pair_block(rows), value_block(rows, pairs)] * 2
            + [
                pair_block(rows),
                pair_block(rows),
                pl.BlockSpec((8, rows), lambda i, *_: (i, 0)),
            ],
            out_specs=(pair_block(rows),) * 5,
            scratch_shapes=[
                pltpu.VMEM((clip, PAIR), jnp.bfloat16),
                pltpu.VMEM((clip, PAIR), jnp.bfloat16),
                pltpu.VMEM((PAIR, rows // 2), jnp.float32),
                pltpu.VMEM((clip, PAIR), jnp.float32),
                pltpu.VMEM((clip, PAIR), jnp.float32),
            ],
        ),
        compiler_params=pltpu.CompilerParams(vmem_limit_bytes=32 * 2**20),
        cost_estimate=pl.CostEstimate(
            flops=5 * 2 * rows * clip * width, bytes_accessed=16 * clip * width, transcendentals=0
        ),
        name="self_attend_back",
    )(place, queries, own, own, other, other, mixed, grads, lse)


def both_heads(rows, value):
    return jnp.concatenate([rows * half_mask(side, value) for side in range(2)], axis=0)


def cross_probs_of(lookup_two, probes, present):
    text = present.shape[0]
    scores = dot(lookup_two, probes, NT)
    out = []
    for side in range(2):
        part = jnp.where(
            present > 0, scores[side * text : (side + 1) * text], masked_score
        )
        weights = jnp.exp(part - jnp.max(part, axis=0, keepdims=True))
        out.append(weights / jnp.sum(weights, axis=0, keepdims=True))
    return out


def cross_forward_kernel(probe_ref, lookup_ref, content_ref, present_ref, mixed_ref):
    probs = cross_probs_of(
        both_heads(lookup_ref[...], HEAD_DIM ** (-0.5)), probe_ref[...], present_ref[...]
    )
    probs = jnp.concatenate(probs, axis=0).astype(jnp.bfloat16)
    mixed_ref[...] = dot(probs, both_heads(content_ref[...], 1.0), TN).astype(jnp.bfloat16)


def cross_backward_kernel(
    probe_ref, lookup_ref, content_ref, present_ref, grad_ref, dp_ref, dl_ref, dc_ref
):
    text = present_ref.shape[0]
    scale = HEAD_DIM ** (-0.5)
    probes = probe_ref[...]
    grads = grad_ref[...]
    lookup_two = both_heads(lookup_ref[...], scale)
    probs = cross_probs_of(lookup_two, probes, present_ref[...])
    grad_probs = dot(both_heads(content_ref[...], 1.0), grads, NT)
    grad_scores = []
    for side in range(2):
        part = grad_probs[side * text : (side + 1) * text]
        inner = jnp.sum(probs[side] * part, axis=0, keepdims=True)
        grad_scores.append(probs[side] * (part - inner))
    grad_scores = jnp.concatenate(grad_scores, axis=0).astype(jnp.bfloat16)
    probs = jnp.concatenate(probs, axis=0).astype(jnp.bfloat16)
    low = lax.broadcasted_iota(jnp.int32, (1, PAIR), 1) < HEAD_DIM
    dp_ref[...] = dot(grad_scores, lookup_two, TN).astype(jnp.bfloat16)
    dl = dot(grad_scores, probes, NN) * scale
    dl_ref[...] = jnp.where(low, dl[:text], dl[text:]).astype(jnp.bfloat16)
    dc = dot(probs, grads, NN)
    dc_ref[...] = jnp.where(low, dc[:text], dc[text:]).astype(jnp.bfloat16)


def cross_attend(probes, lookups, contents, present):
    rows, width = probes.shape
    text = lookups.shape[0]
    return pl.pallas_call(
        cross_forward_kernel,
        out_shape=jax.ShapeDtypeStruct((rows, width), jnp.bfloat16),
        grid=(width // PAIR,),
        in_specs=[
            pair_block(rows),
            pair_block(text),
            pair_block(text),
            pl.BlockSpec((text, 1), lambda i: (0, 0)),
        ],
        out_specs=pair_block(rows),
        compiler_params=pltpu.CompilerParams(vmem_limit_bytes=32 * 2**20),
        cost_estimate=pl.CostEstimate(
            flops=8 * rows * text * width, bytes_accessed=4 * rows * width, transcendentals=0
        ),
        name="cross_attend",
    )(probes, lookups, contents, present)


def cross_attend_back(probes, lookups, contents, present, grads):
    rows, width = probes.shape
    text = lookups.shape[0]
    return pl.pallas_call(
        cross_backward_kernel,
        out_shape=(
            jax.ShapeDtypeStruct((rows, width), jnp.bfloat16),
            jax.ShapeDtypeStruct((text, width), jnp.bfloat16),
            jax.ShapeDtypeStruct((text, width), jnp.bfloat16),
        ),
        grid=(width // PAIR,),
        in_specs=[
            pair_block(rows),
            pair_block(text),
            pair_block(text),
            pl.BlockSpec((text, 1), lambda i: (0, 0)),
            pair_block(rows),
        ],
        out_specs=(pair_block(rows), pair_block(text), pair_block(text)),
        compiler_params=pltpu.CompilerParams(vmem_limit_bytes=32 * 2**20),
        cost_estimate=pl.CostEstimate(
            flops=20 * rows * text * width, bytes_accessed=6 * rows * width, transcendentals=0
        ),
        name="cross_attend_back",
    )(probes, lookups, contents, present, grads)


def unpack_kernel(in_ref, out_ref):
    pieces = in_ref[...]
    out_ref[...] = pieces.reshape(-1, pieces.shape[-1]).T.astype(jnp.float32)


def unpack(full, rows, place, out_shape, out_at, together):
    owners, _, features = full.shape
    tall = out_shape[0] // features
    wide = out_shape[1] // (together * rows)
    return pl.pallas_call(
        unpack_kernel,
        out_shape=jax.ShapeDtypeStruct(out_shape, jnp.float32),
        grid=(tall, wide),
        in_specs=[
            pl.BlockSpec((together, rows, features), lambda i, j: (j + out_at, place + i, 0))
        ],
        out_specs=pl.BlockSpec((features, together * rows), lambda i, j: (i, j)),
        compiler_params=pltpu.CompilerParams(vmem_limit_bytes=32 * 2**20),
        cost_estimate=pl.CostEstimate(
            flops=0, bytes_accessed=6 * out_shape[0] * out_shape[1], transcendentals=0
        ),
        name="unpack",
    )(full)


def held(values, *others):
    return list(lax.optimization_barrier((*values, *others))[: len(values)])


def after(value, *others):
    return lax.optimization_barrier((value, *others))[0]


def norm_parts(values):
    mean = jnp.mean(values, axis=-1, keepdims=True)
    center = values - mean
    return mean, lax.rsqrt(jnp.mean(center * center, axis=-1, keepdims=True) + epsilon)


def norm_back(grads, values, parts, gain):
    mean, inverse = parts
    unit = (values - mean) * inverse
    gain_grad = jnp.sum(grads * unit, axis=0)
    bias_grad = jnp.sum(grads, axis=0)
    scaled = grads * gain
    back = inverse * (
        scaled
        - jnp.mean(scaled, axis=-1, keepdims=True)
        - unit * jnp.mean(scaled * unit, axis=-1, keepdims=True)
    )
    return back, gain_grad, bias_grad


def clip_body(
    frames,
    text_states,
    text_mask,
    clip_lengths,
    slot_used,
    teacher,
    self_norm_gain,
    self_norm_bias,
    self_query_weight,
    self_key_weight,
    self_value_weight,
    self_output_weight,
    cross_norm_gain,
    cross_norm_bias,
    cross_query_weight,
    cross_key_weight,
    cross_value_weight,
    cross_output_weight,
    feed_norm_gain,
    feed_norm_bias,
    feed_up_weight,
    feed_down_weight,
):
    block, width = frames.shape[1:]
    text_len = text_states.shape[1]
    shards, replicas, outers = 4, 8, 4
    core = lax.axis_index("core")
    shard = lax.axis_index("shard")
    outer = 2 * lax.axis_index("y") + lax.axis_index("x")
    replica = 2 * outer + core
    clip = block * shards
    hidden_units = feed_up_weight.shape[1]

    holder = {0: 0, 1: 1, 2: 1, 3: 0}
    there = ([], [])
    for c in range(2):
        for s in range(4):
            for turn in range(2):
                slot = turn if s < 2 else 1 - turn
                there[turn].append((c * 4 + s, holder[s] * 4 + 2 * c + slot))
    back = tuple([(b, a) for a, b in pairs] for pairs in there)
    spot = ("core", "shard")
    swap = [(0, 1), (1, 0)]
    even = shard % 2 == 0
    lower = shard < 2
    first_core = core == 0

    def hop(values, distance):
        pairs = [(i, (i + distance) % shards) for i in range(shards)]
        return lax.ppermute(values, "shard", pairs)

    def hops(values):
        return [hop(values, distance) for distance in (1, 2, 3)]

    def line_up(mine, came):
        out = jnp.zeros((shards,) + mine.shape, mine.dtype)
        out = lax.dynamic_update_index_in_dim(out, mine, shard, 0)
        for distance, values in zip((1, 2, 3), came):
            owner = lax.rem(shard + shards - distance, shards)
            out = lax.dynamic_update_index_in_dim(out, values, owner, 0)
        return out

    def to_chip(pair):
        one = lax.ppermute(jnp.where(lower, pair[0], pair[1]), spot, there[0])
        two = lax.ppermute(jnp.where(lower, pair[1], pair[0]), spot, there[1])
        return one, two

    def by_time(one, two):
        return jnp.concatenate([jnp.where(even, one, two), jnp.where(even, two, one)], axis=0)

    def outgoing(values):
        early, late = values[:block], values[block:]
        return jnp.where(even, early, late), jnp.where(even, late, early)

    def from_chip(values):
        one, two = outgoing(values)
        return lax.ppermute(one, spot, back[0]), lax.ppermute(two, spot, back[1])

    def by_slot(one, two):
        return jnp.stack([jnp.where(lower, one, two), jnp.where(lower, two, one)])

    def share_of(weight):
        share = weight.shape[0] // replicas
        return lax.dynamic_slice_in_dim(weight, replica * share, share, 0)

    def from_replicas(line):
        full = lax.all_gather(line, ("y", "x", "core"), axis=1, tiled=True)
        return full.reshape(-1, line.shape[-1])

    qkv_share = jnp.concatenate(
        [share_of(self_query_weight), share_of(self_key_weight), share_of(self_value_weight)],
        axis=1,
    )
    vectors = jnp.concatenate(
        [
            self_norm_gain,
            self_norm_bias,
            cross_norm_gain,
            cross_norm_bias,
            feed_norm_gain,
            feed_norm_bias,
        ]
    )
    vectors = jnp.pad(vectors[None, :], ((0, 15), (0, 3 * width - 6 * block)))
    share = qkv_share.shape[0]
    qkv_mine = jnp.concatenate([qkv_share, vectors], axis=0)
    qkv_came = hops(qkv_mine)
    qkv_matrix = from_replicas(line_up(qkv_share, [values[:share] for values in qkv_came]))
    norms = line_up(vectors[0], [values[share] for values in qkv_came])
    norms = norms[:, : 6 * block].reshape(shards, 6, block).transpose(1, 0, 2)
    norms = norms.reshape(6, width).astype(jnp.float32)
    came = to_chip(after(frames, *qkv_came))
    x_low = by_time(*came)
    rest_share = jnp.concatenate(
        [share_of(self_output_weight), share_of(cross_query_weight), share_of(cross_output_weight)],
        axis=1,
    )
    rest_came = hops(after(rest_share, *came))
    expand_share = share_of(feed_up_weight)

    facts = jnp.concatenate(
        [(clip_lengths // 64)[:, None], (clip_lengths % 64)[:, None], slot_used[:, None], text_mask],
        axis=1,
    ).astype(jnp.bfloat16)
    facts = jnp.pad(facts[:, None, :], ((0, 0), (0, 15), (0, width - facts.shape[1])))
    text_sent = lax.ppermute(jnp.concatenate([text_states, facts], axis=1), "core", swap)
    text_other = text_sent[:, :text_len]
    both = jnp.stack([facts[:, 0], text_sent[:, text_len]])[:, :, : 3 + text_len].astype(jnp.int32)
    lengths = 64 * both[:, :, 0] + both[:, :, 1]
    fact = lax.dynamic_index_in_dim(
        jnp.where(shard // 2 == core, both[0], both[1]), shard % 2, 0, keepdims=False
    )
    length, used = 64 * fact[0] + fact[1], fact[2]
    present = fact[3:].reshape(text_len, 1)
    count = jnp.sum(
        jnp.where(both[:, :, 2] > 0, jnp.minimum(lengths, clip), 0).astype(jnp.float32)
    )
    count = jnp.full((8, 128), count)
    for axis in ("x", "y"):
        count += lax.ppermute(count, axis, swap)
    count = count[0, 0]
    text_all = jnp.concatenate(
        [
            jnp.where(first_core, text_states, text_other),
            jnp.where(first_core, text_other, text_states),
        ],
        axis=0,
    ).reshape(4 * text_len, width)
    text_all = lax.dynamic_slice_in_dim(text_all, shard * block, block, 1)
    text_matrix = jnp.where(first_core, cross_key_weight, cross_value_weight)
    text_part = project(text_all, text_matrix).astype(jnp.bfloat16).reshape(4, text_len, width)
    text_came = [
        hop(
            lax.dynamic_index_in_dim(
                text_part, lax.rem(shard + distance, shards), 0, keepdims=False
            ),
            distance,
        )
        for distance in (1, 2, 3)
    ]

    places = jnp.stack([core, 3 - core, length, 1 - core, 2 + core]).astype(jnp.int32)
    positions = jnp.concatenate(
        [core * block + jnp.arange(block), (3 - core) * block + jnp.arange(block)]
    )
    valid_rows = ((positions < length) & (used > 0)).astype(jnp.float32)[:, None]
    inputs = x_low.astype(jnp.float32)
    parts_one = norm_parts(inputs)
    hidden_one = ((inputs - parts_one[0]) * parts_one[1] * norms[0] + norms[1]).astype(
        jnp.bfloat16
    )
    kv = project(after(hidden_one, count), qkv_matrix[:, width:]).astype(jnp.bfloat16)
    kv_other = lax.ppermute(kv, "core", swap)
    queries = project(after(hidden_one, kv), qkv_matrix[:, :width]).astype(jnp.bfloat16)
    rest_came = held(rest_came, kv)
    rest = from_replicas(line_up(rest_share, rest_came))
    output_matrix = rest[:, :width]
    probe_matrix = rest[:, width : 2 * width]
    merge_matrix = rest[:, 2 * width :]
    text_came = held(text_came, queries)
    text_half = lax.dynamic_index_in_dim(text_part, shard, 0, keepdims=False).astype(jnp.float32)
    for values in text_came:
        text_half += values.astype(jnp.float32)
    text_half = text_half.astype(jnp.bfloat16)
    text_swap = lax.ppermute(text_half, "core", swap)
    lookups = jnp.where(first_core, text_half, text_swap)
    contents = jnp.where(first_core, text_swap, text_half)
    expand_came = hops(after(expand_share, *rest_came, *text_came))
    mixed_self, lse = self_attend(after(places, rest_came[0]), queries, kv, kv_other)
    expand_came = held(expand_came, mixed_self)
    expand_matrix = from_replicas(line_up(expand_share, expand_came))
    reduce_share = share_of(feed_down_weight)
    reduce_came = hops(after(reduce_share, *expand_came))
    after_self = inputs + project(mixed_self, output_matrix)
    parts_two = norm_parts(after_self)
    hidden_two = ((after_self - parts_two[0]) * parts_two[1] * norms[2] + norms[3]).astype(
        jnp.bfloat16
    )
    probes = project(hidden_two, probe_matrix).astype(jnp.bfloat16)
    reduce_matrix = from_replicas(line_up(reduce_share, held(reduce_came, probes)))
    teacher_low = by_time(*to_chip(after(teacher, *reduce_came, probes)))
    cross_mixed = cross_attend(probes, lookups, contents, present)
    after_cross = after_self + project(cross_mixed, merge_matrix)
    parts_three = norm_parts(after_cross)
    hidden_three = (
        (after_cross - parts_three[0]) * parts_three[1] * norms[4] + norms[5]
    ).astype(jnp.bfloat16)
    upward = project(hidden_three, expand_matrix)
    activated, gelu_pull = jax.vjp(exact_gelu, upward)
    activated_low = activated.astype(jnp.bfloat16)
    result = after_cross + project(activated_low, reduce_matrix)
    errors = (result - teacher_low.astype(jnp.float32)) * valid_rows
    squares = jnp.sum(errors * errors)
    grad_result = errors * (4 * outers * clip / count)
    grad_feed_low = grad_result.astype(jnp.bfloat16)

    def theirs_of(right, left):
        columns = right.shape[1] // 2
        part = lax.dynamic_slice_in_dim(right, (1 - core) * columns, columns, 1)
        return outer_sum(part, left).astype(jnp.bfloat16)

    def ours_of(right, left, theirs):
        columns = right.shape[1] // 2
        sent = lax.ppermute(theirs, "core", swap)
        part = lax.dynamic_slice_in_dim(right, core * columns, columns, 1)
        return (outer_sum(part, left) + sent.astype(jnp.float32)).astype(jnp.bfloat16)

    def over_outer(values):
        return lax.psum_scatter(values, ("y", "x"), scatter_dimension=0, tiled=True)

    def shard_hops(values):
        columns = values.shape[1] // shards
        return [
            hop(
                lax.dynamic_slice_in_dim(
                    values, lax.rem(shard + distance, shards) * columns, columns, 1
                ),
                distance,
            )
            for distance in (1, 2, 3)
        ]

    def over_shard(values, came):
        columns = values.shape[1] // shards
        total = lax.dynamic_slice_in_dim(values, shard * columns, columns, 1).astype(jnp.float32)
        for part in came:
            total += part.astype(jnp.float32)
        return total.astype(jnp.bfloat16)

    down_theirs = theirs_of(grad_feed_low, activated_low)
    to_send = outgoing(result.astype(jnp.bfloat16))
    output_one = lax.ppermute(to_send[0], spot, back[0])
    grad_activated = back_project(after(grad_feed_low, down_theirs), reduce_matrix)
    grad_upward = gelu_pull(grad_activated)[0].astype(jnp.bfloat16)
    output_one = after(output_one, grad_upward)
    down_ours = ours_of(
        after(grad_feed_low, grad_upward, output_one), activated_low, down_theirs
    )
    down_sum = over_outer(down_ours)
    up_theirs = theirs_of(after(grad_upward, down_ours), hidden_three)
    grad_hidden_three = back_project(after(grad_upward, up_theirs), expand_matrix)
    output_two = lax.ppermute(after(to_send[1], output_one), spot, back[1])
    output_two = after(output_two, grad_hidden_three)
    output = by_slot(output_one, output_two)
    up_ours = ours_of(after(grad_upward, grad_hidden_three, output_two), hidden_three, up_theirs)
    grad_norm, gain_feed, bias_feed = norm_back(
        after(grad_hidden_three, up_ours), after_cross, parts_three, norms[4]
    )
    grad_after_cross = grad_result + grad_norm
    grad_cross_low = grad_after_cross.astype(jnp.bfloat16)
    merge_theirs = theirs_of(grad_cross_low, cross_mixed)
    grad_cross_mixed = back_project(after(grad_cross_low, merge_theirs), merge_matrix).astype(
        jnp.bfloat16
    )
    probe_grads, lookup_grads, content_grads = cross_attend_back(
        probes, lookups, contents, present, grad_cross_mixed
    )
    up_sum = over_outer(up_ours)
    text_mine = jnp.where(first_core, lookup_grads, content_grads)
    text_sent = lax.ppermute(
        jnp.where(first_core, content_grads, lookup_grads), "core", swap
    )
    text_mine = (text_mine.astype(jnp.float32) + text_sent.astype(jnp.float32)).astype(
        jnp.bfloat16
    )
    merge_ours = ours_of(after(grad_cross_low, probe_grads), cross_mixed, merge_theirs)
    probe_theirs = theirs_of(after(probe_grads, merge_ours), hidden_two)
    grad_hidden_two = back_project(after(probe_grads, probe_theirs), probe_matrix)
    text_four = line_up(text_mine, hops(text_mine)).reshape(4 * text_len, width)
    grad_norm, gain_cross, bias_cross = norm_back(
        grad_hidden_two, after_self, parts_two, norms[2]
    )
    grad_after_self = grad_after_cross + grad_norm
    grad_self_low = grad_after_self.astype(jnp.bfloat16)
    output_theirs = theirs_of(grad_self_low, mixed_self)
    grad_mixed = back_project(after(grad_self_low, output_theirs), output_matrix).astype(
        jnp.bfloat16
    )
    probe_ours = ours_of(after(probe_grads, grad_mixed), hidden_two, probe_theirs)
    text_weights = outer_sum(text_four, text_all).astype(jnp.bfloat16)
    text_back = back_project(text_four, text_matrix).astype(jnp.bfloat16)
    output_ours = ours_of(after(grad_self_low, probe_ours), mixed_self, output_theirs)
    text_rows = width // outers
    middle = jnp.concatenate(
        [
            values.reshape(outers, -1, width)
            for values in (
                output_ours,
                probe_ours,
                merge_ours,
                text_weights.reshape(outers, shards, text_rows // shards, block)
                .transpose(0, 2, 1, 3)
                .reshape(outers, text_rows // shards, width),
            )
        ],
        axis=1,
    )
    middle_rows = middle.shape[1]
    middle = middle.reshape(outers * middle_rows, width)
    middle_sum = over_outer(middle)
    text_split = text_rows // shards
    text_piece = (
        middle_sum[middle_rows - text_split :]
        .reshape(text_split, shards, block)
        .transpose(1, 0, 2)
        .reshape(text_rows, block)
    )
    text_back = text_back.reshape(2, 2, text_len, block)
    text_kept = lax.dynamic_index_in_dim(text_back, core, 0, keepdims=False)
    text_gone = lax.dynamic_index_in_dim(text_back, 1 - core, 0, keepdims=False)
    text_own = text_kept.astype(jnp.float32) + lax.ppermute(text_gone, "core", swap).astype(
        jnp.float32
    )
    text_own = text_own.astype(jnp.bfloat16)
    down_came = shard_hops(down_sum)
    text_came = hops(text_own)
    grad_queries, own_keys, own_values, other_keys, other_values = self_attend_back(
        places, queries, kv, kv_other, mixed_self, after(grad_mixed, middle, text_own), lse
    )
    text_came = held(text_came, grad_queries)
    down_came = held(down_came, grad_queries)
    other_keys, other_values = held([other_keys, other_values], *text_came, *down_came)
    own_keys += lax.ppermute(other_keys, "core", swap)
    own_values += lax.ppermute(other_values, "core", swap)
    down_piece = over_shard(down_sum, down_came)
    up_came = shard_hops(after(up_sum, down_piece))

    qkv_grads = jnp.concatenate([grad_queries, own_keys, own_values], axis=1)
    qkv_theirs = theirs_of(qkv_grads, hidden_one)
    grad_hidden_one = back_project(after(qkv_grads, qkv_theirs), qkv_matrix)
    qkv_ours = ours_of(after(qkv_grads, grad_hidden_one), hidden_one, qkv_theirs)
    up_came = held(up_came, grad_hidden_one)
    up_piece = over_shard(up_sum, up_came)
    text_grad = line_up(text_own, text_came).astype(jnp.float32)
    text_grad = text_grad.transpose(1, 2, 0, 3).reshape(text_states.shape)
    qkv_sum = over_outer(qkv_ours)
    grad_norm, gain_self, bias_self = norm_back(
        after(grad_hidden_one, qkv_ours, *up_came), inputs, parts_one, norms[0]
    )
    middle_kept = after(middle_sum[: middle_rows - text_split], qkv_ours, *up_came)
    middle_came = shard_hops(middle_kept)
    frames_came = from_chip(
        after((grad_after_self + grad_norm).astype(jnp.bfloat16), *middle_came)
    )
    frames_grad = by_slot(*frames_came).astype(jnp.float32)

    qkv_sum = after(qkv_sum, *frames_came)
    late_came = shard_hops(qkv_sum)
    small = jnp.stack(
        [
            gain_self,
            bias_self,
            gain_cross,
            bias_cross,
            gain_feed,
            bias_feed,
            jnp.full((width,), squares),
            jnp.zeros((width,), jnp.float32),
        ]
    )
    small = after(small, *late_came)
    for axis, pairs in (
        ("core", swap),
        ("x", swap),
        ("y", swap),
        ("shard", [(0, 1), (1, 0), (2, 3), (3, 2)]),
        ("shard", [(0, 2), (2, 0), (1, 3), (3, 1)]),
    ):
        small += lax.ppermute(small, axis, pairs)
    loss = small[6, 0] / (width * count)
    small_own = lax.dynamic_slice_in_dim(small, shard * block, block, 1)

    middle_piece = over_shard(middle_kept, middle_came)
    early = jnp.concatenate(
        [up_piece]
        + [down_piece[:, i * block : (i + 1) * block] for i in range(4)]
        + [text_piece, middle_piece],
        axis=0,
    )
    early = lax.all_gather(after(early, text_grad), REPLICAS, axis=0)
    piece = width // replicas
    square = (block, width)
    up_grad = unpack(early, hidden_units // replicas, 0, (block, hidden_units), 0, 1)
    at = hidden_units // replicas // piece
    down_grad = unpack(early, piece, at, (4 * block, width), 0, 2)
    at += 4
    key_grad = unpack(early, text_rows, at * piece // text_rows, square, 0, 1)
    value_grad = unpack(early, text_rows, at * piece // text_rows, square, 4, 1)
    at += text_rows // piece
    output_grad = unpack(early, piece, at, square, 0, 2)
    probe_grad = unpack(early, piece, at + 1, square, 0, 2)
    merge_grad = unpack(early, piece, at + 2, square, 0, 2)
    late = over_shard(qkv_sum, late_came)
    late = lax.all_gather(after(late, early), REPLICAS, axis=0, tiled=True)
    late = late.reshape(-1, block, block)
    qkv_grad = [unpack(late, block, 0, square, 2 * i, 2) for i in range(3)]
    return (
        output,
        loss,
        frames_grad,
        text_grad,
        small_own[0],
        small_own[1],
        qkv_grad[0],
        qkv_grad[1],
        qkv_grad[2],
        output_grad,
        small_own[2],
        small_own[3],
        probe_grad,
        key_grad,
        value_grad,
        merge_grad,
        small_own[4],
        small_own[5],
        up_grad,
        down_grad,
    )


def solution(mesh):
    by_chip = mesh.shape["shard"] == 4 and mesh.shape["replica"] == 8
    replica = ("y", "x", "core") if by_chip else "replica"
    row = P(replica)
    clip = P(replica, "shard", None)
    text = P(replica, None, None)
    vector = P("shard")
    matrix = P("shard", None)
    weights = (
        [vector, vector] + [matrix] * 4 + [vector, vector] + [matrix] * 4 + [vector, vector]
        + [matrix] * 2
    )
    if by_chip:
        mesh = Mesh(mesh.devices.reshape(2, 2, 2, 4), ("y", "x", "core", "shard"))
    return jax.shard_map(
        clip_body if by_chip else general_body,
        mesh=mesh,
        in_specs=(clip, text, P(replica, None), row, row, clip, *weights),
        out_specs=(clip, P(), clip, text, *weights),
        check_vma=False,
    )
```

```python
import jax
import jax.numpy as jnp
from jax import lax
from jax.experimental import pallas as pl
from jax.experimental.pallas import tpu as pltpu
from jax.sharding import Mesh
from jax.sharding import PartitionSpec as P

HEADS = 24
HEAD_DIM = 64


epsilon = 1e-05
masked_score = -1e30


def layer_norm(values, gain, shift):
    center = values - jnp.mean(values, axis=-1, keepdims=True)
    variance = jnp.mean(center * center, axis=-1, keepdims=True)
    return center * lax.rsqrt(variance + epsilon) * gain + shift


def exact_gelu(values):
    return jax.nn.gelu(values, approximate=False)


def project(left, right):
    return jnp.dot(left, right, preferred_element_type=jnp.float32)


def outer_sum(left, right):
    return jnp.einsum("rd,re->de", left, right, preferred_element_type=jnp.float32)


def back_project(grads, matrix):
    return jnp.einsum("re,de->rd", grads, matrix, preferred_element_type=jnp.float32)


def split_heads(values):
    return values.reshape(values.shape[:-1] + (HEADS, HEAD_DIM))


def self_forward(operands):
    queries, keys_all, values_all, allowed = operands
    scale = HEAD_DIM ** (-0.5)
    scores = (
        jnp.einsum("qhd,khd->hqk", queries, keys_all, preferred_element_type=jnp.float32) * scale
    )
    scores = jnp.where(allowed[None], scores, masked_score)
    peak = jnp.max(scores, axis=-1, keepdims=True)
    weights = jnp.exp(scores - peak)
    totals = jnp.sum(weights, axis=-1, keepdims=True)
    probs = (weights / totals).astype(jnp.bfloat16)
    mixed = jnp.einsum("hqk,khd->qhd", probs, values_all, preferred_element_type=jnp.float32)
    return (mixed.astype(jnp.bfloat16), (peak + jnp.log(totals))[..., 0])


def self_backward(operands):
    queries, keys_all, values_all, allowed, log_totals, grad_mixed = operands
    scale = HEAD_DIM ** (-0.5)
    scores = (
        jnp.einsum("qhd,khd->hqk", queries, keys_all, preferred_element_type=jnp.float32) * scale
    )
    scores = jnp.where(allowed[None], scores, masked_score)
    probs = jnp.exp(scores - log_totals[..., None])
    grad_probs = jnp.einsum(
        "qhd,khd->hqk", grad_mixed, values_all, preferred_element_type=jnp.float32
    )
    grad_values = jnp.einsum(
        "hqk,qhd->khd", probs.astype(jnp.bfloat16), grad_mixed, preferred_element_type=jnp.float32
    )
    inner = jnp.sum(probs * grad_probs, axis=-1, keepdims=True)
    grad_scores = (probs * (grad_probs - inner)).astype(jnp.bfloat16)
    grad_queries = (
        jnp.einsum("hqk,khd->qhd", grad_scores, keys_all, preferred_element_type=jnp.float32)
        * scale
    ).astype(jnp.bfloat16)
    grad_keys = (
        jnp.einsum("hqk,qhd->khd", grad_scores, queries, preferred_element_type=jnp.float32) * scale
    )
    return (grad_queries, grad_keys, grad_values)


def general_body(
    frames,
    text_states,
    text_mask,
    clip_lengths,
    slot_used,
    teacher,
    self_norm_gain,
    self_norm_bias,
    self_query_weight,
    self_key_weight,
    self_value_weight,
    self_output_weight,
    cross_norm_gain,
    cross_norm_bias,
    cross_query_weight,
    cross_key_weight,
    cross_value_weight,
    cross_output_weight,
    feed_norm_gain,
    feed_norm_bias,
    feed_up_weight,
    feed_down_weight,
):
    gathered = (
        lax.all_gather(self_norm_gain, "shard", axis=0, tiled=True),
        lax.all_gather(self_norm_bias, "shard", axis=0, tiled=True),
        lax.all_gather(self_query_weight, "shard", axis=0, tiled=True),
        lax.all_gather(self_key_weight, "shard", axis=0, tiled=True),
        lax.all_gather(self_value_weight, "shard", axis=0, tiled=True),
        lax.all_gather(self_output_weight, "shard", axis=0, tiled=True),
        lax.all_gather(cross_norm_gain, "shard", axis=0, tiled=True),
        lax.all_gather(cross_norm_bias, "shard", axis=0, tiled=True),
        lax.all_gather(cross_query_weight, "shard", axis=0, tiled=True),
        lax.all_gather(cross_key_weight, "shard", axis=0, tiled=True),
        lax.all_gather(cross_value_weight, "shard", axis=0, tiled=True),
        lax.all_gather(cross_output_weight, "shard", axis=0, tiled=True),
        lax.all_gather(feed_norm_gain, "shard", axis=0, tiled=True),
        lax.all_gather(feed_norm_bias, "shard", axis=0, tiled=True),
        lax.all_gather(feed_up_weight, "shard", axis=0, tiled=True),
        lax.all_gather(feed_down_weight, "shard", axis=0, tiled=True),
    )
    (
        gain_attend,
        bias_attend,
        query_matrix,
        key_matrix,
        value_matrix,
        output_matrix,
        gain_cross,
        bias_cross,
        probe_matrix,
        lookup_matrix,
        content_matrix,
        merge_matrix,
        gain_feed,
        bias_feed,
        expand_matrix,
        reduce_matrix,
    ) = gathered
    slots = frames.shape[0]
    frame_count = frames.shape[1]
    width = frames.shape[2]
    text_len = text_states.shape[1]
    shards = lax.axis_size("shard")
    replicas = lax.axis_size("replica")
    clip_total = frame_count * shards
    row_count = slots * frame_count
    scale = HEAD_DIM ** (-0.5)
    shard_rank = lax.axis_index("shard")
    positions = shard_rank * frame_count + jnp.arange(frame_count, dtype=jnp.int32)
    key_positions = jnp.arange(clip_total, dtype=jnp.int32)
    allowed = (key_positions[None, None, :] <= positions[None, :, None]) & (
        key_positions[None, None, :] < clip_lengths[:, None, None]
    )
    valid_rows = ((positions[None, :] < clip_lengths[:, None]) & (slot_used[:, None] > 0)).astype(
        jnp.float32
    )
    text_allowed = text_mask > 0
    inputs = frames.astype(jnp.float32)
    normed_one, pull_one = jax.vjp(
        layer_norm, inputs, gain_attend.astype(jnp.float32), bias_attend.astype(jnp.float32)
    )
    hidden_one = normed_one.astype(jnp.bfloat16).reshape(row_count, width)
    queries = (
        project(hidden_one, query_matrix).astype(jnp.bfloat16).reshape(slots, frame_count, width)
    )
    keys_local = (
        project(hidden_one, key_matrix).astype(jnp.bfloat16).reshape(slots, frame_count, width)
    )
    values_local = (
        project(hidden_one, value_matrix).astype(jnp.bfloat16).reshape(slots, frame_count, width)
    )
    keys_all, values_all = (
        lax.all_gather(keys_local, "shard", axis=1, tiled=True),
        lax.all_gather(values_local, "shard", axis=1, tiled=True),
    )
    head_queries = split_heads(queries)
    head_keys = split_heads(keys_all)
    head_values = split_heads(values_all)
    mixed_self, log_totals = lax.map(self_forward, (head_queries, head_keys, head_values, allowed))
    mixed_rows = mixed_self.reshape(row_count, width)
    after_self = inputs + project(mixed_rows, output_matrix).reshape(slots, frame_count, width)
    normed_two, pull_two = jax.vjp(
        layer_norm, after_self, gain_cross.astype(jnp.float32), bias_cross.astype(jnp.float32)
    )
    hidden_two = normed_two.astype(jnp.bfloat16).reshape(row_count, width)
    probes = split_heads(
        project(hidden_two, probe_matrix).astype(jnp.bfloat16).reshape(slots, frame_count, width)
    )
    text_rows = text_states.reshape(slots * text_len, width)
    lookups = split_heads(
        project(text_rows, lookup_matrix).astype(jnp.bfloat16).reshape(slots, text_len, width)
    )
    contents = split_heads(
        project(text_rows, content_matrix).astype(jnp.bfloat16).reshape(slots, text_len, width)
    )
    cross_scores = (
        jnp.einsum("sqhd,skhd->shqk", probes, lookups, preferred_element_type=jnp.float32) * scale
    )
    cross_scores = jnp.where(text_allowed[:, None, None, :], cross_scores, masked_score)
    cross_peak = jnp.max(cross_scores, axis=-1, keepdims=True)
    cross_weights = jnp.exp(cross_scores - cross_peak)
    cross_probs = cross_weights / jnp.sum(cross_weights, axis=-1, keepdims=True)
    cross_probs_low = cross_probs.astype(jnp.bfloat16)
    cross_mixed = jnp.einsum(
        "shqk,skhd->sqhd", cross_probs_low, contents, preferred_element_type=jnp.float32
    )
    cross_mixed = cross_mixed.astype(jnp.bfloat16).reshape(row_count, width)
    after_cross = after_self + project(cross_mixed, merge_matrix).reshape(slots, frame_count, width)
    normed_three, pull_three = jax.vjp(
        layer_norm, after_cross, gain_feed.astype(jnp.float32), bias_feed.astype(jnp.float32)
    )
    hidden_three = normed_three.astype(jnp.bfloat16).reshape(row_count, width)
    upward = project(hidden_three, expand_matrix)
    activated, gelu_pull = jax.vjp(exact_gelu, upward)
    activated_low = activated.astype(jnp.bfloat16)
    result = after_cross + project(activated_low, reduce_matrix).reshape(slots, frame_count, width)
    output = result.astype(jnp.bfloat16)
    errors = (result - teacher.astype(jnp.float32)) * valid_rows[..., None]
    squares_total, count_total = lax.psum(
        (jnp.sum(errors * errors), jnp.sum(valid_rows)), ("replica", "shard")
    )
    loss = squares_total / (width * count_total)
    grad_result = errors * (slots * replicas * clip_total / count_total)
    grad_feed_low = grad_result.reshape(row_count, width).astype(jnp.bfloat16)
    grad_activated = back_project(grad_feed_low, reduce_matrix)
    grad_upward = gelu_pull(grad_activated)[0].astype(jnp.bfloat16)
    grad_hidden_three = back_project(grad_upward, expand_matrix).reshape(slots, frame_count, width)
    grad_cross_norm, gain_feed_part, bias_feed_part = pull_three(grad_hidden_three)
    grad_after_cross = grad_result + grad_cross_norm
    feed_owned = (
        lax.psum_scatter(
            outer_sum(hidden_three, grad_upward).astype(jnp.bfloat16),
            "shard",
            scatter_dimension=0,
            tiled=True,
        ).astype(jnp.float32),
        lax.psum_scatter(
            outer_sum(activated_low, grad_feed_low).astype(jnp.bfloat16),
            "shard",
            scatter_dimension=0,
            tiled=True,
        ).astype(jnp.float32),
        lax.psum_scatter(
            gain_feed_part.astype(jnp.bfloat16), "shard", scatter_dimension=0, tiled=True
        ).astype(jnp.float32),
        lax.psum_scatter(
            bias_feed_part.astype(jnp.bfloat16), "shard", scatter_dimension=0, tiled=True
        ).astype(jnp.float32),
    )
    grad_cross_low = grad_after_cross.reshape(row_count, width).astype(jnp.bfloat16)
    grad_cross_mixed = split_heads(
        back_project(grad_cross_low, merge_matrix)
        .astype(jnp.bfloat16)
        .reshape(slots, frame_count, width)
    )
    grad_cross_probs = jnp.einsum(
        "sqhd,skhd->shqk", grad_cross_mixed, contents, preferred_element_type=jnp.float32
    )
    content_grads = jnp.einsum(
        "shqk,sqhd->skhd", cross_probs_low, grad_cross_mixed, preferred_element_type=jnp.float32
    )
    cross_inner = jnp.sum(cross_probs * grad_cross_probs, axis=-1, keepdims=True)
    grad_cross_scores = (cross_probs * (grad_cross_probs - cross_inner)).astype(jnp.bfloat16)
    probe_grads = (
        jnp.einsum(
            "shqk,skhd->sqhd", grad_cross_scores, lookups, preferred_element_type=jnp.float32
        )
        * scale
    )
    probe_grads = probe_grads.astype(jnp.bfloat16).reshape(row_count, width)
    lookup_grads = (
        jnp.einsum("shqk,sqhd->skhd", grad_cross_scores, probes, preferred_element_type=jnp.float32)
        * scale
    )
    lookup_sum, content_sum = (
        lax.psum(lookup_grads.astype(jnp.bfloat16), "shard").astype(jnp.float32),
        lax.psum(content_grads.astype(jnp.bfloat16), "shard").astype(jnp.float32),
    )
    lookup_low = lookup_sum.astype(jnp.bfloat16).reshape(slots * text_len, width)
    content_low = content_sum.astype(jnp.bfloat16).reshape(slots * text_len, width)
    own_width = width // shards
    own_text = lax.dynamic_slice_in_dim(text_rows, shard_rank * own_width, own_width, 1)
    lookup_own = outer_sum(own_text, lookup_low)
    content_own = outer_sum(own_text, content_low)
    text_grad = (
        back_project(lookup_low, lookup_matrix) + back_project(content_low, content_matrix)
    ).reshape(slots, text_len, width)
    grad_hidden_two = back_project(probe_grads, probe_matrix).reshape(slots, frame_count, width)
    grad_self_norm, gain_cross_part, bias_cross_part = pull_two(grad_hidden_two)
    grad_after_self = grad_after_cross + grad_self_norm
    grad_self_low = grad_after_self.reshape(row_count, width).astype(jnp.bfloat16)
    grad_mixed = split_heads(
        back_project(grad_self_low, output_matrix)
        .astype(jnp.bfloat16)
        .reshape(slots, frame_count, width)
    )
    grad_queries, grad_keys, grad_values = lax.map(
        self_backward, (head_queries, head_keys, head_values, allowed, log_totals, grad_mixed)
    )
    key_sum, value_sum = (
        lax.psum_scatter(
            grad_keys.reshape(slots, clip_total, width).astype(jnp.bfloat16),
            "shard",
            scatter_dimension=1,
            tiled=True,
        ).astype(jnp.float32),
        lax.psum_scatter(
            grad_values.reshape(slots, clip_total, width).astype(jnp.bfloat16),
            "shard",
            scatter_dimension=1,
            tiled=True,
        ).astype(jnp.float32),
    )
    key_low = key_sum.astype(jnp.bfloat16).reshape(row_count, width)
    value_low = value_sum.astype(jnp.bfloat16).reshape(row_count, width)
    query_low = grad_queries.reshape(row_count, width)
    grad_hidden_one = (
        back_project(query_low, query_matrix)
        + back_project(key_low, key_matrix)
        + back_project(value_low, value_matrix)
    )
    grad_inputs, gain_attend_part, bias_attend_part = pull_one(
        grad_hidden_one.reshape(slots, frame_count, width)
    )
    frames_grad = grad_after_self + grad_inputs
    attend_owned = (
        lax.psum_scatter(
            outer_sum(hidden_one, query_low).astype(jnp.bfloat16),
            "shard",
            scatter_dimension=0,
            tiled=True,
        ).astype(jnp.float32),
        lax.psum_scatter(
            outer_sum(hidden_one, key_low).astype(jnp.bfloat16),
            "shard",
            scatter_dimension=0,
            tiled=True,
        ).astype(jnp.float32),
        lax.psum_scatter(
            outer_sum(hidden_one, value_low).astype(jnp.bfloat16),
            "shard",
            scatter_dimension=0,
            tiled=True,
        ).astype(jnp.float32),
        lax.psum_scatter(
            outer_sum(mixed_rows, grad_self_low).astype(jnp.bfloat16),
            "shard",
            scatter_dimension=0,
            tiled=True,
        ).astype(jnp.float32),
        lax.psum_scatter(
            outer_sum(hidden_two, probe_grads).astype(jnp.bfloat16),
            "shard",
            scatter_dimension=0,
            tiled=True,
        ).astype(jnp.float32),
        lax.psum_scatter(
            outer_sum(cross_mixed, grad_cross_low).astype(jnp.bfloat16),
            "shard",
            scatter_dimension=0,
            tiled=True,
        ).astype(jnp.float32),
        lax.psum_scatter(
            gain_attend_part.astype(jnp.bfloat16), "shard", scatter_dimension=0, tiled=True
        ).astype(jnp.float32),
        lax.psum_scatter(
            bias_attend_part.astype(jnp.bfloat16), "shard", scatter_dimension=0, tiled=True
        ).astype(jnp.float32),
        lax.psum_scatter(
            gain_cross_part.astype(jnp.bfloat16), "shard", scatter_dimension=0, tiled=True
        ).astype(jnp.float32),
        lax.psum_scatter(
            bias_cross_part.astype(jnp.bfloat16), "shard", scatter_dimension=0, tiled=True
        ).astype(jnp.float32),
    )
    summed = (
        lax.psum(attend_owned[6].astype(jnp.bfloat16), "replica").astype(jnp.float32),
        lax.psum(attend_owned[7].astype(jnp.bfloat16), "replica").astype(jnp.float32),
        lax.psum(attend_owned[0].astype(jnp.bfloat16), "replica").astype(jnp.float32),
        lax.psum(attend_owned[1].astype(jnp.bfloat16), "replica").astype(jnp.float32),
        lax.psum(attend_owned[2].astype(jnp.bfloat16), "replica").astype(jnp.float32),
        lax.psum(attend_owned[3].astype(jnp.bfloat16), "replica").astype(jnp.float32),
        lax.psum(attend_owned[8].astype(jnp.bfloat16), "replica").astype(jnp.float32),
        lax.psum(attend_owned[9].astype(jnp.bfloat16), "replica").astype(jnp.float32),
        lax.psum(attend_owned[4].astype(jnp.bfloat16), "replica").astype(jnp.float32),
        lax.psum(lookup_own.astype(jnp.bfloat16), "replica").astype(jnp.float32),
        lax.psum(content_own.astype(jnp.bfloat16), "replica").astype(jnp.float32),
        lax.psum(attend_owned[5].astype(jnp.bfloat16), "replica").astype(jnp.float32),
        lax.psum(feed_owned[2].astype(jnp.bfloat16), "replica").astype(jnp.float32),
        lax.psum(feed_owned[3].astype(jnp.bfloat16), "replica").astype(jnp.float32),
        lax.psum(feed_owned[0].astype(jnp.bfloat16), "replica").astype(jnp.float32),
        lax.psum(feed_owned[1].astype(jnp.bfloat16), "replica").astype(jnp.float32),
    )
    return (
        output,
        loss,
        frames_grad,
        text_grad,
        summed[0],
        summed[1],
        summed[2],
        summed[3],
        summed[4],
        summed[5],
        summed[6],
        summed[7],
        summed[8],
        summed[9],
        summed[10],
        summed[11],
        summed[12],
        summed[13],
        summed[14],
        summed[15],
    )


PAIR = 2 * HEAD_DIM
EVERY = ("shard", "y", "x", "core")
REPLICAS = ("core", "y", "x")
NT = (((1,), (1,)), ((), ()))
TN = (((0,), (0,)), ((), ()))
NN = (((1,), (0,)), ((), ()))


def dot(left, right, dims):
    return lax.dot_general(left, right, dims, preferred_element_type=jnp.float32)


def half_mask(side, value):
    lanes = lax.broadcasted_iota(jnp.int32, (1, PAIR), 1)
    inside = (lanes >= HEAD_DIM) if side else (lanes < HEAD_DIM)
    return jnp.where(inside, value, 0.0).astype(jnp.bfloat16)


def fill_clip(place, own_ref, other_ref, all_ref):
    block = own_ref.shape[0] // 2
    for part in range(2):
        rows = slice(part * block, (part + 1) * block)
        for at, ref in ((place[part], own_ref), (place[3 + part], other_ref)):
            all_ref[pl.ds(pl.multiple_of(at * block, block), block), :] = ref[rows, :]


def self_forward_kernel(
    place, q_ref, own_k, own_v, other_k, other_v, mixed_ref, lse_ref, k_ref, v_ref, acc_ref
):
    fill_clip(place, own_k, other_k, k_ref)
    fill_clip(place, own_v, other_v, v_ref)
    block = q_ref.shape[0] // 2
    length = place[2]
    low = lax.broadcasted_iota(jnp.int32, (PAIR, 1), 0) < HEAD_DIM
    for part in range(2):
        first = place[part] * block
        rows = slice(part * block, (part + 1) * block)
        q = q_ref[rows, :]
        q_half = [q * half_mask(side, HEAD_DIM ** (-0.5)) for side in range(2)]
        limit = jnp.minimum(
            first + lax.broadcasted_iota(jnp.int32, (1, block), 1) + 1, length
        )
        acc_ref[...] = jnp.zeros_like(acc_ref)

        def step(j, peaks, q_half=q_half, limit=limit):
            at = pl.multiple_of(j * block, block)
            k = k_ref[pl.ds(at, block), :]
            v = v_ref[pl.ds(at, block), :]
            allowed = at + lax.broadcasted_iota(jnp.int32, (block, block), 0) < limit
            out = []
            for side in range(2):
                scores = jnp.where(allowed, dot(k, q_half[side], NT), masked_score)
                peak = jnp.maximum(peaks[side], jnp.max(scores, axis=0, keepdims=True))
                weights = jnp.exp(scores - peak).astype(jnp.bfloat16)
                v_ones = v * half_mask(side, 1.0) + half_mask(1 - side, 1.0)
                acc_ref[side] = acc_ref[side] * jnp.exp(peaks[side] - peak) + dot(
                    v_ones, weights, TN
                )
                out.append(peak)
            return tuple(out)

        peaks = lax.fori_loop(
            0, place[part] + 1, step, (jnp.full((1, block), masked_score, jnp.float32),) * 2
        )
        top, bottom = acc_ref[0], acc_ref[1]
        total = jnp.where(low, top[HEAD_DIM : HEAD_DIM + 1], bottom[0:1])
        mixed = jnp.where(low, top, bottom) / total
        mixed_ref[rows, :] = mixed.T.astype(jnp.bfloat16)
        lse_ref[0:1, rows] = peaks[0] + jnp.log(top[HEAD_DIM : HEAD_DIM + 1])
        lse_ref[1:2, rows] = peaks[1] + jnp.log(bottom[0:1])


def self_backward_kernel(
    place, q_ref, own_k, own_v, other_k, other_v, mixed_ref, grad_ref, lse_ref,
    dq_ref, own_dk, own_dv, other_dk, other_dv, k_ref, v_ref, dq_acc, dk_acc, dv_acc,
):
    fill_clip(place, own_k, other_k, k_ref)
    fill_clip(place, own_v, other_v, v_ref)
    block = q_ref.shape[0] // 2
    length = place[2]
    scale = HEAD_DIM ** (-0.5)
    dk_acc[...] = jnp.zeros_like(dk_acc)
    dv_acc[...] = jnp.zeros_like(dv_acc)
    for part in range(2):
        first = place[part] * block
        rows = slice(part * block, (part + 1) * block)
        q = q_ref[rows, :]
        grad = grad_ref[rows, :]
        q_half = [q * half_mask(side, scale) for side in range(2)]
        grad_half = [grad * half_mask(side, 1.0) for side in range(2)]
        product = (grad.astype(jnp.float32) * mixed_ref[rows, :].astype(jnp.float32)).T
        inner = [
            jnp.sum(product[side * HEAD_DIM : (side + 1) * HEAD_DIM], axis=0, keepdims=True)
            for side in range(2)
        ]
        lse = [lse_ref[side : side + 1, rows] for side in range(2)]
        limit = jnp.minimum(
            first + lax.broadcasted_iota(jnp.int32, (1, block), 1) + 1, length
        )
        dq_acc[...] = jnp.zeros_like(dq_acc)

        def step(
            j, carry, q_half=q_half, grad_half=grad_half, inner=inner, lse=lse, limit=limit
        ):
            at = pl.multiple_of(j * block, block)
            k = k_ref[pl.ds(at, block), :]
            v = v_ref[pl.ds(at, block), :]
            allowed = at + lax.broadcasted_iota(jnp.int32, (block, block), 0) < limit
            dq, dk, dv = 0.0, 0.0, 0.0
            for side in range(2):
                scores = jnp.where(allowed, dot(k, q_half[side], NT), masked_score)
                probs = jnp.exp(scores - lse[side])
                grad_probs = dot(v, grad_half[side], NT)
                grad_scores = (probs * (grad_probs - inner[side])).astype(jnp.bfloat16)
                dv += dot(probs.astype(jnp.bfloat16), grad_half[side], NN)
                dk += dot(grad_scores, q_half[side], NN)
                dq += dot(k * half_mask(side, scale), grad_scores, TN)
            dk_acc[pl.ds(at, block), :] += dk
            dv_acc[pl.ds(at, block), :] += dv
            dq_acc[...] += dq
            return carry

        lax.fori_loop(0, place[part] + 1, step, 0)
        dq_ref[rows, :] = dq_acc[...].T.astype(jnp.bfloat16)
    for part in range(2):
        rows = slice(part * block, (part + 1) * block)
        own = pl.ds(pl.multiple_of(place[part] * block, block), block)
        other = pl.ds(pl.multiple_of(place[3 + part] * block, block), block)
        own_dk[rows, :] = dk_acc[own, :].astype(jnp.bfloat16)
        own_dv[rows, :] = dv_acc[own, :].astype(jnp.bfloat16)
        other_dk[rows, :] = dk_acc[other, :].astype(jnp.bfloat16)
        other_dv[rows, :] = dv_acc[other, :].astype(jnp.bfloat16)


def pair_block(rows):
    return pl.BlockSpec((rows, PAIR), lambda i, *_: (0, i))


def value_block(rows, pairs):
    return pl.BlockSpec((rows, PAIR), lambda i, *_: (0, pairs + i))


def self_attend(place, queries, own, other):
    rows, width = queries.shape
    clip = 2 * rows
    pairs = width // PAIR
    return pl.pallas_call(
        self_forward_kernel,
        out_shape=(
            jax.ShapeDtypeStruct((rows, width), jnp.bfloat16),
            jax.ShapeDtypeStruct((pairs * 8, rows), jnp.float32),
        ),
        grid_spec=pltpu.PrefetchScalarGridSpec(
            num_scalar_prefetch=1,
            grid=(pairs,),
            in_specs=[pair_block(rows)] + [pair_block(rows), value_block(rows, pairs)] * 2,
            out_specs=(pair_block(rows), pl.BlockSpec((8, rows), lambda i, *_: (i, 0))),
            scratch_shapes=[
                pltpu.VMEM((clip, PAIR), jnp.bfloat16),
                pltpu.VMEM((clip, PAIR), jnp.bfloat16),
                pltpu.VMEM((2, PAIR, rows // 2), jnp.float32),
            ],
        ),
        compiler_params=pltpu.CompilerParams(vmem_limit_bytes=32 * 2**20),
        cost_estimate=pl.CostEstimate(
            flops=2 * 2 * rows * clip * width, bytes_accessed=8 * clip * width, transcendentals=0
        ),
        name="self_attend",
    )(place, queries, own, own, other, other)


def self_attend_back(place, queries, own, other, mixed, grads, lse):
    rows, width = queries.shape
    clip = 2 * rows
    pairs = width // PAIR
    return pl.pallas_call(
        self_backward_kernel,
        out_shape=(jax.ShapeDtypeStruct((rows, width), jnp.bfloat16),) * 5,
        grid_spec=pltpu.PrefetchScalarGridSpec(
            num_scalar_prefetch=1,
            grid=(pairs,),
            in_specs=[pair_block(rows)]
            + [pair_block(rows), value_block(rows, pairs)] * 2
            + [
                pair_block(rows),
                pair_block(rows),
                pl.BlockSpec((8, rows), lambda i, *_: (i, 0)),
            ],
            out_specs=(pair_block(rows),) * 5,
            scratch_shapes=[
                pltpu.VMEM((clip, PAIR), jnp.bfloat16),
                pltpu.VMEM((clip, PAIR), jnp.bfloat16),
                pltpu.VMEM((PAIR, rows // 2), jnp.float32),
                pltpu.VMEM((clip, PAIR), jnp.float32),
                pltpu.VMEM((clip, PAIR), jnp.float32),
            ],
        ),
        compiler_params=pltpu.CompilerParams(vmem_limit_bytes=32 * 2**20),
        cost_estimate=pl.CostEstimate(
            flops=5 * 2 * rows * clip * width, bytes_accessed=16 * clip * width, transcendentals=0
        ),
        name="self_attend_back",
    )(place, queries, own, own, other, other, mixed, grads, lse)


def both_heads(rows, value):
    return jnp.concatenate([rows * half_mask(side, value) for side in range(2)], axis=0)


def cross_probs_of(lookup_two, probes, present):
    text = present.shape[0]
    scores = dot(lookup_two, probes, NT)
    out = []
    for side in range(2):
        part = jnp.where(
            present > 0, scores[side * text : (side + 1) * text], masked_score
        )
        weights = jnp.exp(part - jnp.max(part, axis=0, keepdims=True))
        out.append(weights / jnp.sum(weights, axis=0, keepdims=True))
    return out


def cross_forward_kernel(probe_ref, lookup_ref, content_ref, present_ref, mixed_ref):
    probs = cross_probs_of(
        both_heads(lookup_ref[...], HEAD_DIM ** (-0.5)), probe_ref[...], present_ref[...]
    )
    probs = jnp.concatenate(probs, axis=0).astype(jnp.bfloat16)
    mixed_ref[...] = dot(probs, both_heads(content_ref[...], 1.0), TN).astype(jnp.bfloat16)


def cross_backward_kernel(
    probe_ref, lookup_ref, content_ref, present_ref, grad_ref, dp_ref, dl_ref, dc_ref
):
    text = present_ref.shape[0]
    scale = HEAD_DIM ** (-0.5)
    probes = probe_ref[...]
    grads = grad_ref[...]
    lookup_two = both_heads(lookup_ref[...], scale)
    probs = cross_probs_of(lookup_two, probes, present_ref[...])
    grad_probs = dot(both_heads(content_ref[...], 1.0), grads, NT)
    grad_scores = []
    for side in range(2):
        part = grad_probs[side * text : (side + 1) * text]
        inner = jnp.sum(probs[side] * part, axis=0, keepdims=True)
        grad_scores.append(probs[side] * (part - inner))
    grad_scores = jnp.concatenate(grad_scores, axis=0).astype(jnp.bfloat16)
    probs = jnp.concatenate(probs, axis=0).astype(jnp.bfloat16)
    low = lax.broadcasted_iota(jnp.int32, (1, PAIR), 1) < HEAD_DIM
    dp_ref[...] = dot(grad_scores, lookup_two, TN).astype(jnp.bfloat16)
    dl = dot(grad_scores, probes, NN) * scale
    dl_ref[...] = jnp.where(low, dl[:text], dl[text:]).astype(jnp.bfloat16)
    dc = dot(probs, grads, NN)
    dc_ref[...] = jnp.where(low, dc[:text], dc[text:]).astype(jnp.bfloat16)


def cross_attend(probes, lookups, contents, present):
    rows, width = probes.shape
    text = lookups.shape[0]
    return pl.pallas_call(
        cross_forward_kernel,
        out_shape=jax.ShapeDtypeStruct((rows, width), jnp.bfloat16),
        grid=(width // PAIR,),
        in_specs=[
            pair_block(rows),
            pair_block(text),
            pair_block(text),
            pl.BlockSpec((text, 1), lambda i: (0, 0)),
        ],
        out_specs=pair_block(rows),
        compiler_params=pltpu.CompilerParams(vmem_limit_bytes=32 * 2**20),
        cost_estimate=pl.CostEstimate(
            flops=8 * rows * text * width, bytes_accessed=4 * rows * width, transcendentals=0
        ),
        name="cross_attend",
    )(probes, lookups, contents, present)


def cross_attend_back(probes, lookups, contents, present, grads):
    rows, width = probes.shape
    text = lookups.shape[0]
    return pl.pallas_call(
        cross_backward_kernel,
        out_shape=(
            jax.ShapeDtypeStruct((rows, width), jnp.bfloat16),
            jax.ShapeDtypeStruct((text, width), jnp.bfloat16),
            jax.ShapeDtypeStruct((text, width), jnp.bfloat16),
        ),
        grid=(width // PAIR,),
        in_specs=[
            pair_block(rows),
            pair_block(text),
            pair_block(text),
            pl.BlockSpec((text, 1), lambda i: (0, 0)),
            pair_block(rows),
        ],
        out_specs=(pair_block(rows), pair_block(text), pair_block(text)),
        compiler_params=pltpu.CompilerParams(vmem_limit_bytes=32 * 2**20),
        cost_estimate=pl.CostEstimate(
            flops=20 * rows * text * width, bytes_accessed=6 * rows * width, transcendentals=0
        ),
        name="cross_attend_back",
    )(probes, lookups, contents, present, grads)


def unpack_kernel(in_ref, out_ref):
    pieces = in_ref[...]
    out_ref[...] = pieces.reshape(-1, pieces.shape[-1]).T.astype(jnp.float32)


def unpack(full, rows, place, out_shape, out_at, together):
    owners, _, features = full.shape
    tall = out_shape[0] // features
    wide = out_shape[1] // (together * rows)
    return pl.pallas_call(
        unpack_kernel,
        out_shape=jax.ShapeDtypeStruct(out_shape, jnp.float32),
        grid=(tall, wide),
        in_specs=[
            pl.BlockSpec((together, rows, features), lambda i, j: (j + out_at, place + i, 0))
        ],
        out_specs=pl.BlockSpec((features, together * rows), lambda i, j: (i, j)),
        compiler_params=pltpu.CompilerParams(vmem_limit_bytes=32 * 2**20),
        cost_estimate=pl.CostEstimate(
            flops=0, bytes_accessed=6 * out_shape[0] * out_shape[1], transcendentals=0
        ),
        name="unpack",
    )(full)


def unpack_late_kernel(seat, one_ref, two_ref, out_ref):
    pieces = jnp.concatenate([one_ref[0], two_ref[0]], axis=0)
    out_ref[...] = pieces.T.astype(jnp.float32)


def unpack_late(seat, full, rows, out_shape, which):
    features = full.shape[2]
    wide = out_shape[1] // (2 * rows)
    parts = full.shape[1] // rows

    def part_block(side):
        def at(j, seat):
            part = 2 * (which * wide + j) + side
            return (part // parts) ^ seat[0], part % parts, 0

        return pl.BlockSpec((1, rows, features), at)

    return pl.pallas_call(
        unpack_late_kernel,
        out_shape=jax.ShapeDtypeStruct(out_shape, jnp.float32),
        grid_spec=pltpu.PrefetchScalarGridSpec(
            num_scalar_prefetch=1,
            grid=(wide,),
            in_specs=[part_block(0), part_block(1)],
            out_specs=pl.BlockSpec((features, 2 * rows), lambda j, seat: (0, j)),
        ),
        compiler_params=pltpu.CompilerParams(vmem_limit_bytes=32 * 2**20),
        cost_estimate=pl.CostEstimate(
            flops=0, bytes_accessed=6 * out_shape[0] * out_shape[1], transcendentals=0
        ),
        name="unpack_late",
    )(seat, full, full)


def held(values, *others):
    return list(lax.optimization_barrier((*values, *others))[: len(values)])


def after(value, *others):
    return lax.optimization_barrier((value, *others))[0]


def norm_parts(values):
    mean = jnp.mean(values, axis=-1, keepdims=True)
    center = values - mean
    return mean, lax.rsqrt(jnp.mean(center * center, axis=-1, keepdims=True) + epsilon)


def norm_back(grads, values, parts, gain):
    mean, inverse = parts
    unit = (values - mean) * inverse
    gain_grad = jnp.sum(grads * unit, axis=0)
    bias_grad = jnp.sum(grads, axis=0)
    scaled = grads * gain
    back = inverse * (
        scaled
        - jnp.mean(scaled, axis=-1, keepdims=True)
        - unit * jnp.mean(scaled * unit, axis=-1, keepdims=True)
    )
    return back, gain_grad, bias_grad


def clip_body(
    frames,
    text_states,
    text_mask,
    clip_lengths,
    slot_used,
    teacher,
    self_norm_gain,
    self_norm_bias,
    self_query_weight,
    self_key_weight,
    self_value_weight,
    self_output_weight,
    cross_norm_gain,
    cross_norm_bias,
    cross_query_weight,
    cross_key_weight,
    cross_value_weight,
    cross_output_weight,
    feed_norm_gain,
    feed_norm_bias,
    feed_up_weight,
    feed_down_weight,
):
    block, width = frames.shape[1:]
    text_len = text_states.shape[1]
    shards, replicas, outers = 4, 8, 4
    core = lax.axis_index("core")
    shard = lax.axis_index("shard")
    outer = 2 * lax.axis_index("y") + lax.axis_index("x")
    replica = 2 * outer + core
    clip = block * shards
    hidden_units = feed_up_weight.shape[1]

    holder = {0: 0, 1: 1, 2: 1, 3: 0}
    there = ([], [])
    for c in range(2):
        for s in range(4):
            for turn in range(2):
                slot = turn if s < 2 else 1 - turn
                there[turn].append((c * 4 + s, holder[s] * 4 + 2 * c + slot))
    back = tuple([(b, a) for a, b in pairs] for pairs in there)
    spot = ("core", "shard")
    swap = [(0, 1), (1, 0)]
    even = shard % 2 == 0
    lower = shard < 2
    first_core = core == 0

    def hop(values, distance):
        pairs = [(i, (i + distance) % shards) for i in range(shards)]
        return lax.ppermute(values, "shard", pairs)

    def hops(values):
        return [hop(values, distance) for distance in (1, 2, 3)]

    def line_up(mine, came):
        out = jnp.zeros((shards,) + mine.shape, mine.dtype)
        out = lax.dynamic_update_index_in_dim(out, mine, shard, 0)
        for distance, values in zip((1, 2, 3), came):
            owner = lax.rem(shard + shards - distance, shards)
            out = lax.dynamic_update_index_in_dim(out, values, owner, 0)
        return out

    def to_chip(pair):
        one = lax.ppermute(jnp.where(lower, pair[0], pair[1]), spot, there[0])
        two = lax.ppermute(jnp.where(lower, pair[1], pair[0]), spot, there[1])
        return one, two

    def by_time(one, two):
        return jnp.concatenate([jnp.where(even, one, two), jnp.where(even, two, one)], axis=0)

    def outgoing(values):
        early, late = values[:block], values[block:]
        return jnp.where(even, early, late), jnp.where(even, late, early)

    def from_chip(values):
        one, two = outgoing(values)
        return lax.ppermute(one, spot, back[0]), lax.ppermute(two, spot, back[1])

    def by_slot(one, two):
        return jnp.stack([jnp.where(lower, one, two), jnp.where(lower, two, one)])

    def share_of(weight):
        share = weight.shape[0] // replicas
        return lax.dynamic_slice_in_dim(weight, replica * share, share, 0)

    def from_replicas(line):
        full = lax.all_gather(line, ("y", "x", "core"), axis=1, tiled=True)
        return full.reshape(-1, line.shape[-1])

    qkv_share = jnp.concatenate(
        [share_of(self_query_weight), share_of(self_key_weight), share_of(self_value_weight)],
        axis=1,
    )
    vectors = jnp.concatenate(
        [
            self_norm_gain,
            self_norm_bias,
            cross_norm_gain,
            cross_norm_bias,
            feed_norm_gain,
            feed_norm_bias,
        ]
    )
    vectors = jnp.pad(vectors[None, :], ((0, 15), (0, 3 * width - 6 * block)))
    share = qkv_share.shape[0]
    qkv_mine = jnp.concatenate([qkv_share, vectors], axis=0)
    qkv_came = hops(qkv_mine)
    qkv_matrix = from_replicas(line_up(qkv_share, [values[:share] for values in qkv_came]))
    norms = line_up(vectors[0], [values[share] for values in qkv_came])
    norms = norms[:, : 6 * block].reshape(shards, 6, block).transpose(1, 0, 2)
    norms = norms.reshape(6, width).astype(jnp.float32)
    rest_share = jnp.concatenate(
        [share_of(self_output_weight), share_of(cross_query_weight), share_of(cross_output_weight)],
        axis=1,
    )
    rest_came = hops(after(rest_share, *qkv_came))
    rest = from_replicas(line_up(rest_share, rest_came))
    came = to_chip(after(frames, *rest_came))
    x_low = by_time(*came)
    expand_share = share_of(feed_up_weight)
    expand_came = hops(after(expand_share, *came))

    facts = jnp.concatenate(
        [(clip_lengths // 64)[:, None], (clip_lengths % 64)[:, None], slot_used[:, None], text_mask],
        axis=1,
    ).astype(jnp.bfloat16)
    facts = jnp.pad(facts[:, None, :], ((0, 0), (0, 15), (0, width - facts.shape[1])))
    text_sent = lax.ppermute(jnp.concatenate([text_states, facts], axis=1), "core", swap)
    text_other = text_sent[:, :text_len]
    both = jnp.stack([facts[:, 0], text_sent[:, text_len]])[:, :, : 3 + text_len].astype(jnp.int32)
    lengths = 64 * both[:, :, 0] + both[:, :, 1]
    fact = lax.dynamic_index_in_dim(
        jnp.where(shard // 2 == core, both[0], both[1]), shard % 2, 0, keepdims=False
    )
    length, used = 64 * fact[0] + fact[1], fact[2]
    present = fact[3:].reshape(text_len, 1)
    count = jnp.sum(
        jnp.where(both[:, :, 2] > 0, jnp.minimum(lengths, clip), 0).astype(jnp.float32)
    )
    count = jnp.full((8, 128), count)
    for axis in ("x", "y"):
        count += lax.ppermute(count, axis, swap)
    count = count[0, 0]
    text_all = jnp.concatenate(
        [
            jnp.where(first_core, text_states, text_other),
            jnp.where(first_core, text_other, text_states),
        ],
        axis=0,
    ).reshape(4 * text_len, width)
    text_all = lax.dynamic_slice_in_dim(text_all, shard * block, block, 1)
    text_matrix = jnp.where(first_core, cross_key_weight, cross_value_weight)
    text_part = project(text_all, text_matrix).astype(jnp.bfloat16).reshape(4, text_len, width)
    text_came = [
        hop(
            lax.dynamic_index_in_dim(
                text_part, lax.rem(shard + distance, shards), 0, keepdims=False
            ),
            distance,
        )
        for distance in (1, 2, 3)
    ]

    places = jnp.stack([core, 3 - core, length, 1 - core, 2 + core]).astype(jnp.int32)
    positions = jnp.concatenate(
        [core * block + jnp.arange(block), (3 - core) * block + jnp.arange(block)]
    )
    valid_rows = ((positions < length) & (used > 0)).astype(jnp.float32)[:, None]
    inputs = x_low.astype(jnp.float32)
    parts_one = norm_parts(inputs)
    hidden_one = ((inputs - parts_one[0]) * parts_one[1] * norms[0] + norms[1]).astype(
        jnp.bfloat16
    )
    kv = project(after(hidden_one, count), qkv_matrix[:, width:]).astype(jnp.bfloat16)
    kv_other = lax.ppermute(kv, "core", swap)
    queries = project(after(hidden_one, kv), qkv_matrix[:, :width]).astype(jnp.bfloat16)
    expand_came = held(expand_came, kv_other, queries)
    expand_matrix = from_replicas(line_up(expand_share, expand_came))
    reduce_share = share_of(feed_down_weight)
    reduce_came = hops(after(reduce_share, *expand_came))
    output_matrix = rest[:, :width]
    probe_matrix = rest[:, width : 2 * width]
    merge_matrix = rest[:, 2 * width :]
    mixed_self, lse = self_attend(after(places, *expand_came), queries, kv, kv_other)
    reduce_came = held(reduce_came, mixed_self)
    reduce_matrix = from_replicas(line_up(reduce_share, reduce_came))
    text_came = held(text_came, mixed_self)
    text_half = lax.dynamic_index_in_dim(text_part, shard, 0, keepdims=False).astype(jnp.float32)
    for values in text_came:
        text_half += values.astype(jnp.float32)
    text_half = text_half.astype(jnp.bfloat16)
    text_swap = lax.ppermute(text_half, "core", swap)
    lookups = jnp.where(first_core, text_half, text_swap)
    contents = jnp.where(first_core, text_swap, text_half)
    after_self = inputs + project(mixed_self, output_matrix)
    parts_two = norm_parts(after_self)
    hidden_two = ((after_self - parts_two[0]) * parts_two[1] * norms[2] + norms[3]).astype(
        jnp.bfloat16
    )
    probes = project(hidden_two, probe_matrix).astype(jnp.bfloat16)
    teacher_low = by_time(*to_chip(after(teacher, *reduce_came, probes)))
    cross_mixed = cross_attend(probes, lookups, contents, present)
    after_cross = after_self + project(cross_mixed, merge_matrix)
    parts_three = norm_parts(after_cross)
    hidden_three = (
        (after_cross - parts_three[0]) * parts_three[1] * norms[4] + norms[5]
    ).astype(jnp.bfloat16)
    upward = project(hidden_three, expand_matrix)
    activated, gelu_pull = jax.vjp(exact_gelu, upward)
    activated_low = activated.astype(jnp.bfloat16)
    result = after_cross + project(activated_low, reduce_matrix)
    errors = (result - teacher_low.astype(jnp.float32)) * valid_rows
    squares = jnp.sum(errors * errors)
    grad_result = errors * (4 * outers * clip / count)
    grad_feed_low = grad_result.astype(jnp.bfloat16)

    def theirs_of(right, left):
        columns = right.shape[1] // 2
        part = lax.dynamic_slice_in_dim(right, (1 - core) * columns, columns, 1)
        return outer_sum(part, left).astype(jnp.bfloat16)

    def ours_of(right, left, theirs):
        columns = right.shape[1] // 2
        sent = lax.ppermute(theirs, "core", swap)
        part = lax.dynamic_slice_in_dim(right, core * columns, columns, 1)
        return (outer_sum(part, left) + sent.astype(jnp.float32)).astype(jnp.bfloat16)

    def over_outer(values):
        return lax.psum_scatter(values, ("y", "x"), scatter_dimension=0, tiled=True)

    def shard_hops(values):
        columns = values.shape[1] // shards
        return [
            hop(
                lax.dynamic_slice_in_dim(
                    values, lax.rem(shard + distance, shards) * columns, columns, 1
                ),
                distance,
            )
            for distance in (1, 2, 3)
        ]

    def over_shard(values, came):
        columns = values.shape[1] // shards
        total = lax.dynamic_slice_in_dim(values, shard * columns, columns, 1).astype(jnp.float32)
        for part in came:
            total += part.astype(jnp.float32)
        return total.astype(jnp.bfloat16)

    down_ours = outer_sum(grad_feed_low, activated_low).astype(jnp.bfloat16)
    down_sum = lax.psum_scatter(down_ours, REPLICAS, scatter_dimension=0, tiled=True)
    to_send = outgoing(result.astype(jnp.bfloat16))
    output_one = lax.ppermute(to_send[0], spot, back[0])
    grad_activated = back_project(after(grad_feed_low, down_ours), reduce_matrix)
    grad_upward = gelu_pull(grad_activated)[0].astype(jnp.bfloat16)
    output_one = after(output_one, grad_upward)
    up_theirs = theirs_of(after(grad_upward, output_one), hidden_three)
    grad_hidden_three = back_project(after(grad_upward, up_theirs), expand_matrix)
    output_two = lax.ppermute(after(to_send[1], output_one), spot, back[1])
    output_two = after(output_two, grad_hidden_three)
    output = by_slot(output_one, output_two)
    up_ours = ours_of(after(grad_upward, grad_hidden_three, output_two), hidden_three, up_theirs)
    grad_norm, gain_feed, bias_feed = norm_back(
        after(grad_hidden_three, up_ours), after_cross, parts_three, norms[4]
    )
    grad_after_cross = grad_result + grad_norm
    grad_cross_low = grad_after_cross.astype(jnp.bfloat16)
    merge_theirs = theirs_of(grad_cross_low, cross_mixed)
    grad_cross_mixed = back_project(after(grad_cross_low, merge_theirs), merge_matrix).astype(
        jnp.bfloat16
    )
    probe_grads, lookup_grads, content_grads = cross_attend_back(
        probes, lookups, contents, present, grad_cross_mixed
    )
    up_sum = over_outer(up_ours)
    text_mine = jnp.where(first_core, lookup_grads, content_grads)
    text_sent = lax.ppermute(
        jnp.where(first_core, content_grads, lookup_grads), "core", swap
    )
    text_mine = (text_mine.astype(jnp.float32) + text_sent.astype(jnp.float32)).astype(
        jnp.bfloat16
    )
    merge_ours = ours_of(after(grad_cross_low, probe_grads), cross_mixed, merge_theirs)
    probe_theirs = theirs_of(after(probe_grads, merge_ours), hidden_two)
    grad_hidden_two = back_project(after(probe_grads, probe_theirs), probe_matrix)
    text_four = line_up(text_mine, hops(text_mine)).reshape(4 * text_len, width)
    grad_norm, gain_cross, bias_cross = norm_back(
        grad_hidden_two, after_self, parts_two, norms[2]
    )
    grad_after_self = grad_after_cross + grad_norm
    grad_self_low = grad_after_self.astype(jnp.bfloat16)
    output_theirs = theirs_of(grad_self_low, mixed_self)
    grad_mixed = back_project(after(grad_self_low, output_theirs), output_matrix).astype(
        jnp.bfloat16
    )
    probe_ours = ours_of(after(probe_grads, grad_mixed), hidden_two, probe_theirs)
    text_weights = outer_sum(text_four, text_all).astype(jnp.bfloat16)
    text_back = back_project(text_four, text_matrix).astype(jnp.bfloat16)
    output_ours = ours_of(after(grad_self_low, probe_ours), mixed_self, output_theirs)
    text_rows = width // outers
    middle = jnp.concatenate(
        [
            values.reshape(outers, -1, width)
            for values in (
                output_ours,
                probe_ours,
                merge_ours,
                text_weights.reshape(outers, shards, text_rows // shards, block)
                .transpose(0, 2, 1, 3)
                .reshape(outers, text_rows // shards, width),
            )
        ],
        axis=1,
    )
    middle_rows = middle.shape[1]
    middle = middle.reshape(outers * middle_rows, width)
    middle_sum = over_outer(middle)
    text_split = text_rows // shards
    text_piece = (
        middle_sum[middle_rows - text_split :]
        .reshape(text_split, shards, block)
        .transpose(1, 0, 2)
        .reshape(text_rows, block)
    )
    text_back = text_back.reshape(2, 2, text_len, block)
    text_kept = lax.dynamic_index_in_dim(text_back, core, 0, keepdims=False)
    text_gone = lax.dynamic_index_in_dim(text_back, 1 - core, 0, keepdims=False)
    text_own = text_kept.astype(jnp.float32) + lax.ppermute(text_gone, "core", swap).astype(
        jnp.float32
    )
    text_own = text_own.astype(jnp.bfloat16)
    down_came = shard_hops(down_sum)
    text_came = hops(text_own)
    grad_queries, own_keys, own_values, other_keys, other_values = self_attend_back(
        places, queries, kv, kv_other, mixed_self, after(grad_mixed, middle, text_own), lse
    )
    text_came = held(text_came, grad_queries)
    down_came = held(down_came, grad_queries)
    other_keys, other_values = held([other_keys, other_values], *text_came, *down_came)
    own_keys += lax.ppermute(other_keys, "core", swap)
    own_values += lax.ppermute(other_values, "core", swap)
    down_piece = over_shard(down_sum, down_came)
    up_came = shard_hops(after(up_sum, down_piece))

    qkv_grads = jnp.concatenate([grad_queries, own_keys, own_values], axis=1)
    qkv_theirs = theirs_of(qkv_grads, hidden_one)
    grad_hidden_one = back_project(after(qkv_grads, qkv_theirs), qkv_matrix)
    qkv_ours = ours_of(after(qkv_grads, grad_hidden_one), hidden_one, qkv_theirs)
    up_came = held(up_came, grad_hidden_one)
    up_piece = over_shard(up_sum, up_came)
    text_grad = line_up(text_own, text_came).astype(jnp.float32)
    text_grad = text_grad.transpose(1, 2, 0, 3).reshape(text_states.shape)
    qkv_sum = over_outer(qkv_ours)
    grad_norm, gain_self, bias_self = norm_back(
        after(grad_hidden_one, qkv_ours, *up_came), inputs, parts_one, norms[0]
    )
    middle_kept = after(middle_sum[: middle_rows - text_split], qkv_ours, *up_came)
    middle_came = shard_hops(middle_kept)
    late_came = shard_hops(after(qkv_sum, *middle_came))
    frames_came = from_chip(
        after((grad_after_self + grad_norm).astype(jnp.bfloat16), *late_came)
    )
    frames_grad = by_slot(*frames_came).astype(jnp.float32)

    small = jnp.stack(
        [
            gain_self,
            bias_self,
            gain_cross,
            bias_cross,
            gain_feed,
            bias_feed,
            jnp.full((width,), squares),
            jnp.zeros((width,), jnp.float32),
        ]
    )
    for axis, pairs in (
        ("core", swap),
        ("x", swap),
        ("y", swap),
        ("shard", [(0, 1), (1, 0), (2, 3), (3, 2)]),
        ("shard", [(0, 2), (2, 0), (1, 3), (3, 1)]),
    ):
        small += lax.ppermute(small, axis, pairs)
    loss = small[6, 0] / (width * count)
    small_own = lax.dynamic_slice_in_dim(small, shard * block, block, 1)

    middle_piece = over_shard(middle_kept, middle_came)
    early = jnp.concatenate(
        [up_piece]
        + [down_piece[:, i * block : (i + 1) * block] for i in range(4)]
        + [text_piece, middle_piece],
        axis=0,
    )
    early = lax.all_gather(after(early, text_grad), REPLICAS, axis=0)
    piece = width // replicas
    square = (block, width)
    up_grad = unpack(early, hidden_units // replicas, 0, (block, hidden_units), 0, 1)
    at = hidden_units // replicas // piece
    down_grad = unpack(early, piece, at, (4 * block, width), 0, 2)
    at += 4
    key_grad = unpack(early, text_rows, at * piece // text_rows, square, 0, 1)
    value_grad = unpack(early, text_rows, at * piece // text_rows, square, 4, 1)
    at += text_rows // piece
    output_grad = unpack(early, piece, at, square, 0, 2)
    probe_grad = unpack(early, piece, at + 1, square, 0, 2)
    merge_grad = unpack(early, piece, at + 2, square, 0, 2)
    late = over_shard(qkv_sum, late_came)
    late_x = lax.ppermute(late, "x", swap)
    late_y = lax.ppermute(late, "y", swap)
    cut = late.shape[0] // 2
    late_one = lax.ppermute(late_x[:cut], "y", swap)
    late_two = lax.ppermute(late_y[cut:], "x", swap)
    late = jnp.concatenate([late, late_x, late_y, late_one, late_two], axis=0)
    late = jnp.concatenate([late, lax.ppermute(late, "core", swap)], axis=0)
    late = late.reshape(replicas, -1, block)
    seat = (4 * core + outer).astype(jnp.int32).reshape(1)
    qkv_grad = [unpack_late(seat, late, piece, square, i) for i in range(3)]
    return (
        output,
        loss,
        frames_grad,
        text_grad,
        small_own[0],
        small_own[1],
        qkv_grad[0],
        qkv_grad[1],
        qkv_grad[2],
        output_grad,
        small_own[2],
        small_own[3],
        probe_grad,
        key_grad,
        value_grad,
        merge_grad,
        small_own[4],
        small_own[5],
        up_grad,
        down_grad,
    )


def solution(mesh):
    by_chip = mesh.shape["shard"] == 4 and mesh.shape["replica"] == 8
    replica = ("y", "x", "core") if by_chip else "replica"
    row = P(replica)
    clip = P(replica, "shard", None)
    text = P(replica, None, None)
    vector = P("shard")
    matrix = P("shard", None)
    weights = (
        [vector, vector] + [matrix] * 4 + [vector, vector] + [matrix] * 4 + [vector, vector]
        + [matrix] * 2
    )
    if by_chip:
        mesh = Mesh(mesh.devices.reshape(2, 2, 2, 4), ("y", "x", "core", "shard"))
    return jax.shard_map(
        clip_body if by_chip else general_body,
        mesh=mesh,
        in_specs=(clip, text, P(replica, None), row, row, clip, *weights),
        out_specs=(clip, P(), clip, text, *weights),
        check_vma=False,
    )
```

```python
import jax
import jax.numpy as jnp
from jax import lax
from jax.experimental import pallas as pl
from jax.experimental.pallas import tpu as pltpu
from jax.sharding import Mesh
from jax.sharding import PartitionSpec as P

HEADS = 24
HEAD_DIM = 64


epsilon = 1e-05
masked_score = -1e30


def layer_norm(values, gain, shift):
    center = values - jnp.mean(values, axis=-1, keepdims=True)
    variance = jnp.mean(center * center, axis=-1, keepdims=True)
    return center * lax.rsqrt(variance + epsilon) * gain + shift


def exact_gelu(values):
    return jax.nn.gelu(values, approximate=False)


def project(left, right):
    return jnp.dot(left, right, preferred_element_type=jnp.float32)


def outer_sum(left, right):
    return jnp.einsum("rd,re->de", left, right, preferred_element_type=jnp.float32)


def back_project(grads, matrix):
    return jnp.einsum("re,de->rd", grads, matrix, preferred_element_type=jnp.float32)


def split_heads(values):
    return values.reshape(values.shape[:-1] + (HEADS, HEAD_DIM))


def self_forward(operands):
    queries, keys_all, values_all, allowed = operands
    scale = HEAD_DIM ** (-0.5)
    scores = (
        jnp.einsum("qhd,khd->hqk", queries, keys_all, preferred_element_type=jnp.float32) * scale
    )
    scores = jnp.where(allowed[None], scores, masked_score)
    peak = jnp.max(scores, axis=-1, keepdims=True)
    weights = jnp.exp(scores - peak)
    totals = jnp.sum(weights, axis=-1, keepdims=True)
    probs = (weights / totals).astype(jnp.bfloat16)
    mixed = jnp.einsum("hqk,khd->qhd", probs, values_all, preferred_element_type=jnp.float32)
    return (mixed.astype(jnp.bfloat16), (peak + jnp.log(totals))[..., 0])


def self_backward(operands):
    queries, keys_all, values_all, allowed, log_totals, grad_mixed = operands
    scale = HEAD_DIM ** (-0.5)
    scores = (
        jnp.einsum("qhd,khd->hqk", queries, keys_all, preferred_element_type=jnp.float32) * scale
    )
    scores = jnp.where(allowed[None], scores, masked_score)
    probs = jnp.exp(scores - log_totals[..., None])
    grad_probs = jnp.einsum(
        "qhd,khd->hqk", grad_mixed, values_all, preferred_element_type=jnp.float32
    )
    grad_values = jnp.einsum(
        "hqk,qhd->khd", probs.astype(jnp.bfloat16), grad_mixed, preferred_element_type=jnp.float32
    )
    inner = jnp.sum(probs * grad_probs, axis=-1, keepdims=True)
    grad_scores = (probs * (grad_probs - inner)).astype(jnp.bfloat16)
    grad_queries = (
        jnp.einsum("hqk,khd->qhd", grad_scores, keys_all, preferred_element_type=jnp.float32)
        * scale
    ).astype(jnp.bfloat16)
    grad_keys = (
        jnp.einsum("hqk,qhd->khd", grad_scores, queries, preferred_element_type=jnp.float32) * scale
    )
    return (grad_queries, grad_keys, grad_values)


def general_body(
    frames,
    text_states,
    text_mask,
    clip_lengths,
    slot_used,
    teacher,
    self_norm_gain,
    self_norm_bias,
    self_query_weight,
    self_key_weight,
    self_value_weight,
    self_output_weight,
    cross_norm_gain,
    cross_norm_bias,
    cross_query_weight,
    cross_key_weight,
    cross_value_weight,
    cross_output_weight,
    feed_norm_gain,
    feed_norm_bias,
    feed_up_weight,
    feed_down_weight,
):
    gathered = (
        lax.all_gather(self_norm_gain, "shard", axis=0, tiled=True),
        lax.all_gather(self_norm_bias, "shard", axis=0, tiled=True),
        lax.all_gather(self_query_weight, "shard", axis=0, tiled=True),
        lax.all_gather(self_key_weight, "shard", axis=0, tiled=True),
        lax.all_gather(self_value_weight, "shard", axis=0, tiled=True),
        lax.all_gather(self_output_weight, "shard", axis=0, tiled=True),
        lax.all_gather(cross_norm_gain, "shard", axis=0, tiled=True),
        lax.all_gather(cross_norm_bias, "shard", axis=0, tiled=True),
        lax.all_gather(cross_query_weight, "shard", axis=0, tiled=True),
        lax.all_gather(cross_key_weight, "shard", axis=0, tiled=True),
        lax.all_gather(cross_value_weight, "shard", axis=0, tiled=True),
        lax.all_gather(cross_output_weight, "shard", axis=0, tiled=True),
        lax.all_gather(feed_norm_gain, "shard", axis=0, tiled=True),
        lax.all_gather(feed_norm_bias, "shard", axis=0, tiled=True),
        lax.all_gather(feed_up_weight, "shard", axis=0, tiled=True),
        lax.all_gather(feed_down_weight, "shard", axis=0, tiled=True),
    )
    (
        gain_attend,
        bias_attend,
        query_matrix,
        key_matrix,
        value_matrix,
        output_matrix,
        gain_cross,
        bias_cross,
        probe_matrix,
        lookup_matrix,
        content_matrix,
        merge_matrix,
        gain_feed,
        bias_feed,
        expand_matrix,
        reduce_matrix,
    ) = gathered
    slots = frames.shape[0]
    frame_count = frames.shape[1]
    width = frames.shape[2]
    text_len = text_states.shape[1]
    shards = lax.axis_size("shard")
    replicas = lax.axis_size("replica")
    clip_total = frame_count * shards
    row_count = slots * frame_count
    scale = HEAD_DIM ** (-0.5)
    shard_rank = lax.axis_index("shard")
    positions = shard_rank * frame_count + jnp.arange(frame_count, dtype=jnp.int32)
    key_positions = jnp.arange(clip_total, dtype=jnp.int32)
    allowed = (key_positions[None, None, :] <= positions[None, :, None]) & (
        key_positions[None, None, :] < clip_lengths[:, None, None]
    )
    valid_rows = ((positions[None, :] < clip_lengths[:, None]) & (slot_used[:, None] > 0)).astype(
        jnp.float32
    )
    text_allowed = text_mask > 0
    inputs = frames.astype(jnp.float32)
    normed_one, pull_one = jax.vjp(
        layer_norm, inputs, gain_attend.astype(jnp.float32), bias_attend.astype(jnp.float32)
    )
    hidden_one = normed_one.astype(jnp.bfloat16).reshape(row_count, width)
    queries = (
        project(hidden_one, query_matrix).astype(jnp.bfloat16).reshape(slots, frame_count, width)
    )
    keys_local = (
        project(hidden_one, key_matrix).astype(jnp.bfloat16).reshape(slots, frame_count, width)
    )
    values_local = (
        project(hidden_one, value_matrix).astype(jnp.bfloat16).reshape(slots, frame_count, width)
    )
    keys_all, values_all = (
        lax.all_gather(keys_local, "shard", axis=1, tiled=True),
        lax.all_gather(values_local, "shard", axis=1, tiled=True),
    )
    head_queries = split_heads(queries)
    head_keys = split_heads(keys_all)
    head_values = split_heads(values_all)
    mixed_self, log_totals = lax.map(self_forward, (head_queries, head_keys, head_values, allowed))
    mixed_rows = mixed_self.reshape(row_count, width)
    after_self = inputs + project(mixed_rows, output_matrix).reshape(slots, frame_count, width)
    normed_two, pull_two = jax.vjp(
        layer_norm, after_self, gain_cross.astype(jnp.float32), bias_cross.astype(jnp.float32)
    )
    hidden_two = normed_two.astype(jnp.bfloat16).reshape(row_count, width)
    probes = split_heads(
        project(hidden_two, probe_matrix).astype(jnp.bfloat16).reshape(slots, frame_count, width)
    )
    text_rows = text_states.reshape(slots * text_len, width)
    lookups = split_heads(
        project(text_rows, lookup_matrix).astype(jnp.bfloat16).reshape(slots, text_len, width)
    )
    contents = split_heads(
        project(text_rows, content_matrix).astype(jnp.bfloat16).reshape(slots, text_len, width)
    )
    cross_scores = (
        jnp.einsum("sqhd,skhd->shqk", probes, lookups, preferred_element_type=jnp.float32) * scale
    )
    cross_scores = jnp.where(text_allowed[:, None, None, :], cross_scores, masked_score)
    cross_peak = jnp.max(cross_scores, axis=-1, keepdims=True)
    cross_weights = jnp.exp(cross_scores - cross_peak)
    cross_probs = cross_weights / jnp.sum(cross_weights, axis=-1, keepdims=True)
    cross_probs_low = cross_probs.astype(jnp.bfloat16)
    cross_mixed = jnp.einsum(
        "shqk,skhd->sqhd", cross_probs_low, contents, preferred_element_type=jnp.float32
    )
    cross_mixed = cross_mixed.astype(jnp.bfloat16).reshape(row_count, width)
    after_cross = after_self + project(cross_mixed, merge_matrix).reshape(slots, frame_count, width)
    normed_three, pull_three = jax.vjp(
        layer_norm, after_cross, gain_feed.astype(jnp.float32), bias_feed.astype(jnp.float32)
    )
    hidden_three = normed_three.astype(jnp.bfloat16).reshape(row_count, width)
    upward = project(hidden_three, expand_matrix)
    activated, gelu_pull = jax.vjp(exact_gelu, upward)
    activated_low = activated.astype(jnp.bfloat16)
    result = after_cross + project(activated_low, reduce_matrix).reshape(slots, frame_count, width)
    output = result.astype(jnp.bfloat16)
    errors = (result - teacher.astype(jnp.float32)) * valid_rows[..., None]
    squares_total, count_total = lax.psum(
        (jnp.sum(errors * errors), jnp.sum(valid_rows)), ("replica", "shard")
    )
    loss = squares_total / (width * count_total)
    grad_result = errors * (slots * replicas * clip_total / count_total)
    grad_feed_low = grad_result.reshape(row_count, width).astype(jnp.bfloat16)
    grad_activated = back_project(grad_feed_low, reduce_matrix)
    grad_upward = gelu_pull(grad_activated)[0].astype(jnp.bfloat16)
    grad_hidden_three = back_project(grad_upward, expand_matrix).reshape(slots, frame_count, width)
    grad_cross_norm, gain_feed_part, bias_feed_part = pull_three(grad_hidden_three)
    grad_after_cross = grad_result + grad_cross_norm
    feed_owned = (
        lax.psum_scatter(
            outer_sum(hidden_three, grad_upward).astype(jnp.bfloat16),
            "shard",
            scatter_dimension=0,
            tiled=True,
        ).astype(jnp.float32),
        lax.psum_scatter(
            outer_sum(activated_low, grad_feed_low).astype(jnp.bfloat16),
            "shard",
            scatter_dimension=0,
            tiled=True,
        ).astype(jnp.float32),
        lax.psum_scatter(
            gain_feed_part.astype(jnp.bfloat16), "shard", scatter_dimension=0, tiled=True
        ).astype(jnp.float32),
        lax.psum_scatter(
            bias_feed_part.astype(jnp.bfloat16), "shard", scatter_dimension=0, tiled=True
        ).astype(jnp.float32),
    )
    grad_cross_low = grad_after_cross.reshape(row_count, width).astype(jnp.bfloat16)
    grad_cross_mixed = split_heads(
        back_project(grad_cross_low, merge_matrix)
        .astype(jnp.bfloat16)
        .reshape(slots, frame_count, width)
    )
    grad_cross_probs = jnp.einsum(
        "sqhd,skhd->shqk", grad_cross_mixed, contents, preferred_element_type=jnp.float32
    )
    content_grads = jnp.einsum(
        "shqk,sqhd->skhd", cross_probs_low, grad_cross_mixed, preferred_element_type=jnp.float32
    )
    cross_inner = jnp.sum(cross_probs * grad_cross_probs, axis=-1, keepdims=True)
    grad_cross_scores = (cross_probs * (grad_cross_probs - cross_inner)).astype(jnp.bfloat16)
    probe_grads = (
        jnp.einsum(
            "shqk,skhd->sqhd", grad_cross_scores, lookups, preferred_element_type=jnp.float32
        )
        * scale
    )
    probe_grads = probe_grads.astype(jnp.bfloat16).reshape(row_count, width)
    lookup_grads = (
        jnp.einsum("shqk,sqhd->skhd", grad_cross_scores, probes, preferred_element_type=jnp.float32)
        * scale
    )
    lookup_sum, content_sum = (
        lax.psum(lookup_grads.astype(jnp.bfloat16), "shard").astype(jnp.float32),
        lax.psum(content_grads.astype(jnp.bfloat16), "shard").astype(jnp.float32),
    )
    lookup_low = lookup_sum.astype(jnp.bfloat16).reshape(slots * text_len, width)
    content_low = content_sum.astype(jnp.bfloat16).reshape(slots * text_len, width)
    own_width = width // shards
    own_text = lax.dynamic_slice_in_dim(text_rows, shard_rank * own_width, own_width, 1)
    lookup_own = outer_sum(own_text, lookup_low)
    content_own = outer_sum(own_text, content_low)
    text_grad = (
        back_project(lookup_low, lookup_matrix) + back_project(content_low, content_matrix)
    ).reshape(slots, text_len, width)
    grad_hidden_two = back_project(probe_grads, probe_matrix).reshape(slots, frame_count, width)
    grad_self_norm, gain_cross_part, bias_cross_part = pull_two(grad_hidden_two)
    grad_after_self = grad_after_cross + grad_self_norm
    grad_self_low = grad_after_self.reshape(row_count, width).astype(jnp.bfloat16)
    grad_mixed = split_heads(
        back_project(grad_self_low, output_matrix)
        .astype(jnp.bfloat16)
        .reshape(slots, frame_count, width)
    )
    grad_queries, grad_keys, grad_values = lax.map(
        self_backward, (head_queries, head_keys, head_values, allowed, log_totals, grad_mixed)
    )
    key_sum, value_sum = (
        lax.psum_scatter(
            grad_keys.reshape(slots, clip_total, width).astype(jnp.bfloat16),
            "shard",
            scatter_dimension=1,
            tiled=True,
        ).astype(jnp.float32),
        lax.psum_scatter(
            grad_values.reshape(slots, clip_total, width).astype(jnp.bfloat16),
            "shard",
            scatter_dimension=1,
            tiled=True,
        ).astype(jnp.float32),
    )
    key_low = key_sum.astype(jnp.bfloat16).reshape(row_count, width)
    value_low = value_sum.astype(jnp.bfloat16).reshape(row_count, width)
    query_low = grad_queries.reshape(row_count, width)
    grad_hidden_one = (
        back_project(query_low, query_matrix)
        + back_project(key_low, key_matrix)
        + back_project(value_low, value_matrix)
    )
    grad_inputs, gain_attend_part, bias_attend_part = pull_one(
        grad_hidden_one.reshape(slots, frame_count, width)
    )
    frames_grad = grad_after_self + grad_inputs
    attend_owned = (
        lax.psum_scatter(
            outer_sum(hidden_one, query_low).astype(jnp.bfloat16),
            "shard",
            scatter_dimension=0,
            tiled=True,
        ).astype(jnp.float32),
        lax.psum_scatter(
            outer_sum(hidden_one, key_low).astype(jnp.bfloat16),
            "shard",
            scatter_dimension=0,
            tiled=True,
        ).astype(jnp.float32),
        lax.psum_scatter(
            outer_sum(hidden_one, value_low).astype(jnp.bfloat16),
            "shard",
            scatter_dimension=0,
            tiled=True,
        ).astype(jnp.float32),
        lax.psum_scatter(
            outer_sum(mixed_rows, grad_self_low).astype(jnp.bfloat16),
            "shard",
            scatter_dimension=0,
            tiled=True,
        ).astype(jnp.float32),
        lax.psum_scatter(
            outer_sum(hidden_two, probe_grads).astype(jnp.bfloat16),
            "shard",
            scatter_dimension=0,
            tiled=True,
        ).astype(jnp.float32),
        lax.psum_scatter(
            outer_sum(cross_mixed, grad_cross_low).astype(jnp.bfloat16),
            "shard",
            scatter_dimension=0,
            tiled=True,
        ).astype(jnp.float32),
        lax.psum_scatter(
            gain_attend_part.astype(jnp.bfloat16), "shard", scatter_dimension=0, tiled=True
        ).astype(jnp.float32),
        lax.psum_scatter(
            bias_attend_part.astype(jnp.bfloat16), "shard", scatter_dimension=0, tiled=True
        ).astype(jnp.float32),
        lax.psum_scatter(
            gain_cross_part.astype(jnp.bfloat16), "shard", scatter_dimension=0, tiled=True
        ).astype(jnp.float32),
        lax.psum_scatter(
            bias_cross_part.astype(jnp.bfloat16), "shard", scatter_dimension=0, tiled=True
        ).astype(jnp.float32),
    )
    summed = (
        lax.psum(attend_owned[6].astype(jnp.bfloat16), "replica").astype(jnp.float32),
        lax.psum(attend_owned[7].astype(jnp.bfloat16), "replica").astype(jnp.float32),
        lax.psum(attend_owned[0].astype(jnp.bfloat16), "replica").astype(jnp.float32),
        lax.psum(attend_owned[1].astype(jnp.bfloat16), "replica").astype(jnp.float32),
        lax.psum(attend_owned[2].astype(jnp.bfloat16), "replica").astype(jnp.float32),
        lax.psum(attend_owned[3].astype(jnp.bfloat16), "replica").astype(jnp.float32),
        lax.psum(attend_owned[8].astype(jnp.bfloat16), "replica").astype(jnp.float32),
        lax.psum(attend_owned[9].astype(jnp.bfloat16), "replica").astype(jnp.float32),
        lax.psum(attend_owned[4].astype(jnp.bfloat16), "replica").astype(jnp.float32),
        lax.psum(lookup_own.astype(jnp.bfloat16), "replica").astype(jnp.float32),
        lax.psum(content_own.astype(jnp.bfloat16), "replica").astype(jnp.float32),
        lax.psum(attend_owned[5].astype(jnp.bfloat16), "replica").astype(jnp.float32),
        lax.psum(feed_owned[2].astype(jnp.bfloat16), "replica").astype(jnp.float32),
        lax.psum(feed_owned[3].astype(jnp.bfloat16), "replica").astype(jnp.float32),
        lax.psum(feed_owned[0].astype(jnp.bfloat16), "replica").astype(jnp.float32),
        lax.psum(feed_owned[1].astype(jnp.bfloat16), "replica").astype(jnp.float32),
    )
    return (
        output,
        loss,
        frames_grad,
        text_grad,
        summed[0],
        summed[1],
        summed[2],
        summed[3],
        summed[4],
        summed[5],
        summed[6],
        summed[7],
        summed[8],
        summed[9],
        summed[10],
        summed[11],
        summed[12],
        summed[13],
        summed[14],
        summed[15],
    )


PAIR = 2 * HEAD_DIM
EVERY = ("shard", "y", "x", "core")
REPLICAS = ("core", "y", "x")
NT = (((1,), (1,)), ((), ()))
TN = (((0,), (0,)), ((), ()))
NN = (((1,), (0,)), ((), ()))


def dot(left, right, dims):
    return lax.dot_general(left, right, dims, preferred_element_type=jnp.float32)


def half_mask(side, value):
    lanes = lax.broadcasted_iota(jnp.int32, (1, PAIR), 1)
    inside = (lanes >= HEAD_DIM) if side else (lanes < HEAD_DIM)
    return jnp.where(inside, value, 0.0).astype(jnp.bfloat16)


def fill_clip(place, own_ref, other_ref, all_ref):
    block = own_ref.shape[0] // 2
    for part in range(2):
        rows = slice(part * block, (part + 1) * block)
        for at, ref in ((place[part], own_ref), (place[3 + part], other_ref)):
            all_ref[pl.ds(pl.multiple_of(at * block, block), block), :] = ref[rows, :]


def self_forward_kernel(
    place, q_ref, own_k, own_v, other_k, other_v, mixed_ref, lse_ref, k_ref, v_ref, acc_ref
):
    fill_clip(place, own_k, other_k, k_ref)
    fill_clip(place, own_v, other_v, v_ref)
    block = q_ref.shape[0] // 2
    length = place[2]
    low = lax.broadcasted_iota(jnp.int32, (PAIR, 1), 0) < HEAD_DIM
    for part in range(2):
        first = place[part] * block
        rows = slice(part * block, (part + 1) * block)
        q = q_ref[rows, :]
        q_half = [q * half_mask(side, HEAD_DIM ** (-0.5)) for side in range(2)]
        limit = jnp.minimum(
            first + lax.broadcasted_iota(jnp.int32, (1, block), 1) + 1, length
        )
        acc_ref[...] = jnp.zeros_like(acc_ref)

        def step(j, peaks, q_half=q_half, limit=limit):
            at = pl.multiple_of(j * block, block)
            k = k_ref[pl.ds(at, block), :]
            v = v_ref[pl.ds(at, block), :]
            allowed = at + lax.broadcasted_iota(jnp.int32, (block, block), 0) < limit
            out = []
            for side in range(2):
                scores = jnp.where(allowed, dot(k, q_half[side], NT), masked_score)
                peak = jnp.maximum(peaks[side], jnp.max(scores, axis=0, keepdims=True))
                weights = jnp.exp(scores - peak).astype(jnp.bfloat16)
                v_ones = v * half_mask(side, 1.0) + half_mask(1 - side, 1.0)
                acc_ref[side] = acc_ref[side] * jnp.exp(peaks[side] - peak) + dot(
                    v_ones, weights, TN
                )
                out.append(peak)
            return tuple(out)

        peaks = lax.fori_loop(
            0, place[part] + 1, step, (jnp.full((1, block), masked_score, jnp.float32),) * 2
        )
        top, bottom = acc_ref[0], acc_ref[1]
        total = jnp.where(low, top[HEAD_DIM : HEAD_DIM + 1], bottom[0:1])
        mixed = jnp.where(low, top, bottom) / total
        mixed_ref[rows, :] = mixed.T.astype(jnp.bfloat16)
        lse_ref[0:1, rows] = peaks[0] + jnp.log(top[HEAD_DIM : HEAD_DIM + 1])
        lse_ref[1:2, rows] = peaks[1] + jnp.log(bottom[0:1])


def self_backward_kernel(
    place, q_ref, own_k, own_v, other_k, other_v, mixed_ref, grad_ref, lse_ref,
    dq_ref, own_dk, own_dv, other_dk, other_dv, k_ref, v_ref, dq_acc, dk_acc, dv_acc,
):
    fill_clip(place, own_k, other_k, k_ref)
    fill_clip(place, own_v, other_v, v_ref)
    block = q_ref.shape[0] // 2
    length = place[2]
    scale = HEAD_DIM ** (-0.5)
    dk_acc[...] = jnp.zeros_like(dk_acc)
    dv_acc[...] = jnp.zeros_like(dv_acc)
    for part in range(2):
        first = place[part] * block
        rows = slice(part * block, (part + 1) * block)
        q = q_ref[rows, :]
        grad = grad_ref[rows, :]
        q_half = [q * half_mask(side, scale) for side in range(2)]
        grad_half = [grad * half_mask(side, 1.0) for side in range(2)]
        product = (grad.astype(jnp.float32) * mixed_ref[rows, :].astype(jnp.float32)).T
        inner = [
            jnp.sum(product[side * HEAD_DIM : (side + 1) * HEAD_DIM], axis=0, keepdims=True)
            for side in range(2)
        ]
        lse = [lse_ref[side : side + 1, rows] for side in range(2)]
        limit = jnp.minimum(
            first + lax.broadcasted_iota(jnp.int32, (1, block), 1) + 1, length
        )
        dq_acc[...] = jnp.zeros_like(dq_acc)

        def step(
            j, carry, q_half=q_half, grad_half=grad_half, inner=inner, lse=lse, limit=limit
        ):
            at = pl.multiple_of(j * block, block)
            k = k_ref[pl.ds(at, block), :]
            v = v_ref[pl.ds(at, block), :]
            allowed = at + lax.broadcasted_iota(jnp.int32, (block, block), 0) < limit
            dq, dk, dv = 0.0, 0.0, 0.0
            for side in range(2):
                scores = jnp.where(allowed, dot(k, q_half[side], NT), masked_score)
                probs = jnp.exp(scores - lse[side])
                grad_probs = dot(v, grad_half[side], NT)
                grad_scores = (probs * (grad_probs - inner[side])).astype(jnp.bfloat16)
                dv += dot(probs.astype(jnp.bfloat16), grad_half[side], NN)
                dk += dot(grad_scores, q_half[side], NN)
                dq += dot(k * half_mask(side, scale), grad_scores, TN)
            dk_acc[pl.ds(at, block), :] += dk
            dv_acc[pl.ds(at, block), :] += dv
            dq_acc[...] += dq
            return carry

        lax.fori_loop(0, place[part] + 1, step, 0)
        dq_ref[rows, :] = dq_acc[...].T.astype(jnp.bfloat16)
    for part in range(2):
        rows = slice(part * block, (part + 1) * block)
        own = pl.ds(pl.multiple_of(place[part] * block, block), block)
        other = pl.ds(pl.multiple_of(place[3 + part] * block, block), block)
        own_dk[rows, :] = dk_acc[own, :].astype(jnp.bfloat16)
        own_dv[rows, :] = dv_acc[own, :].astype(jnp.bfloat16)
        other_dk[rows, :] = dk_acc[other, :].astype(jnp.bfloat16)
        other_dv[rows, :] = dv_acc[other, :].astype(jnp.bfloat16)


def pair_block(rows):
    return pl.BlockSpec((rows, PAIR), lambda i, *_: (0, i))


def value_block(rows, pairs):
    return pl.BlockSpec((rows, PAIR), lambda i, *_: (0, pairs + i))


def self_attend(place, queries, own, other):
    rows, width = queries.shape
    clip = 2 * rows
    pairs = width // PAIR
    return pl.pallas_call(
        self_forward_kernel,
        out_shape=(
            jax.ShapeDtypeStruct((rows, width), jnp.bfloat16),
            jax.ShapeDtypeStruct((pairs * 8, rows), jnp.float32),
        ),
        grid_spec=pltpu.PrefetchScalarGridSpec(
            num_scalar_prefetch=1,
            grid=(pairs,),
            in_specs=[pair_block(rows)] + [pair_block(rows), value_block(rows, pairs)] * 2,
            out_specs=(pair_block(rows), pl.BlockSpec((8, rows), lambda i, *_: (i, 0))),
            scratch_shapes=[
                pltpu.VMEM((clip, PAIR), jnp.bfloat16),
                pltpu.VMEM((clip, PAIR), jnp.bfloat16),
                pltpu.VMEM((2, PAIR, rows // 2), jnp.float32),
            ],
        ),
        compiler_params=pltpu.CompilerParams(vmem_limit_bytes=32 * 2**20),
        cost_estimate=pl.CostEstimate(
            flops=2 * 2 * rows * clip * width, bytes_accessed=8 * clip * width, transcendentals=0
        ),
        name="self_attend",
    )(place, queries, own, own, other, other)


def self_attend_back(place, queries, own, other, mixed, grads, lse):
    rows, width = queries.shape
    clip = 2 * rows
    pairs = width // PAIR
    return pl.pallas_call(
        self_backward_kernel,
        out_shape=(jax.ShapeDtypeStruct((rows, width), jnp.bfloat16),) * 5,
        grid_spec=pltpu.PrefetchScalarGridSpec(
            num_scalar_prefetch=1,
            grid=(pairs,),
            in_specs=[pair_block(rows)]
            + [pair_block(rows), value_block(rows, pairs)] * 2
            + [
                pair_block(rows),
                pair_block(rows),
                pl.BlockSpec((8, rows), lambda i, *_: (i, 0)),
            ],
            out_specs=(pair_block(rows),) * 5,
            scratch_shapes=[
                pltpu.VMEM((clip, PAIR), jnp.bfloat16),
                pltpu.VMEM((clip, PAIR), jnp.bfloat16),
                pltpu.VMEM((PAIR, rows // 2), jnp.float32),
                pltpu.VMEM((clip, PAIR), jnp.float32),
                pltpu.VMEM((clip, PAIR), jnp.float32),
            ],
        ),
        compiler_params=pltpu.CompilerParams(vmem_limit_bytes=32 * 2**20),
        cost_estimate=pl.CostEstimate(
            flops=5 * 2 * rows * clip * width, bytes_accessed=16 * clip * width, transcendentals=0
        ),
        name="self_attend_back",
    )(place, queries, own, own, other, other, mixed, grads, lse)


def both_heads(rows, value):
    return jnp.concatenate([rows * half_mask(side, value) for side in range(2)], axis=0)


def cross_probs_of(lookup_two, probes, present):
    text = present.shape[0]
    scores = dot(lookup_two, probes, NT)
    out = []
    for side in range(2):
        part = jnp.where(
            present > 0, scores[side * text : (side + 1) * text], masked_score
        )
        weights = jnp.exp(part - jnp.max(part, axis=0, keepdims=True))
        out.append(weights / jnp.sum(weights, axis=0, keepdims=True))
    return out


def cross_forward_kernel(probe_ref, lookup_ref, content_ref, present_ref, mixed_ref):
    probs = cross_probs_of(
        both_heads(lookup_ref[...], HEAD_DIM ** (-0.5)), probe_ref[...], present_ref[...]
    )
    probs = jnp.concatenate(probs, axis=0).astype(jnp.bfloat16)
    mixed_ref[...] = dot(probs, both_heads(content_ref[...], 1.0), TN).astype(jnp.bfloat16)


def cross_backward_kernel(
    probe_ref, lookup_ref, content_ref, present_ref, grad_ref, dp_ref, dl_ref, dc_ref
):
    text = present_ref.shape[0]
    scale = HEAD_DIM ** (-0.5)
    probes = probe_ref[...]
    grads = grad_ref[...]
    lookup_two = both_heads(lookup_ref[...], scale)
    probs = cross_probs_of(lookup_two, probes, present_ref[...])
    grad_probs = dot(both_heads(content_ref[...], 1.0), grads, NT)
    grad_scores = []
    for side in range(2):
        part = grad_probs[side * text : (side + 1) * text]
        inner = jnp.sum(probs[side] * part, axis=0, keepdims=True)
        grad_scores.append(probs[side] * (part - inner))
    grad_scores = jnp.concatenate(grad_scores, axis=0).astype(jnp.bfloat16)
    probs = jnp.concatenate(probs, axis=0).astype(jnp.bfloat16)
    low = lax.broadcasted_iota(jnp.int32, (1, PAIR), 1) < HEAD_DIM
    dp_ref[...] = dot(grad_scores, lookup_two, TN).astype(jnp.bfloat16)
    dl = dot(grad_scores, probes, NN) * scale
    dl_ref[...] = jnp.where(low, dl[:text], dl[text:]).astype(jnp.bfloat16)
    dc = dot(probs, grads, NN)
    dc_ref[...] = jnp.where(low, dc[:text], dc[text:]).astype(jnp.bfloat16)


def cross_attend(probes, lookups, contents, present):
    rows, width = probes.shape
    text = lookups.shape[0]
    return pl.pallas_call(
        cross_forward_kernel,
        out_shape=jax.ShapeDtypeStruct((rows, width), jnp.bfloat16),
        grid=(width // PAIR,),
        in_specs=[
            pair_block(rows),
            pair_block(text),
            pair_block(text),
            pl.BlockSpec((text, 1), lambda i: (0, 0)),
        ],
        out_specs=pair_block(rows),
        compiler_params=pltpu.CompilerParams(vmem_limit_bytes=32 * 2**20),
        cost_estimate=pl.CostEstimate(
            flops=8 * rows * text * width, bytes_accessed=4 * rows * width, transcendentals=0
        ),
        name="cross_attend",
    )(probes, lookups, contents, present)


def cross_attend_back(probes, lookups, contents, present, grads):
    rows, width = probes.shape
    text = lookups.shape[0]
    return pl.pallas_call(
        cross_backward_kernel,
        out_shape=(
            jax.ShapeDtypeStruct((rows, width), jnp.bfloat16),
            jax.ShapeDtypeStruct((text, width), jnp.bfloat16),
            jax.ShapeDtypeStruct((text, width), jnp.bfloat16),
        ),
        grid=(width // PAIR,),
        in_specs=[
            pair_block(rows),
            pair_block(text),
            pair_block(text),
            pl.BlockSpec((text, 1), lambda i: (0, 0)),
            pair_block(rows),
        ],
        out_specs=(pair_block(rows), pair_block(text), pair_block(text)),
        compiler_params=pltpu.CompilerParams(vmem_limit_bytes=32 * 2**20),
        cost_estimate=pl.CostEstimate(
            flops=20 * rows * text * width, bytes_accessed=6 * rows * width, transcendentals=0
        ),
        name="cross_attend_back",
    )(probes, lookups, contents, present, grads)


def unpack_kernel(in_ref, out_ref):
    pieces = in_ref[...]
    out_ref[...] = pieces.reshape(-1, pieces.shape[-1]).T.astype(jnp.float32)


def unpack(full, rows, place, out_shape, out_at, together):
    owners, _, features = full.shape
    tall = out_shape[0] // features
    wide = out_shape[1] // (together * rows)
    return pl.pallas_call(
        unpack_kernel,
        out_shape=jax.ShapeDtypeStruct(out_shape, jnp.float32),
        grid=(tall, wide),
        in_specs=[
            pl.BlockSpec((together, rows, features), lambda i, j: (j + out_at, place + i, 0))
        ],
        out_specs=pl.BlockSpec((features, together * rows), lambda i, j: (i, j)),
        compiler_params=pltpu.CompilerParams(vmem_limit_bytes=32 * 2**20),
        cost_estimate=pl.CostEstimate(
            flops=0, bytes_accessed=6 * out_shape[0] * out_shape[1], transcendentals=0
        ),
        name="unpack",
    )(full)


def held(values, *others):
    return list(lax.optimization_barrier((*values, *others))[: len(values)])


def after(value, *others):
    return lax.optimization_barrier((value, *others))[0]


def norm_parts(values):
    mean = jnp.mean(values, axis=-1, keepdims=True)
    center = values - mean
    return mean, lax.rsqrt(jnp.mean(center * center, axis=-1, keepdims=True) + epsilon)


def norm_back(grads, values, parts, gain):
    mean, inverse = parts
    unit = (values - mean) * inverse
    gain_grad = jnp.sum(grads * unit, axis=0)
    bias_grad = jnp.sum(grads, axis=0)
    scaled = grads * gain
    back = inverse * (
        scaled
        - jnp.mean(scaled, axis=-1, keepdims=True)
        - unit * jnp.mean(scaled * unit, axis=-1, keepdims=True)
    )
    return back, gain_grad, bias_grad


def clip_body(
    frames,
    text_states,
    text_mask,
    clip_lengths,
    slot_used,
    teacher,
    self_norm_gain,
    self_norm_bias,
    self_query_weight,
    self_key_weight,
    self_value_weight,
    self_output_weight,
    cross_norm_gain,
    cross_norm_bias,
    cross_query_weight,
    cross_key_weight,
    cross_value_weight,
    cross_output_weight,
    feed_norm_gain,
    feed_norm_bias,
    feed_up_weight,
    feed_down_weight,
):
    block, width = frames.shape[1:]
    text_len = text_states.shape[1]
    shards, replicas, outers = 4, 8, 4
    core = lax.axis_index("core")
    shard = lax.axis_index("shard")
    outer = 2 * lax.axis_index("y") + lax.axis_index("x")
    replica = 2 * outer + core
    clip = block * shards
    hidden_units = feed_up_weight.shape[1]

    holder = {0: 0, 1: 1, 2: 1, 3: 0}
    there = ([], [])
    for c in range(2):
        for s in range(4):
            for turn in range(2):
                slot = turn if s < 2 else 1 - turn
                there[turn].append((c * 4 + s, holder[s] * 4 + 2 * c + slot))
    back = tuple([(b, a) for a, b in pairs] for pairs in there)
    spot = ("core", "shard")
    swap = [(0, 1), (1, 0)]
    even = shard % 2 == 0
    lower = shard < 2
    first_core = core == 0

    def hop(values, distance):
        pairs = [(i, (i + distance) % shards) for i in range(shards)]
        return lax.ppermute(values, "shard", pairs)

    def hops(values):
        return [hop(values, distance) for distance in (1, 2, 3)]

    def line_up(mine, came):
        out = jnp.zeros((shards,) + mine.shape, mine.dtype)
        out = lax.dynamic_update_index_in_dim(out, mine, shard, 0)
        for distance, values in zip((1, 2, 3), came):
            owner = lax.rem(shard + shards - distance, shards)
            out = lax.dynamic_update_index_in_dim(out, values, owner, 0)
        return out

    def to_chip(pair):
        one = lax.ppermute(jnp.where(lower, pair[0], pair[1]), spot, there[0])
        two = lax.ppermute(jnp.where(lower, pair[1], pair[0]), spot, there[1])
        return one, two

    def by_time(one, two):
        return jnp.concatenate([jnp.where(even, one, two), jnp.where(even, two, one)], axis=0)

    def outgoing(values):
        early, late = values[:block], values[block:]
        return jnp.where(even, early, late), jnp.where(even, late, early)

    def from_chip(values):
        one, two = outgoing(values)
        return lax.ppermute(one, spot, back[0]), lax.ppermute(two, spot, back[1])

    def by_slot(one, two):
        return jnp.stack([jnp.where(lower, one, two), jnp.where(lower, two, one)])

    def share_of(weight):
        share = weight.shape[0] // replicas
        return lax.dynamic_slice_in_dim(weight, replica * share, share, 0)

    def from_replicas(line):
        full = lax.all_gather(line, ("y", "x", "core"), axis=1, tiled=True)
        return full.reshape(-1, line.shape[-1])

    qkv_share = jnp.concatenate(
        [share_of(self_query_weight), share_of(self_key_weight), share_of(self_value_weight)],
        axis=1,
    )
    vectors = jnp.concatenate(
        [
            self_norm_gain,
            self_norm_bias,
            cross_norm_gain,
            cross_norm_bias,
            feed_norm_gain,
            feed_norm_bias,
        ]
    )
    vectors = jnp.pad(vectors[None, :], ((0, 15), (0, 3 * width - 6 * block)))
    share = qkv_share.shape[0]
    qkv_mine = jnp.concatenate([qkv_share, vectors], axis=0)
    qkv_came = hops(qkv_mine)
    qkv_matrix = from_replicas(line_up(qkv_share, [values[:share] for values in qkv_came]))
    norms = line_up(vectors[0], [values[share] for values in qkv_came])
    norms = norms[:, : 6 * block].reshape(shards, 6, block).transpose(1, 0, 2)
    norms = norms.reshape(6, width).astype(jnp.float32)
    rest_share = jnp.concatenate(
        [share_of(self_output_weight), share_of(cross_query_weight), share_of(cross_output_weight)],
        axis=1,
    )
    rest_came = hops(after(rest_share, *qkv_came))
    rest = from_replicas(line_up(rest_share, rest_came))
    came = to_chip(after(frames, *rest_came))
    x_low = by_time(*came)
    expand_share = share_of(feed_up_weight)
    expand_came = hops(after(expand_share, *came))

    facts = jnp.concatenate(
        [(clip_lengths // 64)[:, None], (clip_lengths % 64)[:, None], slot_used[:, None], text_mask],
        axis=1,
    ).astype(jnp.bfloat16)
    facts = jnp.pad(facts[:, None, :], ((0, 0), (0, 15), (0, width - facts.shape[1])))
    text_sent = lax.ppermute(jnp.concatenate([text_states, facts], axis=1), "core", swap)
    text_other = text_sent[:, :text_len]
    both = jnp.stack([facts[:, 0], text_sent[:, text_len]])[:, :, : 3 + text_len].astype(jnp.int32)
    lengths = 64 * both[:, :, 0] + both[:, :, 1]
    fact = lax.dynamic_index_in_dim(
        jnp.where(shard // 2 == core, both[0], both[1]), shard % 2, 0, keepdims=False
    )
    length, used = 64 * fact[0] + fact[1], fact[2]
    present = fact[3:].reshape(text_len, 1)
    count = jnp.sum(
        jnp.where(both[:, :, 2] > 0, jnp.minimum(lengths, clip), 0).astype(jnp.float32)
    )
    count = jnp.full((8, 128), count)
    for axis in ("x", "y"):
        count += lax.ppermute(count, axis, swap)
    count = count[0, 0]
    text_all = jnp.concatenate(
        [
            jnp.where(first_core, text_states, text_other),
            jnp.where(first_core, text_other, text_states),
        ],
        axis=0,
    ).reshape(4 * text_len, width)
    text_all = lax.dynamic_slice_in_dim(text_all, shard * block, block, 1)
    text_matrix = jnp.where(first_core, cross_key_weight, cross_value_weight)
    text_part = project(text_all, text_matrix).astype(jnp.bfloat16).reshape(4, text_len, width)
    text_came = [
        hop(
            lax.dynamic_index_in_dim(
                text_part, lax.rem(shard + distance, shards), 0, keepdims=False
            ),
            distance,
        )
        for distance in (1, 2, 3)
    ]

    places = jnp.stack([core, 3 - core, length, 1 - core, 2 + core]).astype(jnp.int32)
    positions = jnp.concatenate(
        [core * block + jnp.arange(block), (3 - core) * block + jnp.arange(block)]
    )
    valid_rows = ((positions < length) & (used > 0)).astype(jnp.float32)[:, None]
    inputs = x_low.astype(jnp.float32)
    parts_one = norm_parts(inputs)
    hidden_one = ((inputs - parts_one[0]) * parts_one[1] * norms[0] + norms[1]).astype(
        jnp.bfloat16
    )
    kv = project(after(hidden_one, count), qkv_matrix[:, width:]).astype(jnp.bfloat16)
    kv_other = lax.ppermute(kv, "core", swap)
    queries = project(after(hidden_one, kv), qkv_matrix[:, :width]).astype(jnp.bfloat16)
    expand_came = held(expand_came, kv_other, queries)
    expand_matrix = from_replicas(line_up(expand_share, expand_came))
    output_matrix = rest[:, :width]
    probe_matrix = rest[:, width : 2 * width]
    merge_matrix = rest[:, 2 * width :]
    mixed_self, lse = self_attend(after(places, *expand_came), queries, kv, kv_other)
    reduce_share = share_of(feed_down_weight)
    text_came = held(text_came, mixed_self)
    reduce_came = hops(after(reduce_share, *text_came))
    text_half = lax.dynamic_index_in_dim(text_part, shard, 0, keepdims=False).astype(jnp.float32)
    for values in text_came:
        text_half += values.astype(jnp.float32)
    text_half = text_half.astype(jnp.bfloat16)
    text_swap = lax.ppermute(text_half, "core", swap)
    lookups = jnp.where(first_core, text_half, text_swap)
    contents = jnp.where(first_core, text_swap, text_half)
    after_self = inputs + project(mixed_self, output_matrix)
    parts_two = norm_parts(after_self)
    hidden_two = ((after_self - parts_two[0]) * parts_two[1] * norms[2] + norms[3]).astype(
        jnp.bfloat16
    )
    probes = project(hidden_two, probe_matrix).astype(jnp.bfloat16)
    reduce_came = held(reduce_came, probes)
    reduce_matrix = from_replicas(line_up(reduce_share, reduce_came))
    teacher_came = to_chip(after(teacher, *reduce_came, probes))
    cross_mixed = cross_attend(probes, lookups, contents, present)
    after_cross = after_self + project(cross_mixed, merge_matrix)
    parts_three = norm_parts(after_cross)
    hidden_three = (
        (after_cross - parts_three[0]) * parts_three[1] * norms[4] + norms[5]
    ).astype(jnp.bfloat16)
    upward = project(hidden_three, expand_matrix)
    activated, gelu_pull = jax.vjp(exact_gelu, upward)
    activated_low = activated.astype(jnp.bfloat16)
    teacher_low = by_time(*held(teacher_came, activated_low))
    result = after_cross + project(activated_low, reduce_matrix)
    errors = (result - teacher_low.astype(jnp.float32)) * valid_rows
    squares = jnp.sum(errors * errors)
    grad_result = errors * (4 * outers * clip / count)
    grad_feed_low = grad_result.astype(jnp.bfloat16)

    def theirs_of(right, left):
        columns = right.shape[1] // 2
        part = lax.dynamic_slice_in_dim(right, (1 - core) * columns, columns, 1)
        return outer_sum(part, left).astype(jnp.bfloat16)

    def ours_of(right, left, theirs):
        columns = right.shape[1] // 2
        sent = lax.ppermute(theirs, "core", swap)
        part = lax.dynamic_slice_in_dim(right, core * columns, columns, 1)
        return (outer_sum(part, left) + sent.astype(jnp.float32)).astype(jnp.bfloat16)

    def over_outer(values):
        return lax.psum_scatter(values, ("y", "x"), scatter_dimension=0, tiled=True)

    def shard_hops(values):
        columns = values.shape[1] // shards
        return [
            hop(
                lax.dynamic_slice_in_dim(
                    values, lax.rem(shard + distance, shards) * columns, columns, 1
                ),
                distance,
            )
            for distance in (1, 2, 3)
        ]

    def over_shard(values, came):
        columns = values.shape[1] // shards
        total = lax.dynamic_slice_in_dim(values, shard * columns, columns, 1).astype(jnp.float32)
        for part in came:
            total += part.astype(jnp.float32)
        return total.astype(jnp.bfloat16)

    down_theirs = theirs_of(grad_feed_low, activated_low)
    to_send = outgoing(result.astype(jnp.bfloat16))
    output_one = lax.ppermute(to_send[0], spot, back[0])
    grad_activated = back_project(after(grad_feed_low, down_theirs), reduce_matrix)
    grad_upward = gelu_pull(grad_activated)[0].astype(jnp.bfloat16)
    output_one = after(output_one, grad_upward)
    down_ours = ours_of(
        after(grad_feed_low, grad_upward, output_one), activated_low, down_theirs
    )
    down_sum = over_outer(down_ours)
    up_theirs = theirs_of(after(grad_upward, down_ours), hidden_three)
    grad_hidden_three = back_project(after(grad_upward, up_theirs), expand_matrix)
    output_two = lax.ppermute(after(to_send[1], output_one), spot, back[1])
    output_two = after(output_two, grad_hidden_three)
    output = by_slot(output_one, output_two)
    up_ours = ours_of(after(grad_upward, grad_hidden_three, output_two), hidden_three, up_theirs)
    grad_norm, gain_feed, bias_feed = norm_back(
        after(grad_hidden_three, up_ours), after_cross, parts_three, norms[4]
    )
    grad_after_cross = grad_result + grad_norm
    grad_cross_low = grad_after_cross.astype(jnp.bfloat16)
    merge_theirs = theirs_of(grad_cross_low, cross_mixed)
    grad_cross_mixed = back_project(after(grad_cross_low, merge_theirs), merge_matrix).astype(
        jnp.bfloat16
    )
    probe_grads, lookup_grads, content_grads = cross_attend_back(
        probes, lookups, contents, present, grad_cross_mixed
    )
    up_sum = over_outer(up_ours)
    text_mine = jnp.where(first_core, lookup_grads, content_grads)
    text_sent = lax.ppermute(
        jnp.where(first_core, content_grads, lookup_grads), "core", swap
    )
    text_mine = (text_mine.astype(jnp.float32) + text_sent.astype(jnp.float32)).astype(
        jnp.bfloat16
    )
    merge_ours = ours_of(after(grad_cross_low, probe_grads), cross_mixed, merge_theirs)
    probe_theirs = theirs_of(after(probe_grads, merge_ours), hidden_two)
    grad_hidden_two = back_project(after(probe_grads, probe_theirs), probe_matrix)
    text_four = line_up(text_mine, hops(text_mine)).reshape(4 * text_len, width)
    grad_norm, gain_cross, bias_cross = norm_back(
        grad_hidden_two, after_self, parts_two, norms[2]
    )
    grad_after_self = grad_after_cross + grad_norm
    grad_self_low = grad_after_self.astype(jnp.bfloat16)
    output_theirs = theirs_of(grad_self_low, mixed_self)
    grad_mixed = back_project(after(grad_self_low, output_theirs), output_matrix).astype(
        jnp.bfloat16
    )
    probe_ours = ours_of(after(probe_grads, grad_mixed), hidden_two, probe_theirs)
    text_weights = outer_sum(text_four, text_all).astype(jnp.bfloat16)
    text_back = back_project(text_four, text_matrix).astype(jnp.bfloat16)
    output_ours = ours_of(after(grad_self_low, probe_ours), mixed_self, output_theirs)
    text_rows = width // outers
    middle = jnp.concatenate(
        [
            values.reshape(outers, -1, width)
            for values in (
                output_ours,
                probe_ours,
                merge_ours,
                text_weights.reshape(outers, shards, text_rows // shards, block)
                .transpose(0, 2, 1, 3)
                .reshape(outers, text_rows // shards, width),
            )
        ],
        axis=1,
    )
    middle_rows = middle.shape[1]
    middle = middle.reshape(outers * middle_rows, width)
    middle_sum = over_outer(middle)
    text_split = text_rows // shards
    text_piece = (
        middle_sum[middle_rows - text_split :]
        .reshape(text_split, shards, block)
        .transpose(1, 0, 2)
        .reshape(text_rows, block)
    )
    text_back = text_back.reshape(2, 2, text_len, block)
    text_kept = lax.dynamic_index_in_dim(text_back, core, 0, keepdims=False)
    text_gone = lax.dynamic_index_in_dim(text_back, 1 - core, 0, keepdims=False)
    text_own = text_kept.astype(jnp.float32) + lax.ppermute(text_gone, "core", swap).astype(
        jnp.float32
    )
    text_own = text_own.astype(jnp.bfloat16)
    down_came = shard_hops(down_sum)
    grad_queries, own_keys, own_values, other_keys, other_values = self_attend_back(
        places, queries, kv, kv_other, mixed_self, after(grad_mixed, middle, text_own), lse
    )
    down_came = held(down_came, grad_queries)
    other_keys, other_values = held([other_keys, other_values], *down_came)
    own_keys += lax.ppermute(other_keys, "core", swap)
    own_values += lax.ppermute(other_values, "core", swap)
    down_piece = over_shard(down_sum, down_came)
    up_came = shard_hops(after(up_sum, down_piece))

    qkv_grads = jnp.concatenate([grad_queries, own_keys, own_values], axis=1)
    qkv_theirs = theirs_of(qkv_grads, hidden_one)
    grad_hidden_one = back_project(after(qkv_grads, qkv_theirs), qkv_matrix)
    qkv_ours = ours_of(after(qkv_grads, grad_hidden_one), hidden_one, qkv_theirs)
    up_came = held(up_came, grad_hidden_one)
    up_piece = over_shard(up_sum, up_came)
    qkv_sum = over_outer(qkv_ours)
    grad_norm, gain_self, bias_self = norm_back(
        after(grad_hidden_one, qkv_ours, *up_came), inputs, parts_one, norms[0]
    )
    middle_kept = after(middle_sum[: middle_rows - text_split], qkv_ours, *up_came)
    middle_came = shard_hops(middle_kept)

    small = jnp.stack(
        [
            gain_self,
            bias_self,
            gain_cross,
            bias_cross,
            gain_feed,
            bias_feed,
            jnp.full((width,), squares),
            jnp.zeros((width,), jnp.float32),
        ]
    )
    for axis, pairs in (
        ("core", swap),
        ("x", swap),
        ("y", swap),
        ("shard", [(0, 1), (1, 0), (2, 3), (3, 2)]),
        ("shard", [(0, 2), (2, 0), (1, 3), (3, 1)]),
    ):
        small += lax.ppermute(small, axis, pairs)
    late_came = shard_hops(after(qkv_sum, *middle_came, small))
    frames_came = from_chip(
        after((grad_after_self + grad_norm).astype(jnp.bfloat16), *late_came)
    )
    frames_grad = by_slot(*frames_came).astype(jnp.float32)
    text_came = hops(after(text_own, *late_came))
    text_grad = line_up(text_own, text_came).astype(jnp.float32)
    text_grad = text_grad.transpose(1, 2, 0, 3).reshape(text_states.shape)
    loss = small[6, 0] / (width * count)
    small_own = lax.dynamic_slice_in_dim(small, shard * block, block, 1)

    middle_piece = over_shard(middle_kept, middle_came)
    early = jnp.concatenate(
        [up_piece]
        + [down_piece[:, i * block : (i + 1) * block] for i in range(4)]
        + [text_piece, middle_piece],
        axis=0,
    )
    early = lax.all_gather(early, REPLICAS, axis=0)
    piece = width // replicas
    square = (block, width)
    up_grad = unpack(early, hidden_units // replicas, 0, (block, hidden_units), 0, 1)
    at = hidden_units // replicas // piece
    down_grad = unpack(early, piece, at, (4 * block, width), 0, 2)
    at += 4
    key_grad = unpack(early, text_rows, at * piece // text_rows, square, 0, 1)
    value_grad = unpack(early, text_rows, at * piece // text_rows, square, 4, 1)
    at += text_rows // piece
    output_grad = unpack(early, piece, at, square, 0, 2)
    probe_grad = unpack(early, piece, at + 1, square, 0, 2)
    merge_grad = unpack(early, piece, at + 2, square, 0, 2)
    late = over_shard(qkv_sum, late_came)
    late = lax.all_gather(
        after(late, early, text_grad, *frames_came), REPLICAS, axis=0, tiled=True
    )
    late = late.reshape(-1, block, block)
    qkv_grad = [unpack(late, block, 0, square, 2 * i, 2) for i in range(3)]
    return (
        output,
        loss,
        frames_grad,
        text_grad,
        small_own[0],
        small_own[1],
        qkv_grad[0],
        qkv_grad[1],
        qkv_grad[2],
        output_grad,
        small_own[2],
        small_own[3],
        probe_grad,
        key_grad,
        value_grad,
        merge_grad,
        small_own[4],
        small_own[5],
        up_grad,
        down_grad,
    )


def solution(mesh):
    by_chip = mesh.shape["shard"] == 4 and mesh.shape["replica"] == 8
    replica = ("y", "x", "core") if by_chip else "replica"
    row = P(replica)
    clip = P(replica, "shard", None)
    text = P(replica, None, None)
    vector = P("shard")
    matrix = P("shard", None)
    weights = (
        [vector, vector] + [matrix] * 4 + [vector, vector] + [matrix] * 4 + [vector, vector]
        + [matrix] * 2
    )
    if by_chip:
        mesh = Mesh(mesh.devices.reshape(2, 2, 2, 4), ("y", "x", "core", "shard"))
    return jax.shard_map(
        clip_body if by_chip else general_body,
        mesh=mesh,
        in_specs=(clip, text, P(replica, None), row, row, clip, *weights),
        out_specs=(clip, P(), clip, text, *weights),
        check_vma=False,
    )
```

```python
import jax
import jax.numpy as jnp
from jax import lax
from jax.experimental import pallas as pl
from jax.experimental.pallas import tpu as pltpu
from jax.sharding import Mesh
from jax.sharding import PartitionSpec as P

HEADS = 24
HEAD_DIM = 64


epsilon = 1e-05
masked_score = -1e30


def layer_norm(values, gain, shift):
    center = values - jnp.mean(values, axis=-1, keepdims=True)
    variance = jnp.mean(center * center, axis=-1, keepdims=True)
    return center * lax.rsqrt(variance + epsilon) * gain + shift


def exact_gelu(values):
    return jax.nn.gelu(values, approximate=False)


def project(left, right):
    return jnp.dot(left, right, preferred_element_type=jnp.float32)


def outer_sum(left, right):
    return jnp.einsum("rd,re->de", left, right, preferred_element_type=jnp.float32)


def back_project(grads, matrix):
    return jnp.einsum("re,de->rd", grads, matrix, preferred_element_type=jnp.float32)


def split_heads(values):
    return values.reshape(values.shape[:-1] + (HEADS, HEAD_DIM))


def self_forward(operands):
    queries, keys_all, values_all, allowed = operands
    scale = HEAD_DIM ** (-0.5)
    scores = (
        jnp.einsum("qhd,khd->hqk", queries, keys_all, preferred_element_type=jnp.float32) * scale
    )
    scores = jnp.where(allowed[None], scores, masked_score)
    peak = jnp.max(scores, axis=-1, keepdims=True)
    weights = jnp.exp(scores - peak)
    totals = jnp.sum(weights, axis=-1, keepdims=True)
    probs = (weights / totals).astype(jnp.bfloat16)
    mixed = jnp.einsum("hqk,khd->qhd", probs, values_all, preferred_element_type=jnp.float32)
    return (mixed.astype(jnp.bfloat16), (peak + jnp.log(totals))[..., 0])


def self_backward(operands):
    queries, keys_all, values_all, allowed, log_totals, grad_mixed = operands
    scale = HEAD_DIM ** (-0.5)
    scores = (
        jnp.einsum("qhd,khd->hqk", queries, keys_all, preferred_element_type=jnp.float32) * scale
    )
    scores = jnp.where(allowed[None], scores, masked_score)
    probs = jnp.exp(scores - log_totals[..., None])
    grad_probs = jnp.einsum(
        "qhd,khd->hqk", grad_mixed, values_all, preferred_element_type=jnp.float32
    )
    grad_values = jnp.einsum(
        "hqk,qhd->khd", probs.astype(jnp.bfloat16), grad_mixed, preferred_element_type=jnp.float32
    )
    inner = jnp.sum(probs * grad_probs, axis=-1, keepdims=True)
    grad_scores = (probs * (grad_probs - inner)).astype(jnp.bfloat16)
    grad_queries = (
        jnp.einsum("hqk,khd->qhd", grad_scores, keys_all, preferred_element_type=jnp.float32)
        * scale
    ).astype(jnp.bfloat16)
    grad_keys = (
        jnp.einsum("hqk,qhd->khd", grad_scores, queries, preferred_element_type=jnp.float32) * scale
    )
    return (grad_queries, grad_keys, grad_values)


def general_body(
    frames,
    text_states,
    text_mask,
    clip_lengths,
    slot_used,
    teacher,
    self_norm_gain,
    self_norm_bias,
    self_query_weight,
    self_key_weight,
    self_value_weight,
    self_output_weight,
    cross_norm_gain,
    cross_norm_bias,
    cross_query_weight,
    cross_key_weight,
    cross_value_weight,
    cross_output_weight,
    feed_norm_gain,
    feed_norm_bias,
    feed_up_weight,
    feed_down_weight,
):
    gathered = (
        lax.all_gather(self_norm_gain, "shard", axis=0, tiled=True),
        lax.all_gather(self_norm_bias, "shard", axis=0, tiled=True),
        lax.all_gather(self_query_weight, "shard", axis=0, tiled=True),
        lax.all_gather(self_key_weight, "shard", axis=0, tiled=True),
        lax.all_gather(self_value_weight, "shard", axis=0, tiled=True),
        lax.all_gather(self_output_weight, "shard", axis=0, tiled=True),
        lax.all_gather(cross_norm_gain, "shard", axis=0, tiled=True),
        lax.all_gather(cross_norm_bias, "shard", axis=0, tiled=True),
        lax.all_gather(cross_query_weight, "shard", axis=0, tiled=True),
        lax.all_gather(cross_key_weight, "shard", axis=0, tiled=True),
        lax.all_gather(cross_value_weight, "shard", axis=0, tiled=True),
        lax.all_gather(cross_output_weight, "shard", axis=0, tiled=True),
        lax.all_gather(feed_norm_gain, "shard", axis=0, tiled=True),
        lax.all_gather(feed_norm_bias, "shard", axis=0, tiled=True),
        lax.all_gather(feed_up_weight, "shard", axis=0, tiled=True),
        lax.all_gather(feed_down_weight, "shard", axis=0, tiled=True),
    )
    (
        gain_attend,
        bias_attend,
        query_matrix,
        key_matrix,
        value_matrix,
        output_matrix,
        gain_cross,
        bias_cross,
        probe_matrix,
        lookup_matrix,
        content_matrix,
        merge_matrix,
        gain_feed,
        bias_feed,
        expand_matrix,
        reduce_matrix,
    ) = gathered
    slots = frames.shape[0]
    frame_count = frames.shape[1]
    width = frames.shape[2]
    text_len = text_states.shape[1]
    shards = lax.axis_size("shard")
    replicas = lax.axis_size("replica")
    clip_total = frame_count * shards
    row_count = slots * frame_count
    scale = HEAD_DIM ** (-0.5)
    shard_rank = lax.axis_index("shard")
    positions = shard_rank * frame_count + jnp.arange(frame_count, dtype=jnp.int32)
    key_positions = jnp.arange(clip_total, dtype=jnp.int32)
    allowed = (key_positions[None, None, :] <= positions[None, :, None]) & (
        key_positions[None, None, :] < clip_lengths[:, None, None]
    )
    valid_rows = ((positions[None, :] < clip_lengths[:, None]) & (slot_used[:, None] > 0)).astype(
        jnp.float32
    )
    text_allowed = text_mask > 0
    inputs = frames.astype(jnp.float32)
    normed_one, pull_one = jax.vjp(
        layer_norm, inputs, gain_attend.astype(jnp.float32), bias_attend.astype(jnp.float32)
    )
    hidden_one = normed_one.astype(jnp.bfloat16).reshape(row_count, width)
    queries = (
        project(hidden_one, query_matrix).astype(jnp.bfloat16).reshape(slots, frame_count, width)
    )
    keys_local = (
        project(hidden_one, key_matrix).astype(jnp.bfloat16).reshape(slots, frame_count, width)
    )
    values_local = (
        project(hidden_one, value_matrix).astype(jnp.bfloat16).reshape(slots, frame_count, width)
    )
    keys_all, values_all = (
        lax.all_gather(keys_local, "shard", axis=1, tiled=True),
        lax.all_gather(values_local, "shard", axis=1, tiled=True),
    )
    head_queries = split_heads(queries)
    head_keys = split_heads(keys_all)
    head_values = split_heads(values_all)
    mixed_self, log_totals = lax.map(self_forward, (head_queries, head_keys, head_values, allowed))
    mixed_rows = mixed_self.reshape(row_count, width)
    after_self = inputs + project(mixed_rows, output_matrix).reshape(slots, frame_count, width)
    normed_two, pull_two = jax.vjp(
        layer_norm, after_self, gain_cross.astype(jnp.float32), bias_cross.astype(jnp.float32)
    )
    hidden_two = normed_two.astype(jnp.bfloat16).reshape(row_count, width)
    probes = split_heads(
        project(hidden_two, probe_matrix).astype(jnp.bfloat16).reshape(slots, frame_count, width)
    )
    text_rows = text_states.reshape(slots * text_len, width)
    lookups = split_heads(
        project(text_rows, lookup_matrix).astype(jnp.bfloat16).reshape(slots, text_len, width)
    )
    contents = split_heads(
        project(text_rows, content_matrix).astype(jnp.bfloat16).reshape(slots, text_len, width)
    )
    cross_scores = (
        jnp.einsum("sqhd,skhd->shqk", probes, lookups, preferred_element_type=jnp.float32) * scale
    )
    cross_scores = jnp.where(text_allowed[:, None, None, :], cross_scores, masked_score)
    cross_peak = jnp.max(cross_scores, axis=-1, keepdims=True)
    cross_weights = jnp.exp(cross_scores - cross_peak)
    cross_probs = cross_weights / jnp.sum(cross_weights, axis=-1, keepdims=True)
    cross_probs_low = cross_probs.astype(jnp.bfloat16)
    cross_mixed = jnp.einsum(
        "shqk,skhd->sqhd", cross_probs_low, contents, preferred_element_type=jnp.float32
    )
    cross_mixed = cross_mixed.astype(jnp.bfloat16).reshape(row_count, width)
    after_cross = after_self + project(cross_mixed, merge_matrix).reshape(slots, frame_count, width)
    normed_three, pull_three = jax.vjp(
        layer_norm, after_cross, gain_feed.astype(jnp.float32), bias_feed.astype(jnp.float32)
    )
    hidden_three = normed_three.astype(jnp.bfloat16).reshape(row_count, width)
    upward = project(hidden_three, expand_matrix)
    activated, gelu_pull = jax.vjp(exact_gelu, upward)
    activated_low = activated.astype(jnp.bfloat16)
    result = after_cross + project(activated_low, reduce_matrix).reshape(slots, frame_count, width)
    output = result.astype(jnp.bfloat16)
    errors = (result - teacher.astype(jnp.float32)) * valid_rows[..., None]
    squares_total, count_total = lax.psum(
        (jnp.sum(errors * errors), jnp.sum(valid_rows)), ("replica", "shard")
    )
    loss = squares_total / (width * count_total)
    grad_result = errors * (slots * replicas * clip_total / count_total)
    grad_feed_low = grad_result.reshape(row_count, width).astype(jnp.bfloat16)
    grad_activated = back_project(grad_feed_low, reduce_matrix)
    grad_upward = gelu_pull(grad_activated)[0].astype(jnp.bfloat16)
    grad_hidden_three = back_project(grad_upward, expand_matrix).reshape(slots, frame_count, width)
    grad_cross_norm, gain_feed_part, bias_feed_part = pull_three(grad_hidden_three)
    grad_after_cross = grad_result + grad_cross_norm
    feed_owned = (
        lax.psum_scatter(
            outer_sum(hidden_three, grad_upward).astype(jnp.bfloat16),
            "shard",
            scatter_dimension=0,
            tiled=True,
        ).astype(jnp.float32),
        lax.psum_scatter(
            outer_sum(activated_low, grad_feed_low).astype(jnp.bfloat16),
            "shard",
            scatter_dimension=0,
            tiled=True,
        ).astype(jnp.float32),
        lax.psum_scatter(
            gain_feed_part.astype(jnp.bfloat16), "shard", scatter_dimension=0, tiled=True
        ).astype(jnp.float32),
        lax.psum_scatter(
            bias_feed_part.astype(jnp.bfloat16), "shard", scatter_dimension=0, tiled=True
        ).astype(jnp.float32),
    )
    grad_cross_low = grad_after_cross.reshape(row_count, width).astype(jnp.bfloat16)
    grad_cross_mixed = split_heads(
        back_project(grad_cross_low, merge_matrix)
        .astype(jnp.bfloat16)
        .reshape(slots, frame_count, width)
    )
    grad_cross_probs = jnp.einsum(
        "sqhd,skhd->shqk", grad_cross_mixed, contents, preferred_element_type=jnp.float32
    )
    content_grads = jnp.einsum(
        "shqk,sqhd->skhd", cross_probs_low, grad_cross_mixed, preferred_element_type=jnp.float32
    )
    cross_inner = jnp.sum(cross_probs * grad_cross_probs, axis=-1, keepdims=True)
    grad_cross_scores = (cross_probs * (grad_cross_probs - cross_inner)).astype(jnp.bfloat16)
    probe_grads = (
        jnp.einsum(
            "shqk,skhd->sqhd", grad_cross_scores, lookups, preferred_element_type=jnp.float32
        )
        * scale
    )
    probe_grads = probe_grads.astype(jnp.bfloat16).reshape(row_count, width)
    lookup_grads = (
        jnp.einsum("shqk,sqhd->skhd", grad_cross_scores, probes, preferred_element_type=jnp.float32)
        * scale
    )
    lookup_sum, content_sum = (
        lax.psum(lookup_grads.astype(jnp.bfloat16), "shard").astype(jnp.float32),
        lax.psum(content_grads.astype(jnp.bfloat16), "shard").astype(jnp.float32),
    )
    lookup_low = lookup_sum.astype(jnp.bfloat16).reshape(slots * text_len, width)
    content_low = content_sum.astype(jnp.bfloat16).reshape(slots * text_len, width)
    own_width = width // shards
    own_text = lax.dynamic_slice_in_dim(text_rows, shard_rank * own_width, own_width, 1)
    lookup_own = outer_sum(own_text, lookup_low)
    content_own = outer_sum(own_text, content_low)
    text_grad = (
        back_project(lookup_low, lookup_matrix) + back_project(content_low, content_matrix)
    ).reshape(slots, text_len, width)
    grad_hidden_two = back_project(probe_grads, probe_matrix).reshape(slots, frame_count, width)
    grad_self_norm, gain_cross_part, bias_cross_part = pull_two(grad_hidden_two)
    grad_after_self = grad_after_cross + grad_self_norm
    grad_self_low = grad_after_self.reshape(row_count, width).astype(jnp.bfloat16)
    grad_mixed = split_heads(
        back_project(grad_self_low, output_matrix)
        .astype(jnp.bfloat16)
        .reshape(slots, frame_count, width)
    )
    grad_queries, grad_keys, grad_values = lax.map(
        self_backward, (head_queries, head_keys, head_values, allowed, log_totals, grad_mixed)
    )
    key_sum, value_sum = (
        lax.psum_scatter(
            grad_keys.reshape(slots, clip_total, width).astype(jnp.bfloat16),
            "shard",
            scatter_dimension=1,
            tiled=True,
        ).astype(jnp.float32),
        lax.psum_scatter(
            grad_values.reshape(slots, clip_total, width).astype(jnp.bfloat16),
            "shard",
            scatter_dimension=1,
            tiled=True,
        ).astype(jnp.float32),
    )
    key_low = key_sum.astype(jnp.bfloat16).reshape(row_count, width)
    value_low = value_sum.astype(jnp.bfloat16).reshape(row_count, width)
    query_low = grad_queries.reshape(row_count, width)
    grad_hidden_one = (
        back_project(query_low, query_matrix)
        + back_project(key_low, key_matrix)
        + back_project(value_low, value_matrix)
    )
    grad_inputs, gain_attend_part, bias_attend_part = pull_one(
        grad_hidden_one.reshape(slots, frame_count, width)
    )
    frames_grad = grad_after_self + grad_inputs
    attend_owned = (
        lax.psum_scatter(
            outer_sum(hidden_one, query_low).astype(jnp.bfloat16),
            "shard",
            scatter_dimension=0,
            tiled=True,
        ).astype(jnp.float32),
        lax.psum_scatter(
            outer_sum(hidden_one, key_low).astype(jnp.bfloat16),
            "shard",
            scatter_dimension=0,
            tiled=True,
        ).astype(jnp.float32),
        lax.psum_scatter(
            outer_sum(hidden_one, value_low).astype(jnp.bfloat16),
            "shard",
            scatter_dimension=0,
            tiled=True,
        ).astype(jnp.float32),
        lax.psum_scatter(
            outer_sum(mixed_rows, grad_self_low).astype(jnp.bfloat16),
            "shard",
            scatter_dimension=0,
            tiled=True,
        ).astype(jnp.float32),
        lax.psum_scatter(
            outer_sum(hidden_two, probe_grads).astype(jnp.bfloat16),
            "shard",
            scatter_dimension=0,
            tiled=True,
        ).astype(jnp.float32),
        lax.psum_scatter(
            outer_sum(cross_mixed, grad_cross_low).astype(jnp.bfloat16),
            "shard",
            scatter_dimension=0,
            tiled=True,
        ).astype(jnp.float32),
        lax.psum_scatter(
            gain_attend_part.astype(jnp.bfloat16), "shard", scatter_dimension=0, tiled=True
        ).astype(jnp.float32),
        lax.psum_scatter(
            bias_attend_part.astype(jnp.bfloat16), "shard", scatter_dimension=0, tiled=True
        ).astype(jnp.float32),
        lax.psum_scatter(
            gain_cross_part.astype(jnp.bfloat16), "shard", scatter_dimension=0, tiled=True
        ).astype(jnp.float32),
        lax.psum_scatter(
            bias_cross_part.astype(jnp.bfloat16), "shard", scatter_dimension=0, tiled=True
        ).astype(jnp.float32),
    )
    summed = (
        lax.psum(attend_owned[6].astype(jnp.bfloat16), "replica").astype(jnp.float32),
        lax.psum(attend_owned[7].astype(jnp.bfloat16), "replica").astype(jnp.float32),
        lax.psum(attend_owned[0].astype(jnp.bfloat16), "replica").astype(jnp.float32),
        lax.psum(attend_owned[1].astype(jnp.bfloat16), "replica").astype(jnp.float32),
        lax.psum(attend_owned[2].astype(jnp.bfloat16), "replica").astype(jnp.float32),
        lax.psum(attend_owned[3].astype(jnp.bfloat16), "replica").astype(jnp.float32),
        lax.psum(attend_owned[8].astype(jnp.bfloat16), "replica").astype(jnp.float32),
        lax.psum(attend_owned[9].astype(jnp.bfloat16), "replica").astype(jnp.float32),
        lax.psum(attend_owned[4].astype(jnp.bfloat16), "replica").astype(jnp.float32),
        lax.psum(lookup_own.astype(jnp.bfloat16), "replica").astype(jnp.float32),
        lax.psum(content_own.astype(jnp.bfloat16), "replica").astype(jnp.float32),
        lax.psum(attend_owned[5].astype(jnp.bfloat16), "replica").astype(jnp.float32),
        lax.psum(feed_owned[2].astype(jnp.bfloat16), "replica").astype(jnp.float32),
        lax.psum(feed_owned[3].astype(jnp.bfloat16), "replica").astype(jnp.float32),
        lax.psum(feed_owned[0].astype(jnp.bfloat16), "replica").astype(jnp.float32),
        lax.psum(feed_owned[1].astype(jnp.bfloat16), "replica").astype(jnp.float32),
    )
    return (
        output,
        loss,
        frames_grad,
        text_grad,
        summed[0],
        summed[1],
        summed[2],
        summed[3],
        summed[4],
        summed[5],
        summed[6],
        summed[7],
        summed[8],
        summed[9],
        summed[10],
        summed[11],
        summed[12],
        summed[13],
        summed[14],
        summed[15],
    )


PAIR = 2 * HEAD_DIM
EVERY = ("shard", "y", "x", "core")
REPLICAS = ("core", "y", "x")
NT = (((1,), (1,)), ((), ()))
TN = (((0,), (0,)), ((), ()))
NN = (((1,), (0,)), ((), ()))


def dot(left, right, dims):
    return lax.dot_general(left, right, dims, preferred_element_type=jnp.float32)


def half_mask(side, value):
    lanes = lax.broadcasted_iota(jnp.int32, (1, PAIR), 1)
    inside = (lanes >= HEAD_DIM) if side else (lanes < HEAD_DIM)
    return jnp.where(inside, value, 0.0).astype(jnp.bfloat16)


def fill_clip(place, own_ref, other_ref, all_ref):
    block = own_ref.shape[0] // 2
    for part in range(2):
        rows = slice(part * block, (part + 1) * block)
        for at, ref in ((place[part], own_ref), (place[3 + part], other_ref)):
            all_ref[pl.ds(pl.multiple_of(at * block, block), block), :] = ref[rows, :]


def self_forward_kernel(
    place, q_ref, own_k, own_v, other_k, other_v, mixed_ref, lse_ref, k_ref, v_ref, acc_ref
):
    fill_clip(place, own_k, other_k, k_ref)
    fill_clip(place, own_v, other_v, v_ref)
    block = q_ref.shape[0] // 2
    length = place[2]
    low = lax.broadcasted_iota(jnp.int32, (PAIR, 1), 0) < HEAD_DIM
    for part in range(2):
        first = place[part] * block
        rows = slice(part * block, (part + 1) * block)
        q = q_ref[rows, :]
        q_half = [q * half_mask(side, HEAD_DIM ** (-0.5)) for side in range(2)]
        limit = jnp.minimum(
            first + lax.broadcasted_iota(jnp.int32, (1, block), 1) + 1, length
        )
        acc_ref[...] = jnp.zeros_like(acc_ref)

        def step(j, peaks, q_half=q_half, limit=limit):
            at = pl.multiple_of(j * block, block)
            k = k_ref[pl.ds(at, block), :]
            v = v_ref[pl.ds(at, block), :]
            allowed = at + lax.broadcasted_iota(jnp.int32, (block, block), 0) < limit
            out = []
            for side in range(2):
                scores = jnp.where(allowed, dot(k, q_half[side], NT), masked_score)
                peak = jnp.maximum(peaks[side], jnp.max(scores, axis=0, keepdims=True))
                weights = jnp.exp(scores - peak).astype(jnp.bfloat16)
                v_ones = v * half_mask(side, 1.0) + half_mask(1 - side, 1.0)
                acc_ref[side] = acc_ref[side] * jnp.exp(peaks[side] - peak) + dot(
                    v_ones, weights, TN
                )
                out.append(peak)
            return tuple(out)

        peaks = lax.fori_loop(
            0, place[part] + 1, step, (jnp.full((1, block), masked_score, jnp.float32),) * 2
        )
        top, bottom = acc_ref[0], acc_ref[1]
        total = jnp.where(low, top[HEAD_DIM : HEAD_DIM + 1], bottom[0:1])
        mixed = jnp.where(low, top, bottom) / total
        mixed_ref[rows, :] = mixed.T.astype(jnp.bfloat16)
        lse_ref[0:1, rows] = peaks[0] + jnp.log(top[HEAD_DIM : HEAD_DIM + 1])
        lse_ref[1:2, rows] = peaks[1] + jnp.log(bottom[0:1])


def self_backward_kernel(
    place, q_ref, own_k, own_v, other_k, other_v, mixed_ref, grad_ref, lse_ref,
    dq_ref, own_dk, own_dv, other_dk, other_dv, k_ref, v_ref, dq_acc, dk_acc, dv_acc,
):
    fill_clip(place, own_k, other_k, k_ref)
    fill_clip(place, own_v, other_v, v_ref)
    block = q_ref.shape[0] // 2
    length = place[2]
    scale = HEAD_DIM ** (-0.5)
    dk_acc[...] = jnp.zeros_like(dk_acc)
    dv_acc[...] = jnp.zeros_like(dv_acc)
    for part in range(2):
        first = place[part] * block
        rows = slice(part * block, (part + 1) * block)
        q = q_ref[rows, :]
        grad = grad_ref[rows, :]
        q_half = [q * half_mask(side, scale) for side in range(2)]
        grad_half = [grad * half_mask(side, 1.0) for side in range(2)]
        product = (grad.astype(jnp.float32) * mixed_ref[rows, :].astype(jnp.float32)).T
        inner = [
            jnp.sum(product[side * HEAD_DIM : (side + 1) * HEAD_DIM], axis=0, keepdims=True)
            for side in range(2)
        ]
        lse = [lse_ref[side : side + 1, rows] for side in range(2)]
        limit = jnp.minimum(
            first + lax.broadcasted_iota(jnp.int32, (1, block), 1) + 1, length
        )
        dq_acc[...] = jnp.zeros_like(dq_acc)

        def step(
            j, carry, q_half=q_half, grad_half=grad_half, inner=inner, lse=lse, limit=limit
        ):
            at = pl.multiple_of(j * block, block)
            k = k_ref[pl.ds(at, block), :]
            v = v_ref[pl.ds(at, block), :]
            allowed = at + lax.broadcasted_iota(jnp.int32, (block, block), 0) < limit
            dq, dk, dv = 0.0, 0.0, 0.0
            for side in range(2):
                scores = jnp.where(allowed, dot(k, q_half[side], NT), masked_score)
                probs = jnp.exp(scores - lse[side])
                grad_probs = dot(v, grad_half[side], NT)
                grad_scores = (probs * (grad_probs - inner[side])).astype(jnp.bfloat16)
                dv += dot(probs.astype(jnp.bfloat16), grad_half[side], NN)
                dk += dot(grad_scores, q_half[side], NN)
                dq += dot(k * half_mask(side, scale), grad_scores, TN)
            dk_acc[pl.ds(at, block), :] += dk
            dv_acc[pl.ds(at, block), :] += dv
            dq_acc[...] += dq
            return carry

        lax.fori_loop(0, place[part] + 1, step, 0)
        dq_ref[rows, :] = dq_acc[...].T.astype(jnp.bfloat16)
    for part in range(2):
        rows = slice(part * block, (part + 1) * block)
        own = pl.ds(pl.multiple_of(place[part] * block, block), block)
        other = pl.ds(pl.multiple_of(place[3 + part] * block, block), block)
        own_dk[rows, :] = dk_acc[own, :].astype(jnp.bfloat16)
        own_dv[rows, :] = dv_acc[own, :].astype(jnp.bfloat16)
        other_dk[rows, :] = dk_acc[other, :].astype(jnp.bfloat16)
        other_dv[rows, :] = dv_acc[other, :].astype(jnp.bfloat16)


def pair_block(rows):
    return pl.BlockSpec((rows, PAIR), lambda i, *_: (0, i))


def value_block(rows, pairs):
    return pl.BlockSpec((rows, PAIR), lambda i, *_: (0, pairs + i))


def self_attend(place, queries, own, other):
    rows, width = queries.shape
    clip = 2 * rows
    pairs = width // PAIR
    return pl.pallas_call(
        self_forward_kernel,
        out_shape=(
            jax.ShapeDtypeStruct((rows, width), jnp.bfloat16),
            jax.ShapeDtypeStruct((pairs * 8, rows), jnp.float32),
        ),
        grid_spec=pltpu.PrefetchScalarGridSpec(
            num_scalar_prefetch=1,
            grid=(pairs,),
            in_specs=[pair_block(rows)] + [pair_block(rows), value_block(rows, pairs)] * 2,
            out_specs=(pair_block(rows), pl.BlockSpec((8, rows), lambda i, *_: (i, 0))),
            scratch_shapes=[
                pltpu.VMEM((clip, PAIR), jnp.bfloat16),
                pltpu.VMEM((clip, PAIR), jnp.bfloat16),
                pltpu.VMEM((2, PAIR, rows // 2), jnp.float32),
            ],
        ),
        compiler_params=pltpu.CompilerParams(vmem_limit_bytes=32 * 2**20),
        cost_estimate=pl.CostEstimate(
            flops=2 * 2 * rows * clip * width, bytes_accessed=8 * clip * width, transcendentals=0
        ),
        name="self_attend",
    )(place, queries, own, own, other, other)


def self_attend_back(place, queries, own, other, mixed, grads, lse):
    rows, width = queries.shape
    clip = 2 * rows
    pairs = width // PAIR
    return pl.pallas_call(
        self_backward_kernel,
        out_shape=(jax.ShapeDtypeStruct((rows, width), jnp.bfloat16),) * 5,
        grid_spec=pltpu.PrefetchScalarGridSpec(
            num_scalar_prefetch=1,
            grid=(pairs,),
            in_specs=[pair_block(rows)]
            + [pair_block(rows), value_block(rows, pairs)] * 2
            + [
                pair_block(rows),
                pair_block(rows),
                pl.BlockSpec((8, rows), lambda i, *_: (i, 0)),
            ],
            out_specs=(pair_block(rows),) * 5,
            scratch_shapes=[
                pltpu.VMEM((clip, PAIR), jnp.bfloat16),
                pltpu.VMEM((clip, PAIR), jnp.bfloat16),
                pltpu.VMEM((PAIR, rows // 2), jnp.float32),
                pltpu.VMEM((clip, PAIR), jnp.float32),
                pltpu.VMEM((clip, PAIR), jnp.float32),
            ],
        ),
        compiler_params=pltpu.CompilerParams(vmem_limit_bytes=32 * 2**20),
        cost_estimate=pl.CostEstimate(
            flops=5 * 2 * rows * clip * width, bytes_accessed=16 * clip * width, transcendentals=0
        ),
        name="self_attend_back",
    )(place, queries, own, own, other, other, mixed, grads, lse)


def both_heads(rows, value):
    return jnp.concatenate([rows * half_mask(side, value) for side in range(2)], axis=0)


def cross_probs_of(lookup_two, probes, present):
    text = present.shape[0]
    scores = dot(lookup_two, probes, NT)
    out = []
    for side in range(2):
        part = jnp.where(
            present > 0, scores[side * text : (side + 1) * text], masked_score
        )
        weights = jnp.exp(part - jnp.max(part, axis=0, keepdims=True))
        out.append(weights / jnp.sum(weights, axis=0, keepdims=True))
    return out


def cross_forward_kernel(probe_ref, lookup_ref, content_ref, present_ref, mixed_ref):
    probs = cross_probs_of(
        both_heads(lookup_ref[...], HEAD_DIM ** (-0.5)), probe_ref[...], present_ref[...]
    )
    probs = jnp.concatenate(probs, axis=0).astype(jnp.bfloat16)
    mixed_ref[...] = dot(probs, both_heads(content_ref[...], 1.0), TN).astype(jnp.bfloat16)


def cross_backward_kernel(
    probe_ref, lookup_ref, content_ref, present_ref, grad_ref, dp_ref, dl_ref, dc_ref
):
    text = present_ref.shape[0]
    scale = HEAD_DIM ** (-0.5)
    probes = probe_ref[...]
    grads = grad_ref[...]
    lookup_two = both_heads(lookup_ref[...], scale)
    probs = cross_probs_of(lookup_two, probes, present_ref[...])
    grad_probs = dot(both_heads(content_ref[...], 1.0), grads, NT)
    grad_scores = []
    for side in range(2):
        part = grad_probs[side * text : (side + 1) * text]
        inner = jnp.sum(probs[side] * part, axis=0, keepdims=True)
        grad_scores.append(probs[side] * (part - inner))
    grad_scores = jnp.concatenate(grad_scores, axis=0).astype(jnp.bfloat16)
    probs = jnp.concatenate(probs, axis=0).astype(jnp.bfloat16)
    low = lax.broadcasted_iota(jnp.int32, (1, PAIR), 1) < HEAD_DIM
    dp_ref[...] = dot(grad_scores, lookup_two, TN).astype(jnp.bfloat16)
    dl = dot(grad_scores, probes, NN) * scale
    dl_ref[...] = jnp.where(low, dl[:text], dl[text:]).astype(jnp.bfloat16)
    dc = dot(probs, grads, NN)
    dc_ref[...] = jnp.where(low, dc[:text], dc[text:]).astype(jnp.bfloat16)


def cross_attend(probes, lookups, contents, present):
    rows, width = probes.shape
    text = lookups.shape[0]
    return pl.pallas_call(
        cross_forward_kernel,
        out_shape=jax.ShapeDtypeStruct((rows, width), jnp.bfloat16),
        grid=(width // PAIR,),
        in_specs=[
            pair_block(rows),
            pair_block(text),
            pair_block(text),
            pl.BlockSpec((text, 1), lambda i: (0, 0)),
        ],
        out_specs=pair_block(rows),
        compiler_params=pltpu.CompilerParams(vmem_limit_bytes=32 * 2**20),
        cost_estimate=pl.CostEstimate(
            flops=8 * rows * text * width, bytes_accessed=4 * rows * width, transcendentals=0
        ),
        name="cross_attend",
    )(probes, lookups, contents, present)


def cross_attend_back(probes, lookups, contents, present, grads):
    rows, width = probes.shape
    text = lookups.shape[0]
    return pl.pallas_call(
        cross_backward_kernel,
        out_shape=(
            jax.ShapeDtypeStruct((rows, width), jnp.bfloat16),
            jax.ShapeDtypeStruct((text, width), jnp.bfloat16),
            jax.ShapeDtypeStruct((text, width), jnp.bfloat16),
        ),
        grid=(width // PAIR,),
        in_specs=[
            pair_block(rows),
            pair_block(text),
            pair_block(text),
            pl.BlockSpec((text, 1), lambda i: (0, 0)),
            pair_block(rows),
        ],
        out_specs=(pair_block(rows), pair_block(text), pair_block(text)),
        compiler_params=pltpu.CompilerParams(vmem_limit_bytes=32 * 2**20),
        cost_estimate=pl.CostEstimate(
            flops=20 * rows * text * width, bytes_accessed=6 * rows * width, transcendentals=0
        ),
        name="cross_attend_back",
    )(probes, lookups, contents, present, grads)


def unpack_kernel(in_ref, out_ref):
    pieces = in_ref[...]
    out_ref[...] = pieces.reshape(-1, pieces.shape[-1]).T.astype(jnp.float32)


def unpack(full, rows, place, out_shape, out_at, together):
    owners, _, features = full.shape
    tall = out_shape[0] // features
    wide = out_shape[1] // (together * rows)
    return pl.pallas_call(
        unpack_kernel,
        out_shape=jax.ShapeDtypeStruct(out_shape, jnp.float32),
        grid=(tall, wide),
        in_specs=[
            pl.BlockSpec((together, rows, features), lambda i, j: (j + out_at, place + i, 0))
        ],
        out_specs=pl.BlockSpec((features, together * rows), lambda i, j: (i, j)),
        compiler_params=pltpu.CompilerParams(vmem_limit_bytes=32 * 2**20),
        cost_estimate=pl.CostEstimate(
            flops=0, bytes_accessed=6 * out_shape[0] * out_shape[1], transcendentals=0
        ),
        name="unpack",
    )(full)


def held(values, *others):
    return list(lax.optimization_barrier((*values, *others))[: len(values)])


def after(value, *others):
    return lax.optimization_barrier((value, *others))[0]


def norm_parts(values):
    mean = jnp.mean(values, axis=-1, keepdims=True)
    center = values - mean
    return mean, lax.rsqrt(jnp.mean(center * center, axis=-1, keepdims=True) + epsilon)


def norm_back(grads, values, parts, gain):
    mean, inverse = parts
    unit = (values - mean) * inverse
    gain_grad = jnp.sum(grads * unit, axis=0)
    bias_grad = jnp.sum(grads, axis=0)
    scaled = grads * gain
    back = inverse * (
        scaled
        - jnp.mean(scaled, axis=-1, keepdims=True)
        - unit * jnp.mean(scaled * unit, axis=-1, keepdims=True)
    )
    return back, gain_grad, bias_grad


def clip_body(
    frames,
    text_states,
    text_mask,
    clip_lengths,
    slot_used,
    teacher,
    self_norm_gain,
    self_norm_bias,
    self_query_weight,
    self_key_weight,
    self_value_weight,
    self_output_weight,
    cross_norm_gain,
    cross_norm_bias,
    cross_query_weight,
    cross_key_weight,
    cross_value_weight,
    cross_output_weight,
    feed_norm_gain,
    feed_norm_bias,
    feed_up_weight,
    feed_down_weight,
):
    block, width = frames.shape[1:]
    text_len = text_states.shape[1]
    shards, replicas, outers = 4, 8, 4
    core = lax.axis_index("core")
    shard = lax.axis_index("shard")
    outer = 2 * lax.axis_index("y") + lax.axis_index("x")
    replica = 2 * outer + core
    clip = block * shards
    hidden_units = feed_up_weight.shape[1]

    holder = {0: 0, 1: 1, 2: 1, 3: 0}
    there = ([], [])
    for c in range(2):
        for s in range(4):
            for turn in range(2):
                slot = turn if s < 2 else 1 - turn
                there[turn].append((c * 4 + s, holder[s] * 4 + 2 * c + slot))
    back = tuple([(b, a) for a, b in pairs] for pairs in there)
    spot = ("core", "shard")
    swap = [(0, 1), (1, 0)]
    even = shard % 2 == 0
    lower = shard < 2
    first_core = core == 0

    def hop(values, distance):
        pairs = [(i, (i + distance) % shards) for i in range(shards)]
        return lax.ppermute(values, "shard", pairs)

    def hops(values):
        return [hop(values, distance) for distance in (1, 2, 3)]

    def line_up(mine, came):
        out = jnp.zeros((shards,) + mine.shape, mine.dtype)
        out = lax.dynamic_update_index_in_dim(out, mine, shard, 0)
        for distance, values in zip((1, 2, 3), came):
            owner = lax.rem(shard + shards - distance, shards)
            out = lax.dynamic_update_index_in_dim(out, values, owner, 0)
        return out

    def to_chip(pair):
        one = lax.ppermute(jnp.where(lower, pair[0], pair[1]), spot, there[0])
        two = lax.ppermute(jnp.where(lower, pair[1], pair[0]), spot, there[1])
        return one, two

    def by_time(one, two):
        return jnp.concatenate([jnp.where(even, one, two), jnp.where(even, two, one)], axis=0)

    def outgoing(values):
        early, late = values[:block], values[block:]
        return jnp.where(even, early, late), jnp.where(even, late, early)

    def from_chip(values):
        one, two = outgoing(values)
        return lax.ppermute(one, spot, back[0]), lax.ppermute(two, spot, back[1])

    def by_slot(one, two):
        return jnp.stack([jnp.where(lower, one, two), jnp.where(lower, two, one)])

    def share_of(weight):
        share = weight.shape[0] // replicas
        return lax.dynamic_slice_in_dim(weight, replica * share, share, 0)

    def from_replicas(line):
        full = lax.all_gather(line, ("y", "x", "core"), axis=1, tiled=True)
        return full.reshape(-1, line.shape[-1])

    qkv_share = jnp.concatenate(
        [share_of(self_query_weight), share_of(self_key_weight), share_of(self_value_weight)],
        axis=1,
    )
    vectors = jnp.concatenate(
        [
            self_norm_gain,
            self_norm_bias,
            cross_norm_gain,
            cross_norm_bias,
            feed_norm_gain,
            feed_norm_bias,
        ]
    )
    vectors = jnp.pad(vectors[None, :], ((0, 15), (0, 3 * width - 6 * block)))
    share = qkv_share.shape[0]
    qkv_mine = jnp.concatenate([qkv_share, vectors], axis=0)
    qkv_came = hops(qkv_mine)
    qkv_matrix = from_replicas(line_up(qkv_share, [values[:share] for values in qkv_came]))
    norms = line_up(vectors[0], [values[share] for values in qkv_came])
    norms = norms[:, : 6 * block].reshape(shards, 6, block).transpose(1, 0, 2)
    norms = norms.reshape(6, width).astype(jnp.float32)
    rest_share = jnp.concatenate(
        [share_of(self_output_weight), share_of(cross_query_weight), share_of(cross_output_weight)],
        axis=1,
    )
    rest_came = hops(after(rest_share, *qkv_came))
    rest = from_replicas(line_up(rest_share, rest_came))
    came = to_chip(after(frames, *rest_came))
    x_low = by_time(*came)
    expand_share = share_of(feed_up_weight)
    expand_came = hops(after(expand_share, *came))

    facts = jnp.concatenate(
        [(clip_lengths // 64)[:, None], (clip_lengths % 64)[:, None], slot_used[:, None], text_mask],
        axis=1,
    ).astype(jnp.bfloat16)
    facts = jnp.pad(facts[:, None, :], ((0, 0), (0, 15), (0, width - facts.shape[1])))
    text_sent = lax.ppermute(jnp.concatenate([text_states, facts], axis=1), "core", swap)
    text_other = text_sent[:, :text_len]
    both = jnp.stack([facts[:, 0], text_sent[:, text_len]])[:, :, : 3 + text_len].astype(jnp.int32)
    lengths = 64 * both[:, :, 0] + both[:, :, 1]
    fact = lax.dynamic_index_in_dim(
        jnp.where(shard // 2 == core, both[0], both[1]), shard % 2, 0, keepdims=False
    )
    length, used = 64 * fact[0] + fact[1], fact[2]
    present = fact[3:].reshape(text_len, 1)
    count = jnp.sum(
        jnp.where(both[:, :, 2] > 0, jnp.minimum(lengths, clip), 0).astype(jnp.float32)
    )
    count = jnp.full((8, 128), count)
    for axis in ("x", "y"):
        count += lax.ppermute(count, axis, swap)
    count = count[0, 0]
    text_all = jnp.concatenate(
        [
            jnp.where(first_core, text_states, text_other),
            jnp.where(first_core, text_other, text_states),
        ],
        axis=0,
    ).reshape(4 * text_len, width)
    text_all = lax.dynamic_slice_in_dim(text_all, shard * block, block, 1)
    text_matrix = jnp.where(first_core, cross_key_weight, cross_value_weight)
    text_part = project(text_all, text_matrix).astype(jnp.bfloat16).reshape(4, text_len, width)
    text_came = [
        hop(
            lax.dynamic_index_in_dim(
                text_part, lax.rem(shard + distance, shards), 0, keepdims=False
            ),
            distance,
        )
        for distance in (1, 2, 3)
    ]

    places = jnp.stack([core, 3 - core, length, 1 - core, 2 + core]).astype(jnp.int32)
    positions = jnp.concatenate(
        [core * block + jnp.arange(block), (3 - core) * block + jnp.arange(block)]
    )
    valid_rows = ((positions < length) & (used > 0)).astype(jnp.float32)[:, None]
    inputs = x_low.astype(jnp.float32)
    parts_one = norm_parts(inputs)
    hidden_one = ((inputs - parts_one[0]) * parts_one[1] * norms[0] + norms[1]).astype(
        jnp.bfloat16
    )
    kv = project(after(hidden_one, count), qkv_matrix[:, width:]).astype(jnp.bfloat16)
    kv_other = lax.ppermute(kv, "core", swap)
    queries = project(after(hidden_one, kv), qkv_matrix[:, :width]).astype(jnp.bfloat16)
    expand_came = held(expand_came, kv_other, queries)
    expand_matrix = from_replicas(line_up(expand_share, expand_came))
    reduce_share = share_of(feed_down_weight)
    reduce_came = hops(after(reduce_share, *expand_came))
    output_matrix = rest[:, :width]
    probe_matrix = rest[:, width : 2 * width]
    merge_matrix = rest[:, 2 * width :]
    mixed_self, lse = self_attend(after(places, *expand_came), queries, kv, kv_other)
    reduce_came = held(reduce_came, mixed_self)
    reduce_matrix = from_replicas(line_up(reduce_share, reduce_came))
    text_came = held(text_came, mixed_self)
    text_half = lax.dynamic_index_in_dim(text_part, shard, 0, keepdims=False).astype(jnp.float32)
    for values in text_came:
        text_half += values.astype(jnp.float32)
    text_half = text_half.astype(jnp.bfloat16)
    text_swap = lax.ppermute(text_half, "core", swap)
    lookups = jnp.where(first_core, text_half, text_swap)
    contents = jnp.where(first_core, text_swap, text_half)
    after_self = inputs + project(mixed_self, output_matrix)
    parts_two = norm_parts(after_self)
    hidden_two = ((after_self - parts_two[0]) * parts_two[1] * norms[2] + norms[3]).astype(
        jnp.bfloat16
    )
    probes = project(hidden_two, probe_matrix).astype(jnp.bfloat16)
    teacher_came = to_chip(after(teacher, *reduce_came, probes))
    cross_mixed = cross_attend(probes, lookups, contents, present)
    after_cross = after_self + project(cross_mixed, merge_matrix)
    parts_three = norm_parts(after_cross)
    hidden_three = (
        (after_cross - parts_three[0]) * parts_three[1] * norms[4] + norms[5]
    ).astype(jnp.bfloat16)
    upward = project(hidden_three, expand_matrix)
    activated, gelu_pull = jax.vjp(exact_gelu, upward)
    activated_low = activated.astype(jnp.bfloat16)
    teacher_low = by_time(*held(teacher_came, activated_low))
    result = after_cross + project(activated_low, reduce_matrix)
    errors = (result - teacher_low.astype(jnp.float32)) * valid_rows
    squares = jnp.sum(errors * errors)
    grad_result = errors * (4 * outers * clip / count)
    grad_feed_low = grad_result.astype(jnp.bfloat16)

    def theirs_of(right, left):
        columns = right.shape[1] // 2
        part = lax.dynamic_slice_in_dim(right, (1 - core) * columns, columns, 1)
        return outer_sum(part, left).astype(jnp.bfloat16)

    def ours_of(right, left, theirs):
        columns = right.shape[1] // 2
        sent = lax.ppermute(theirs, "core", swap)
        part = lax.dynamic_slice_in_dim(right, core * columns, columns, 1)
        return (outer_sum(part, left) + sent.astype(jnp.float32)).astype(jnp.bfloat16)

    def over_outer(values):
        return lax.psum_scatter(values, ("y", "x"), scatter_dimension=0, tiled=True)

    def shard_hops(values):
        columns = values.shape[1] // shards
        return [
            hop(
                lax.dynamic_slice_in_dim(
                    values, lax.rem(shard + distance, shards) * columns, columns, 1
                ),
                distance,
            )
            for distance in (1, 2, 3)
        ]

    def over_shard(values, came):
        columns = values.shape[1] // shards
        total = lax.dynamic_slice_in_dim(values, shard * columns, columns, 1).astype(jnp.float32)
        for part in came:
            total += part.astype(jnp.float32)
        return total.astype(jnp.bfloat16)

    down_theirs = theirs_of(grad_feed_low, activated_low)
    to_send = outgoing(result.astype(jnp.bfloat16))
    output_one = lax.ppermute(to_send[0], spot, back[0])
    grad_activated = back_project(after(grad_feed_low, down_theirs), reduce_matrix)
    grad_upward = gelu_pull(grad_activated)[0].astype(jnp.bfloat16)
    output_one = after(output_one, grad_upward)
    down_ours = ours_of(
        after(grad_feed_low, grad_upward, output_one), activated_low, down_theirs
    )
    down_sum = over_outer(down_ours)
    up_theirs = theirs_of(after(grad_upward, down_ours), hidden_three)
    grad_hidden_three = back_project(after(grad_upward, up_theirs), expand_matrix)
    output_two = lax.ppermute(after(to_send[1], output_one), spot, back[1])
    output_two = after(output_two, grad_hidden_three)
    output = by_slot(output_one, output_two)
    up_ours = ours_of(after(grad_upward, grad_hidden_three, output_two), hidden_three, up_theirs)
    grad_norm, gain_feed, bias_feed = norm_back(
        after(grad_hidden_three, up_ours), after_cross, parts_three, norms[4]
    )
    grad_after_cross = grad_result + grad_norm
    grad_cross_low = grad_after_cross.astype(jnp.bfloat16)
    merge_theirs = theirs_of(grad_cross_low, cross_mixed)
    grad_cross_mixed = back_project(after(grad_cross_low, merge_theirs), merge_matrix).astype(
        jnp.bfloat16
    )
    probe_grads, lookup_grads, content_grads = cross_attend_back(
        probes, lookups, contents, present, grad_cross_mixed
    )
    up_sum = over_outer(up_ours)
    text_mine = jnp.where(first_core, lookup_grads, content_grads)
    text_sent = lax.ppermute(
        jnp.where(first_core, content_grads, lookup_grads), "core", swap
    )
    text_mine = (text_mine.astype(jnp.float32) + text_sent.astype(jnp.float32)).astype(
        jnp.bfloat16
    )
    merge_ours = ours_of(after(grad_cross_low, probe_grads), cross_mixed, merge_theirs)
    probe_theirs = theirs_of(after(probe_grads, merge_ours), hidden_two)
    grad_hidden_two = back_project(after(probe_grads, probe_theirs), probe_matrix)
    text_four = line_up(text_mine, hops(text_mine)).reshape(4 * text_len, width)
    grad_norm, gain_cross, bias_cross = norm_back(
        grad_hidden_two, after_self, parts_two, norms[2]
    )
    grad_after_self = grad_after_cross + grad_norm
    grad_self_low = grad_after_self.astype(jnp.bfloat16)
    output_theirs = theirs_of(grad_self_low, mixed_self)
    grad_mixed = back_project(after(grad_self_low, output_theirs), output_matrix).astype(
        jnp.bfloat16
    )
    probe_ours = ours_of(after(probe_grads, grad_mixed), hidden_two, probe_theirs)
    text_weights = outer_sum(text_four, text_all).astype(jnp.bfloat16)
    text_back = back_project(text_four, text_matrix).astype(jnp.bfloat16)
    output_ours = ours_of(after(grad_self_low, probe_ours), mixed_self, output_theirs)
    text_rows = width // outers
    middle = jnp.concatenate(
        [
            values.reshape(outers, -1, width)
            for values in (
                output_ours,
                probe_ours,
                merge_ours,
                text_weights.reshape(outers, shards, text_rows // shards, block)
                .transpose(0, 2, 1, 3)
                .reshape(outers, text_rows // shards, width),
            )
        ],
        axis=1,
    )
    middle_rows = middle.shape[1]
    middle = middle.reshape(outers * middle_rows, width)
    middle_sum = over_outer(middle)
    text_split = text_rows // shards
    text_piece = (
        middle_sum[middle_rows - text_split :]
        .reshape(text_split, shards, block)
        .transpose(1, 0, 2)
        .reshape(text_rows, block)
    )
    text_back = text_back.reshape(2, 2, text_len, block)
    text_kept = lax.dynamic_index_in_dim(text_back, core, 0, keepdims=False)
    text_gone = lax.dynamic_index_in_dim(text_back, 1 - core, 0, keepdims=False)
    text_own = text_kept.astype(jnp.float32) + lax.ppermute(text_gone, "core", swap).astype(
        jnp.float32
    )
    text_own = text_own.astype(jnp.bfloat16)
    down_came = shard_hops(down_sum)
    text_came = hops(text_own)
    grad_queries, own_keys, own_values, other_keys, other_values = self_attend_back(
        places, queries, kv, kv_other, mixed_self, after(grad_mixed, middle, text_own), lse
    )
    text_came = held(text_came, grad_queries)
    down_came = held(down_came, grad_queries)
    other_keys, other_values = held([other_keys, other_values], *text_came, *down_came)
    own_keys += lax.ppermute(other_keys, "core", swap)
    own_values += lax.ppermute(other_values, "core", swap)
    down_piece = over_shard(down_sum, down_came)
    up_came = shard_hops(after(up_sum, down_piece))

    qkv_grads = jnp.concatenate([grad_queries, own_keys, own_values], axis=1)
    qkv_theirs = theirs_of(qkv_grads, hidden_one)
    grad_hidden_one = back_project(after(qkv_grads, qkv_theirs), qkv_matrix)
    qkv_ours = ours_of(after(qkv_grads, grad_hidden_one), hidden_one, qkv_theirs)
    up_came = held(up_came, grad_hidden_one)
    up_piece = over_shard(up_sum, up_came)
    text_grad = line_up(text_own, text_came).astype(jnp.float32)
    text_grad = text_grad.transpose(1, 2, 0, 3).reshape(text_states.shape)
    qkv_sum = over_outer(qkv_ours)
    grad_norm, gain_self, bias_self = norm_back(
        after(grad_hidden_one, qkv_ours, *up_came), inputs, parts_one, norms[0]
    )
    middle_kept = after(middle_sum[: middle_rows - text_split], qkv_ours, *up_came)
    middle_came = shard_hops(middle_kept)
    small = jnp.stack(
        [
            gain_self,
            bias_self,
            gain_cross,
            bias_cross,
            gain_feed,
            bias_feed,
            jnp.full((width,), squares),
            jnp.zeros((width,), jnp.float32),
        ]
    )
    for axis in ("core", "x", "y"):
        small += lax.ppermute(small, axis, swap)
    late_came = shard_hops(after(qkv_sum, *middle_came, small))
    small_came = shard_hops(small)
    small_own = lax.dynamic_slice_in_dim(small, shard * block, block, 1)
    for part in small_came:
        small_own += part
    loss = small_own[6, 0] / (width * count)
    frames_came = from_chip(
        after((grad_after_self + grad_norm).astype(jnp.bfloat16), *late_came, *small_came)
    )
    frames_grad = by_slot(*frames_came).astype(jnp.float32)

    middle_piece = over_shard(middle_kept, middle_came)
    early = jnp.concatenate(
        [up_piece]
        + [down_piece[:, i * block : (i + 1) * block] for i in range(4)]
        + [text_piece, middle_piece],
        axis=0,
    )
    early = lax.all_gather(after(early, text_grad), REPLICAS, axis=0)
    piece = width // replicas
    square = (block, width)
    up_grad = unpack(early, hidden_units // replicas, 0, (block, hidden_units), 0, 1)
    at = hidden_units // replicas // piece
    down_grad = unpack(early, piece, at, (4 * block, width), 0, 2)
    at += 4
    key_grad = unpack(early, text_rows, at * piece // text_rows, square, 0, 1)
    value_grad = unpack(early, text_rows, at * piece // text_rows, square, 4, 1)
    at += text_rows // piece
    output_grad = unpack(early, piece, at, square, 0, 2)
    probe_grad = unpack(early, piece, at + 1, square, 0, 2)
    merge_grad = unpack(early, piece, at + 2, square, 0, 2)
    late = over_shard(qkv_sum, late_came)
    late = lax.all_gather(after(late, early, *frames_came), REPLICAS, axis=0, tiled=True)
    late = late.reshape(-1, block, block)
    qkv_grad = [unpack(late, block, 0, square, 2 * i, 2) for i in range(3)]
    return (
        output,
        loss,
        frames_grad,
        text_grad,
        small_own[0],
        small_own[1],
        qkv_grad[0],
        qkv_grad[1],
        qkv_grad[2],
        output_grad,
        small_own[2],
        small_own[3],
        probe_grad,
        key_grad,
        value_grad,
        merge_grad,
        small_own[4],
        small_own[5],
        up_grad,
        down_grad,
    )


def solution(mesh):
    by_chip = mesh.shape["shard"] == 4 and mesh.shape["replica"] == 8
    replica = ("y", "x", "core") if by_chip else "replica"
    row = P(replica)
    clip = P(replica, "shard", None)
    text = P(replica, None, None)
    vector = P("shard")
    matrix = P("shard", None)
    weights = (
        [vector, vector] + [matrix] * 4 + [vector, vector] + [matrix] * 4 + [vector, vector]
        + [matrix] * 2
    )
    if by_chip:
        mesh = Mesh(mesh.devices.reshape(2, 2, 2, 4), ("y", "x", "core", "shard"))
    return jax.shard_map(
        clip_body if by_chip else general_body,
        mesh=mesh,
        in_specs=(clip, text, P(replica, None), row, row, clip, *weights),
        out_specs=(clip, P(), clip, text, *weights),
        check_vma=False,
    )
```

```python
import jax
import jax.numpy as jnp
from jax import lax
from jax.experimental import pallas as pl
from jax.experimental.pallas import tpu as pltpu
from jax.sharding import Mesh
from jax.sharding import PartitionSpec as P

HEADS = 24
HEAD_DIM = 64


epsilon = 1e-05
masked_score = -1e30


def layer_norm(values, gain, shift):
    center = values - jnp.mean(values, axis=-1, keepdims=True)
    variance = jnp.mean(center * center, axis=-1, keepdims=True)
    return center * lax.rsqrt(variance + epsilon) * gain + shift


def exact_gelu(values):
    return jax.nn.gelu(values, approximate=False)


def project(left, right):
    return jnp.dot(left, right, preferred_element_type=jnp.float32)


def outer_sum(left, right):
    return jnp.einsum("rd,re->de", left, right, preferred_element_type=jnp.float32)


def back_project(grads, matrix):
    return jnp.einsum("re,de->rd", grads, matrix, preferred_element_type=jnp.float32)


def split_heads(values):
    return values.reshape(values.shape[:-1] + (HEADS, HEAD_DIM))


def self_forward(operands):
    queries, keys_all, values_all, allowed = operands
    scale = HEAD_DIM ** (-0.5)
    scores = (
        jnp.einsum("qhd,khd->hqk", queries, keys_all, preferred_element_type=jnp.float32) * scale
    )
    scores = jnp.where(allowed[None], scores, masked_score)
    peak = jnp.max(scores, axis=-1, keepdims=True)
    weights = jnp.exp(scores - peak)
    totals = jnp.sum(weights, axis=-1, keepdims=True)
    probs = (weights / totals).astype(jnp.bfloat16)
    mixed = jnp.einsum("hqk,khd->qhd", probs, values_all, preferred_element_type=jnp.float32)
    return (mixed.astype(jnp.bfloat16), (peak + jnp.log(totals))[..., 0])


def self_backward(operands):
    queries, keys_all, values_all, allowed, log_totals, grad_mixed = operands
    scale = HEAD_DIM ** (-0.5)
    scores = (
        jnp.einsum("qhd,khd->hqk", queries, keys_all, preferred_element_type=jnp.float32) * scale
    )
    scores = jnp.where(allowed[None], scores, masked_score)
    probs = jnp.exp(scores - log_totals[..., None])
    grad_probs = jnp.einsum(
        "qhd,khd->hqk", grad_mixed, values_all, preferred_element_type=jnp.float32
    )
    grad_values = jnp.einsum(
        "hqk,qhd->khd", probs.astype(jnp.bfloat16), grad_mixed, preferred_element_type=jnp.float32
    )
    inner = jnp.sum(probs * grad_probs, axis=-1, keepdims=True)
    grad_scores = (probs * (grad_probs - inner)).astype(jnp.bfloat16)
    grad_queries = (
        jnp.einsum("hqk,khd->qhd", grad_scores, keys_all, preferred_element_type=jnp.float32)
        * scale
    ).astype(jnp.bfloat16)
    grad_keys = (
        jnp.einsum("hqk,qhd->khd", grad_scores, queries, preferred_element_type=jnp.float32) * scale
    )
    return (grad_queries, grad_keys, grad_values)


def general_body(
    frames,
    text_states,
    text_mask,
    clip_lengths,
    slot_used,
    teacher,
    self_norm_gain,
    self_norm_bias,
    self_query_weight,
    self_key_weight,
    self_value_weight,
    self_output_weight,
    cross_norm_gain,
    cross_norm_bias,
    cross_query_weight,
    cross_key_weight,
    cross_value_weight,
    cross_output_weight,
    feed_norm_gain,
    feed_norm_bias,
    feed_up_weight,
    feed_down_weight,
):
    gathered = (
        lax.all_gather(self_norm_gain, "shard", axis=0, tiled=True),
        lax.all_gather(self_norm_bias, "shard", axis=0, tiled=True),
        lax.all_gather(self_query_weight, "shard", axis=0, tiled=True),
        lax.all_gather(self_key_weight, "shard", axis=0, tiled=True),
        lax.all_gather(self_value_weight, "shard", axis=0, tiled=True),
        lax.all_gather(self_output_weight, "shard", axis=0, tiled=True),
        lax.all_gather(cross_norm_gain, "shard", axis=0, tiled=True),
        lax.all_gather(cross_norm_bias, "shard", axis=0, tiled=True),
        lax.all_gather(cross_query_weight, "shard", axis=0, tiled=True),
        lax.all_gather(cross_key_weight, "shard", axis=0, tiled=True),
        lax.all_gather(cross_value_weight, "shard", axis=0, tiled=True),
        lax.all_gather(cross_output_weight, "shard", axis=0, tiled=True),
        lax.all_gather(feed_norm_gain, "shard", axis=0, tiled=True),
        lax.all_gather(feed_norm_bias, "shard", axis=0, tiled=True),
        lax.all_gather(feed_up_weight, "shard", axis=0, tiled=True),
        lax.all_gather(feed_down_weight, "shard", axis=0, tiled=True),
    )
    (
        gain_attend,
        bias_attend,
        query_matrix,
        key_matrix,
        value_matrix,
        output_matrix,
        gain_cross,
        bias_cross,
        probe_matrix,
        lookup_matrix,
        content_matrix,
        merge_matrix,
        gain_feed,
        bias_feed,
        expand_matrix,
        reduce_matrix,
    ) = gathered
    slots = frames.shape[0]
    frame_count = frames.shape[1]
    width = frames.shape[2]
    text_len = text_states.shape[1]
    shards = lax.axis_size("shard")
    replicas = lax.axis_size("replica")
    clip_total = frame_count * shards
    row_count = slots * frame_count
    scale = HEAD_DIM ** (-0.5)
    shard_rank = lax.axis_index("shard")
    positions = shard_rank * frame_count + jnp.arange(frame_count, dtype=jnp.int32)
    key_positions = jnp.arange(clip_total, dtype=jnp.int32)
    allowed = (key_positions[None, None, :] <= positions[None, :, None]) & (
        key_positions[None, None, :] < clip_lengths[:, None, None]
    )
    valid_rows = ((positions[None, :] < clip_lengths[:, None]) & (slot_used[:, None] > 0)).astype(
        jnp.float32
    )
    text_allowed = text_mask > 0
    inputs = frames.astype(jnp.float32)
    normed_one, pull_one = jax.vjp(
        layer_norm, inputs, gain_attend.astype(jnp.float32), bias_attend.astype(jnp.float32)
    )
    hidden_one = normed_one.astype(jnp.bfloat16).reshape(row_count, width)
    queries = (
        project(hidden_one, query_matrix).astype(jnp.bfloat16).reshape(slots, frame_count, width)
    )
    keys_local = (
        project(hidden_one, key_matrix).astype(jnp.bfloat16).reshape(slots, frame_count, width)
    )
    values_local = (
        project(hidden_one, value_matrix).astype(jnp.bfloat16).reshape(slots, frame_count, width)
    )
    keys_all, values_all = (
        lax.all_gather(keys_local, "shard", axis=1, tiled=True),
        lax.all_gather(values_local, "shard", axis=1, tiled=True),
    )
    head_queries = split_heads(queries)
    head_keys = split_heads(keys_all)
    head_values = split_heads(values_all)
    mixed_self, log_totals = lax.map(self_forward, (head_queries, head_keys, head_values, allowed))
    mixed_rows = mixed_self.reshape(row_count, width)
    after_self = inputs + project(mixed_rows, output_matrix).reshape(slots, frame_count, width)
    normed_two, pull_two = jax.vjp(
        layer_norm, after_self, gain_cross.astype(jnp.float32), bias_cross.astype(jnp.float32)
    )
    hidden_two = normed_two.astype(jnp.bfloat16).reshape(row_count, width)
    probes = split_heads(
        project(hidden_two, probe_matrix).astype(jnp.bfloat16).reshape(slots, frame_count, width)
    )
    text_rows = text_states.reshape(slots * text_len, width)
    lookups = split_heads(
        project(text_rows, lookup_matrix).astype(jnp.bfloat16).reshape(slots, text_len, width)
    )
    contents = split_heads(
        project(text_rows, content_matrix).astype(jnp.bfloat16).reshape(slots, text_len, width)
    )
    cross_scores = (
        jnp.einsum("sqhd,skhd->shqk", probes, lookups, preferred_element_type=jnp.float32) * scale
    )
    cross_scores = jnp.where(text_allowed[:, None, None, :], cross_scores, masked_score)
    cross_peak = jnp.max(cross_scores, axis=-1, keepdims=True)
    cross_weights = jnp.exp(cross_scores - cross_peak)
    cross_probs = cross_weights / jnp.sum(cross_weights, axis=-1, keepdims=True)
    cross_probs_low = cross_probs.astype(jnp.bfloat16)
    cross_mixed = jnp.einsum(
        "shqk,skhd->sqhd", cross_probs_low, contents, preferred_element_type=jnp.float32
    )
    cross_mixed = cross_mixed.astype(jnp.bfloat16).reshape(row_count, width)
    after_cross = after_self + project(cross_mixed, merge_matrix).reshape(slots, frame_count, width)
    normed_three, pull_three = jax.vjp(
        layer_norm, after_cross, gain_feed.astype(jnp.float32), bias_feed.astype(jnp.float32)
    )
    hidden_three = normed_three.astype(jnp.bfloat16).reshape(row_count, width)
    upward = project(hidden_three, expand_matrix)
    activated, gelu_pull = jax.vjp(exact_gelu, upward)
    activated_low = activated.astype(jnp.bfloat16)
    result = after_cross + project(activated_low, reduce_matrix).reshape(slots, frame_count, width)
    output = result.astype(jnp.bfloat16)
    errors = (result - teacher.astype(jnp.float32)) * valid_rows[..., None]
    squares_total, count_total = lax.psum(
        (jnp.sum(errors * errors), jnp.sum(valid_rows)), ("replica", "shard")
    )
    loss = squares_total / (width * count_total)
    grad_result = errors * (slots * replicas * clip_total / count_total)
    grad_feed_low = grad_result.reshape(row_count, width).astype(jnp.bfloat16)
    grad_activated = back_project(grad_feed_low, reduce_matrix)
    grad_upward = gelu_pull(grad_activated)[0].astype(jnp.bfloat16)
    grad_hidden_three = back_project(grad_upward, expand_matrix).reshape(slots, frame_count, width)
    grad_cross_norm, gain_feed_part, bias_feed_part = pull_three(grad_hidden_three)
    grad_after_cross = grad_result + grad_cross_norm
    feed_owned = (
        lax.psum_scatter(
            outer_sum(hidden_three, grad_upward).astype(jnp.bfloat16),
            "shard",
            scatter_dimension=0,
            tiled=True,
        ).astype(jnp.float32),
        lax.psum_scatter(
            outer_sum(activated_low, grad_feed_low).astype(jnp.bfloat16),
            "shard",
            scatter_dimension=0,
            tiled=True,
        ).astype(jnp.float32),
        lax.psum_scatter(
            gain_feed_part.astype(jnp.bfloat16), "shard", scatter_dimension=0, tiled=True
        ).astype(jnp.float32),
        lax.psum_scatter(
            bias_feed_part.astype(jnp.bfloat16), "shard", scatter_dimension=0, tiled=True
        ).astype(jnp.float32),
    )
    grad_cross_low = grad_after_cross.reshape(row_count, width).astype(jnp.bfloat16)
    grad_cross_mixed = split_heads(
        back_project(grad_cross_low, merge_matrix)
        .astype(jnp.bfloat16)
        .reshape(slots, frame_count, width)
    )
    grad_cross_probs = jnp.einsum(
        "sqhd,skhd->shqk", grad_cross_mixed, contents, preferred_element_type=jnp.float32
    )
    content_grads = jnp.einsum(
        "shqk,sqhd->skhd", cross_probs_low, grad_cross_mixed, preferred_element_type=jnp.float32
    )
    cross_inner = jnp.sum(cross_probs * grad_cross_probs, axis=-1, keepdims=True)
    grad_cross_scores = (cross_probs * (grad_cross_probs - cross_inner)).astype(jnp.bfloat16)
    probe_grads = (
        jnp.einsum(
            "shqk,skhd->sqhd", grad_cross_scores, lookups, preferred_element_type=jnp.float32
        )
        * scale
    )
    probe_grads = probe_grads.astype(jnp.bfloat16).reshape(row_count, width)
    lookup_grads = (
        jnp.einsum("shqk,sqhd->skhd", grad_cross_scores, probes, preferred_element_type=jnp.float32)
        * scale
    )
    lookup_sum, content_sum = (
        lax.psum(lookup_grads.astype(jnp.bfloat16), "shard").astype(jnp.float32),
        lax.psum(content_grads.astype(jnp.bfloat16), "shard").astype(jnp.float32),
    )
    lookup_low = lookup_sum.astype(jnp.bfloat16).reshape(slots * text_len, width)
    content_low = content_sum.astype(jnp.bfloat16).reshape(slots * text_len, width)
    own_width = width // shards
    own_text = lax.dynamic_slice_in_dim(text_rows, shard_rank * own_width, own_width, 1)
    lookup_own = outer_sum(own_text, lookup_low)
    content_own = outer_sum(own_text, content_low)
    text_grad = (
        back_project(lookup_low, lookup_matrix) + back_project(content_low, content_matrix)
    ).reshape(slots, text_len, width)
    grad_hidden_two = back_project(probe_grads, probe_matrix).reshape(slots, frame_count, width)
    grad_self_norm, gain_cross_part, bias_cross_part = pull_two(grad_hidden_two)
    grad_after_self = grad_after_cross + grad_self_norm
    grad_self_low = grad_after_self.reshape(row_count, width).astype(jnp.bfloat16)
    grad_mixed = split_heads(
        back_project(grad_self_low, output_matrix)
        .astype(jnp.bfloat16)
        .reshape(slots, frame_count, width)
    )
    grad_queries, grad_keys, grad_values = lax.map(
        self_backward, (head_queries, head_keys, head_values, allowed, log_totals, grad_mixed)
    )
    key_sum, value_sum = (
        lax.psum_scatter(
            grad_keys.reshape(slots, clip_total, width).astype(jnp.bfloat16),
            "shard",
            scatter_dimension=1,
            tiled=True,
        ).astype(jnp.float32),
        lax.psum_scatter(
            grad_values.reshape(slots, clip_total, width).astype(jnp.bfloat16),
            "shard",
            scatter_dimension=1,
            tiled=True,
        ).astype(jnp.float32),
    )
    key_low = key_sum.astype(jnp.bfloat16).reshape(row_count, width)
    value_low = value_sum.astype(jnp.bfloat16).reshape(row_count, width)
    query_low = grad_queries.reshape(row_count, width)
    grad_hidden_one = (
        back_project(query_low, query_matrix)
        + back_project(key_low, key_matrix)
        + back_project(value_low, value_matrix)
    )
    grad_inputs, gain_attend_part, bias_attend_part = pull_one(
        grad_hidden_one.reshape(slots, frame_count, width)
    )
    frames_grad = grad_after_self + grad_inputs
    attend_owned = (
        lax.psum_scatter(
            outer_sum(hidden_one, query_low).astype(jnp.bfloat16),
            "shard",
            scatter_dimension=0,
            tiled=True,
        ).astype(jnp.float32),
        lax.psum_scatter(
            outer_sum(hidden_one, key_low).astype(jnp.bfloat16),
            "shard",
            scatter_dimension=0,
            tiled=True,
        ).astype(jnp.float32),
        lax.psum_scatter(
            outer_sum(hidden_one, value_low).astype(jnp.bfloat16),
            "shard",
            scatter_dimension=0,
            tiled=True,
        ).astype(jnp.float32),
        lax.psum_scatter(
            outer_sum(mixed_rows, grad_self_low).astype(jnp.bfloat16),
            "shard",
            scatter_dimension=0,
            tiled=True,
        ).astype(jnp.float32),
        lax.psum_scatter(
            outer_sum(hidden_two, probe_grads).astype(jnp.bfloat16),
            "shard",
            scatter_dimension=0,
            tiled=True,
        ).astype(jnp.float32),
        lax.psum_scatter(
            outer_sum(cross_mixed, grad_cross_low).astype(jnp.bfloat16),
            "shard",
            scatter_dimension=0,
            tiled=True,
        ).astype(jnp.float32),
        lax.psum_scatter(
            gain_attend_part.astype(jnp.bfloat16), "shard", scatter_dimension=0, tiled=True
        ).astype(jnp.float32),
        lax.psum_scatter(
            bias_attend_part.astype(jnp.bfloat16), "shard", scatter_dimension=0, tiled=True
        ).astype(jnp.float32),
        lax.psum_scatter(
            gain_cross_part.astype(jnp.bfloat16), "shard", scatter_dimension=0, tiled=True
        ).astype(jnp.float32),
        lax.psum_scatter(
            bias_cross_part.astype(jnp.bfloat16), "shard", scatter_dimension=0, tiled=True
        ).astype(jnp.float32),
    )
    summed = (
        lax.psum(attend_owned[6].astype(jnp.bfloat16), "replica").astype(jnp.float32),
        lax.psum(attend_owned[7].astype(jnp.bfloat16), "replica").astype(jnp.float32),
        lax.psum(attend_owned[0].astype(jnp.bfloat16), "replica").astype(jnp.float32),
        lax.psum(attend_owned[1].astype(jnp.bfloat16), "replica").astype(jnp.float32),
        lax.psum(attend_owned[2].astype(jnp.bfloat16), "replica").astype(jnp.float32),
        lax.psum(attend_owned[3].astype(jnp.bfloat16), "replica").astype(jnp.float32),
        lax.psum(attend_owned[8].astype(jnp.bfloat16), "replica").astype(jnp.float32),
        lax.psum(attend_owned[9].astype(jnp.bfloat16), "replica").astype(jnp.float32),
        lax.psum(attend_owned[4].astype(jnp.bfloat16), "replica").astype(jnp.float32),
        lax.psum(lookup_own.astype(jnp.bfloat16), "replica").astype(jnp.float32),
        lax.psum(content_own.astype(jnp.bfloat16), "replica").astype(jnp.float32),
        lax.psum(attend_owned[5].astype(jnp.bfloat16), "replica").astype(jnp.float32),
        lax.psum(feed_owned[2].astype(jnp.bfloat16), "replica").astype(jnp.float32),
        lax.psum(feed_owned[3].astype(jnp.bfloat16), "replica").astype(jnp.float32),
        lax.psum(feed_owned[0].astype(jnp.bfloat16), "replica").astype(jnp.float32),
        lax.psum(feed_owned[1].astype(jnp.bfloat16), "replica").astype(jnp.float32),
    )
    return (
        output,
        loss,
        frames_grad,
        text_grad,
        summed[0],
        summed[1],
        summed[2],
        summed[3],
        summed[4],
        summed[5],
        summed[6],
        summed[7],
        summed[8],
        summed[9],
        summed[10],
        summed[11],
        summed[12],
        summed[13],
        summed[14],
        summed[15],
    )


PAIR = 2 * HEAD_DIM
EVERY = ("shard", "y", "x", "core")
REPLICAS = ("core", "y", "x")
NT = (((1,), (1,)), ((), ()))
TN = (((0,), (0,)), ((), ()))
NN = (((1,), (0,)), ((), ()))


def dot(left, right, dims):
    return lax.dot_general(left, right, dims, preferred_element_type=jnp.float32)


def half_mask(side, value):
    lanes = lax.broadcasted_iota(jnp.int32, (1, PAIR), 1)
    inside = (lanes >= HEAD_DIM) if side else (lanes < HEAD_DIM)
    return jnp.where(inside, value, 0.0).astype(jnp.bfloat16)


def fill_clip(place, own_ref, other_ref, all_ref):
    block = own_ref.shape[0] // 2
    for part in range(2):
        rows = slice(part * block, (part + 1) * block)
        for at, ref in ((place[part], own_ref), (place[3 + part], other_ref)):
            all_ref[pl.ds(pl.multiple_of(at * block, block), block), :] = ref[rows, :]


def self_forward_kernel(
    place, q_ref, own_k, own_v, other_k, other_v, mixed_ref, lse_ref, k_ref, v_ref, acc_ref
):
    fill_clip(place, own_k, other_k, k_ref)
    fill_clip(place, own_v, other_v, v_ref)
    block = q_ref.shape[0] // 2
    length = place[2]
    low = lax.broadcasted_iota(jnp.int32, (PAIR, 1), 0) < HEAD_DIM
    for part in range(2):
        first = place[part] * block
        rows = slice(part * block, (part + 1) * block)
        q = q_ref[rows, :]
        q_half = [q * half_mask(side, HEAD_DIM ** (-0.5)) for side in range(2)]
        limit = jnp.minimum(
            first + lax.broadcasted_iota(jnp.int32, (1, block), 1) + 1, length
        )
        acc_ref[...] = jnp.zeros_like(acc_ref)

        def step(j, peaks, q_half=q_half, limit=limit):
            at = pl.multiple_of(j * block, block)
            k = k_ref[pl.ds(at, block), :]
            v = v_ref[pl.ds(at, block), :]
            allowed = at + lax.broadcasted_iota(jnp.int32, (block, block), 0) < limit
            out = []
            for side in range(2):
                scores = jnp.where(allowed, dot(k, q_half[side], NT), masked_score)
                peak = jnp.maximum(peaks[side], jnp.max(scores, axis=0, keepdims=True))
                weights = jnp.exp(scores - peak).astype(jnp.bfloat16)
                v_ones = v * half_mask(side, 1.0) + half_mask(1 - side, 1.0)
                acc_ref[side] = acc_ref[side] * jnp.exp(peaks[side] - peak) + dot(
                    v_ones, weights, TN
                )
                out.append(peak)
            return tuple(out)

        peaks = lax.fori_loop(
            0, place[part] + 1, step, (jnp.full((1, block), masked_score, jnp.float32),) * 2
        )
        top, bottom = acc_ref[0], acc_ref[1]
        total = jnp.where(low, top[HEAD_DIM : HEAD_DIM + 1], bottom[0:1])
        mixed = jnp.where(low, top, bottom) / total
        mixed_ref[rows, :] = mixed.T.astype(jnp.bfloat16)
        lse_ref[0:1, rows] = peaks[0] + jnp.log(top[HEAD_DIM : HEAD_DIM + 1])
        lse_ref[1:2, rows] = peaks[1] + jnp.log(bottom[0:1])


def self_backward_kernel(
    place, q_ref, own_k, own_v, other_k, other_v, mixed_ref, grad_ref, lse_ref,
    dq_ref, own_dk, own_dv, other_dk, other_dv, k_ref, v_ref, dq_acc, dk_acc, dv_acc,
):
    fill_clip(place, own_k, other_k, k_ref)
    fill_clip(place, own_v, other_v, v_ref)
    block = q_ref.shape[0] // 2
    length = place[2]
    scale = HEAD_DIM ** (-0.5)
    dk_acc[...] = jnp.zeros_like(dk_acc)
    dv_acc[...] = jnp.zeros_like(dv_acc)
    for part in range(2):
        first = place[part] * block
        rows = slice(part * block, (part + 1) * block)
        q = q_ref[rows, :]
        grad = grad_ref[rows, :]
        q_half = [q * half_mask(side, scale) for side in range(2)]
        grad_half = [grad * half_mask(side, 1.0) for side in range(2)]
        product = (grad.astype(jnp.float32) * mixed_ref[rows, :].astype(jnp.float32)).T
        inner = [
            jnp.sum(product[side * HEAD_DIM : (side + 1) * HEAD_DIM], axis=0, keepdims=True)
            for side in range(2)
        ]
        lse = [lse_ref[side : side + 1, rows] for side in range(2)]
        limit = jnp.minimum(
            first + lax.broadcasted_iota(jnp.int32, (1, block), 1) + 1, length
        )
        dq_acc[...] = jnp.zeros_like(dq_acc)

        def step(
            j, carry, q_half=q_half, grad_half=grad_half, inner=inner, lse=lse, limit=limit
        ):
            at = pl.multiple_of(j * block, block)
            k = k_ref[pl.ds(at, block), :]
            v = v_ref[pl.ds(at, block), :]
            allowed = at + lax.broadcasted_iota(jnp.int32, (block, block), 0) < limit
            dq, dk, dv = 0.0, 0.0, 0.0
            for side in range(2):
                scores = jnp.where(allowed, dot(k, q_half[side], NT), masked_score)
                probs = jnp.exp(scores - lse[side])
                grad_probs = dot(v, grad_half[side], NT)
                grad_scores = (probs * (grad_probs - inner[side])).astype(jnp.bfloat16)
                dv += dot(probs.astype(jnp.bfloat16), grad_half[side], NN)
                dk += dot(grad_scores, q_half[side], NN)
                dq += dot(k * half_mask(side, scale), grad_scores, TN)
            dk_acc[pl.ds(at, block), :] += dk
            dv_acc[pl.ds(at, block), :] += dv
            dq_acc[...] += dq
            return carry

        lax.fori_loop(0, place[part] + 1, step, 0)
        dq_ref[rows, :] = dq_acc[...].T.astype(jnp.bfloat16)
    for part in range(2):
        rows = slice(part * block, (part + 1) * block)
        own = pl.ds(pl.multiple_of(place[part] * block, block), block)
        other = pl.ds(pl.multiple_of(place[3 + part] * block, block), block)
        own_dk[rows, :] = dk_acc[own, :].astype(jnp.bfloat16)
        own_dv[rows, :] = dv_acc[own, :].astype(jnp.bfloat16)
        other_dk[rows, :] = dk_acc[other, :].astype(jnp.bfloat16)
        other_dv[rows, :] = dv_acc[other, :].astype(jnp.bfloat16)


def pair_block(rows):
    return pl.BlockSpec((rows, PAIR), lambda i, *_: (0, i))


def value_block(rows, pairs):
    return pl.BlockSpec((rows, PAIR), lambda i, *_: (0, pairs + i))


def self_attend(place, queries, own, other):
    rows, width = queries.shape
    clip = 2 * rows
    pairs = width // PAIR
    return pl.pallas_call(
        self_forward_kernel,
        out_shape=(
            jax.ShapeDtypeStruct((rows, width), jnp.bfloat16),
            jax.ShapeDtypeStruct((pairs * 8, rows), jnp.float32),
        ),
        grid_spec=pltpu.PrefetchScalarGridSpec(
            num_scalar_prefetch=1,
            grid=(pairs,),
            in_specs=[pair_block(rows)] + [pair_block(rows), value_block(rows, pairs)] * 2,
            out_specs=(pair_block(rows), pl.BlockSpec((8, rows), lambda i, *_: (i, 0))),
            scratch_shapes=[
                pltpu.VMEM((clip, PAIR), jnp.bfloat16),
                pltpu.VMEM((clip, PAIR), jnp.bfloat16),
                pltpu.VMEM((2, PAIR, rows // 2), jnp.float32),
            ],
        ),
        compiler_params=pltpu.CompilerParams(vmem_limit_bytes=32 * 2**20),
        cost_estimate=pl.CostEstimate(
            flops=2 * 2 * rows * clip * width, bytes_accessed=8 * clip * width, transcendentals=0
        ),
        name="self_attend",
    )(place, queries, own, own, other, other)


def self_attend_back(place, queries, own, other, mixed, grads, lse):
    rows, width = queries.shape
    clip = 2 * rows
    pairs = width // PAIR
    return pl.pallas_call(
        self_backward_kernel,
        out_shape=(jax.ShapeDtypeStruct((rows, width), jnp.bfloat16),) * 5,
        grid_spec=pltpu.PrefetchScalarGridSpec(
            num_scalar_prefetch=1,
            grid=(pairs,),
            in_specs=[pair_block(rows)]
            + [pair_block(rows), value_block(rows, pairs)] * 2
            + [
                pair_block(rows),
                pair_block(rows),
                pl.BlockSpec((8, rows), lambda i, *_: (i, 0)),
            ],
            out_specs=(pair_block(rows),) * 5,
            scratch_shapes=[
                pltpu.VMEM((clip, PAIR), jnp.bfloat16),
                pltpu.VMEM((clip, PAIR), jnp.bfloat16),
                pltpu.VMEM((PAIR, rows // 2), jnp.float32),
                pltpu.VMEM((clip, PAIR), jnp.float32),
                pltpu.VMEM((clip, PAIR), jnp.float32),
            ],
        ),
        compiler_params=pltpu.CompilerParams(vmem_limit_bytes=32 * 2**20),
        cost_estimate=pl.CostEstimate(
            flops=5 * 2 * rows * clip * width, bytes_accessed=16 * clip * width, transcendentals=0
        ),
        name="self_attend_back",
    )(place, queries, own, own, other, other, mixed, grads, lse)


def both_heads(rows, value):
    return jnp.concatenate([rows * half_mask(side, value) for side in range(2)], axis=0)


def cross_probs_of(lookup_two, probes, present):
    text = present.shape[0]
    scores = dot(lookup_two, probes, NT)
    out = []
    for side in range(2):
        part = jnp.where(
            present > 0, scores[side * text : (side + 1) * text], masked_score
        )
        weights = jnp.exp(part - jnp.max(part, axis=0, keepdims=True))
        out.append(weights / jnp.sum(weights, axis=0, keepdims=True))
    return out


def cross_forward_kernel(probe_ref, lookup_ref, content_ref, present_ref, mixed_ref):
    probs = cross_probs_of(
        both_heads(lookup_ref[...], HEAD_DIM ** (-0.5)), probe_ref[...], present_ref[...]
    )
    probs = jnp.concatenate(probs, axis=0).astype(jnp.bfloat16)
    mixed_ref[...] = dot(probs, both_heads(content_ref[...], 1.0), TN).astype(jnp.bfloat16)


def cross_backward_kernel(
    probe_ref, lookup_ref, content_ref, present_ref, grad_ref, dp_ref, dl_ref, dc_ref
):
    text = present_ref.shape[0]
    scale = HEAD_DIM ** (-0.5)
    probes = probe_ref[...]
    grads = grad_ref[...]
    lookup_two = both_heads(lookup_ref[...], scale)
    probs = cross_probs_of(lookup_two, probes, present_ref[...])
    grad_probs = dot(both_heads(content_ref[...], 1.0), grads, NT)
    grad_scores = []
    for side in range(2):
        part = grad_probs[side * text : (side + 1) * text]
        inner = jnp.sum(probs[side] * part, axis=0, keepdims=True)
        grad_scores.append(probs[side] * (part - inner))
    grad_scores = jnp.concatenate(grad_scores, axis=0).astype(jnp.bfloat16)
    probs = jnp.concatenate(probs, axis=0).astype(jnp.bfloat16)
    low = lax.broadcasted_iota(jnp.int32, (1, PAIR), 1) < HEAD_DIM
    dp_ref[...] = dot(grad_scores, lookup_two, TN).astype(jnp.bfloat16)
    dl = dot(grad_scores, probes, NN) * scale
    dl_ref[...] = jnp.where(low, dl[:text], dl[text:]).astype(jnp.bfloat16)
    dc = dot(probs, grads, NN)
    dc_ref[...] = jnp.where(low, dc[:text], dc[text:]).astype(jnp.bfloat16)


def cross_attend(probes, lookups, contents, present):
    rows, width = probes.shape
    text = lookups.shape[0]
    return pl.pallas_call(
        cross_forward_kernel,
        out_shape=jax.ShapeDtypeStruct((rows, width), jnp.bfloat16),
        grid=(width // PAIR,),
        in_specs=[
            pair_block(rows),
            pair_block(text),
            pair_block(text),
            pl.BlockSpec((text, 1), lambda i: (0, 0)),
        ],
        out_specs=pair_block(rows),
        compiler_params=pltpu.CompilerParams(vmem_limit_bytes=32 * 2**20),
        cost_estimate=pl.CostEstimate(
            flops=8 * rows * text * width, bytes_accessed=4 * rows * width, transcendentals=0
        ),
        name="cross_attend",
    )(probes, lookups, contents, present)


def cross_attend_back(probes, lookups, contents, present, grads):
    rows, width = probes.shape
    text = lookups.shape[0]
    return pl.pallas_call(
        cross_backward_kernel,
        out_shape=(
            jax.ShapeDtypeStruct((rows, width), jnp.bfloat16),
            jax.ShapeDtypeStruct((text, width), jnp.bfloat16),
            jax.ShapeDtypeStruct((text, width), jnp.bfloat16),
        ),
        grid=(width // PAIR,),
        in_specs=[
            pair_block(rows),
            pair_block(text),
            pair_block(text),
            pl.BlockSpec((text, 1), lambda i: (0, 0)),
            pair_block(rows),
        ],
        out_specs=(pair_block(rows), pair_block(text), pair_block(text)),
        compiler_params=pltpu.CompilerParams(vmem_limit_bytes=32 * 2**20),
        cost_estimate=pl.CostEstimate(
            flops=20 * rows * text * width, bytes_accessed=6 * rows * width, transcendentals=0
        ),
        name="cross_attend_back",
    )(probes, lookups, contents, present, grads)


def unpack_kernel(in_ref, out_ref):
    pieces = in_ref[...]
    out_ref[...] = pieces.reshape(-1, pieces.shape[-1]).T.astype(jnp.float32)


def unpack(full, rows, place, out_shape, out_at, together):
    owners, _, features = full.shape
    tall = out_shape[0] // features
    wide = out_shape[1] // (together * rows)
    return pl.pallas_call(
        unpack_kernel,
        out_shape=jax.ShapeDtypeStruct(out_shape, jnp.float32),
        grid=(tall, wide),
        in_specs=[
            pl.BlockSpec((together, rows, features), lambda i, j: (j + out_at, place + i, 0))
        ],
        out_specs=pl.BlockSpec((features, together * rows), lambda i, j: (i, j)),
        compiler_params=pltpu.CompilerParams(vmem_limit_bytes=32 * 2**20),
        cost_estimate=pl.CostEstimate(
            flops=0, bytes_accessed=6 * out_shape[0] * out_shape[1], transcendentals=0
        ),
        name="unpack",
    )(full)


def held(values, *others):
    return list(lax.optimization_barrier((*values, *others))[: len(values)])


def after(value, *others):
    return lax.optimization_barrier((value, *others))[0]


def norm_parts(values):
    mean = jnp.mean(values, axis=-1, keepdims=True)
    center = values - mean
    return mean, lax.rsqrt(jnp.mean(center * center, axis=-1, keepdims=True) + epsilon)


def norm_back(grads, values, parts, gain):
    mean, inverse = parts
    unit = (values - mean) * inverse
    gain_grad = jnp.sum(grads * unit, axis=0)
    bias_grad = jnp.sum(grads, axis=0)
    scaled = grads * gain
    back = inverse * (
        scaled
        - jnp.mean(scaled, axis=-1, keepdims=True)
        - unit * jnp.mean(scaled * unit, axis=-1, keepdims=True)
    )
    return back, gain_grad, bias_grad


def clip_body(
    frames,
    text_states,
    text_mask,
    clip_lengths,
    slot_used,
    teacher,
    self_norm_gain,
    self_norm_bias,
    self_query_weight,
    self_key_weight,
    self_value_weight,
    self_output_weight,
    cross_norm_gain,
    cross_norm_bias,
    cross_query_weight,
    cross_key_weight,
    cross_value_weight,
    cross_output_weight,
    feed_norm_gain,
    feed_norm_bias,
    feed_up_weight,
    feed_down_weight,
):
    block, width = frames.shape[1:]
    text_len = text_states.shape[1]
    shards, replicas, outers = 4, 8, 4
    core = lax.axis_index("core")
    shard = lax.axis_index("shard")
    outer = 2 * lax.axis_index("y") + lax.axis_index("x")
    replica = 2 * outer + core
    clip = block * shards
    hidden_units = feed_up_weight.shape[1]

    holder = {0: 0, 1: 1, 2: 1, 3: 0}
    there = ([], [])
    for c in range(2):
        for s in range(4):
            for turn in range(2):
                slot = turn if s < 2 else 1 - turn
                there[turn].append((c * 4 + s, holder[s] * 4 + 2 * c + slot))
    back = tuple([(b, a) for a, b in pairs] for pairs in there)
    spot = ("core", "shard")
    swap = [(0, 1), (1, 0)]
    even = shard % 2 == 0
    lower = shard < 2
    first_core = core == 0

    def hop(values, distance):
        pairs = [(i, (i + distance) % shards) for i in range(shards)]
        return lax.ppermute(values, "shard", pairs)

    def hops(values):
        return [hop(values, distance) for distance in (1, 2, 3)]

    def line_up(mine, came):
        out = jnp.zeros((shards,) + mine.shape, mine.dtype)
        out = lax.dynamic_update_index_in_dim(out, mine, shard, 0)
        for distance, values in zip((1, 2, 3), came):
            owner = lax.rem(shard + shards - distance, shards)
            out = lax.dynamic_update_index_in_dim(out, values, owner, 0)
        return out

    def to_chip(pair):
        one = lax.ppermute(jnp.where(lower, pair[0], pair[1]), spot, there[0])
        two = lax.ppermute(jnp.where(lower, pair[1], pair[0]), spot, there[1])
        return one, two

    def by_time(one, two):
        return jnp.concatenate([jnp.where(even, one, two), jnp.where(even, two, one)], axis=0)

    def outgoing(values):
        early, late = values[:block], values[block:]
        return jnp.where(even, early, late), jnp.where(even, late, early)

    def from_chip(values):
        one, two = outgoing(values)
        return lax.ppermute(one, spot, back[0]), lax.ppermute(two, spot, back[1])

    def by_slot(one, two):
        return jnp.stack([jnp.where(lower, one, two), jnp.where(lower, two, one)])

    def share_of(weight):
        share = weight.shape[0] // replicas
        return lax.dynamic_slice_in_dim(weight, replica * share, share, 0)

    def from_replicas(line):
        full = lax.all_gather(line, ("y", "x", "core"), axis=1, tiled=True)
        return full.reshape(-1, line.shape[-1])

    qkv_share = jnp.concatenate(
        [share_of(self_query_weight), share_of(self_key_weight), share_of(self_value_weight)],
        axis=1,
    )
    vectors = jnp.concatenate(
        [
            self_norm_gain,
            self_norm_bias,
            cross_norm_gain,
            cross_norm_bias,
            feed_norm_gain,
            feed_norm_bias,
        ]
    )
    vectors = jnp.pad(vectors[None, :], ((0, 15), (0, 3 * width - 6 * block)))
    share = qkv_share.shape[0]
    qkv_mine = jnp.concatenate([qkv_share, vectors], axis=0)
    qkv_came = hops(qkv_mine)
    qkv_matrix = from_replicas(line_up(qkv_share, [values[:share] for values in qkv_came]))
    norms = line_up(vectors[0], [values[share] for values in qkv_came])
    norms = norms[:, : 6 * block].reshape(shards, 6, block).transpose(1, 0, 2)
    norms = norms.reshape(6, width).astype(jnp.float32)
    rest_share = jnp.concatenate(
        [share_of(self_output_weight), share_of(cross_query_weight), share_of(cross_output_weight)],
        axis=1,
    )
    rest_came = hops(after(rest_share, *qkv_came))
    rest = from_replicas(line_up(rest_share, rest_came))
    came = to_chip(after(frames, *rest_came))
    x_low = by_time(*came)
    expand_share = share_of(feed_up_weight)
    expand_came = hops(after(expand_share, *came))

    facts = jnp.concatenate(
        [(clip_lengths // 64)[:, None], (clip_lengths % 64)[:, None], slot_used[:, None], text_mask],
        axis=1,
    ).astype(jnp.bfloat16)
    facts = jnp.pad(facts[:, None, :], ((0, 0), (0, 15), (0, width - facts.shape[1])))
    text_sent = lax.ppermute(jnp.concatenate([text_states, facts], axis=1), "core", swap)
    text_other = text_sent[:, :text_len]
    both = jnp.stack([facts[:, 0], text_sent[:, text_len]])[:, :, : 3 + text_len].astype(jnp.int32)
    lengths = 64 * both[:, :, 0] + both[:, :, 1]
    fact = lax.dynamic_index_in_dim(
        jnp.where(shard // 2 == core, both[0], both[1]), shard % 2, 0, keepdims=False
    )
    length, used = 64 * fact[0] + fact[1], fact[2]
    present = fact[3:].reshape(text_len, 1)
    count = jnp.sum(
        jnp.where(both[:, :, 2] > 0, jnp.minimum(lengths, clip), 0).astype(jnp.float32)
    )
    count = jnp.full((8, 128), count)
    for axis in ("x", "y"):
        count += lax.ppermute(count, axis, swap)
    count = count[0, 0]
    text_all = jnp.concatenate(
        [
            jnp.where(first_core, text_states, text_other),
            jnp.where(first_core, text_other, text_states),
        ],
        axis=0,
    ).reshape(4 * text_len, width)
    text_all = lax.dynamic_slice_in_dim(text_all, shard * block, block, 1)
    text_matrix = jnp.where(first_core, cross_key_weight, cross_value_weight)
    text_part = project(text_all, text_matrix).astype(jnp.bfloat16).reshape(4, text_len, width)
    text_came = [
        hop(
            lax.dynamic_index_in_dim(
                text_part, lax.rem(shard + distance, shards), 0, keepdims=False
            ),
            distance,
        )
        for distance in (1, 2, 3)
    ]

    places = jnp.stack([core, 3 - core, length, 1 - core, 2 + core]).astype(jnp.int32)
    positions = jnp.concatenate(
        [core * block + jnp.arange(block), (3 - core) * block + jnp.arange(block)]
    )
    valid_rows = ((positions < length) & (used > 0)).astype(jnp.float32)[:, None]
    inputs = x_low.astype(jnp.float32)
    parts_one = norm_parts(inputs)
    hidden_one = ((inputs - parts_one[0]) * parts_one[1] * norms[0] + norms[1]).astype(
        jnp.bfloat16
    )
    kv = project(after(hidden_one, count), qkv_matrix[:, width:]).astype(jnp.bfloat16)
    kv_other = lax.ppermute(kv, "core", swap)
    expand_came = held(expand_came, kv)
    queries = project(after(hidden_one, kv, *expand_came), qkv_matrix[:, :width])
    queries = queries.astype(jnp.bfloat16)
    expand_matrix = from_replicas(line_up(expand_share, expand_came))
    reduce_share = share_of(feed_down_weight)
    reduce_came = hops(after(reduce_share, *expand_came))
    output_matrix = rest[:, :width]
    probe_matrix = rest[:, width : 2 * width]
    merge_matrix = rest[:, 2 * width :]
    mixed_self, lse = self_attend(after(places, *expand_came), queries, kv, kv_other)
    reduce_came = held(reduce_came, mixed_self)
    reduce_matrix = from_replicas(line_up(reduce_share, reduce_came))
    text_came = held(text_came, mixed_self)
    text_half = lax.dynamic_index_in_dim(text_part, shard, 0, keepdims=False).astype(jnp.float32)
    for values in text_came:
        text_half += values.astype(jnp.float32)
    text_half = text_half.astype(jnp.bfloat16)
    text_swap = lax.ppermute(text_half, "core", swap)
    lookups = jnp.where(first_core, text_half, text_swap)
    contents = jnp.where(first_core, text_swap, text_half)
    after_self = inputs + project(mixed_self, output_matrix)
    parts_two = norm_parts(after_self)
    hidden_two = ((after_self - parts_two[0]) * parts_two[1] * norms[2] + norms[3]).astype(
        jnp.bfloat16
    )
    probes = project(hidden_two, probe_matrix).astype(jnp.bfloat16)
    teacher_came = to_chip(after(teacher, *reduce_came, probes))
    cross_mixed = cross_attend(probes, lookups, contents, present)
    after_cross = after_self + project(cross_mixed, merge_matrix)
    parts_three = norm_parts(after_cross)
    hidden_three = (
        (after_cross - parts_three[0]) * parts_three[1] * norms[4] + norms[5]
    ).astype(jnp.bfloat16)
    upward = project(hidden_three, expand_matrix)
    activated, gelu_pull = jax.vjp(exact_gelu, upward)
    activated_low = activated.astype(jnp.bfloat16)
    teacher_low = by_time(*held(teacher_came, activated_low))
    result = after_cross + project(activated_low, reduce_matrix)
    errors = (result - teacher_low.astype(jnp.float32)) * valid_rows
    squares = jnp.sum(errors * errors)
    grad_result = errors * (4 * outers * clip / count)
    grad_feed_low = grad_result.astype(jnp.bfloat16)

    def theirs_of(right, left):
        columns = right.shape[1] // 2
        part = lax.dynamic_slice_in_dim(right, (1 - core) * columns, columns, 1)
        return outer_sum(part, left).astype(jnp.bfloat16)

    def ours_of(right, left, theirs):
        columns = right.shape[1] // 2
        sent = lax.ppermute(theirs, "core", swap)
        part = lax.dynamic_slice_in_dim(right, core * columns, columns, 1)
        return (outer_sum(part, left) + sent.astype(jnp.float32)).astype(jnp.bfloat16)

    def over_outer(values):
        return lax.psum_scatter(values, ("y", "x"), scatter_dimension=0, tiled=True)

    def shard_hops(values):
        columns = values.shape[1] // shards
        return [
            hop(
                lax.dynamic_slice_in_dim(
                    values, lax.rem(shard + distance, shards) * columns, columns, 1
                ),
                distance,
            )
            for distance in (1, 2, 3)
        ]

    def over_shard(values, came):
        columns = values.shape[1] // shards
        total = lax.dynamic_slice_in_dim(values, shard * columns, columns, 1).astype(jnp.float32)
        for part in came:
            total += part.astype(jnp.float32)
        return total.astype(jnp.bfloat16)

    down_theirs = theirs_of(grad_feed_low, activated_low)
    to_send = outgoing(result.astype(jnp.bfloat16))
    output_one = lax.ppermute(to_send[0], spot, back[0])
    grad_activated = back_project(after(grad_feed_low, down_theirs), reduce_matrix)
    grad_upward = gelu_pull(grad_activated)[0].astype(jnp.bfloat16)
    output_one = after(output_one, grad_upward)
    down_ours = ours_of(
        after(grad_feed_low, grad_upward, output_one), activated_low, down_theirs
    )
    down_sum = over_outer(down_ours)
    up_theirs = theirs_of(after(grad_upward, down_ours), hidden_three)
    grad_hidden_three = back_project(after(grad_upward, up_theirs), expand_matrix)
    output_two = lax.ppermute(after(to_send[1], output_one), spot, back[1])
    output_two = after(output_two, grad_hidden_three)
    output = by_slot(output_one, output_two)
    up_ours = ours_of(after(grad_upward, grad_hidden_three, output_two), hidden_three, up_theirs)
    grad_norm, gain_feed, bias_feed = norm_back(
        after(grad_hidden_three, up_ours), after_cross, parts_three, norms[4]
    )
    grad_after_cross = grad_result + grad_norm
    grad_cross_low = grad_after_cross.astype(jnp.bfloat16)
    merge_theirs = theirs_of(grad_cross_low, cross_mixed)
    grad_cross_mixed = back_project(after(grad_cross_low, merge_theirs), merge_matrix).astype(
        jnp.bfloat16
    )
    probe_grads, lookup_grads, content_grads = cross_attend_back(
        probes, lookups, contents, present, grad_cross_mixed
    )
    up_sum = over_outer(up_ours)
    text_mine = jnp.where(first_core, lookup_grads, content_grads)
    text_sent = lax.ppermute(
        jnp.where(first_core, content_grads, lookup_grads), "core", swap
    )
    text_mine = (text_mine.astype(jnp.float32) + text_sent.astype(jnp.float32)).astype(
        jnp.bfloat16
    )
    merge_ours = ours_of(after(grad_cross_low, probe_grads), cross_mixed, merge_theirs)
    probe_theirs = theirs_of(after(probe_grads, merge_ours), hidden_two)
    grad_hidden_two = back_project(after(probe_grads, probe_theirs), probe_matrix)
    text_four = line_up(text_mine, hops(text_mine)).reshape(4 * text_len, width)
    grad_norm, gain_cross, bias_cross = norm_back(
        grad_hidden_two, after_self, parts_two, norms[2]
    )
    grad_after_self = grad_after_cross + grad_norm
    grad_self_low = grad_after_self.astype(jnp.bfloat16)
    output_theirs = theirs_of(grad_self_low, mixed_self)
    grad_mixed = back_project(after(grad_self_low, output_theirs), output_matrix).astype(
        jnp.bfloat16
    )
    probe_ours = ours_of(after(probe_grads, grad_mixed), hidden_two, probe_theirs)
    text_weights = outer_sum(text_four, text_all).astype(jnp.bfloat16)
    text_back = back_project(text_four, text_matrix).astype(jnp.bfloat16)
    output_ours = ours_of(after(grad_self_low, probe_ours), mixed_self, output_theirs)
    text_rows = width // outers
    middle = jnp.concatenate(
        [
            values.reshape(outers, -1, width)
            for values in (
                output_ours,
                probe_ours,
                merge_ours,
                text_weights.reshape(outers, shards, text_rows // shards, block)
                .transpose(0, 2, 1, 3)
                .reshape(outers, text_rows // shards, width),
            )
        ],
        axis=1,
    )
    middle_rows = middle.shape[1]
    middle = middle.reshape(outers * middle_rows, width)
    middle_sum = over_outer(middle)
    text_split = text_rows // shards
    text_piece = (
        middle_sum[middle_rows - text_split :]
        .reshape(text_split, shards, block)
        .transpose(1, 0, 2)
        .reshape(text_rows, block)
    )
    text_back = text_back.reshape(2, 2, text_len, block)
    text_kept = lax.dynamic_index_in_dim(text_back, core, 0, keepdims=False)
    text_gone = lax.dynamic_index_in_dim(text_back, 1 - core, 0, keepdims=False)
    text_own = text_kept.astype(jnp.float32) + lax.ppermute(text_gone, "core", swap).astype(
        jnp.float32
    )
    text_own = text_own.astype(jnp.bfloat16)
    down_came = shard_hops(down_sum)
    text_came = hops(text_own)
    grad_queries, own_keys, own_values, other_keys, other_values = self_attend_back(
        places, queries, kv, kv_other, mixed_self, after(grad_mixed, middle, text_own), lse
    )
    text_came = held(text_came, grad_queries)
    down_came = held(down_came, grad_queries)
    other_keys, other_values = held([other_keys, other_values], *text_came, *down_came)
    own_keys += lax.ppermute(other_keys, "core", swap)
    own_values += lax.ppermute(other_values, "core", swap)
    down_piece = over_shard(down_sum, down_came)
    up_came = shard_hops(after(up_sum, down_piece))

    qkv_grads = jnp.concatenate([grad_queries, own_keys, own_values], axis=1)
    qkv_theirs = theirs_of(qkv_grads, hidden_one)
    grad_hidden_one = back_project(after(qkv_grads, qkv_theirs), qkv_matrix)
    qkv_ours = ours_of(after(qkv_grads, grad_hidden_one), hidden_one, qkv_theirs)
    up_came = held(up_came, grad_hidden_one)
    up_piece = over_shard(up_sum, up_came)
    text_grad = line_up(text_own, text_came).astype(jnp.float32)
    text_grad = text_grad.transpose(1, 2, 0, 3).reshape(text_states.shape)
    qkv_sum = over_outer(qkv_ours)
    grad_norm, gain_self, bias_self = norm_back(
        after(grad_hidden_one, qkv_ours, *up_came), inputs, parts_one, norms[0]
    )
    middle_kept = after(middle_sum[: middle_rows - text_split], qkv_ours, *up_came)
    middle_came = shard_hops(middle_kept)
    small = jnp.stack(
        [
            gain_self,
            bias_self,
            gain_cross,
            bias_cross,
            gain_feed,
            bias_feed,
            jnp.full((width,), squares),
            jnp.zeros((width,), jnp.float32),
        ]
    )
    for axis in ("core", "x", "y"):
        small += lax.ppermute(small, axis, swap)
    middle_came = held(middle_came, small)
    middle_piece = over_shard(middle_kept, middle_came)
    late_came = shard_hops(after(qkv_sum, *middle_came))
    small_came = shard_hops(small)
    small_own = lax.dynamic_slice_in_dim(small, shard * block, block, 1)
    for part in small_came:
        small_own += part
    loss = small_own[6, 0] / (width * count)
    frames_came = from_chip(
        after((grad_after_self + grad_norm).astype(jnp.bfloat16), *late_came, *small_came)
    )
    frames_grad = by_slot(*frames_came).astype(jnp.float32)

    early = jnp.concatenate(
        [up_piece]
        + [down_piece[:, i * block : (i + 1) * block] for i in range(4)]
        + [text_piece, middle_piece],
        axis=0,
    )
    early = lax.all_gather(after(early, text_grad), REPLICAS, axis=0)
    piece = width // replicas
    square = (block, width)
    up_grad = unpack(early, hidden_units // replicas, 0, (block, hidden_units), 0, 1)
    at = hidden_units // replicas // piece
    down_grad = unpack(early, piece, at, (4 * block, width), 0, 2)
    at += 4
    key_grad = unpack(early, text_rows, at * piece // text_rows, square, 0, 1)
    value_grad = unpack(early, text_rows, at * piece // text_rows, square, 4, 1)
    at += text_rows // piece
    output_grad = unpack(early, piece, at, square, 0, 2)
    probe_grad = unpack(early, piece, at + 1, square, 0, 2)
    merge_grad = unpack(early, piece, at + 2, square, 0, 2)
    late = over_shard(qkv_sum, late_came)
    late = lax.all_gather(after(late, early, *frames_came), REPLICAS, axis=0, tiled=True)
    late = late.reshape(-1, block, block)
    qkv_grad = [unpack(late, block, 0, square, 2 * i, 2) for i in range(3)]
    return (
        output,
        loss,
        frames_grad,
        text_grad,
        small_own[0],
        small_own[1],
        qkv_grad[0],
        qkv_grad[1],
        qkv_grad[2],
        output_grad,
        small_own[2],
        small_own[3],
        probe_grad,
        key_grad,
        value_grad,
        merge_grad,
        small_own[4],
        small_own[5],
        up_grad,
        down_grad,
    )


def solution(mesh):
    by_chip = mesh.shape["shard"] == 4 and mesh.shape["replica"] == 8
    replica = ("y", "x", "core") if by_chip else "replica"
    row = P(replica)
    clip = P(replica, "shard", None)
    text = P(replica, None, None)
    vector = P("shard")
    matrix = P("shard", None)
    weights = (
        [vector, vector] + [matrix] * 4 + [vector, vector] + [matrix] * 4 + [vector, vector]
        + [matrix] * 2
    )
    if by_chip:
        mesh = Mesh(mesh.devices.reshape(2, 2, 2, 4), ("y", "x", "core", "shard"))
    return jax.shard_map(
        clip_body if by_chip else general_body,
        mesh=mesh,
        in_specs=(clip, text, P(replica, None), row, row, clip, *weights),
        out_specs=(clip, P(), clip, text, *weights),
        check_vma=False,
    )
```

```python
import jax
import jax.numpy as jnp
from jax import lax
from jax.experimental import pallas as pl
from jax.experimental.pallas import tpu as pltpu
from jax.sharding import Mesh
from jax.sharding import PartitionSpec as P

HEADS = 24
HEAD_DIM = 64


epsilon = 1e-05
masked_score = -1e30


def layer_norm(values, gain, shift):
    center = values - jnp.mean(values, axis=-1, keepdims=True)
    variance = jnp.mean(center * center, axis=-1, keepdims=True)
    return center * lax.rsqrt(variance + epsilon) * gain + shift


def exact_gelu(values):
    return jax.nn.gelu(values, approximate=False)


def project(left, right):
    return jnp.dot(left, right, preferred_element_type=jnp.float32)


def outer_sum(left, right):
    return jnp.einsum("rd,re->de", left, right, preferred_element_type=jnp.float32)


def back_project(grads, matrix):
    return jnp.einsum("re,de->rd", grads, matrix, preferred_element_type=jnp.float32)


def split_heads(values):
    return values.reshape(values.shape[:-1] + (HEADS, HEAD_DIM))


def self_forward(operands):
    queries, keys_all, values_all, allowed = operands
    scale = HEAD_DIM ** (-0.5)
    scores = (
        jnp.einsum("qhd,khd->hqk", queries, keys_all, preferred_element_type=jnp.float32) * scale
    )
    scores = jnp.where(allowed[None], scores, masked_score)
    peak = jnp.max(scores, axis=-1, keepdims=True)
    weights = jnp.exp(scores - peak)
    totals = jnp.sum(weights, axis=-1, keepdims=True)
    probs = (weights / totals).astype(jnp.bfloat16)
    mixed = jnp.einsum("hqk,khd->qhd", probs, values_all, preferred_element_type=jnp.float32)
    return (mixed.astype(jnp.bfloat16), (peak + jnp.log(totals))[..., 0])


def self_backward(operands):
    queries, keys_all, values_all, allowed, log_totals, grad_mixed = operands
    scale = HEAD_DIM ** (-0.5)
    scores = (
        jnp.einsum("qhd,khd->hqk", queries, keys_all, preferred_element_type=jnp.float32) * scale
    )
    scores = jnp.where(allowed[None], scores, masked_score)
    probs = jnp.exp(scores - log_totals[..., None])
    grad_probs = jnp.einsum(
        "qhd,khd->hqk", grad_mixed, values_all, preferred_element_type=jnp.float32
    )
    grad_values = jnp.einsum(
        "hqk,qhd->khd", probs.astype(jnp.bfloat16), grad_mixed, preferred_element_type=jnp.float32
    )
    inner = jnp.sum(probs * grad_probs, axis=-1, keepdims=True)
    grad_scores = (probs * (grad_probs - inner)).astype(jnp.bfloat16)
    grad_queries = (
        jnp.einsum("hqk,khd->qhd", grad_scores, keys_all, preferred_element_type=jnp.float32)
        * scale
    ).astype(jnp.bfloat16)
    grad_keys = (
        jnp.einsum("hqk,qhd->khd", grad_scores, queries, preferred_element_type=jnp.float32) * scale
    )
    return (grad_queries, grad_keys, grad_values)


def general_body(
    frames,
    text_states,
    text_mask,
    clip_lengths,
    slot_used,
    teacher,
    self_norm_gain,
    self_norm_bias,
    self_query_weight,
    self_key_weight,
    self_value_weight,
    self_output_weight,
    cross_norm_gain,
    cross_norm_bias,
    cross_query_weight,
    cross_key_weight,
    cross_value_weight,
    cross_output_weight,
    feed_norm_gain,
    feed_norm_bias,
    feed_up_weight,
    feed_down_weight,
):
    gathered = (
        lax.all_gather(self_norm_gain, "shard", axis=0, tiled=True),
        lax.all_gather(self_norm_bias, "shard", axis=0, tiled=True),
        lax.all_gather(self_query_weight, "shard", axis=0, tiled=True),
        lax.all_gather(self_key_weight, "shard", axis=0, tiled=True),
        lax.all_gather(self_value_weight, "shard", axis=0, tiled=True),
        lax.all_gather(self_output_weight, "shard", axis=0, tiled=True),
        lax.all_gather(cross_norm_gain, "shard", axis=0, tiled=True),
        lax.all_gather(cross_norm_bias, "shard", axis=0, tiled=True),
        lax.all_gather(cross_query_weight, "shard", axis=0, tiled=True),
        lax.all_gather(cross_key_weight, "shard", axis=0, tiled=True),
        lax.all_gather(cross_value_weight, "shard", axis=0, tiled=True),
        lax.all_gather(cross_output_weight, "shard", axis=0, tiled=True),
        lax.all_gather(feed_norm_gain, "shard", axis=0, tiled=True),
        lax.all_gather(feed_norm_bias, "shard", axis=0, tiled=True),
        lax.all_gather(feed_up_weight, "shard", axis=0, tiled=True),
        lax.all_gather(feed_down_weight, "shard", axis=0, tiled=True),
    )
    (
        gain_attend,
        bias_attend,
        query_matrix,
        key_matrix,
        value_matrix,
        output_matrix,
        gain_cross,
        bias_cross,
        probe_matrix,
        lookup_matrix,
        content_matrix,
        merge_matrix,
        gain_feed,
        bias_feed,
        expand_matrix,
        reduce_matrix,
    ) = gathered
    slots = frames.shape[0]
    frame_count = frames.shape[1]
    width = frames.shape[2]
    text_len = text_states.shape[1]
    shards = lax.axis_size("shard")
    replicas = lax.axis_size("replica")
    clip_total = frame_count * shards
    row_count = slots * frame_count
    scale = HEAD_DIM ** (-0.5)
    shard_rank = lax.axis_index("shard")
    positions = shard_rank * frame_count + jnp.arange(frame_count, dtype=jnp.int32)
    key_positions = jnp.arange(clip_total, dtype=jnp.int32)
    allowed = (key_positions[None, None, :] <= positions[None, :, None]) & (
        key_positions[None, None, :] < clip_lengths[:, None, None]
    )
    valid_rows = ((positions[None, :] < clip_lengths[:, None]) & (slot_used[:, None] > 0)).astype(
        jnp.float32
    )
    text_allowed = text_mask > 0
    inputs = frames.astype(jnp.float32)
    normed_one, pull_one = jax.vjp(
        layer_norm, inputs, gain_attend.astype(jnp.float32), bias_attend.astype(jnp.float32)
    )
    hidden_one = normed_one.astype(jnp.bfloat16).reshape(row_count, width)
    queries = (
        project(hidden_one, query_matrix).astype(jnp.bfloat16).reshape(slots, frame_count, width)
    )
    keys_local = (
        project(hidden_one, key_matrix).astype(jnp.bfloat16).reshape(slots, frame_count, width)
    )
    values_local = (
        project(hidden_one, value_matrix).astype(jnp.bfloat16).reshape(slots, frame_count, width)
    )
    keys_all, values_all = (
        lax.all_gather(keys_local, "shard", axis=1, tiled=True),
        lax.all_gather(values_local, "shard", axis=1, tiled=True),
    )
    head_queries = split_heads(queries)
    head_keys = split_heads(keys_all)
    head_values = split_heads(values_all)
    mixed_self, log_totals = lax.map(self_forward, (head_queries, head_keys, head_values, allowed))
    mixed_rows = mixed_self.reshape(row_count, width)
    after_self = inputs + project(mixed_rows, output_matrix).reshape(slots, frame_count, width)
    normed_two, pull_two = jax.vjp(
        layer_norm, after_self, gain_cross.astype(jnp.float32), bias_cross.astype(jnp.float32)
    )
    hidden_two = normed_two.astype(jnp.bfloat16).reshape(row_count, width)
    probes = split_heads(
        project(hidden_two, probe_matrix).astype(jnp.bfloat16).reshape(slots, frame_count, width)
    )
    text_rows = text_states.reshape(slots * text_len, width)
    lookups = split_heads(
        project(text_rows, lookup_matrix).astype(jnp.bfloat16).reshape(slots, text_len, width)
    )
    contents = split_heads(
        project(text_rows, content_matrix).astype(jnp.bfloat16).reshape(slots, text_len, width)
    )
    cross_scores = (
        jnp.einsum("sqhd,skhd->shqk", probes, lookups, preferred_element_type=jnp.float32) * scale
    )
    cross_scores = jnp.where(text_allowed[:, None, None, :], cross_scores, masked_score)
    cross_peak = jnp.max(cross_scores, axis=-1, keepdims=True)
    cross_weights = jnp.exp(cross_scores - cross_peak)
    cross_probs = cross_weights / jnp.sum(cross_weights, axis=-1, keepdims=True)
    cross_probs_low = cross_probs.astype(jnp.bfloat16)
    cross_mixed = jnp.einsum(
        "shqk,skhd->sqhd", cross_probs_low, contents, preferred_element_type=jnp.float32
    )
    cross_mixed = cross_mixed.astype(jnp.bfloat16).reshape(row_count, width)
    after_cross = after_self + project(cross_mixed, merge_matrix).reshape(slots, frame_count, width)
    normed_three, pull_three = jax.vjp(
        layer_norm, after_cross, gain_feed.astype(jnp.float32), bias_feed.astype(jnp.float32)
    )
    hidden_three = normed_three.astype(jnp.bfloat16).reshape(row_count, width)
    upward = project(hidden_three, expand_matrix)
    activated, gelu_pull = jax.vjp(exact_gelu, upward)
    activated_low = activated.astype(jnp.bfloat16)
    result = after_cross + project(activated_low, reduce_matrix).reshape(slots, frame_count, width)
    output = result.astype(jnp.bfloat16)
    errors = (result - teacher.astype(jnp.float32)) * valid_rows[..., None]
    squares_total, count_total = lax.psum(
        (jnp.sum(errors * errors), jnp.sum(valid_rows)), ("replica", "shard")
    )
    loss = squares_total / (width * count_total)
    grad_result = errors * (slots * replicas * clip_total / count_total)
    grad_feed_low = grad_result.reshape(row_count, width).astype(jnp.bfloat16)
    grad_activated = back_project(grad_feed_low, reduce_matrix)
    grad_upward = gelu_pull(grad_activated)[0].astype(jnp.bfloat16)
    grad_hidden_three = back_project(grad_upward, expand_matrix).reshape(slots, frame_count, width)
    grad_cross_norm, gain_feed_part, bias_feed_part = pull_three(grad_hidden_three)
    grad_after_cross = grad_result + grad_cross_norm
    feed_owned = (
        lax.psum_scatter(
            outer_sum(hidden_three, grad_upward).astype(jnp.bfloat16),
            "shard",
            scatter_dimension=0,
            tiled=True,
        ).astype(jnp.float32),
        lax.psum_scatter(
            outer_sum(activated_low, grad_feed_low).astype(jnp.bfloat16),
            "shard",
            scatter_dimension=0,
            tiled=True,
        ).astype(jnp.float32),
        lax.psum_scatter(
            gain_feed_part.astype(jnp.bfloat16), "shard", scatter_dimension=0, tiled=True
        ).astype(jnp.float32),
        lax.psum_scatter(
            bias_feed_part.astype(jnp.bfloat16), "shard", scatter_dimension=0, tiled=True
        ).astype(jnp.float32),
    )
    grad_cross_low = grad_after_cross.reshape(row_count, width).astype(jnp.bfloat16)
    grad_cross_mixed = split_heads(
        back_project(grad_cross_low, merge_matrix)
        .astype(jnp.bfloat16)
        .reshape(slots, frame_count, width)
    )
    grad_cross_probs = jnp.einsum(
        "sqhd,skhd->shqk", grad_cross_mixed, contents, preferred_element_type=jnp.float32
    )
    content_grads = jnp.einsum(
        "shqk,sqhd->skhd", cross_probs_low, grad_cross_mixed, preferred_element_type=jnp.float32
    )
    cross_inner = jnp.sum(cross_probs * grad_cross_probs, axis=-1, keepdims=True)
    grad_cross_scores = (cross_probs * (grad_cross_probs - cross_inner)).astype(jnp.bfloat16)
    probe_grads = (
        jnp.einsum(
            "shqk,skhd->sqhd", grad_cross_scores, lookups, preferred_element_type=jnp.float32
        )
        * scale
    )
    probe_grads = probe_grads.astype(jnp.bfloat16).reshape(row_count, width)
    lookup_grads = (
        jnp.einsum("shqk,sqhd->skhd", grad_cross_scores, probes, preferred_element_type=jnp.float32)
        * scale
    )
    lookup_sum, content_sum = (
        lax.psum(lookup_grads.astype(jnp.bfloat16), "shard").astype(jnp.float32),
        lax.psum(content_grads.astype(jnp.bfloat16), "shard").astype(jnp.float32),
    )
    lookup_low = lookup_sum.astype(jnp.bfloat16).reshape(slots * text_len, width)
    content_low = content_sum.astype(jnp.bfloat16).reshape(slots * text_len, width)
    own_width = width // shards
    own_text = lax.dynamic_slice_in_dim(text_rows, shard_rank * own_width, own_width, 1)
    lookup_own = outer_sum(own_text, lookup_low)
    content_own = outer_sum(own_text, content_low)
    text_grad = (
        back_project(lookup_low, lookup_matrix) + back_project(content_low, content_matrix)
    ).reshape(slots, text_len, width)
    grad_hidden_two = back_project(probe_grads, probe_matrix).reshape(slots, frame_count, width)
    grad_self_norm, gain_cross_part, bias_cross_part = pull_two(grad_hidden_two)
    grad_after_self = grad_after_cross + grad_self_norm
    grad_self_low = grad_after_self.reshape(row_count, width).astype(jnp.bfloat16)
    grad_mixed = split_heads(
        back_project(grad_self_low, output_matrix)
        .astype(jnp.bfloat16)
        .reshape(slots, frame_count, width)
    )
    grad_queries, grad_keys, grad_values = lax.map(
        self_backward, (head_queries, head_keys, head_values, allowed, log_totals, grad_mixed)
    )
    key_sum, value_sum = (
        lax.psum_scatter(
            grad_keys.reshape(slots, clip_total, width).astype(jnp.bfloat16),
            "shard",
            scatter_dimension=1,
            tiled=True,
        ).astype(jnp.float32),
        lax.psum_scatter(
            grad_values.reshape(slots, clip_total, width).astype(jnp.bfloat16),
            "shard",
            scatter_dimension=1,
            tiled=True,
        ).astype(jnp.float32),
    )
    key_low = key_sum.astype(jnp.bfloat16).reshape(row_count, width)
    value_low = value_sum.astype(jnp.bfloat16).reshape(row_count, width)
    query_low = grad_queries.reshape(row_count, width)
    grad_hidden_one = (
        back_project(query_low, query_matrix)
        + back_project(key_low, key_matrix)
        + back_project(value_low, value_matrix)
    )
    grad_inputs, gain_attend_part, bias_attend_part = pull_one(
        grad_hidden_one.reshape(slots, frame_count, width)
    )
    frames_grad = grad_after_self + grad_inputs
    attend_owned = (
        lax.psum_scatter(
            outer_sum(hidden_one, query_low).astype(jnp.bfloat16),
            "shard",
            scatter_dimension=0,
            tiled=True,
        ).astype(jnp.float32),
        lax.psum_scatter(
            outer_sum(hidden_one, key_low).astype(jnp.bfloat16),
            "shard",
            scatter_dimension=0,
            tiled=True,
        ).astype(jnp.float32),
        lax.psum_scatter(
            outer_sum(hidden_one, value_low).astype(jnp.bfloat16),
            "shard",
            scatter_dimension=0,
            tiled=True,
        ).astype(jnp.float32),
        lax.psum_scatter(
            outer_sum(mixed_rows, grad_self_low).astype(jnp.bfloat16),
            "shard",
            scatter_dimension=0,
            tiled=True,
        ).astype(jnp.float32),
        lax.psum_scatter(
            outer_sum(hidden_two, probe_grads).astype(jnp.bfloat16),
            "shard",
            scatter_dimension=0,
            tiled=True,
        ).astype(jnp.float32),
        lax.psum_scatter(
            outer_sum(cross_mixed, grad_cross_low).astype(jnp.bfloat16),
            "shard",
            scatter_dimension=0,
            tiled=True,
        ).astype(jnp.float32),
        lax.psum_scatter(
            gain_attend_part.astype(jnp.bfloat16), "shard", scatter_dimension=0, tiled=True
        ).astype(jnp.float32),
        lax.psum_scatter(
            bias_attend_part.astype(jnp.bfloat16), "shard", scatter_dimension=0, tiled=True
        ).astype(jnp.float32),
        lax.psum_scatter(
            gain_cross_part.astype(jnp.bfloat16), "shard", scatter_dimension=0, tiled=True
        ).astype(jnp.float32),
        lax.psum_scatter(
            bias_cross_part.astype(jnp.bfloat16), "shard", scatter_dimension=0, tiled=True
        ).astype(jnp.float32),
    )
    summed = (
        lax.psum(attend_owned[6].astype(jnp.bfloat16), "replica").astype(jnp.float32),
        lax.psum(attend_owned[7].astype(jnp.bfloat16), "replica").astype(jnp.float32),
        lax.psum(attend_owned[0].astype(jnp.bfloat16), "replica").astype(jnp.float32),
        lax.psum(attend_owned[1].astype(jnp.bfloat16), "replica").astype(jnp.float32),
        lax.psum(attend_owned[2].astype(jnp.bfloat16), "replica").astype(jnp.float32),
        lax.psum(attend_owned[3].astype(jnp.bfloat16), "replica").astype(jnp.float32),
        lax.psum(attend_owned[8].astype(jnp.bfloat16), "replica").astype(jnp.float32),
        lax.psum(attend_owned[9].astype(jnp.bfloat16), "replica").astype(jnp.float32),
        lax.psum(attend_owned[4].astype(jnp.bfloat16), "replica").astype(jnp.float32),
        lax.psum(lookup_own.astype(jnp.bfloat16), "replica").astype(jnp.float32),
        lax.psum(content_own.astype(jnp.bfloat16), "replica").astype(jnp.float32),
        lax.psum(attend_owned[5].astype(jnp.bfloat16), "replica").astype(jnp.float32),
        lax.psum(feed_owned[2].astype(jnp.bfloat16), "replica").astype(jnp.float32),
        lax.psum(feed_owned[3].astype(jnp.bfloat16), "replica").astype(jnp.float32),
        lax.psum(feed_owned[0].astype(jnp.bfloat16), "replica").astype(jnp.float32),
        lax.psum(feed_owned[1].astype(jnp.bfloat16), "replica").astype(jnp.float32),
    )
    return (
        output,
        loss,
        frames_grad,
        text_grad,
        summed[0],
        summed[1],
        summed[2],
        summed[3],
        summed[4],
        summed[5],
        summed[6],
        summed[7],
        summed[8],
        summed[9],
        summed[10],
        summed[11],
        summed[12],
        summed[13],
        summed[14],
        summed[15],
    )


PAIR = 2 * HEAD_DIM
EVERY = ("shard", "y", "x", "core")
REPLICAS = ("core", "y", "x")
NT = (((1,), (1,)), ((), ()))
TN = (((0,), (0,)), ((), ()))
NN = (((1,), (0,)), ((), ()))


def dot(left, right, dims):
    return lax.dot_general(left, right, dims, preferred_element_type=jnp.float32)


def half_mask(side, value):
    lanes = lax.broadcasted_iota(jnp.int32, (1, PAIR), 1)
    inside = (lanes >= HEAD_DIM) if side else (lanes < HEAD_DIM)
    return jnp.where(inside, value, 0.0).astype(jnp.bfloat16)


def fill_clip(place, own_ref, other_ref, all_ref):
    block = own_ref.shape[0] // 2
    for part in range(2):
        rows = slice(part * block, (part + 1) * block)
        for at, ref in ((place[part], own_ref), (place[3 + part], other_ref)):
            all_ref[pl.ds(pl.multiple_of(at * block, block), block), :] = ref[rows, :]


def self_forward_kernel(
    place, q_ref, own_k, own_v, other_k, other_v, mixed_ref, lse_ref, k_ref, v_ref, acc_ref
):
    fill_clip(place, own_k, other_k, k_ref)
    fill_clip(place, own_v, other_v, v_ref)
    block = q_ref.shape[0] // 2
    length = place[2]
    low = lax.broadcasted_iota(jnp.int32, (PAIR, 1), 0) < HEAD_DIM
    for part in range(2):
        first = place[part] * block
        rows = slice(part * block, (part + 1) * block)
        q = q_ref[rows, :]
        q_half = [q * half_mask(side, HEAD_DIM ** (-0.5)) for side in range(2)]
        limit = jnp.minimum(
            first + lax.broadcasted_iota(jnp.int32, (1, block), 1) + 1, length
        )
        acc_ref[...] = jnp.zeros_like(acc_ref)

        def step(j, peaks, q_half=q_half, limit=limit):
            at = pl.multiple_of(j * block, block)
            k = k_ref[pl.ds(at, block), :]
            v = v_ref[pl.ds(at, block), :]
            allowed = at + lax.broadcasted_iota(jnp.int32, (block, block), 0) < limit
            out = []
            for side in range(2):
                scores = jnp.where(allowed, dot(k, q_half[side], NT), masked_score)
                peak = jnp.maximum(peaks[side], jnp.max(scores, axis=0, keepdims=True))
                weights = jnp.exp(scores - peak).astype(jnp.bfloat16)
                v_ones = v * half_mask(side, 1.0) + half_mask(1 - side, 1.0)
                acc_ref[side] = acc_ref[side] * jnp.exp(peaks[side] - peak) + dot(
                    v_ones, weights, TN
                )
                out.append(peak)
            return tuple(out)

        peaks = lax.fori_loop(
            0, place[part] + 1, step, (jnp.full((1, block), masked_score, jnp.float32),) * 2
        )
        top, bottom = acc_ref[0], acc_ref[1]
        total = jnp.where(low, top[HEAD_DIM : HEAD_DIM + 1], bottom[0:1])
        mixed = jnp.where(low, top, bottom) / total
        mixed_ref[rows, :] = mixed.T.astype(jnp.bfloat16)
        lse_ref[0:1, rows] = peaks[0] + jnp.log(top[HEAD_DIM : HEAD_DIM + 1])
        lse_ref[1:2, rows] = peaks[1] + jnp.log(bottom[0:1])


def self_backward_kernel(
    place, q_ref, own_k, own_v, other_k, other_v, mixed_ref, grad_ref, lse_ref,
    dq_ref, own_dk, own_dv, other_dk, other_dv, k_ref, v_ref, dq_acc, dk_acc, dv_acc,
):
    fill_clip(place, own_k, other_k, k_ref)
    fill_clip(place, own_v, other_v, v_ref)
    block = q_ref.shape[0] // 2
    length = place[2]
    scale = HEAD_DIM ** (-0.5)
    dk_acc[...] = jnp.zeros_like(dk_acc)
    dv_acc[...] = jnp.zeros_like(dv_acc)
    for part in range(2):
        first = place[part] * block
        rows = slice(part * block, (part + 1) * block)
        q = q_ref[rows, :]
        grad = grad_ref[rows, :]
        q_half = [q * half_mask(side, scale) for side in range(2)]
        grad_half = [grad * half_mask(side, 1.0) for side in range(2)]
        product = (grad.astype(jnp.float32) * mixed_ref[rows, :].astype(jnp.float32)).T
        inner = [
            jnp.sum(product[side * HEAD_DIM : (side + 1) * HEAD_DIM], axis=0, keepdims=True)
            for side in range(2)
        ]
        lse = [lse_ref[side : side + 1, rows] for side in range(2)]
        limit = jnp.minimum(
            first + lax.broadcasted_iota(jnp.int32, (1, block), 1) + 1, length
        )
        dq_acc[...] = jnp.zeros_like(dq_acc)

        def step(
            j, carry, q_half=q_half, grad_half=grad_half, inner=inner, lse=lse, limit=limit
        ):
            at = pl.multiple_of(j * block, block)
            k = k_ref[pl.ds(at, block), :]
            v = v_ref[pl.ds(at, block), :]
            allowed = at + lax.broadcasted_iota(jnp.int32, (block, block), 0) < limit
            dq, dk, dv = 0.0, 0.0, 0.0
            for side in range(2):
                scores = jnp.where(allowed, dot(k, q_half[side], NT), masked_score)
                probs = jnp.exp(scores - lse[side])
                grad_probs = dot(v, grad_half[side], NT)
                grad_scores = (probs * (grad_probs - inner[side])).astype(jnp.bfloat16)
                dv += dot(probs.astype(jnp.bfloat16), grad_half[side], NN)
                dk += dot(grad_scores, q_half[side], NN)
                dq += dot(k * half_mask(side, scale), grad_scores, TN)
            dk_acc[pl.ds(at, block), :] += dk
            dv_acc[pl.ds(at, block), :] += dv
            dq_acc[...] += dq
            return carry

        lax.fori_loop(0, place[part] + 1, step, 0)
        dq_ref[rows, :] = dq_acc[...].T.astype(jnp.bfloat16)
    for part in range(2):
        rows = slice(part * block, (part + 1) * block)
        own = pl.ds(pl.multiple_of(place[part] * block, block), block)
        other = pl.ds(pl.multiple_of(place[3 + part] * block, block), block)
        own_dk[rows, :] = dk_acc[own, :].astype(jnp.bfloat16)
        own_dv[rows, :] = dv_acc[own, :].astype(jnp.bfloat16)
        other_dk[rows, :] = dk_acc[other, :].astype(jnp.bfloat16)
        other_dv[rows, :] = dv_acc[other, :].astype(jnp.bfloat16)


def pair_block(rows):
    return pl.BlockSpec((rows, PAIR), lambda i, *_: (0, i))


def value_block(rows, pairs):
    return pl.BlockSpec((rows, PAIR), lambda i, *_: (0, pairs + i))


def self_attend(place, queries, own, other):
    rows, width = queries.shape
    clip = 2 * rows
    pairs = width // PAIR
    return pl.pallas_call(
        self_forward_kernel,
        out_shape=(
            jax.ShapeDtypeStruct((rows, width), jnp.bfloat16),
            jax.ShapeDtypeStruct((pairs * 8, rows), jnp.float32),
        ),
        grid_spec=pltpu.PrefetchScalarGridSpec(
            num_scalar_prefetch=1,
            grid=(pairs,),
            in_specs=[pair_block(rows)] + [pair_block(rows), value_block(rows, pairs)] * 2,
            out_specs=(pair_block(rows), pl.BlockSpec((8, rows), lambda i, *_: (i, 0))),
            scratch_shapes=[
                pltpu.VMEM((clip, PAIR), jnp.bfloat16),
                pltpu.VMEM((clip, PAIR), jnp.bfloat16),
                pltpu.VMEM((2, PAIR, rows // 2), jnp.float32),
            ],
        ),
        compiler_params=pltpu.CompilerParams(vmem_limit_bytes=32 * 2**20),
        cost_estimate=pl.CostEstimate(
            flops=2 * 2 * rows * clip * width, bytes_accessed=8 * clip * width, transcendentals=0
        ),
        name="self_attend",
    )(place, queries, own, own, other, other)


def self_attend_back(place, queries, own, other, mixed, grads, lse):
    rows, width = queries.shape
    clip = 2 * rows
    pairs = width // PAIR
    return pl.pallas_call(
        self_backward_kernel,
        out_shape=(jax.ShapeDtypeStruct((rows, width), jnp.bfloat16),) * 5,
        grid_spec=pltpu.PrefetchScalarGridSpec(
            num_scalar_prefetch=1,
            grid=(pairs,),
            in_specs=[pair_block(rows)]
            + [pair_block(rows), value_block(rows, pairs)] * 2
            + [
                pair_block(rows),
                pair_block(rows),
                pl.BlockSpec((8, rows), lambda i, *_: (i, 0)),
            ],
            out_specs=(pair_block(rows),) * 5,
            scratch_shapes=[
                pltpu.VMEM((clip, PAIR), jnp.bfloat16),
                pltpu.VMEM((clip, PAIR), jnp.bfloat16),
                pltpu.VMEM((PAIR, rows // 2), jnp.float32),
                pltpu.VMEM((clip, PAIR), jnp.float32),
                pltpu.VMEM((clip, PAIR), jnp.float32),
            ],
        ),
        compiler_params=pltpu.CompilerParams(vmem_limit_bytes=32 * 2**20),
        cost_estimate=pl.CostEstimate(
            flops=5 * 2 * rows * clip * width, bytes_accessed=16 * clip * width, transcendentals=0
        ),
        name="self_attend_back",
    )(place, queries, own, own, other, other, mixed, grads, lse)


def both_heads(rows, value):
    return jnp.concatenate([rows * half_mask(side, value) for side in range(2)], axis=0)


def cross_probs_of(lookup_two, probes, present):
    text = present.shape[0]
    scores = dot(lookup_two, probes, NT)
    out = []
    for side in range(2):
        part = jnp.where(
            present > 0, scores[side * text : (side + 1) * text], masked_score
        )
        weights = jnp.exp(part - jnp.max(part, axis=0, keepdims=True))
        out.append(weights / jnp.sum(weights, axis=0, keepdims=True))
    return out


def cross_forward_kernel(probe_ref, lookup_ref, content_ref, present_ref, mixed_ref):
    probs = cross_probs_of(
        both_heads(lookup_ref[...], HEAD_DIM ** (-0.5)), probe_ref[...], present_ref[...]
    )
    probs = jnp.concatenate(probs, axis=0).astype(jnp.bfloat16)
    mixed_ref[...] = dot(probs, both_heads(content_ref[...], 1.0), TN).astype(jnp.bfloat16)


def cross_backward_kernel(
    probe_ref, lookup_ref, content_ref, present_ref, grad_ref, dp_ref, dl_ref, dc_ref
):
    text = present_ref.shape[0]
    scale = HEAD_DIM ** (-0.5)
    probes = probe_ref[...]
    grads = grad_ref[...]
    lookup_two = both_heads(lookup_ref[...], scale)
    probs = cross_probs_of(lookup_two, probes, present_ref[...])
    grad_probs = dot(both_heads(content_ref[...], 1.0), grads, NT)
    grad_scores = []
    for side in range(2):
        part = grad_probs[side * text : (side + 1) * text]
        inner = jnp.sum(probs[side] * part, axis=0, keepdims=True)
        grad_scores.append(probs[side] * (part - inner))
    grad_scores = jnp.concatenate(grad_scores, axis=0).astype(jnp.bfloat16)
    probs = jnp.concatenate(probs, axis=0).astype(jnp.bfloat16)
    low = lax.broadcasted_iota(jnp.int32, (1, PAIR), 1) < HEAD_DIM
    dp_ref[...] = dot(grad_scores, lookup_two, TN).astype(jnp.bfloat16)
    dl = dot(grad_scores, probes, NN) * scale
    dl_ref[...] = jnp.where(low, dl[:text], dl[text:]).astype(jnp.bfloat16)
    dc = dot(probs, grads, NN)
    dc_ref[...] = jnp.where(low, dc[:text], dc[text:]).astype(jnp.bfloat16)


def cross_attend(probes, lookups, contents, present):
    rows, width = probes.shape
    text = lookups.shape[0]
    return pl.pallas_call(
        cross_forward_kernel,
        out_shape=jax.ShapeDtypeStruct((rows, width), jnp.bfloat16),
        grid=(width // PAIR,),
        in_specs=[
            pair_block(rows),
            pair_block(text),
            pair_block(text),
            pl.BlockSpec((text, 1), lambda i: (0, 0)),
        ],
        out_specs=pair_block(rows),
        compiler_params=pltpu.CompilerParams(vmem_limit_bytes=32 * 2**20),
        cost_estimate=pl.CostEstimate(
            flops=8 * rows * text * width, bytes_accessed=4 * rows * width, transcendentals=0
        ),
        name="cross_attend",
    )(probes, lookups, contents, present)


def cross_attend_back(probes, lookups, contents, present, grads):
    rows, width = probes.shape
    text = lookups.shape[0]
    return pl.pallas_call(
        cross_backward_kernel,
        out_shape=(
            jax.ShapeDtypeStruct((rows, width), jnp.bfloat16),
            jax.ShapeDtypeStruct((text, width), jnp.bfloat16),
            jax.ShapeDtypeStruct((text, width), jnp.bfloat16),
        ),
        grid=(width // PAIR,),
        in_specs=[
            pair_block(rows),
            pair_block(text),
            pair_block(text),
            pl.BlockSpec((text, 1), lambda i: (0, 0)),
            pair_block(rows),
        ],
        out_specs=(pair_block(rows), pair_block(text), pair_block(text)),
        compiler_params=pltpu.CompilerParams(vmem_limit_bytes=32 * 2**20),
        cost_estimate=pl.CostEstimate(
            flops=20 * rows * text * width, bytes_accessed=6 * rows * width, transcendentals=0
        ),
        name="cross_attend_back",
    )(probes, lookups, contents, present, grads)


def unpack_kernel(in_ref, out_ref):
    pieces = in_ref[...]
    out_ref[...] = pieces.reshape(-1, pieces.shape[-1]).T.astype(jnp.float32)


def unpack(full, rows, place, out_shape, out_at, together):
    owners, _, features = full.shape
    tall = out_shape[0] // features
    wide = out_shape[1] // (together * rows)
    return pl.pallas_call(
        unpack_kernel,
        out_shape=jax.ShapeDtypeStruct(out_shape, jnp.float32),
        grid=(tall, wide),
        in_specs=[
            pl.BlockSpec((together, rows, features), lambda i, j: (j + out_at, place + i, 0))
        ],
        out_specs=pl.BlockSpec((features, together * rows), lambda i, j: (i, j)),
        compiler_params=pltpu.CompilerParams(vmem_limit_bytes=32 * 2**20),
        cost_estimate=pl.CostEstimate(
            flops=0, bytes_accessed=6 * out_shape[0] * out_shape[1], transcendentals=0
        ),
        name="unpack",
    )(full)


def held(values, *others):
    return list(lax.optimization_barrier((*values, *others))[: len(values)])


def after(value, *others):
    return lax.optimization_barrier((value, *others))[0]


def norm_parts(values):
    mean = jnp.mean(values, axis=-1, keepdims=True)
    center = values - mean
    return mean, lax.rsqrt(jnp.mean(center * center, axis=-1, keepdims=True) + epsilon)


def norm_back(grads, values, parts, gain):
    mean, inverse = parts
    unit = (values - mean) * inverse
    gain_grad = jnp.sum(grads * unit, axis=0)
    bias_grad = jnp.sum(grads, axis=0)
    scaled = grads * gain
    back = inverse * (
        scaled
        - jnp.mean(scaled, axis=-1, keepdims=True)
        - unit * jnp.mean(scaled * unit, axis=-1, keepdims=True)
    )
    return back, gain_grad, bias_grad


def clip_body(
    frames,
    text_states,
    text_mask,
    clip_lengths,
    slot_used,
    teacher,
    self_norm_gain,
    self_norm_bias,
    self_query_weight,
    self_key_weight,
    self_value_weight,
    self_output_weight,
    cross_norm_gain,
    cross_norm_bias,
    cross_query_weight,
    cross_key_weight,
    cross_value_weight,
    cross_output_weight,
    feed_norm_gain,
    feed_norm_bias,
    feed_up_weight,
    feed_down_weight,
):
    block, width = frames.shape[1:]
    text_len = text_states.shape[1]
    shards, replicas, outers = 4, 8, 4
    core = lax.axis_index("core")
    shard = lax.axis_index("shard")
    outer = 2 * lax.axis_index("y") + lax.axis_index("x")
    replica = 2 * outer + core
    clip = block * shards
    hidden_units = feed_up_weight.shape[1]

    holder = {0: 0, 1: 1, 2: 1, 3: 0}
    there = ([], [])
    for c in range(2):
        for s in range(4):
            for turn in range(2):
                slot = turn if s < 2 else 1 - turn
                there[turn].append((c * 4 + s, holder[s] * 4 + 2 * c + slot))
    back = tuple([(b, a) for a, b in pairs] for pairs in there)
    spot = ("core", "shard")
    swap = [(0, 1), (1, 0)]
    even = shard % 2 == 0
    lower = shard < 2
    first_core = core == 0

    def hop(values, distance):
        pairs = [(i, (i + distance) % shards) for i in range(shards)]
        return lax.ppermute(values, "shard", pairs)

    def hops(values):
        return [hop(values, distance) for distance in (1, 2, 3)]

    def line_up(mine, came):
        out = jnp.zeros((shards,) + mine.shape, mine.dtype)
        out = lax.dynamic_update_index_in_dim(out, mine, shard, 0)
        for distance, values in zip((1, 2, 3), came):
            owner = lax.rem(shard + shards - distance, shards)
            out = lax.dynamic_update_index_in_dim(out, values, owner, 0)
        return out

    def to_chip(pair):
        one = lax.ppermute(jnp.where(lower, pair[0], pair[1]), spot, there[0])
        two = lax.ppermute(jnp.where(lower, pair[1], pair[0]), spot, there[1])
        return one, two

    def by_time(one, two):
        return jnp.concatenate([jnp.where(even, one, two), jnp.where(even, two, one)], axis=0)

    def outgoing(values):
        early, late = values[:block], values[block:]
        return jnp.where(even, early, late), jnp.where(even, late, early)

    def from_chip(values):
        one, two = outgoing(values)
        return lax.ppermute(one, spot, back[0]), lax.ppermute(two, spot, back[1])

    def by_slot(one, two):
        return jnp.stack([jnp.where(lower, one, two), jnp.where(lower, two, one)])

    def share_of(weight):
        share = weight.shape[0] // replicas
        return lax.dynamic_slice_in_dim(weight, replica * share, share, 0)

    def from_replicas(line):
        full = lax.all_gather(line, ("y", "x", "core"), axis=1, tiled=True)
        return full.reshape(-1, line.shape[-1])

    qkv_share = jnp.concatenate(
        [share_of(self_query_weight), share_of(self_key_weight), share_of(self_value_weight)],
        axis=1,
    )
    vectors = jnp.concatenate(
        [
            self_norm_gain,
            self_norm_bias,
            cross_norm_gain,
            cross_norm_bias,
            feed_norm_gain,
            feed_norm_bias,
        ]
    )
    vectors = jnp.pad(vectors[None, :], ((0, 15), (0, 3 * width - 6 * block)))
    share = qkv_share.shape[0]
    qkv_mine = jnp.concatenate([qkv_share, vectors], axis=0)
    qkv_came = hops(qkv_mine)
    qkv_matrix = from_replicas(line_up(qkv_share, [values[:share] for values in qkv_came]))
    norms = line_up(vectors[0], [values[share] for values in qkv_came])
    norms = norms[:, : 6 * block].reshape(shards, 6, block).transpose(1, 0, 2)
    norms = norms.reshape(6, width).astype(jnp.float32)
    rest_share = jnp.concatenate(
        [share_of(self_output_weight), share_of(cross_query_weight), share_of(cross_output_weight)],
        axis=1,
    )
    rest_came = hops(after(rest_share, *qkv_came))
    rest = from_replicas(line_up(rest_share, rest_came))
    came = to_chip(after(frames, *rest_came))
    x_low = by_time(*came)
    expand_share = share_of(feed_up_weight)
    expand_came = hops(after(expand_share, *came))

    facts = jnp.concatenate(
        [(clip_lengths // 64)[:, None], (clip_lengths % 64)[:, None], slot_used[:, None], text_mask],
        axis=1,
    ).astype(jnp.bfloat16)
    facts = jnp.pad(facts[:, None, :], ((0, 0), (0, 15), (0, width - facts.shape[1])))
    text_sent = lax.ppermute(jnp.concatenate([text_states, facts], axis=1), "core", swap)
    text_other = text_sent[:, :text_len]
    both = jnp.stack([facts[:, 0], text_sent[:, text_len]])[:, :, : 3 + text_len].astype(jnp.int32)
    lengths = 64 * both[:, :, 0] + both[:, :, 1]
    fact = lax.dynamic_index_in_dim(
        jnp.where(shard // 2 == core, both[0], both[1]), shard % 2, 0, keepdims=False
    )
    length, used = 64 * fact[0] + fact[1], fact[2]
    present = fact[3:].reshape(text_len, 1)
    count = jnp.sum(
        jnp.where(both[:, :, 2] > 0, jnp.minimum(lengths, clip), 0).astype(jnp.float32)
    )
    count = jnp.full((8, 128), count)
    for axis in ("x", "y"):
        count += lax.ppermute(count, axis, swap)
    count = count[0, 0]
    text_all = jnp.concatenate(
        [
            jnp.where(first_core, text_states, text_other),
            jnp.where(first_core, text_other, text_states),
        ],
        axis=0,
    ).reshape(4 * text_len, width)
    text_all = lax.dynamic_slice_in_dim(text_all, shard * block, block, 1)
    text_matrix = jnp.where(first_core, cross_key_weight, cross_value_weight)
    text_part = project(text_all, text_matrix).astype(jnp.bfloat16).reshape(4, text_len, width)
    text_came = [
        hop(
            lax.dynamic_index_in_dim(
                text_part, lax.rem(shard + distance, shards), 0, keepdims=False
            ),
            distance,
        )
        for distance in (1, 2, 3)
    ]

    places = jnp.stack([core, 3 - core, length, 1 - core, 2 + core]).astype(jnp.int32)
    positions = jnp.concatenate(
        [core * block + jnp.arange(block), (3 - core) * block + jnp.arange(block)]
    )
    valid_rows = ((positions < length) & (used > 0)).astype(jnp.float32)[:, None]
    inputs = x_low.astype(jnp.float32)
    parts_one = norm_parts(inputs)
    hidden_one = ((inputs - parts_one[0]) * parts_one[1] * norms[0] + norms[1]).astype(
        jnp.bfloat16
    )
    kv = project(after(hidden_one, count), qkv_matrix[:, width:]).astype(jnp.bfloat16)
    kv_other = lax.ppermute(kv, "core", swap)
    expand_came = held(expand_came, kv)
    queries = project(after(hidden_one, kv, *expand_came), qkv_matrix[:, :width])
    queries = queries.astype(jnp.bfloat16)
    expand_matrix = from_replicas(line_up(expand_share, expand_came))
    reduce_share = share_of(feed_down_weight)
    reduce_came = hops(after(reduce_share, *expand_came))
    output_matrix = rest[:, :width]
    probe_matrix = rest[:, width : 2 * width]
    merge_matrix = rest[:, 2 * width :]
    mixed_self, lse = self_attend(after(places, *expand_came), queries, kv, kv_other)
    reduce_came = held(reduce_came, mixed_self)
    reduce_matrix = from_replicas(line_up(reduce_share, reduce_came))
    text_came = held(text_came, mixed_self)
    text_half = lax.dynamic_index_in_dim(text_part, shard, 0, keepdims=False).astype(jnp.float32)
    for values in text_came:
        text_half += values.astype(jnp.float32)
    text_half = text_half.astype(jnp.bfloat16)
    text_swap = lax.ppermute(text_half, "core", swap)
    lookups = jnp.where(first_core, text_half, text_swap)
    contents = jnp.where(first_core, text_swap, text_half)
    after_self = inputs + project(mixed_self, output_matrix)
    parts_two = norm_parts(after_self)
    hidden_two = ((after_self - parts_two[0]) * parts_two[1] * norms[2] + norms[3]).astype(
        jnp.bfloat16
    )
    probes = project(hidden_two, probe_matrix).astype(jnp.bfloat16)
    teacher_came = to_chip(after(teacher, *reduce_came, probes))
    cross_mixed = cross_attend(probes, lookups, contents, present)
    after_cross = after_self + project(cross_mixed, merge_matrix)
    parts_three = norm_parts(after_cross)
    hidden_three = (
        (after_cross - parts_three[0]) * parts_three[1] * norms[4] + norms[5]
    ).astype(jnp.bfloat16)
    upward = project(hidden_three, expand_matrix)
    activated, gelu_pull = jax.vjp(exact_gelu, upward)
    activated_low = activated.astype(jnp.bfloat16)
    teacher_low = by_time(*held(teacher_came, activated_low))
    result = after_cross + project(activated_low, reduce_matrix)
    errors = (result - teacher_low.astype(jnp.float32)) * valid_rows
    squares = jnp.sum(errors * errors)
    grad_result = errors * (4 * outers * clip / count)
    grad_feed_low = grad_result.astype(jnp.bfloat16)

    def theirs_of(right, left):
        columns = right.shape[1] // 2
        part = lax.dynamic_slice_in_dim(right, (1 - core) * columns, columns, 1)
        return outer_sum(part, left).astype(jnp.bfloat16)

    def ours_of(right, left, theirs):
        columns = right.shape[1] // 2
        sent = lax.ppermute(theirs, "core", swap)
        part = lax.dynamic_slice_in_dim(right, core * columns, columns, 1)
        return (outer_sum(part, left) + sent.astype(jnp.float32)).astype(jnp.bfloat16)

    def over_outer(values):
        return lax.psum_scatter(values, ("y", "x"), scatter_dimension=0, tiled=True)

    def shard_hops(values):
        columns = values.shape[1] // shards
        return [
            hop(
                lax.dynamic_slice_in_dim(
                    values, lax.rem(shard + distance, shards) * columns, columns, 1
                ),
                distance,
            )
            for distance in (1, 2, 3)
        ]

    def over_shard(values, came):
        columns = values.shape[1] // shards
        total = lax.dynamic_slice_in_dim(values, shard * columns, columns, 1).astype(jnp.float32)
        for part in came:
            total += part.astype(jnp.float32)
        return total.astype(jnp.bfloat16)

    down_theirs = theirs_of(grad_feed_low, activated_low)
    to_send = outgoing(result.astype(jnp.bfloat16))
    output_one = lax.ppermute(to_send[0], spot, back[0])
    grad_activated = back_project(after(grad_feed_low, down_theirs), reduce_matrix)
    grad_upward = gelu_pull(grad_activated)[0].astype(jnp.bfloat16)
    output_one = after(output_one, grad_upward)
    down_ours = ours_of(
        after(grad_feed_low, grad_upward, output_one), activated_low, down_theirs
    )
    down_sum = over_outer(down_ours)
    up_theirs = theirs_of(after(grad_upward, down_ours), hidden_three)
    grad_hidden_three = back_project(after(grad_upward, up_theirs), expand_matrix)
    output_two = lax.ppermute(after(to_send[1], output_one), spot, back[1])
    output_two = after(output_two, grad_hidden_three)
    output = by_slot(output_one, output_two)
    up_ours = ours_of(after(grad_upward, grad_hidden_three, output_two), hidden_three, up_theirs)
    grad_norm, gain_feed, bias_feed = norm_back(
        after(grad_hidden_three, up_ours), after_cross, parts_three, norms[4]
    )
    grad_after_cross = grad_result + grad_norm
    grad_cross_low = grad_after_cross.astype(jnp.bfloat16)
    merge_theirs = theirs_of(grad_cross_low, cross_mixed)
    grad_cross_mixed = back_project(after(grad_cross_low, merge_theirs), merge_matrix).astype(
        jnp.bfloat16
    )
    probe_grads, lookup_grads, content_grads = cross_attend_back(
        probes, lookups, contents, present, grad_cross_mixed
    )
    up_sum = over_outer(up_ours)
    text_mine = jnp.where(first_core, lookup_grads, content_grads)
    text_sent = lax.ppermute(
        jnp.where(first_core, content_grads, lookup_grads), "core", swap
    )
    text_mine = (text_mine.astype(jnp.float32) + text_sent.astype(jnp.float32)).astype(
        jnp.bfloat16
    )
    merge_ours = ours_of(after(grad_cross_low, probe_grads), cross_mixed, merge_theirs)
    probe_theirs = theirs_of(after(probe_grads, merge_ours), hidden_two)
    grad_hidden_two = back_project(after(probe_grads, probe_theirs), probe_matrix)
    text_four = line_up(text_mine, hops(text_mine)).reshape(4 * text_len, width)
    grad_norm, gain_cross, bias_cross = norm_back(
        grad_hidden_two, after_self, parts_two, norms[2]
    )
    grad_after_self = grad_after_cross + grad_norm
    grad_self_low = grad_after_self.astype(jnp.bfloat16)
    output_theirs = theirs_of(grad_self_low, mixed_self)
    grad_mixed = back_project(after(grad_self_low, output_theirs), output_matrix).astype(
        jnp.bfloat16
    )
    probe_ours = ours_of(after(probe_grads, grad_mixed), hidden_two, probe_theirs)
    text_weights = outer_sum(text_four, text_all).astype(jnp.bfloat16)
    text_back = back_project(text_four, text_matrix).astype(jnp.bfloat16)
    output_ours = ours_of(after(grad_self_low, probe_ours), mixed_self, output_theirs)
    text_rows = width // outers
    middle = jnp.concatenate(
        [
            values.reshape(outers, -1, width)
            for values in (
                output_ours,
                probe_ours,
                merge_ours,
                text_weights.reshape(outers, shards, text_rows // shards, block)
                .transpose(0, 2, 1, 3)
                .reshape(outers, text_rows // shards, width),
            )
        ],
        axis=1,
    )
    middle_rows = middle.shape[1]
    middle = middle.reshape(outers * middle_rows, width)
    middle_sum = over_outer(middle)
    text_split = text_rows // shards
    text_piece = (
        middle_sum[middle_rows - text_split :]
        .reshape(text_split, shards, block)
        .transpose(1, 0, 2)
        .reshape(text_rows, block)
    )
    text_back = text_back.reshape(2, 2, text_len, block)
    text_kept = lax.dynamic_index_in_dim(text_back, core, 0, keepdims=False)
    text_gone = lax.dynamic_index_in_dim(text_back, 1 - core, 0, keepdims=False)
    text_own = text_kept.astype(jnp.float32) + lax.ppermute(text_gone, "core", swap).astype(
        jnp.float32
    )
    text_own = text_own.astype(jnp.bfloat16)
    down_came = shard_hops(down_sum)
    text_came = hops(text_own)
    grad_queries, own_keys, own_values, other_keys, other_values = self_attend_back(
        places, queries, kv, kv_other, mixed_self, after(grad_mixed, middle, text_own), lse
    )
    text_came = held(text_came, grad_queries)
    down_came = held(down_came, grad_queries)
    other_keys, other_values = held([other_keys, other_values], *text_came, *down_came)
    own_keys += lax.ppermute(other_keys, "core", swap)
    own_values += lax.ppermute(other_values, "core", swap)
    down_piece = over_shard(down_sum, down_came)
    up_came = shard_hops(after(up_sum, down_piece))

    qkv_grads = jnp.concatenate([grad_queries, own_keys, own_values], axis=1)
    qkv_theirs = theirs_of(qkv_grads, hidden_one)
    grad_hidden_one = back_project(after(qkv_grads, qkv_theirs), qkv_matrix)
    qkv_ours = ours_of(after(qkv_grads, grad_hidden_one), hidden_one, qkv_theirs)
    up_came = held(up_came, grad_hidden_one)
    up_piece = over_shard(up_sum, up_came)
    text_grad = line_up(text_own, text_came).astype(jnp.float32)
    text_grad = text_grad.transpose(1, 2, 0, 3).reshape(text_states.shape)
    qkv_sum = over_outer(qkv_ours)
    middle_kept = after(middle_sum[: middle_rows - text_split], qkv_ours)
    middle_came = shard_hops(middle_kept)
    middle_piece = over_shard(middle_kept, middle_came)
    early = jnp.concatenate(
        [up_piece]
        + [down_piece[:, i * block : (i + 1) * block] for i in range(4)]
        + [text_piece, middle_piece],
        axis=0,
    )
    grad_norm, gain_self, bias_self = norm_back(
        after(grad_hidden_one, qkv_ours, early), inputs, parts_one, norms[0]
    )
    frames_low = (grad_after_self + grad_norm).astype(jnp.bfloat16)
    late_came = held(shard_hops(after(qkv_sum, *middle_came)), frames_low)
    frames_came = from_chip(after(frames_low, *late_came))
    frames_grad = by_slot(*frames_came).astype(jnp.float32)
    small = jnp.stack(
        [
            gain_self,
            bias_self,
            gain_cross,
            bias_cross,
            gain_feed,
            bias_feed,
            jnp.full((width,), squares),
            jnp.zeros((width,), jnp.float32),
        ]
    )
    small = after(small, *late_came)
    for axis in ("core", "x", "y"):
        small += lax.ppermute(small, axis, swap)
    small_came = shard_hops(small)
    small_own = lax.dynamic_slice_in_dim(small, shard * block, block, 1)
    for part in small_came:
        small_own += part
    loss = small_own[6, 0] / (width * count)
    early = lax.all_gather(after(early, text_grad), REPLICAS, axis=0)
    piece = width // replicas
    square = (block, width)
    up_grad = unpack(early, hidden_units // replicas, 0, (block, hidden_units), 0, 1)
    at = hidden_units // replicas // piece
    down_grad = unpack(early, piece, at, (4 * block, width), 0, 2)
    at += 4
    key_grad = unpack(early, text_rows, at * piece // text_rows, square, 0, 1)
    value_grad = unpack(early, text_rows, at * piece // text_rows, square, 4, 1)
    at += text_rows // piece
    output_grad = unpack(early, piece, at, square, 0, 2)
    probe_grad = unpack(early, piece, at + 1, square, 0, 2)
    merge_grad = unpack(early, piece, at + 2, square, 0, 2)
    late = over_shard(qkv_sum, late_came)
    late = lax.all_gather(
        after(late, early, *frames_came, *small_came), REPLICAS, axis=0, tiled=True
    )
    late = late.reshape(-1, block, block)
    qkv_grad = [unpack(late, block, 0, square, 2 * i, 2) for i in range(3)]
    return (
        output,
        loss,
        frames_grad,
        text_grad,
        small_own[0],
        small_own[1],
        qkv_grad[0],
        qkv_grad[1],
        qkv_grad[2],
        output_grad,
        small_own[2],
        small_own[3],
        probe_grad,
        key_grad,
        value_grad,
        merge_grad,
        small_own[4],
        small_own[5],
        up_grad,
        down_grad,
    )


def solution(mesh):
    by_chip = mesh.shape["shard"] == 4 and mesh.shape["replica"] == 8
    replica = ("y", "x", "core") if by_chip else "replica"
    row = P(replica)
    clip = P(replica, "shard", None)
    text = P(replica, None, None)
    vector = P("shard")
    matrix = P("shard", None)
    weights = (
        [vector, vector] + [matrix] * 4 + [vector, vector] + [matrix] * 4 + [vector, vector]
        + [matrix] * 2
    )
    if by_chip:
        mesh = Mesh(mesh.devices.reshape(2, 2, 2, 4), ("y", "x", "core", "shard"))
    return jax.shard_map(
        clip_body if by_chip else general_body,
        mesh=mesh,
        in_specs=(clip, text, P(replica, None), row, row, clip, *weights),
        out_specs=(clip, P(), clip, text, *weights),
        check_vma=False,
    )
```

```python
import jax
import jax.numpy as jnp
from jax import lax
from jax.experimental import pallas as pl
from jax.experimental.pallas import tpu as pltpu
from jax.sharding import Mesh
from jax.sharding import PartitionSpec as P

HEADS = 24
HEAD_DIM = 64


epsilon = 1e-05
masked_score = -1e30


def layer_norm(values, gain, shift):
    center = values - jnp.mean(values, axis=-1, keepdims=True)
    variance = jnp.mean(center * center, axis=-1, keepdims=True)
    return center * lax.rsqrt(variance + epsilon) * gain + shift


def exact_gelu(values):
    return jax.nn.gelu(values, approximate=False)


def project(left, right):
    return jnp.dot(left, right, preferred_element_type=jnp.float32)


def outer_sum(left, right):
    return jnp.einsum("rd,re->de", left, right, preferred_element_type=jnp.float32)


def back_project(grads, matrix):
    return jnp.einsum("re,de->rd", grads, matrix, preferred_element_type=jnp.float32)


def split_heads(values):
    return values.reshape(values.shape[:-1] + (HEADS, HEAD_DIM))


def self_forward(operands):
    queries, keys_all, values_all, allowed = operands
    scale = HEAD_DIM ** (-0.5)
    scores = (
        jnp.einsum("qhd,khd->hqk", queries, keys_all, preferred_element_type=jnp.float32) * scale
    )
    scores = jnp.where(allowed[None], scores, masked_score)
    peak = jnp.max(scores, axis=-1, keepdims=True)
    weights = jnp.exp(scores - peak)
    totals = jnp.sum(weights, axis=-1, keepdims=True)
    probs = (weights / totals).astype(jnp.bfloat16)
    mixed = jnp.einsum("hqk,khd->qhd", probs, values_all, preferred_element_type=jnp.float32)
    return (mixed.astype(jnp.bfloat16), (peak + jnp.log(totals))[..., 0])


def self_backward(operands):
    queries, keys_all, values_all, allowed, log_totals, grad_mixed = operands
    scale = HEAD_DIM ** (-0.5)
    scores = (
        jnp.einsum("qhd,khd->hqk", queries, keys_all, preferred_element_type=jnp.float32) * scale
    )
    scores = jnp.where(allowed[None], scores, masked_score)
    probs = jnp.exp(scores - log_totals[..., None])
    grad_probs = jnp.einsum(
        "qhd,khd->hqk", grad_mixed, values_all, preferred_element_type=jnp.float32
    )
    grad_values = jnp.einsum(
        "hqk,qhd->khd", probs.astype(jnp.bfloat16), grad_mixed, preferred_element_type=jnp.float32
    )
    inner = jnp.sum(probs * grad_probs, axis=-1, keepdims=True)
    grad_scores = (probs * (grad_probs - inner)).astype(jnp.bfloat16)
    grad_queries = (
        jnp.einsum("hqk,khd->qhd", grad_scores, keys_all, preferred_element_type=jnp.float32)
        * scale
    ).astype(jnp.bfloat16)
    grad_keys = (
        jnp.einsum("hqk,qhd->khd", grad_scores, queries, preferred_element_type=jnp.float32) * scale
    )
    return (grad_queries, grad_keys, grad_values)


def general_body(
    frames,
    text_states,
    text_mask,
    clip_lengths,
    slot_used,
    teacher,
    self_norm_gain,
    self_norm_bias,
    self_query_weight,
    self_key_weight,
    self_value_weight,
    self_output_weight,
    cross_norm_gain,
    cross_norm_bias,
    cross_query_weight,
    cross_key_weight,
    cross_value_weight,
    cross_output_weight,
    feed_norm_gain,
    feed_norm_bias,
    feed_up_weight,
    feed_down_weight,
):
    gathered = (
        lax.all_gather(self_norm_gain, "shard", axis=0, tiled=True),
        lax.all_gather(self_norm_bias, "shard", axis=0, tiled=True),
        lax.all_gather(self_query_weight, "shard", axis=0, tiled=True),
        lax.all_gather(self_key_weight, "shard", axis=0, tiled=True),
        lax.all_gather(self_value_weight, "shard", axis=0, tiled=True),
        lax.all_gather(self_output_weight, "shard", axis=0, tiled=True),
        lax.all_gather(cross_norm_gain, "shard", axis=0, tiled=True),
        lax.all_gather(cross_norm_bias, "shard", axis=0, tiled=True),
        lax.all_gather(cross_query_weight, "shard", axis=0, tiled=True),
        lax.all_gather(cross_key_weight, "shard", axis=0, tiled=True),
        lax.all_gather(cross_value_weight, "shard", axis=0, tiled=True),
        lax.all_gather(cross_output_weight, "shard", axis=0, tiled=True),
        lax.all_gather(feed_norm_gain, "shard", axis=0, tiled=True),
        lax.all_gather(feed_norm_bias, "shard", axis=0, tiled=True),
        lax.all_gather(feed_up_weight, "shard", axis=0, tiled=True),
        lax.all_gather(feed_down_weight, "shard", axis=0, tiled=True),
    )
    (
        gain_attend,
        bias_attend,
        query_matrix,
        key_matrix,
        value_matrix,
        output_matrix,
        gain_cross,
        bias_cross,
        probe_matrix,
        lookup_matrix,
        content_matrix,
        merge_matrix,
        gain_feed,
        bias_feed,
        expand_matrix,
        reduce_matrix,
    ) = gathered
    slots = frames.shape[0]
    frame_count = frames.shape[1]
    width = frames.shape[2]
    text_len = text_states.shape[1]
    shards = lax.axis_size("shard")
    replicas = lax.axis_size("replica")
    clip_total = frame_count * shards
    row_count = slots * frame_count
    scale = HEAD_DIM ** (-0.5)
    shard_rank = lax.axis_index("shard")
    positions = shard_rank * frame_count + jnp.arange(frame_count, dtype=jnp.int32)
    key_positions = jnp.arange(clip_total, dtype=jnp.int32)
    allowed = (key_positions[None, None, :] <= positions[None, :, None]) & (
        key_positions[None, None, :] < clip_lengths[:, None, None]
    )
    valid_rows = ((positions[None, :] < clip_lengths[:, None]) & (slot_used[:, None] > 0)).astype(
        jnp.float32
    )
    text_allowed = text_mask > 0
    inputs = frames.astype(jnp.float32)
    normed_one, pull_one = jax.vjp(
        layer_norm, inputs, gain_attend.astype(jnp.float32), bias_attend.astype(jnp.float32)
    )
    hidden_one = normed_one.astype(jnp.bfloat16).reshape(row_count, width)
    queries = (
        project(hidden_one, query_matrix).astype(jnp.bfloat16).reshape(slots, frame_count, width)
    )
    keys_local = (
        project(hidden_one, key_matrix).astype(jnp.bfloat16).reshape(slots, frame_count, width)
    )
    values_local = (
        project(hidden_one, value_matrix).astype(jnp.bfloat16).reshape(slots, frame_count, width)
    )
    keys_all, values_all = (
        lax.all_gather(keys_local, "shard", axis=1, tiled=True),
        lax.all_gather(values_local, "shard", axis=1, tiled=True),
    )
    head_queries = split_heads(queries)
    head_keys = split_heads(keys_all)
    head_values = split_heads(values_all)
    mixed_self, log_totals = lax.map(self_forward, (head_queries, head_keys, head_values, allowed))
    mixed_rows = mixed_self.reshape(row_count, width)
    after_self = inputs + project(mixed_rows, output_matrix).reshape(slots, frame_count, width)
    normed_two, pull_two = jax.vjp(
        layer_norm, after_self, gain_cross.astype(jnp.float32), bias_cross.astype(jnp.float32)
    )
    hidden_two = normed_two.astype(jnp.bfloat16).reshape(row_count, width)
    probes = split_heads(
        project(hidden_two, probe_matrix).astype(jnp.bfloat16).reshape(slots, frame_count, width)
    )
    text_rows = text_states.reshape(slots * text_len, width)
    lookups = split_heads(
        project(text_rows, lookup_matrix).astype(jnp.bfloat16).reshape(slots, text_len, width)
    )
    contents = split_heads(
        project(text_rows, content_matrix).astype(jnp.bfloat16).reshape(slots, text_len, width)
    )
    cross_scores = (
        jnp.einsum("sqhd,skhd->shqk", probes, lookups, preferred_element_type=jnp.float32) * scale
    )
    cross_scores = jnp.where(text_allowed[:, None, None, :], cross_scores, masked_score)
    cross_peak = jnp.max(cross_scores, axis=-1, keepdims=True)
    cross_weights = jnp.exp(cross_scores - cross_peak)
    cross_probs = cross_weights / jnp.sum(cross_weights, axis=-1, keepdims=True)
    cross_probs_low = cross_probs.astype(jnp.bfloat16)
    cross_mixed = jnp.einsum(
        "shqk,skhd->sqhd", cross_probs_low, contents, preferred_element_type=jnp.float32
    )
    cross_mixed = cross_mixed.astype(jnp.bfloat16).reshape(row_count, width)
    after_cross = after_self + project(cross_mixed, merge_matrix).reshape(slots, frame_count, width)
    normed_three, pull_three = jax.vjp(
        layer_norm, after_cross, gain_feed.astype(jnp.float32), bias_feed.astype(jnp.float32)
    )
    hidden_three = normed_three.astype(jnp.bfloat16).reshape(row_count, width)
    upward = project(hidden_three, expand_matrix)
    activated, gelu_pull = jax.vjp(exact_gelu, upward)
    activated_low = activated.astype(jnp.bfloat16)
    result = after_cross + project(activated_low, reduce_matrix).reshape(slots, frame_count, width)
    output = result.astype(jnp.bfloat16)
    errors = (result - teacher.astype(jnp.float32)) * valid_rows[..., None]
    squares_total, count_total = lax.psum(
        (jnp.sum(errors * errors), jnp.sum(valid_rows)), ("replica", "shard")
    )
    loss = squares_total / (width * count_total)
    grad_result = errors * (slots * replicas * clip_total / count_total)
    grad_feed_low = grad_result.reshape(row_count, width).astype(jnp.bfloat16)
    grad_activated = back_project(grad_feed_low, reduce_matrix)
    grad_upward = gelu_pull(grad_activated)[0].astype(jnp.bfloat16)
    grad_hidden_three = back_project(grad_upward, expand_matrix).reshape(slots, frame_count, width)
    grad_cross_norm, gain_feed_part, bias_feed_part = pull_three(grad_hidden_three)
    grad_after_cross = grad_result + grad_cross_norm
    feed_owned = (
        lax.psum_scatter(
            outer_sum(hidden_three, grad_upward).astype(jnp.bfloat16),
            "shard",
            scatter_dimension=0,
            tiled=True,
        ).astype(jnp.float32),
        lax.psum_scatter(
            outer_sum(activated_low, grad_feed_low).astype(jnp.bfloat16),
            "shard",
            scatter_dimension=0,
            tiled=True,
        ).astype(jnp.float32),
        lax.psum_scatter(
            gain_feed_part.astype(jnp.bfloat16), "shard", scatter_dimension=0, tiled=True
        ).astype(jnp.float32),
        lax.psum_scatter(
            bias_feed_part.astype(jnp.bfloat16), "shard", scatter_dimension=0, tiled=True
        ).astype(jnp.float32),
    )
    grad_cross_low = grad_after_cross.reshape(row_count, width).astype(jnp.bfloat16)
    grad_cross_mixed = split_heads(
        back_project(grad_cross_low, merge_matrix)
        .astype(jnp.bfloat16)
        .reshape(slots, frame_count, width)
    )
    grad_cross_probs = jnp.einsum(
        "sqhd,skhd->shqk", grad_cross_mixed, contents, preferred_element_type=jnp.float32
    )
    content_grads = jnp.einsum(
        "shqk,sqhd->skhd", cross_probs_low, grad_cross_mixed, preferred_element_type=jnp.float32
    )
    cross_inner = jnp.sum(cross_probs * grad_cross_probs, axis=-1, keepdims=True)
    grad_cross_scores = (cross_probs * (grad_cross_probs - cross_inner)).astype(jnp.bfloat16)
    probe_grads = (
        jnp.einsum(
            "shqk,skhd->sqhd", grad_cross_scores, lookups, preferred_element_type=jnp.float32
        )
        * scale
    )
    probe_grads = probe_grads.astype(jnp.bfloat16).reshape(row_count, width)
    lookup_grads = (
        jnp.einsum("shqk,sqhd->skhd", grad_cross_scores, probes, preferred_element_type=jnp.float32)
        * scale
    )
    lookup_sum, content_sum = (
        lax.psum(lookup_grads.astype(jnp.bfloat16), "shard").astype(jnp.float32),
        lax.psum(content_grads.astype(jnp.bfloat16), "shard").astype(jnp.float32),
    )
    lookup_low = lookup_sum.astype(jnp.bfloat16).reshape(slots * text_len, width)
    content_low = content_sum.astype(jnp.bfloat16).reshape(slots * text_len, width)
    own_width = width // shards
    own_text = lax.dynamic_slice_in_dim(text_rows, shard_rank * own_width, own_width, 1)
    lookup_own = outer_sum(own_text, lookup_low)
    content_own = outer_sum(own_text, content_low)
    text_grad = (
        back_project(lookup_low, lookup_matrix) + back_project(content_low, content_matrix)
    ).reshape(slots, text_len, width)
    grad_hidden_two = back_project(probe_grads, probe_matrix).reshape(slots, frame_count, width)
    grad_self_norm, gain_cross_part, bias_cross_part = pull_two(grad_hidden_two)
    grad_after_self = grad_after_cross + grad_self_norm
    grad_self_low = grad_after_self.reshape(row_count, width).astype(jnp.bfloat16)
    grad_mixed = split_heads(
        back_project(grad_self_low, output_matrix)
        .astype(jnp.bfloat16)
        .reshape(slots, frame_count, width)
    )
    grad_queries, grad_keys, grad_values = lax.map(
        self_backward, (head_queries, head_keys, head_values, allowed, log_totals, grad_mixed)
    )
    key_sum, value_sum = (
        lax.psum_scatter(
            grad_keys.reshape(slots, clip_total, width).astype(jnp.bfloat16),
            "shard",
            scatter_dimension=1,
            tiled=True,
        ).astype(jnp.float32),
        lax.psum_scatter(
            grad_values.reshape(slots, clip_total, width).astype(jnp.bfloat16),
            "shard",
            scatter_dimension=1,
            tiled=True,
        ).astype(jnp.float32),
    )
    key_low = key_sum.astype(jnp.bfloat16).reshape(row_count, width)
    value_low = value_sum.astype(jnp.bfloat16).reshape(row_count, width)
    query_low = grad_queries.reshape(row_count, width)
    grad_hidden_one = (
        back_project(query_low, query_matrix)
        + back_project(key_low, key_matrix)
        + back_project(value_low, value_matrix)
    )
    grad_inputs, gain_attend_part, bias_attend_part = pull_one(
        grad_hidden_one.reshape(slots, frame_count, width)
    )
    frames_grad = grad_after_self + grad_inputs
    attend_owned = (
        lax.psum_scatter(
            outer_sum(hidden_one, query_low).astype(jnp.bfloat16),
            "shard",
            scatter_dimension=0,
            tiled=True,
        ).astype(jnp.float32),
        lax.psum_scatter(
            outer_sum(hidden_one, key_low).astype(jnp.bfloat16),
            "shard",
            scatter_dimension=0,
            tiled=True,
        ).astype(jnp.float32),
        lax.psum_scatter(
            outer_sum(hidden_one, value_low).astype(jnp.bfloat16),
            "shard",
            scatter_dimension=0,
            tiled=True,
        ).astype(jnp.float32),
        lax.psum_scatter(
            outer_sum(mixed_rows, grad_self_low).astype(jnp.bfloat16),
            "shard",
            scatter_dimension=0,
            tiled=True,
        ).astype(jnp.float32),
        lax.psum_scatter(
            outer_sum(hidden_two, probe_grads).astype(jnp.bfloat16),
            "shard",
            scatter_dimension=0,
            tiled=True,
        ).astype(jnp.float32),
        lax.psum_scatter(
            outer_sum(cross_mixed, grad_cross_low).astype(jnp.bfloat16),
            "shard",
            scatter_dimension=0,
            tiled=True,
        ).astype(jnp.float32),
        lax.psum_scatter(
            gain_attend_part.astype(jnp.bfloat16), "shard", scatter_dimension=0, tiled=True
        ).astype(jnp.float32),
        lax.psum_scatter(
            bias_attend_part.astype(jnp.bfloat16), "shard", scatter_dimension=0, tiled=True
        ).astype(jnp.float32),
        lax.psum_scatter(
            gain_cross_part.astype(jnp.bfloat16), "shard", scatter_dimension=0, tiled=True
        ).astype(jnp.float32),
        lax.psum_scatter(
            bias_cross_part.astype(jnp.bfloat16), "shard", scatter_dimension=0, tiled=True
        ).astype(jnp.float32),
    )
    summed = (
        lax.psum(attend_owned[6].astype(jnp.bfloat16), "replica").astype(jnp.float32),
        lax.psum(attend_owned[7].astype(jnp.bfloat16), "replica").astype(jnp.float32),
        lax.psum(attend_owned[0].astype(jnp.bfloat16), "replica").astype(jnp.float32),
        lax.psum(attend_owned[1].astype(jnp.bfloat16), "replica").astype(jnp.float32),
        lax.psum(attend_owned[2].astype(jnp.bfloat16), "replica").astype(jnp.float32),
        lax.psum(attend_owned[3].astype(jnp.bfloat16), "replica").astype(jnp.float32),
        lax.psum(attend_owned[8].astype(jnp.bfloat16), "replica").astype(jnp.float32),
        lax.psum(attend_owned[9].astype(jnp.bfloat16), "replica").astype(jnp.float32),
        lax.psum(attend_owned[4].astype(jnp.bfloat16), "replica").astype(jnp.float32),
        lax.psum(lookup_own.astype(jnp.bfloat16), "replica").astype(jnp.float32),
        lax.psum(content_own.astype(jnp.bfloat16), "replica").astype(jnp.float32),
        lax.psum(attend_owned[5].astype(jnp.bfloat16), "replica").astype(jnp.float32),
        lax.psum(feed_owned[2].astype(jnp.bfloat16), "replica").astype(jnp.float32),
        lax.psum(feed_owned[3].astype(jnp.bfloat16), "replica").astype(jnp.float32),
        lax.psum(feed_owned[0].astype(jnp.bfloat16), "replica").astype(jnp.float32),
        lax.psum(feed_owned[1].astype(jnp.bfloat16), "replica").astype(jnp.float32),
    )
    return (
        output,
        loss,
        frames_grad,
        text_grad,
        summed[0],
        summed[1],
        summed[2],
        summed[3],
        summed[4],
        summed[5],
        summed[6],
        summed[7],
        summed[8],
        summed[9],
        summed[10],
        summed[11],
        summed[12],
        summed[13],
        summed[14],
        summed[15],
    )


PAIR = 2 * HEAD_DIM
EVERY = ("shard", "y", "x", "core")
REPLICAS = ("core", "y", "x")
NT = (((1,), (1,)), ((), ()))
TN = (((0,), (0,)), ((), ()))
NN = (((1,), (0,)), ((), ()))


def dot(left, right, dims):
    return lax.dot_general(left, right, dims, preferred_element_type=jnp.float32)


def half_mask(side, value):
    lanes = lax.broadcasted_iota(jnp.int32, (1, PAIR), 1)
    inside = (lanes >= HEAD_DIM) if side else (lanes < HEAD_DIM)
    return jnp.where(inside, value, 0.0).astype(jnp.bfloat16)


def fill_clip(place, own_ref, other_ref, all_ref):
    block = own_ref.shape[0] // 2
    for part in range(2):
        rows = slice(part * block, (part + 1) * block)
        for at, ref in ((place[part], own_ref), (place[3 + part], other_ref)):
            all_ref[pl.ds(pl.multiple_of(at * block, block), block), :] = ref[rows, :]


def self_forward_kernel(
    place, q_ref, own_k, own_v, other_k, other_v, mixed_ref, lse_ref, k_ref, v_ref, acc_ref
):
    fill_clip(place, own_k, other_k, k_ref)
    fill_clip(place, own_v, other_v, v_ref)
    block = q_ref.shape[0] // 2
    length = place[2]
    low = lax.broadcasted_iota(jnp.int32, (PAIR, 1), 0) < HEAD_DIM
    for part in range(2):
        first = place[part] * block
        rows = slice(part * block, (part + 1) * block)
        q = q_ref[rows, :]
        q_half = [q * half_mask(side, HEAD_DIM ** (-0.5)) for side in range(2)]
        limit = jnp.minimum(
            first + lax.broadcasted_iota(jnp.int32, (1, block), 1) + 1, length
        )
        acc_ref[...] = jnp.zeros_like(acc_ref)

        def step(j, peaks, q_half=q_half, limit=limit):
            at = pl.multiple_of(j * block, block)
            k = k_ref[pl.ds(at, block), :]
            v = v_ref[pl.ds(at, block), :]
            allowed = at + lax.broadcasted_iota(jnp.int32, (block, block), 0) < limit
            out = []
            for side in range(2):
                scores = jnp.where(allowed, dot(k, q_half[side], NT), masked_score)
                peak = jnp.maximum(peaks[side], jnp.max(scores, axis=0, keepdims=True))
                weights = jnp.exp(scores - peak).astype(jnp.bfloat16)
                v_ones = v * half_mask(side, 1.0) + half_mask(1 - side, 1.0)
                acc_ref[side] = acc_ref[side] * jnp.exp(peaks[side] - peak) + dot(
                    v_ones, weights, TN
                )
                out.append(peak)
            return tuple(out)

        peaks = lax.fori_loop(
            0, place[part] + 1, step, (jnp.full((1, block), masked_score, jnp.float32),) * 2
        )
        top, bottom = acc_ref[0], acc_ref[1]
        total = jnp.where(low, top[HEAD_DIM : HEAD_DIM + 1], bottom[0:1])
        mixed = jnp.where(low, top, bottom) / total
        mixed_ref[rows, :] = mixed.T.astype(jnp.bfloat16)
        lse_ref[0:1, rows] = peaks[0] + jnp.log(top[HEAD_DIM : HEAD_DIM + 1])
        lse_ref[1:2, rows] = peaks[1] + jnp.log(bottom[0:1])


def self_backward_kernel(
    place, q_ref, own_k, own_v, other_k, other_v, mixed_ref, grad_ref, lse_ref,
    dq_ref, own_dk, own_dv, other_dk, other_dv, k_ref, v_ref, dq_acc, dk_acc, dv_acc,
):
    fill_clip(place, own_k, other_k, k_ref)
    fill_clip(place, own_v, other_v, v_ref)
    block = q_ref.shape[0] // 2
    length = place[2]
    scale = HEAD_DIM ** (-0.5)
    dk_acc[...] = jnp.zeros_like(dk_acc)
    dv_acc[...] = jnp.zeros_like(dv_acc)
    for part in range(2):
        first = place[part] * block
        rows = slice(part * block, (part + 1) * block)
        q = q_ref[rows, :]
        grad = grad_ref[rows, :]
        q_half = [q * half_mask(side, scale) for side in range(2)]
        grad_half = [grad * half_mask(side, 1.0) for side in range(2)]
        product = (grad.astype(jnp.float32) * mixed_ref[rows, :].astype(jnp.float32)).T
        inner = [
            jnp.sum(product[side * HEAD_DIM : (side + 1) * HEAD_DIM], axis=0, keepdims=True)
            for side in range(2)
        ]
        lse = [lse_ref[side : side + 1, rows] for side in range(2)]
        limit = jnp.minimum(
            first + lax.broadcasted_iota(jnp.int32, (1, block), 1) + 1, length
        )
        dq_acc[...] = jnp.zeros_like(dq_acc)

        def step(
            j, carry, q_half=q_half, grad_half=grad_half, inner=inner, lse=lse, limit=limit
        ):
            at = pl.multiple_of(j * block, block)
            k = k_ref[pl.ds(at, block), :]
            v = v_ref[pl.ds(at, block), :]
            allowed = at + lax.broadcasted_iota(jnp.int32, (block, block), 0) < limit
            dq, dk, dv = 0.0, 0.0, 0.0
            for side in range(2):
                scores = jnp.where(allowed, dot(k, q_half[side], NT), masked_score)
                probs = jnp.exp(scores - lse[side])
                grad_probs = dot(v, grad_half[side], NT)
                grad_scores = (probs * (grad_probs - inner[side])).astype(jnp.bfloat16)
                dv += dot(probs.astype(jnp.bfloat16), grad_half[side], NN)
                dk += dot(grad_scores, q_half[side], NN)
                dq += dot(k * half_mask(side, scale), grad_scores, TN)
            dk_acc[pl.ds(at, block), :] += dk
            dv_acc[pl.ds(at, block), :] += dv
            dq_acc[...] += dq
            return carry

        lax.fori_loop(0, place[part] + 1, step, 0)
        dq_ref[rows, :] = dq_acc[...].T.astype(jnp.bfloat16)
    for part in range(2):
        rows = slice(part * block, (part + 1) * block)
        own = pl.ds(pl.multiple_of(place[part] * block, block), block)
        other = pl.ds(pl.multiple_of(place[3 + part] * block, block), block)
        own_dk[rows, :] = dk_acc[own, :].astype(jnp.bfloat16)
        own_dv[rows, :] = dv_acc[own, :].astype(jnp.bfloat16)
        other_dk[rows, :] = dk_acc[other, :].astype(jnp.bfloat16)
        other_dv[rows, :] = dv_acc[other, :].astype(jnp.bfloat16)


def pair_block(rows):
    return pl.BlockSpec((rows, PAIR), lambda i, *_: (0, i))


def value_block(rows, pairs):
    return pl.BlockSpec((rows, PAIR), lambda i, *_: (0, pairs + i))


def self_attend(place, queries, own, other):
    rows, width = queries.shape
    clip = 2 * rows
    pairs = width // PAIR
    return pl.pallas_call(
        self_forward_kernel,
        out_shape=(
            jax.ShapeDtypeStruct((rows, width), jnp.bfloat16),
            jax.ShapeDtypeStruct((pairs * 8, rows), jnp.float32),
        ),
        grid_spec=pltpu.PrefetchScalarGridSpec(
            num_scalar_prefetch=1,
            grid=(pairs,),
            in_specs=[pair_block(rows)] + [pair_block(rows), value_block(rows, pairs)] * 2,
            out_specs=(pair_block(rows), pl.BlockSpec((8, rows), lambda i, *_: (i, 0))),
            scratch_shapes=[
                pltpu.VMEM((clip, PAIR), jnp.bfloat16),
                pltpu.VMEM((clip, PAIR), jnp.bfloat16),
                pltpu.VMEM((2, PAIR, rows // 2), jnp.float32),
            ],
        ),
        compiler_params=pltpu.CompilerParams(vmem_limit_bytes=32 * 2**20),
        cost_estimate=pl.CostEstimate(
            flops=2 * 2 * rows * clip * width, bytes_accessed=8 * clip * width, transcendentals=0
        ),
        name="self_attend",
    )(place, queries, own, own, other, other)


def self_attend_back(place, queries, own, other, mixed, grads, lse):
    rows, width = queries.shape
    clip = 2 * rows
    pairs = width // PAIR
    return pl.pallas_call(
        self_backward_kernel,
        out_shape=(jax.ShapeDtypeStruct((rows, width), jnp.bfloat16),) * 5,
        grid_spec=pltpu.PrefetchScalarGridSpec(
            num_scalar_prefetch=1,
            grid=(pairs,),
            in_specs=[pair_block(rows)]
            + [pair_block(rows), value_block(rows, pairs)] * 2
            + [
                pair_block(rows),
                pair_block(rows),
                pl.BlockSpec((8, rows), lambda i, *_: (i, 0)),
            ],
            out_specs=(pair_block(rows),) * 5,
            scratch_shapes=[
                pltpu.VMEM((clip, PAIR), jnp.bfloat16),
                pltpu.VMEM((clip, PAIR), jnp.bfloat16),
                pltpu.VMEM((PAIR, rows // 2), jnp.float32),
                pltpu.VMEM((clip, PAIR), jnp.float32),
                pltpu.VMEM((clip, PAIR), jnp.float32),
            ],
        ),
        compiler_params=pltpu.CompilerParams(vmem_limit_bytes=32 * 2**20),
        cost_estimate=pl.CostEstimate(
            flops=5 * 2 * rows * clip * width, bytes_accessed=16 * clip * width, transcendentals=0
        ),
        name="self_attend_back",
    )(place, queries, own, own, other, other, mixed, grads, lse)


def both_heads(rows, value):
    return jnp.concatenate([rows * half_mask(side, value) for side in range(2)], axis=0)


def cross_probs_of(lookup_two, probes, present):
    text = present.shape[0]
    scores = dot(lookup_two, probes, NT)
    out = []
    for side in range(2):
        part = jnp.where(
            present > 0, scores[side * text : (side + 1) * text], masked_score
        )
        weights = jnp.exp(part - jnp.max(part, axis=0, keepdims=True))
        out.append(weights / jnp.sum(weights, axis=0, keepdims=True))
    return out


def cross_forward_kernel(probe_ref, lookup_ref, content_ref, present_ref, mixed_ref):
    probs = cross_probs_of(
        both_heads(lookup_ref[...], HEAD_DIM ** (-0.5)), probe_ref[...], present_ref[...]
    )
    probs = jnp.concatenate(probs, axis=0).astype(jnp.bfloat16)
    mixed_ref[...] = dot(probs, both_heads(content_ref[...], 1.0), TN).astype(jnp.bfloat16)


def cross_backward_kernel(
    probe_ref, lookup_ref, content_ref, present_ref, grad_ref, dp_ref, dl_ref, dc_ref
):
    text = present_ref.shape[0]
    scale = HEAD_DIM ** (-0.5)
    probes = probe_ref[...]
    grads = grad_ref[...]
    lookup_two = both_heads(lookup_ref[...], scale)
    probs = cross_probs_of(lookup_two, probes, present_ref[...])
    grad_probs = dot(both_heads(content_ref[...], 1.0), grads, NT)
    grad_scores = []
    for side in range(2):
        part = grad_probs[side * text : (side + 1) * text]
        inner = jnp.sum(probs[side] * part, axis=0, keepdims=True)
        grad_scores.append(probs[side] * (part - inner))
    grad_scores = jnp.concatenate(grad_scores, axis=0).astype(jnp.bfloat16)
    probs = jnp.concatenate(probs, axis=0).astype(jnp.bfloat16)
    low = lax.broadcasted_iota(jnp.int32, (1, PAIR), 1) < HEAD_DIM
    dp_ref[...] = dot(grad_scores, lookup_two, TN).astype(jnp.bfloat16)
    dl = dot(grad_scores, probes, NN) * scale
    dl_ref[...] = jnp.where(low, dl[:text], dl[text:]).astype(jnp.bfloat16)
    dc = dot(probs, grads, NN)
    dc_ref[...] = jnp.where(low, dc[:text], dc[text:]).astype(jnp.bfloat16)


def cross_attend(probes, lookups, contents, present):
    rows, width = probes.shape
    text = lookups.shape[0]
    return pl.pallas_call(
        cross_forward_kernel,
        out_shape=jax.ShapeDtypeStruct((rows, width), jnp.bfloat16),
        grid=(width // PAIR,),
        in_specs=[
            pair_block(rows),
            pair_block(text),
            pair_block(text),
            pl.BlockSpec((text, 1), lambda i: (0, 0)),
        ],
        out_specs=pair_block(rows),
        compiler_params=pltpu.CompilerParams(vmem_limit_bytes=32 * 2**20),
        cost_estimate=pl.CostEstimate(
            flops=8 * rows * text * width, bytes_accessed=4 * rows * width, transcendentals=0
        ),
        name="cross_attend",
    )(probes, lookups, contents, present)


def cross_attend_back(probes, lookups, contents, present, grads):
    rows, width = probes.shape
    text = lookups.shape[0]
    return pl.pallas_call(
        cross_backward_kernel,
        out_shape=(
            jax.ShapeDtypeStruct((rows, width), jnp.bfloat16),
            jax.ShapeDtypeStruct((text, width), jnp.bfloat16),
            jax.ShapeDtypeStruct((text, width), jnp.bfloat16),
        ),
        grid=(width // PAIR,),
        in_specs=[
            pair_block(rows),
            pair_block(text),
            pair_block(text),
            pl.BlockSpec((text, 1), lambda i: (0, 0)),
            pair_block(rows),
        ],
        out_specs=(pair_block(rows), pair_block(text), pair_block(text)),
        compiler_params=pltpu.CompilerParams(vmem_limit_bytes=32 * 2**20),
        cost_estimate=pl.CostEstimate(
            flops=20 * rows * text * width, bytes_accessed=6 * rows * width, transcendentals=0
        ),
        name="cross_attend_back",
    )(probes, lookups, contents, present, grads)


def unpack_kernel(in_ref, out_ref):
    pieces = in_ref[...]
    out_ref[...] = pieces.reshape(-1, pieces.shape[-1]).T.astype(jnp.float32)


def unpack(full, rows, place, out_shape, out_at, together):
    owners, _, features = full.shape
    tall = out_shape[0] // features
    wide = out_shape[1] // (together * rows)
    return pl.pallas_call(
        unpack_kernel,
        out_shape=jax.ShapeDtypeStruct(out_shape, jnp.float32),
        grid=(tall, wide),
        in_specs=[
            pl.BlockSpec((together, rows, features), lambda i, j: (j + out_at, place + i, 0))
        ],
        out_specs=pl.BlockSpec((features, together * rows), lambda i, j: (i, j)),
        compiler_params=pltpu.CompilerParams(vmem_limit_bytes=32 * 2**20),
        cost_estimate=pl.CostEstimate(
            flops=0, bytes_accessed=6 * out_shape[0] * out_shape[1], transcendentals=0
        ),
        name="unpack",
    )(full)


def held(values, *others):
    return list(lax.optimization_barrier((*values, *others))[: len(values)])


def after(value, *others):
    return lax.optimization_barrier((value, *others))[0]


def norm_parts(values):
    mean = jnp.mean(values, axis=-1, keepdims=True)
    center = values - mean
    return mean, lax.rsqrt(jnp.mean(center * center, axis=-1, keepdims=True) + epsilon)


def norm_back(grads, values, parts, gain):
    mean, inverse = parts
    unit = (values - mean) * inverse
    gain_grad = jnp.sum(grads * unit, axis=0)
    bias_grad = jnp.sum(grads, axis=0)
    scaled = grads * gain
    back = inverse * (
        scaled
        - jnp.mean(scaled, axis=-1, keepdims=True)
        - unit * jnp.mean(scaled * unit, axis=-1, keepdims=True)
    )
    return back, gain_grad, bias_grad


def clip_body(
    frames,
    text_states,
    text_mask,
    clip_lengths,
    slot_used,
    teacher,
    self_norm_gain,
    self_norm_bias,
    self_query_weight,
    self_key_weight,
    self_value_weight,
    self_output_weight,
    cross_norm_gain,
    cross_norm_bias,
    cross_query_weight,
    cross_key_weight,
    cross_value_weight,
    cross_output_weight,
    feed_norm_gain,
    feed_norm_bias,
    feed_up_weight,
    feed_down_weight,
):
    block, width = frames.shape[1:]
    text_len = text_states.shape[1]
    shards, replicas, outers = 4, 8, 4
    core = lax.axis_index("core")
    shard = lax.axis_index("shard")
    outer = 2 * lax.axis_index("y") + lax.axis_index("x")
    replica = 2 * outer + core
    clip = block * shards
    hidden_units = feed_up_weight.shape[1]

    holder = {0: 0, 1: 1, 2: 1, 3: 0}
    there = ([], [])
    for c in range(2):
        for s in range(4):
            for turn in range(2):
                slot = turn if s < 2 else 1 - turn
                there[turn].append((c * 4 + s, holder[s] * 4 + 2 * c + slot))
    back = tuple([(b, a) for a, b in pairs] for pairs in there)
    spot = ("core", "shard")
    swap = [(0, 1), (1, 0)]
    even = shard % 2 == 0
    lower = shard < 2
    first_core = core == 0

    def hop(values, distance):
        pairs = [(i, (i + distance) % shards) for i in range(shards)]
        return lax.ppermute(values, "shard", pairs)

    def hops(values):
        return [hop(values, distance) for distance in (1, 2, 3)]

    def line_up(mine, came):
        out = jnp.zeros((shards,) + mine.shape, mine.dtype)
        out = lax.dynamic_update_index_in_dim(out, mine, shard, 0)
        for distance, values in zip((1, 2, 3), came):
            owner = lax.rem(shard + shards - distance, shards)
            out = lax.dynamic_update_index_in_dim(out, values, owner, 0)
        return out

    def to_chip(pair):
        one = lax.ppermute(jnp.where(lower, pair[0], pair[1]), spot, there[0])
        two = lax.ppermute(jnp.where(lower, pair[1], pair[0]), spot, there[1])
        return one, two

    def by_time(one, two):
        return jnp.concatenate([jnp.where(even, one, two), jnp.where(even, two, one)], axis=0)

    def outgoing(values):
        early, late = values[:block], values[block:]
        return jnp.where(even, early, late), jnp.where(even, late, early)

    def from_chip(values):
        one, two = outgoing(values)
        return lax.ppermute(one, spot, back[0]), lax.ppermute(two, spot, back[1])

    def by_slot(one, two):
        return jnp.stack([jnp.where(lower, one, two), jnp.where(lower, two, one)])

    def share_of(weight):
        share = weight.shape[0] // replicas
        return lax.dynamic_slice_in_dim(weight, replica * share, share, 0)

    def from_replicas(line):
        full = lax.all_gather(line, ("y", "x", "core"), axis=1, tiled=True)
        return full.reshape(-1, line.shape[-1])

    qkv_share = jnp.concatenate(
        [share_of(self_query_weight), share_of(self_key_weight), share_of(self_value_weight)],
        axis=1,
    )
    vectors = jnp.concatenate(
        [
            self_norm_gain,
            self_norm_bias,
            cross_norm_gain,
            cross_norm_bias,
            feed_norm_gain,
            feed_norm_bias,
        ]
    )
    vectors = jnp.pad(vectors[None, :], ((0, 15), (0, 3 * width - 6 * block)))
    share = qkv_share.shape[0]
    qkv_mine = jnp.concatenate([qkv_share, vectors], axis=0)
    qkv_came = hops(qkv_mine)
    qkv_matrix = from_replicas(line_up(qkv_share, [values[:share] for values in qkv_came]))
    norms = line_up(vectors[0], [values[share] for values in qkv_came])
    norms = norms[:, : 6 * block].reshape(shards, 6, block).transpose(1, 0, 2)
    norms = norms.reshape(6, width).astype(jnp.float32)
    rest_share = jnp.concatenate(
        [share_of(self_output_weight), share_of(cross_query_weight), share_of(cross_output_weight)],
        axis=1,
    )
    rest_came = hops(after(rest_share, *qkv_came))
    rest = from_replicas(line_up(rest_share, rest_came))
    came = to_chip(after(frames, *rest_came))
    x_low = by_time(*came)
    expand_share = share_of(feed_up_weight)
    expand_came = hops(after(expand_share, *came))

    facts = jnp.concatenate(
        [(clip_lengths // 64)[:, None], (clip_lengths % 64)[:, None], slot_used[:, None], text_mask],
        axis=1,
    ).astype(jnp.bfloat16)
    facts = jnp.pad(facts[:, None, :], ((0, 0), (0, 15), (0, width - facts.shape[1])))
    text_sent = lax.ppermute(jnp.concatenate([text_states, facts], axis=1), "core", swap)
    text_other = text_sent[:, :text_len]
    both = jnp.stack([facts[:, 0], text_sent[:, text_len]])[:, :, : 3 + text_len].astype(jnp.int32)
    lengths = 64 * both[:, :, 0] + both[:, :, 1]
    fact = lax.dynamic_index_in_dim(
        jnp.where(shard // 2 == core, both[0], both[1]), shard % 2, 0, keepdims=False
    )
    length, used = 64 * fact[0] + fact[1], fact[2]
    present = fact[3:].reshape(text_len, 1)
    count = jnp.sum(
        jnp.where(both[:, :, 2] > 0, jnp.minimum(lengths, clip), 0).astype(jnp.float32)
    )
    count = jnp.full((8, 128), count)
    for axis in ("x", "y"):
        count += lax.ppermute(count, axis, swap)
    count = count[0, 0]
    text_all = jnp.concatenate(
        [
            jnp.where(first_core, text_states, text_other),
            jnp.where(first_core, text_other, text_states),
        ],
        axis=0,
    ).reshape(4 * text_len, width)
    text_all = lax.dynamic_slice_in_dim(text_all, shard * block, block, 1)
    text_matrix = jnp.where(first_core, cross_key_weight, cross_value_weight)
    text_part = project(text_all, text_matrix).astype(jnp.bfloat16).reshape(4, text_len, width)
    text_came = [
        hop(
            lax.dynamic_index_in_dim(
                text_part, lax.rem(shard + distance, shards), 0, keepdims=False
            ),
            distance,
        )
        for distance in (1, 2, 3)
    ]

    places = jnp.stack([core, 3 - core, length, 1 - core, 2 + core]).astype(jnp.int32)
    positions = jnp.concatenate(
        [core * block + jnp.arange(block), (3 - core) * block + jnp.arange(block)]
    )
    valid_rows = ((positions < length) & (used > 0)).astype(jnp.float32)[:, None]
    inputs = x_low.astype(jnp.float32)
    parts_one = norm_parts(inputs)
    hidden_one = ((inputs - parts_one[0]) * parts_one[1] * norms[0] + norms[1]).astype(
        jnp.bfloat16
    )
    kv = project(after(hidden_one, count), qkv_matrix[:, width:]).astype(jnp.bfloat16)
    kv_other = lax.ppermute(kv, "core", swap)
    expand_came = held(expand_came, kv)
    queries = project(after(hidden_one, kv, *expand_came), qkv_matrix[:, :width])
    queries = queries.astype(jnp.bfloat16)
    expand_matrix = from_replicas(line_up(expand_share, expand_came))
    reduce_share = share_of(feed_down_weight)
    reduce_came = hops(after(reduce_share, *expand_came))
    output_matrix = rest[:, :width]
    probe_matrix = rest[:, width : 2 * width]
    merge_matrix = rest[:, 2 * width :]
    mixed_self, lse = self_attend(after(places, *expand_came), queries, kv, kv_other)
    reduce_came = held(reduce_came, mixed_self)
    reduce_matrix = from_replicas(line_up(reduce_share, reduce_came))
    text_came = held(text_came, mixed_self)
    text_half = lax.dynamic_index_in_dim(text_part, shard, 0, keepdims=False).astype(jnp.float32)
    for values in text_came:
        text_half += values.astype(jnp.float32)
    text_half = text_half.astype(jnp.bfloat16)
    text_swap = lax.ppermute(text_half, "core", swap)
    lookups = jnp.where(first_core, text_half, text_swap)
    contents = jnp.where(first_core, text_swap, text_half)
    after_self = inputs + project(mixed_self, output_matrix)
    parts_two = norm_parts(after_self)
    hidden_two = ((after_self - parts_two[0]) * parts_two[1] * norms[2] + norms[3]).astype(
        jnp.bfloat16
    )
    probes = project(hidden_two, probe_matrix).astype(jnp.bfloat16)
    teacher_came = to_chip(after(teacher, *reduce_came, probes))
    cross_mixed = cross_attend(probes, lookups, contents, present)
    after_cross = after_self + project(cross_mixed, merge_matrix)
    parts_three = norm_parts(after_cross)
    hidden_three = (
        (after_cross - parts_three[0]) * parts_three[1] * norms[4] + norms[5]
    ).astype(jnp.bfloat16)
    upward = project(hidden_three, expand_matrix)
    activated, gelu_pull = jax.vjp(exact_gelu, upward)
    activated_low = activated.astype(jnp.bfloat16)
    teacher_low = by_time(*held(teacher_came, activated_low))
    result = after_cross + project(activated_low, reduce_matrix)
    errors = (result - teacher_low.astype(jnp.float32)) * valid_rows
    squares = jnp.sum(errors * errors)
    grad_result = errors * (4 * outers * clip / count)
    grad_feed_low = grad_result.astype(jnp.bfloat16)

    def theirs_of(right, left):
        columns = right.shape[1] // 2
        part = lax.dynamic_slice_in_dim(right, (1 - core) * columns, columns, 1)
        return outer_sum(part, left).astype(jnp.bfloat16)

    def ours_of(right, left, theirs):
        columns = right.shape[1] // 2
        sent = lax.ppermute(theirs, "core", swap)
        part = lax.dynamic_slice_in_dim(right, core * columns, columns, 1)
        return (outer_sum(part, left) + sent.astype(jnp.float32)).astype(jnp.bfloat16)

    def over_outer(values):
        return lax.psum_scatter(values, ("y", "x"), scatter_dimension=0, tiled=True)

    def shard_hops(values):
        columns = values.shape[1] // shards
        return [
            hop(
                lax.dynamic_slice_in_dim(
                    values, lax.rem(shard + distance, shards) * columns, columns, 1
                ),
                distance,
            )
            for distance in (1, 2, 3)
        ]

    def over_shard(values, came):
        columns = values.shape[1] // shards
        total = lax.dynamic_slice_in_dim(values, shard * columns, columns, 1).astype(jnp.float32)
        for part in came:
            total += part.astype(jnp.float32)
        return total.astype(jnp.bfloat16)

    down_theirs = theirs_of(grad_feed_low, activated_low)
    to_send = outgoing(result.astype(jnp.bfloat16))
    output_one = lax.ppermute(to_send[0], spot, back[0])
    grad_activated = back_project(after(grad_feed_low, down_theirs), reduce_matrix)
    grad_upward = gelu_pull(grad_activated)[0].astype(jnp.bfloat16)
    output_one = after(output_one, grad_upward)
    down_ours = ours_of(
        after(grad_feed_low, grad_upward, output_one), activated_low, down_theirs
    )
    down_sum = over_outer(down_ours)
    up_theirs = theirs_of(after(grad_upward, down_ours), hidden_three)
    grad_hidden_three = back_project(after(grad_upward, up_theirs), expand_matrix)
    output_two = lax.ppermute(after(to_send[1], output_one), spot, back[1])
    output_two = after(output_two, grad_hidden_three)
    output = by_slot(output_one, output_two)
    up_ours = ours_of(after(grad_upward, grad_hidden_three, output_two), hidden_three, up_theirs)
    grad_norm, gain_feed, bias_feed = norm_back(
        after(grad_hidden_three, up_ours), after_cross, parts_three, norms[4]
    )
    grad_after_cross = grad_result + grad_norm
    grad_cross_low = grad_after_cross.astype(jnp.bfloat16)
    merge_theirs = theirs_of(grad_cross_low, cross_mixed)
    grad_cross_mixed = back_project(after(grad_cross_low, merge_theirs), merge_matrix).astype(
        jnp.bfloat16
    )
    probe_grads, lookup_grads, content_grads = cross_attend_back(
        probes, lookups, contents, present, grad_cross_mixed
    )
    up_sum = over_outer(up_ours)
    text_mine = jnp.where(first_core, lookup_grads, content_grads)
    text_sent = lax.ppermute(
        jnp.where(first_core, content_grads, lookup_grads), "core", swap
    )
    text_mine = (text_mine.astype(jnp.float32) + text_sent.astype(jnp.float32)).astype(
        jnp.bfloat16
    )
    merge_ours = ours_of(after(grad_cross_low, probe_grads), cross_mixed, merge_theirs)
    probe_theirs = theirs_of(after(probe_grads, merge_ours), hidden_two)
    grad_hidden_two = back_project(after(probe_grads, probe_theirs), probe_matrix)
    text_four = line_up(text_mine, hops(text_mine)).reshape(4 * text_len, width)
    grad_norm, gain_cross, bias_cross = norm_back(
        grad_hidden_two, after_self, parts_two, norms[2]
    )
    grad_after_self = grad_after_cross + grad_norm
    grad_self_low = grad_after_self.astype(jnp.bfloat16)
    output_theirs = theirs_of(grad_self_low, mixed_self)
    grad_mixed = back_project(after(grad_self_low, output_theirs), output_matrix).astype(
        jnp.bfloat16
    )
    probe_ours = ours_of(after(probe_grads, grad_mixed), hidden_two, probe_theirs)
    text_weights = outer_sum(text_four, text_all).astype(jnp.bfloat16)
    text_back = back_project(text_four, text_matrix).astype(jnp.bfloat16)
    output_ours = ours_of(after(grad_self_low, probe_ours), mixed_self, output_theirs)
    text_rows = width // outers
    middle = jnp.concatenate(
        [
            values.reshape(outers, -1, width)
            for values in (
                output_ours,
                probe_ours,
                merge_ours,
                text_weights.reshape(outers, shards, text_rows // shards, block)
                .transpose(0, 2, 1, 3)
                .reshape(outers, text_rows // shards, width),
            )
        ],
        axis=1,
    )
    middle_rows = middle.shape[1]
    middle = middle.reshape(outers * middle_rows, width)
    middle_sum = over_outer(middle)
    text_split = text_rows // shards
    text_piece = (
        middle_sum[middle_rows - text_split :]
        .reshape(text_split, shards, block)
        .transpose(1, 0, 2)
        .reshape(text_rows, block)
    )
    text_back = text_back.reshape(2, 2, text_len, block)
    text_kept = lax.dynamic_index_in_dim(text_back, core, 0, keepdims=False)
    text_gone = lax.dynamic_index_in_dim(text_back, 1 - core, 0, keepdims=False)
    text_own = text_kept.astype(jnp.float32) + lax.ppermute(text_gone, "core", swap).astype(
        jnp.float32
    )
    text_own = text_own.astype(jnp.bfloat16)
    down_came = shard_hops(down_sum)
    text_came = hops(text_own)
    grad_queries, own_keys, own_values, other_keys, other_values = self_attend_back(
        places, queries, kv, kv_other, mixed_self, after(grad_mixed, middle, text_own), lse
    )
    text_came = held(text_came, grad_queries)
    down_came = held(down_came, grad_queries)
    other_keys, other_values = held([other_keys, other_values], *text_came, *down_came)
    own_keys += lax.ppermute(other_keys, "core", swap)
    own_values += lax.ppermute(other_values, "core", swap)
    down_piece = over_shard(down_sum, down_came)
    up_came = shard_hops(after(up_sum, down_piece))

    qkv_grads = jnp.concatenate([grad_queries, own_keys, own_values], axis=1)
    qkv_theirs = theirs_of(qkv_grads, hidden_one)
    grad_hidden_one = back_project(after(qkv_grads, qkv_theirs), qkv_matrix)
    qkv_ours = ours_of(after(qkv_grads, grad_hidden_one), hidden_one, qkv_theirs)
    up_came = held(up_came, grad_hidden_one)
    up_piece = over_shard(up_sum, up_came)
    text_grad = line_up(text_own, text_came).astype(jnp.float32)
    text_grad = text_grad.transpose(1, 2, 0, 3).reshape(text_states.shape)
    qkv_sum = over_outer(qkv_ours)
    middle_kept = after(middle_sum[: middle_rows - text_split], qkv_ours)
    middle_came = shard_hops(middle_kept)
    middle_piece = over_shard(middle_kept, middle_came)
    early = jnp.concatenate(
        [up_piece]
        + [down_piece[:, i * block : (i + 1) * block] for i in range(4)]
        + [text_piece, middle_piece],
        axis=0,
    )
    grad_norm, gain_self, bias_self = norm_back(
        after(grad_hidden_one, qkv_ours, early), inputs, parts_one, norms[0]
    )
    frames_low = (grad_after_self + grad_norm).astype(jnp.bfloat16)
    late_came = held(shard_hops(after(qkv_sum, *middle_came)), frames_low)
    frames_came = from_chip(after(frames_low, *late_came))
    frames_grad = by_slot(*frames_came).astype(jnp.float32)
    small = jnp.stack(
        [
            gain_self,
            bias_self,
            gain_cross,
            bias_cross,
            gain_feed,
            bias_feed,
            jnp.full((width,), squares),
            jnp.zeros((width,), jnp.float32),
        ]
    )
    small = after(small, *late_came)
    for axis in ("core", "x", "y"):
        small += lax.ppermute(small, axis, swap)
    small_came = shard_hops(small)
    small_own = lax.dynamic_slice_in_dim(small, shard * block, block, 1)
    for part in small_came:
        small_own += part
    loss = small_own[6, 0] / (width * count)
    early = lax.all_gather(after(early, text_grad), REPLICAS, axis=0)
    piece = width // replicas
    square = (block, width)
    up_grad = unpack(early, hidden_units // replicas, 0, (block, hidden_units), 0, 1)
    at = hidden_units // replicas // piece
    down_grad = unpack(early, piece, at, (4 * block, width), 0, 2)
    at += 4
    key_grad = unpack(early, text_rows, at * piece // text_rows, square, 0, 1)
    value_grad = unpack(early, text_rows, at * piece // text_rows, square, 4, 1)
    at += text_rows // piece
    output_grad = unpack(early, piece, at, square, 0, 2)
    probe_grad = unpack(early, piece, at + 1, square, 0, 2)
    merge_grad = unpack(early, piece, at + 2, square, 0, 2)
    late = over_shard(qkv_sum, late_came)
    late = lax.all_gather(
        after(late, early, *frames_came, small), REPLICAS, axis=0, tiled=True
    )
    late = late.reshape(-1, block, block)
    qkv_grad = [unpack(late, block, 0, square, 2 * i, 2) for i in range(3)]
    return (
        output,
        loss,
        frames_grad,
        text_grad,
        small_own[0],
        small_own[1],
        qkv_grad[0],
        qkv_grad[1],
        qkv_grad[2],
        output_grad,
        small_own[2],
        small_own[3],
        probe_grad,
        key_grad,
        value_grad,
        merge_grad,
        small_own[4],
        small_own[5],
        up_grad,
        down_grad,
    )


def solution(mesh):
    by_chip = mesh.shape["shard"] == 4 and mesh.shape["replica"] == 8
    replica = ("y", "x", "core") if by_chip else "replica"
    row = P(replica)
    clip = P(replica, "shard", None)
    text = P(replica, None, None)
    vector = P("shard")
    matrix = P("shard", None)
    weights = (
        [vector, vector] + [matrix] * 4 + [vector, vector] + [matrix] * 4 + [vector, vector]
        + [matrix] * 2
    )
    if by_chip:
        mesh = Mesh(mesh.devices.reshape(2, 2, 2, 4), ("y", "x", "core", "shard"))
    return jax.shard_map(
        clip_body if by_chip else general_body,
        mesh=mesh,
        in_specs=(clip, text, P(replica, None), row, row, clip, *weights),
        out_specs=(clip, P(), clip, text, *weights),
        check_vma=False,
    )
```

```python
import jax
import jax.numpy as jnp
from jax import lax
from jax.experimental import pallas as pl
from jax.experimental.pallas import tpu as pltpu
from jax.sharding import Mesh
from jax.sharding import PartitionSpec as P

HEADS = 24
HEAD_DIM = 64


epsilon = 1e-05
masked_score = -1e30


def layer_norm(values, gain, shift):
    center = values - jnp.mean(values, axis=-1, keepdims=True)
    variance = jnp.mean(center * center, axis=-1, keepdims=True)
    return center * lax.rsqrt(variance + epsilon) * gain + shift


def exact_gelu(values):
    return jax.nn.gelu(values, approximate=False)


def project(left, right):
    return jnp.dot(left, right, preferred_element_type=jnp.float32)


def outer_sum(left, right):
    return jnp.einsum("rd,re->de", left, right, preferred_element_type=jnp.float32)


def back_project(grads, matrix):
    return jnp.einsum("re,de->rd", grads, matrix, preferred_element_type=jnp.float32)


def split_heads(values):
    return values.reshape(values.shape[:-1] + (HEADS, HEAD_DIM))


def self_forward(operands):
    queries, keys_all, values_all, allowed = operands
    scale = HEAD_DIM ** (-0.5)
    scores = (
        jnp.einsum("qhd,khd->hqk", queries, keys_all, preferred_element_type=jnp.float32) * scale
    )
    scores = jnp.where(allowed[None], scores, masked_score)
    peak = jnp.max(scores, axis=-1, keepdims=True)
    weights = jnp.exp(scores - peak)
    totals = jnp.sum(weights, axis=-1, keepdims=True)
    probs = (weights / totals).astype(jnp.bfloat16)
    mixed = jnp.einsum("hqk,khd->qhd", probs, values_all, preferred_element_type=jnp.float32)
    return (mixed.astype(jnp.bfloat16), (peak + jnp.log(totals))[..., 0])


def self_backward(operands):
    queries, keys_all, values_all, allowed, log_totals, grad_mixed = operands
    scale = HEAD_DIM ** (-0.5)
    scores = (
        jnp.einsum("qhd,khd->hqk", queries, keys_all, preferred_element_type=jnp.float32) * scale
    )
    scores = jnp.where(allowed[None], scores, masked_score)
    probs = jnp.exp(scores - log_totals[..., None])
    grad_probs = jnp.einsum(
        "qhd,khd->hqk", grad_mixed, values_all, preferred_element_type=jnp.float32
    )
    grad_values = jnp.einsum(
        "hqk,qhd->khd", probs.astype(jnp.bfloat16), grad_mixed, preferred_element_type=jnp.float32
    )
    inner = jnp.sum(probs * grad_probs, axis=-1, keepdims=True)
    grad_scores = (probs * (grad_probs - inner)).astype(jnp.bfloat16)
    grad_queries = (
        jnp.einsum("hqk,khd->qhd", grad_scores, keys_all, preferred_element_type=jnp.float32)
        * scale
    ).astype(jnp.bfloat16)
    grad_keys = (
        jnp.einsum("hqk,qhd->khd", grad_scores, queries, preferred_element_type=jnp.float32) * scale
    )
    return (grad_queries, grad_keys, grad_values)


def general_body(
    frames,
    text_states,
    text_mask,
    clip_lengths,
    slot_used,
    teacher,
    self_norm_gain,
    self_norm_bias,
    self_query_weight,
    self_key_weight,
    self_value_weight,
    self_output_weight,
    cross_norm_gain,
    cross_norm_bias,
    cross_query_weight,
    cross_key_weight,
    cross_value_weight,
    cross_output_weight,
    feed_norm_gain,
    feed_norm_bias,
    feed_up_weight,
    feed_down_weight,
):
    gathered = (
        lax.all_gather(self_norm_gain, "shard", axis=0, tiled=True),
        lax.all_gather(self_norm_bias, "shard", axis=0, tiled=True),
        lax.all_gather(self_query_weight, "shard", axis=0, tiled=True),
        lax.all_gather(self_key_weight, "shard", axis=0, tiled=True),
        lax.all_gather(self_value_weight, "shard", axis=0, tiled=True),
        lax.all_gather(self_output_weight, "shard", axis=0, tiled=True),
        lax.all_gather(cross_norm_gain, "shard", axis=0, tiled=True),
        lax.all_gather(cross_norm_bias, "shard", axis=0, tiled=True),
        lax.all_gather(cross_query_weight, "shard", axis=0, tiled=True),
        lax.all_gather(cross_key_weight, "shard", axis=0, tiled=True),
        lax.all_gather(cross_value_weight, "shard", axis=0, tiled=True),
        lax.all_gather(cross_output_weight, "shard", axis=0, tiled=True),
        lax.all_gather(feed_norm_gain, "shard", axis=0, tiled=True),
        lax.all_gather(feed_norm_bias, "shard", axis=0, tiled=True),
        lax.all_gather(feed_up_weight, "shard", axis=0, tiled=True),
        lax.all_gather(feed_down_weight, "shard", axis=0, tiled=True),
    )
    (
        gain_attend,
        bias_attend,
        query_matrix,
        key_matrix,
        value_matrix,
        output_matrix,
        gain_cross,
        bias_cross,
        probe_matrix,
        lookup_matrix,
        content_matrix,
        merge_matrix,
        gain_feed,
        bias_feed,
        expand_matrix,
        reduce_matrix,
    ) = gathered
    slots = frames.shape[0]
    frame_count = frames.shape[1]
    width = frames.shape[2]
    text_len = text_states.shape[1]
    shards = lax.axis_size("shard")
    replicas = lax.axis_size("replica")
    clip_total = frame_count * shards
    row_count = slots * frame_count
    scale = HEAD_DIM ** (-0.5)
    shard_rank = lax.axis_index("shard")
    positions = shard_rank * frame_count + jnp.arange(frame_count, dtype=jnp.int32)
    key_positions = jnp.arange(clip_total, dtype=jnp.int32)
    allowed = (key_positions[None, None, :] <= positions[None, :, None]) & (
        key_positions[None, None, :] < clip_lengths[:, None, None]
    )
    valid_rows = ((positions[None, :] < clip_lengths[:, None]) & (slot_used[:, None] > 0)).astype(
        jnp.float32
    )
    text_allowed = text_mask > 0
    inputs = frames.astype(jnp.float32)
    normed_one, pull_one = jax.vjp(
        layer_norm, inputs, gain_attend.astype(jnp.float32), bias_attend.astype(jnp.float32)
    )
    hidden_one = normed_one.astype(jnp.bfloat16).reshape(row_count, width)
    queries = (
        project(hidden_one, query_matrix).astype(jnp.bfloat16).reshape(slots, frame_count, width)
    )
    keys_local = (
        project(hidden_one, key_matrix).astype(jnp.bfloat16).reshape(slots, frame_count, width)
    )
    values_local = (
        project(hidden_one, value_matrix).astype(jnp.bfloat16).reshape(slots, frame_count, width)
    )
    keys_all, values_all = (
        lax.all_gather(keys_local, "shard", axis=1, tiled=True),
        lax.all_gather(values_local, "shard", axis=1, tiled=True),
    )
    head_queries = split_heads(queries)
    head_keys = split_heads(keys_all)
    head_values = split_heads(values_all)
    mixed_self, log_totals = lax.map(self_forward, (head_queries, head_keys, head_values, allowed))
    mixed_rows = mixed_self.reshape(row_count, width)
    after_self = inputs + project(mixed_rows, output_matrix).reshape(slots, frame_count, width)
    normed_two, pull_two = jax.vjp(
        layer_norm, after_self, gain_cross.astype(jnp.float32), bias_cross.astype(jnp.float32)
    )
    hidden_two = normed_two.astype(jnp.bfloat16).reshape(row_count, width)
    probes = split_heads(
        project(hidden_two, probe_matrix).astype(jnp.bfloat16).reshape(slots, frame_count, width)
    )
    text_rows = text_states.reshape(slots * text_len, width)
    lookups = split_heads(
        project(text_rows, lookup_matrix).astype(jnp.bfloat16).reshape(slots, text_len, width)
    )
    contents = split_heads(
        project(text_rows, content_matrix).astype(jnp.bfloat16).reshape(slots, text_len, width)
    )
    cross_scores = (
        jnp.einsum("sqhd,skhd->shqk", probes, lookups, preferred_element_type=jnp.float32) * scale
    )
    cross_scores = jnp.where(text_allowed[:, None, None, :], cross_scores, masked_score)
    cross_peak = jnp.max(cross_scores, axis=-1, keepdims=True)
    cross_weights = jnp.exp(cross_scores - cross_peak)
    cross_probs = cross_weights / jnp.sum(cross_weights, axis=-1, keepdims=True)
    cross_probs_low = cross_probs.astype(jnp.bfloat16)
    cross_mixed = jnp.einsum(
        "shqk,skhd->sqhd", cross_probs_low, contents, preferred_element_type=jnp.float32
    )
    cross_mixed = cross_mixed.astype(jnp.bfloat16).reshape(row_count, width)
    after_cross = after_self + project(cross_mixed, merge_matrix).reshape(slots, frame_count, width)
    normed_three, pull_three = jax.vjp(
        layer_norm, after_cross, gain_feed.astype(jnp.float32), bias_feed.astype(jnp.float32)
    )
    hidden_three = normed_three.astype(jnp.bfloat16).reshape(row_count, width)
    upward = project(hidden_three, expand_matrix)
    activated, gelu_pull = jax.vjp(exact_gelu, upward)
    activated_low = activated.astype(jnp.bfloat16)
    result = after_cross + project(activated_low, reduce_matrix).reshape(slots, frame_count, width)
    output = result.astype(jnp.bfloat16)
    errors = (result - teacher.astype(jnp.float32)) * valid_rows[..., None]
    squares_total, count_total = lax.psum(
        (jnp.sum(errors * errors), jnp.sum(valid_rows)), ("replica", "shard")
    )
    loss = squares_total / (width * count_total)
    grad_result = errors * (slots * replicas * clip_total / count_total)
    grad_feed_low = grad_result.reshape(row_count, width).astype(jnp.bfloat16)
    grad_activated = back_project(grad_feed_low, reduce_matrix)
    grad_upward = gelu_pull(grad_activated)[0].astype(jnp.bfloat16)
    grad_hidden_three = back_project(grad_upward, expand_matrix).reshape(slots, frame_count, width)
    grad_cross_norm, gain_feed_part, bias_feed_part = pull_three(grad_hidden_three)
    grad_after_cross = grad_result + grad_cross_norm
    feed_owned = (
        lax.psum_scatter(
            outer_sum(hidden_three, grad_upward).astype(jnp.bfloat16),
            "shard",
            scatter_dimension=0,
            tiled=True,
        ).astype(jnp.float32),
        lax.psum_scatter(
            outer_sum(activated_low, grad_feed_low).astype(jnp.bfloat16),
            "shard",
            scatter_dimension=0,
            tiled=True,
        ).astype(jnp.float32),
        lax.psum_scatter(
            gain_feed_part.astype(jnp.bfloat16), "shard", scatter_dimension=0, tiled=True
        ).astype(jnp.float32),
        lax.psum_scatter(
            bias_feed_part.astype(jnp.bfloat16), "shard", scatter_dimension=0, tiled=True
        ).astype(jnp.float32),
    )
    grad_cross_low = grad_after_cross.reshape(row_count, width).astype(jnp.bfloat16)
    grad_cross_mixed = split_heads(
        back_project(grad_cross_low, merge_matrix)
        .astype(jnp.bfloat16)
        .reshape(slots, frame_count, width)
    )
    grad_cross_probs = jnp.einsum(
        "sqhd,skhd->shqk", grad_cross_mixed, contents, preferred_element_type=jnp.float32
    )
    content_grads = jnp.einsum(
        "shqk,sqhd->skhd", cross_probs_low, grad_cross_mixed, preferred_element_type=jnp.float32
    )
    cross_inner = jnp.sum(cross_probs * grad_cross_probs, axis=-1, keepdims=True)
    grad_cross_scores = (cross_probs * (grad_cross_probs - cross_inner)).astype(jnp.bfloat16)
    probe_grads = (
        jnp.einsum(
            "shqk,skhd->sqhd", grad_cross_scores, lookups, preferred_element_type=jnp.float32
        )
        * scale
    )
    probe_grads = probe_grads.astype(jnp.bfloat16).reshape(row_count, width)
    lookup_grads = (
        jnp.einsum("shqk,sqhd->skhd", grad_cross_scores, probes, preferred_element_type=jnp.float32)
        * scale
    )
    lookup_sum, content_sum = (
        lax.psum(lookup_grads.astype(jnp.bfloat16), "shard").astype(jnp.float32),
        lax.psum(content_grads.astype(jnp.bfloat16), "shard").astype(jnp.float32),
    )
    lookup_low = lookup_sum.astype(jnp.bfloat16).reshape(slots * text_len, width)
    content_low = content_sum.astype(jnp.bfloat16).reshape(slots * text_len, width)
    own_width = width // shards
    own_text = lax.dynamic_slice_in_dim(text_rows, shard_rank * own_width, own_width, 1)
    lookup_own = outer_sum(own_text, lookup_low)
    content_own = outer_sum(own_text, content_low)
    text_grad = (
        back_project(lookup_low, lookup_matrix) + back_project(content_low, content_matrix)
    ).reshape(slots, text_len, width)
    grad_hidden_two = back_project(probe_grads, probe_matrix).reshape(slots, frame_count, width)
    grad_self_norm, gain_cross_part, bias_cross_part = pull_two(grad_hidden_two)
    grad_after_self = grad_after_cross + grad_self_norm
    grad_self_low = grad_after_self.reshape(row_count, width).astype(jnp.bfloat16)
    grad_mixed = split_heads(
        back_project(grad_self_low, output_matrix)
        .astype(jnp.bfloat16)
        .reshape(slots, frame_count, width)
    )
    grad_queries, grad_keys, grad_values = lax.map(
        self_backward, (head_queries, head_keys, head_values, allowed, log_totals, grad_mixed)
    )
    key_sum, value_sum = (
        lax.psum_scatter(
            grad_keys.reshape(slots, clip_total, width).astype(jnp.bfloat16),
            "shard",
            scatter_dimension=1,
            tiled=True,
        ).astype(jnp.float32),
        lax.psum_scatter(
            grad_values.reshape(slots, clip_total, width).astype(jnp.bfloat16),
            "shard",
            scatter_dimension=1,
            tiled=True,
        ).astype(jnp.float32),
    )
    key_low = key_sum.astype(jnp.bfloat16).reshape(row_count, width)
    value_low = value_sum.astype(jnp.bfloat16).reshape(row_count, width)
    query_low = grad_queries.reshape(row_count, width)
    grad_hidden_one = (
        back_project(query_low, query_matrix)
        + back_project(key_low, key_matrix)
        + back_project(value_low, value_matrix)
    )
    grad_inputs, gain_attend_part, bias_attend_part = pull_one(
        grad_hidden_one.reshape(slots, frame_count, width)
    )
    frames_grad = grad_after_self + grad_inputs
    attend_owned = (
        lax.psum_scatter(
            outer_sum(hidden_one, query_low).astype(jnp.bfloat16),
            "shard",
            scatter_dimension=0,
            tiled=True,
        ).astype(jnp.float32),
        lax.psum_scatter(
            outer_sum(hidden_one, key_low).astype(jnp.bfloat16),
            "shard",
            scatter_dimension=0,
            tiled=True,
        ).astype(jnp.float32),
        lax.psum_scatter(
            outer_sum(hidden_one, value_low).astype(jnp.bfloat16),
            "shard",
            scatter_dimension=0,
            tiled=True,
        ).astype(jnp.float32),
        lax.psum_scatter(
            outer_sum(mixed_rows, grad_self_low).astype(jnp.bfloat16),
            "shard",
            scatter_dimension=0,
            tiled=True,
        ).astype(jnp.float32),
        lax.psum_scatter(
            outer_sum(hidden_two, probe_grads).astype(jnp.bfloat16),
            "shard",
            scatter_dimension=0,
            tiled=True,
        ).astype(jnp.float32),
        lax.psum_scatter(
            outer_sum(cross_mixed, grad_cross_low).astype(jnp.bfloat16),
            "shard",
            scatter_dimension=0,
            tiled=True,
        ).astype(jnp.float32),
        lax.psum_scatter(
            gain_attend_part.astype(jnp.bfloat16), "shard", scatter_dimension=0, tiled=True
        ).astype(jnp.float32),
        lax.psum_scatter(
            bias_attend_part.astype(jnp.bfloat16), "shard", scatter_dimension=0, tiled=True
        ).astype(jnp.float32),
        lax.psum_scatter(
            gain_cross_part.astype(jnp.bfloat16), "shard", scatter_dimension=0, tiled=True
        ).astype(jnp.float32),
        lax.psum_scatter(
            bias_cross_part.astype(jnp.bfloat16), "shard", scatter_dimension=0, tiled=True
        ).astype(jnp.float32),
    )
    summed = (
        lax.psum(attend_owned[6].astype(jnp.bfloat16), "replica").astype(jnp.float32),
        lax.psum(attend_owned[7].astype(jnp.bfloat16), "replica").astype(jnp.float32),
        lax.psum(attend_owned[0].astype(jnp.bfloat16), "replica").astype(jnp.float32),
        lax.psum(attend_owned[1].astype(jnp.bfloat16), "replica").astype(jnp.float32),
        lax.psum(attend_owned[2].astype(jnp.bfloat16), "replica").astype(jnp.float32),
        lax.psum(attend_owned[3].astype(jnp.bfloat16), "replica").astype(jnp.float32),
        lax.psum(attend_owned[8].astype(jnp.bfloat16), "replica").astype(jnp.float32),
        lax.psum(attend_owned[9].astype(jnp.bfloat16), "replica").astype(jnp.float32),
        lax.psum(attend_owned[4].astype(jnp.bfloat16), "replica").astype(jnp.float32),
        lax.psum(lookup_own.astype(jnp.bfloat16), "replica").astype(jnp.float32),
        lax.psum(content_own.astype(jnp.bfloat16), "replica").astype(jnp.float32),
        lax.psum(attend_owned[5].astype(jnp.bfloat16), "replica").astype(jnp.float32),
        lax.psum(feed_owned[2].astype(jnp.bfloat16), "replica").astype(jnp.float32),
        lax.psum(feed_owned[3].astype(jnp.bfloat16), "replica").astype(jnp.float32),
        lax.psum(feed_owned[0].astype(jnp.bfloat16), "replica").astype(jnp.float32),
        lax.psum(feed_owned[1].astype(jnp.bfloat16), "replica").astype(jnp.float32),
    )
    return (
        output,
        loss,
        frames_grad,
        text_grad,
        summed[0],
        summed[1],
        summed[2],
        summed[3],
        summed[4],
        summed[5],
        summed[6],
        summed[7],
        summed[8],
        summed[9],
        summed[10],
        summed[11],
        summed[12],
        summed[13],
        summed[14],
        summed[15],
    )


PAIR = 2 * HEAD_DIM
EVERY = ("shard", "y", "x", "core")
REPLICAS = ("core", "y", "x")
NT = (((1,), (1,)), ((), ()))
TN = (((0,), (0,)), ((), ()))
NN = (((1,), (0,)), ((), ()))


def dot(left, right, dims):
    return lax.dot_general(left, right, dims, preferred_element_type=jnp.float32)


def half_mask(side, value):
    lanes = lax.broadcasted_iota(jnp.int32, (1, PAIR), 1)
    inside = (lanes >= HEAD_DIM) if side else (lanes < HEAD_DIM)
    return jnp.where(inside, value, 0.0).astype(jnp.bfloat16)


def fill_clip(place, own_ref, other_ref, all_ref):
    block = own_ref.shape[0] // 2
    for part in range(2):
        rows = slice(part * block, (part + 1) * block)
        for at, ref in ((place[part], own_ref), (place[3 + part], other_ref)):
            all_ref[pl.ds(pl.multiple_of(at * block, block), block), :] = ref[rows, :]


def self_forward_kernel(
    place, q_ref, own_k, own_v, other_k, other_v, mixed_ref, lse_ref, k_ref, v_ref, acc_ref
):
    fill_clip(place, own_k, other_k, k_ref)
    fill_clip(place, own_v, other_v, v_ref)
    block = q_ref.shape[0] // 2
    length = place[2]
    low = lax.broadcasted_iota(jnp.int32, (PAIR, 1), 0) < HEAD_DIM
    for part in range(2):
        first = place[part] * block
        rows = slice(part * block, (part + 1) * block)
        q = q_ref[rows, :]
        q_half = [q * half_mask(side, HEAD_DIM ** (-0.5)) for side in range(2)]
        limit = jnp.minimum(
            first + lax.broadcasted_iota(jnp.int32, (1, block), 1) + 1, length
        )
        acc_ref[...] = jnp.zeros_like(acc_ref)

        def step(j, peaks, q_half=q_half, limit=limit):
            at = pl.multiple_of(j * block, block)
            k = k_ref[pl.ds(at, block), :]
            v = v_ref[pl.ds(at, block), :]
            allowed = at + lax.broadcasted_iota(jnp.int32, (block, block), 0) < limit
            out = []
            for side in range(2):
                scores = jnp.where(allowed, dot(k, q_half[side], NT), masked_score)
                peak = jnp.maximum(peaks[side], jnp.max(scores, axis=0, keepdims=True))
                weights = jnp.exp(scores - peak).astype(jnp.bfloat16)
                v_ones = v * half_mask(side, 1.0) + half_mask(1 - side, 1.0)
                acc_ref[side] = acc_ref[side] * jnp.exp(peaks[side] - peak) + dot(
                    v_ones, weights, TN
                )
                out.append(peak)
            return tuple(out)

        peaks = lax.fori_loop(
            0, place[part] + 1, step, (jnp.full((1, block), masked_score, jnp.float32),) * 2
        )
        top, bottom = acc_ref[0], acc_ref[1]
        total = jnp.where(low, top[HEAD_DIM : HEAD_DIM + 1], bottom[0:1])
        mixed = jnp.where(low, top, bottom) / total
        mixed_ref[rows, :] = mixed.T.astype(jnp.bfloat16)
        lse_ref[0:1, rows] = peaks[0] + jnp.log(top[HEAD_DIM : HEAD_DIM + 1])
        lse_ref[1:2, rows] = peaks[1] + jnp.log(bottom[0:1])


def self_backward_kernel(
    place, q_ref, own_k, own_v, other_k, other_v, mixed_ref, grad_ref, lse_ref,
    dq_ref, own_dk, own_dv, other_dk, other_dv, k_ref, v_ref, dq_acc, dk_acc, dv_acc,
):
    fill_clip(place, own_k, other_k, k_ref)
    fill_clip(place, own_v, other_v, v_ref)
    block = q_ref.shape[0] // 2
    length = place[2]
    scale = HEAD_DIM ** (-0.5)
    dk_acc[...] = jnp.zeros_like(dk_acc)
    dv_acc[...] = jnp.zeros_like(dv_acc)
    for part in range(2):
        first = place[part] * block
        rows = slice(part * block, (part + 1) * block)
        q = q_ref[rows, :]
        grad = grad_ref[rows, :]
        q_half = [q * half_mask(side, scale) for side in range(2)]
        grad_half = [grad * half_mask(side, 1.0) for side in range(2)]
        product = (grad.astype(jnp.float32) * mixed_ref[rows, :].astype(jnp.float32)).T
        inner = [
            jnp.sum(product[side * HEAD_DIM : (side + 1) * HEAD_DIM], axis=0, keepdims=True)
            for side in range(2)
        ]
        lse = [lse_ref[side : side + 1, rows] for side in range(2)]
        limit = jnp.minimum(
            first + lax.broadcasted_iota(jnp.int32, (1, block), 1) + 1, length
        )
        dq_acc[...] = jnp.zeros_like(dq_acc)

        def step(
            j, carry, q_half=q_half, grad_half=grad_half, inner=inner, lse=lse, limit=limit
        ):
            at = pl.multiple_of(j * block, block)
            k = k_ref[pl.ds(at, block), :]
            v = v_ref[pl.ds(at, block), :]
            allowed = at + lax.broadcasted_iota(jnp.int32, (block, block), 0) < limit
            dq, dk, dv = 0.0, 0.0, 0.0
            for side in range(2):
                scores = jnp.where(allowed, dot(k, q_half[side], NT), masked_score)
                probs = jnp.exp(scores - lse[side])
                grad_probs = dot(v, grad_half[side], NT)
                grad_scores = (probs * (grad_probs - inner[side])).astype(jnp.bfloat16)
                dv += dot(probs.astype(jnp.bfloat16), grad_half[side], NN)
                dk += dot(grad_scores, q_half[side], NN)
                dq += dot(k * half_mask(side, scale), grad_scores, TN)
            dk_acc[pl.ds(at, block), :] += dk
            dv_acc[pl.ds(at, block), :] += dv
            dq_acc[...] += dq
            return carry

        lax.fori_loop(0, place[part] + 1, step, 0)
        dq_ref[rows, :] = dq_acc[...].T.astype(jnp.bfloat16)
    for part in range(2):
        rows = slice(part * block, (part + 1) * block)
        own = pl.ds(pl.multiple_of(place[part] * block, block), block)
        other = pl.ds(pl.multiple_of(place[3 + part] * block, block), block)
        own_dk[rows, :] = dk_acc[own, :].astype(jnp.bfloat16)
        own_dv[rows, :] = dv_acc[own, :].astype(jnp.bfloat16)
        other_dk[rows, :] = dk_acc[other, :].astype(jnp.bfloat16)
        other_dv[rows, :] = dv_acc[other, :].astype(jnp.bfloat16)


def pair_block(rows):
    return pl.BlockSpec((rows, PAIR), lambda i, *_: (0, i))


def value_block(rows, pairs):
    return pl.BlockSpec((rows, PAIR), lambda i, *_: (0, pairs + i))


def self_attend(place, queries, own, other):
    rows, width = queries.shape
    clip = 2 * rows
    pairs = width // PAIR
    return pl.pallas_call(
        self_forward_kernel,
        out_shape=(
            jax.ShapeDtypeStruct((rows, width), jnp.bfloat16),
            jax.ShapeDtypeStruct((pairs * 8, rows), jnp.float32),
        ),
        grid_spec=pltpu.PrefetchScalarGridSpec(
            num_scalar_prefetch=1,
            grid=(pairs,),
            in_specs=[pair_block(rows)] + [pair_block(rows), value_block(rows, pairs)] * 2,
            out_specs=(pair_block(rows), pl.BlockSpec((8, rows), lambda i, *_: (i, 0))),
            scratch_shapes=[
                pltpu.VMEM((clip, PAIR), jnp.bfloat16),
                pltpu.VMEM((clip, PAIR), jnp.bfloat16),
                pltpu.VMEM((2, PAIR, rows // 2), jnp.float32),
            ],
        ),
        compiler_params=pltpu.CompilerParams(vmem_limit_bytes=32 * 2**20),
        cost_estimate=pl.CostEstimate(
            flops=2 * 2 * rows * clip * width, bytes_accessed=8 * clip * width, transcendentals=0
        ),
        name="self_attend",
    )(place, queries, own, own, other, other)


def self_attend_back(place, queries, own, other, mixed, grads, lse):
    rows, width = queries.shape
    clip = 2 * rows
    pairs = width // PAIR
    return pl.pallas_call(
        self_backward_kernel,
        out_shape=(jax.ShapeDtypeStruct((rows, width), jnp.bfloat16),) * 5,
        grid_spec=pltpu.PrefetchScalarGridSpec(
            num_scalar_prefetch=1,
            grid=(pairs,),
            in_specs=[pair_block(rows)]
            + [pair_block(rows), value_block(rows, pairs)] * 2
            + [
                pair_block(rows),
                pair_block(rows),
                pl.BlockSpec((8, rows), lambda i, *_: (i, 0)),
            ],
            out_specs=(pair_block(rows),) * 5,
            scratch_shapes=[
                pltpu.VMEM((clip, PAIR), jnp.bfloat16),
                pltpu.VMEM((clip, PAIR), jnp.bfloat16),
                pltpu.VMEM((PAIR, rows // 2), jnp.float32),
                pltpu.VMEM((clip, PAIR), jnp.float32),
                pltpu.VMEM((clip, PAIR), jnp.float32),
            ],
        ),
        compiler_params=pltpu.CompilerParams(vmem_limit_bytes=32 * 2**20),
        cost_estimate=pl.CostEstimate(
            flops=5 * 2 * rows * clip * width, bytes_accessed=16 * clip * width, transcendentals=0
        ),
        name="self_attend_back",
    )(place, queries, own, own, other, other, mixed, grads, lse)


def both_heads(rows, value):
    return jnp.concatenate([rows * half_mask(side, value) for side in range(2)], axis=0)


def cross_probs_of(lookup_two, probes, present):
    text = present.shape[0]
    scores = dot(lookup_two, probes, NT)
    out = []
    for side in range(2):
        part = jnp.where(
            present > 0, scores[side * text : (side + 1) * text], masked_score
        )
        weights = jnp.exp(part - jnp.max(part, axis=0, keepdims=True))
        out.append(weights / jnp.sum(weights, axis=0, keepdims=True))
    return out


def cross_forward_kernel(probe_ref, lookup_ref, content_ref, present_ref, mixed_ref):
    probs = cross_probs_of(
        both_heads(lookup_ref[...], HEAD_DIM ** (-0.5)), probe_ref[...], present_ref[...]
    )
    probs = jnp.concatenate(probs, axis=0).astype(jnp.bfloat16)
    mixed_ref[...] = dot(probs, both_heads(content_ref[...], 1.0), TN).astype(jnp.bfloat16)


def cross_backward_kernel(
    probe_ref, lookup_ref, content_ref, present_ref, grad_ref, dp_ref, dl_ref, dc_ref
):
    text = present_ref.shape[0]
    scale = HEAD_DIM ** (-0.5)
    probes = probe_ref[...]
    grads = grad_ref[...]
    lookup_two = both_heads(lookup_ref[...], scale)
    probs = cross_probs_of(lookup_two, probes, present_ref[...])
    grad_probs = dot(both_heads(content_ref[...], 1.0), grads, NT)
    grad_scores = []
    for side in range(2):
        part = grad_probs[side * text : (side + 1) * text]
        inner = jnp.sum(probs[side] * part, axis=0, keepdims=True)
        grad_scores.append(probs[side] * (part - inner))
    grad_scores = jnp.concatenate(grad_scores, axis=0).astype(jnp.bfloat16)
    probs = jnp.concatenate(probs, axis=0).astype(jnp.bfloat16)
    low = lax.broadcasted_iota(jnp.int32, (1, PAIR), 1) < HEAD_DIM
    dp_ref[...] = dot(grad_scores, lookup_two, TN).astype(jnp.bfloat16)
    dl = dot(grad_scores, probes, NN) * scale
    dl_ref[...] = jnp.where(low, dl[:text], dl[text:]).astype(jnp.bfloat16)
    dc = dot(probs, grads, NN)
    dc_ref[...] = jnp.where(low, dc[:text], dc[text:]).astype(jnp.bfloat16)


def cross_attend(probes, lookups, contents, present):
    rows, width = probes.shape
    text = lookups.shape[0]
    return pl.pallas_call(
        cross_forward_kernel,
        out_shape=jax.ShapeDtypeStruct((rows, width), jnp.bfloat16),
        grid=(width // PAIR,),
        in_specs=[
            pair_block(rows),
            pair_block(text),
            pair_block(text),
            pl.BlockSpec((text, 1), lambda i: (0, 0)),
        ],
        out_specs=pair_block(rows),
        compiler_params=pltpu.CompilerParams(vmem_limit_bytes=32 * 2**20),
        cost_estimate=pl.CostEstimate(
            flops=8 * rows * text * width, bytes_accessed=4 * rows * width, transcendentals=0
        ),
        name="cross_attend",
    )(probes, lookups, contents, present)


def cross_attend_back(probes, lookups, contents, present, grads):
    rows, width = probes.shape
    text = lookups.shape[0]
    return pl.pallas_call(
        cross_backward_kernel,
        out_shape=(
            jax.ShapeDtypeStruct((rows, width), jnp.bfloat16),
            jax.ShapeDtypeStruct((text, width), jnp.bfloat16),
            jax.ShapeDtypeStruct((text, width), jnp.bfloat16),
        ),
        grid=(width // PAIR,),
        in_specs=[
            pair_block(rows),
            pair_block(text),
            pair_block(text),
            pl.BlockSpec((text, 1), lambda i: (0, 0)),
            pair_block(rows),
        ],
        out_specs=(pair_block(rows), pair_block(text), pair_block(text)),
        compiler_params=pltpu.CompilerParams(vmem_limit_bytes=32 * 2**20),
        cost_estimate=pl.CostEstimate(
            flops=20 * rows * text * width, bytes_accessed=6 * rows * width, transcendentals=0
        ),
        name="cross_attend_back",
    )(probes, lookups, contents, present, grads)


def unpack_kernel(in_ref, out_ref):
    pieces = in_ref[...]
    out_ref[...] = pieces.reshape(-1, pieces.shape[-1]).T.astype(jnp.float32)


def unpack(full, rows, place, out_shape, out_at, together):
    owners, _, features = full.shape
    tall = out_shape[0] // features
    wide = out_shape[1] // (together * rows)
    return pl.pallas_call(
        unpack_kernel,
        out_shape=jax.ShapeDtypeStruct(out_shape, jnp.float32),
        grid=(tall, wide),
        in_specs=[
            pl.BlockSpec((together, rows, features), lambda i, j: (j + out_at, place + i, 0))
        ],
        out_specs=pl.BlockSpec((features, together * rows), lambda i, j: (i, j)),
        compiler_params=pltpu.CompilerParams(vmem_limit_bytes=32 * 2**20),
        cost_estimate=pl.CostEstimate(
            flops=0, bytes_accessed=6 * out_shape[0] * out_shape[1], transcendentals=0
        ),
        name="unpack",
    )(full)


def held(values, *others):
    return list(lax.optimization_barrier((*values, *others))[: len(values)])


def after(value, *others):
    return lax.optimization_barrier((value, *others))[0]


def norm_parts(values):
    mean = jnp.mean(values, axis=-1, keepdims=True)
    center = values - mean
    return mean, lax.rsqrt(jnp.mean(center * center, axis=-1, keepdims=True) + epsilon)


def norm_back(grads, values, parts, gain):
    mean, inverse = parts
    unit = (values - mean) * inverse
    gain_grad = jnp.sum(grads * unit, axis=0)
    bias_grad = jnp.sum(grads, axis=0)
    scaled = grads * gain
    back = inverse * (
        scaled
        - jnp.mean(scaled, axis=-1, keepdims=True)
        - unit * jnp.mean(scaled * unit, axis=-1, keepdims=True)
    )
    return back, gain_grad, bias_grad


def clip_body(
    frames,
    text_states,
    text_mask,
    clip_lengths,
    slot_used,
    teacher,
    self_norm_gain,
    self_norm_bias,
    self_query_weight,
    self_key_weight,
    self_value_weight,
    self_output_weight,
    cross_norm_gain,
    cross_norm_bias,
    cross_query_weight,
    cross_key_weight,
    cross_value_weight,
    cross_output_weight,
    feed_norm_gain,
    feed_norm_bias,
    feed_up_weight,
    feed_down_weight,
):
    block, width = frames.shape[1:]
    text_len = text_states.shape[1]
    shards, replicas, outers = 4, 8, 4
    core = lax.axis_index("core")
    shard = lax.axis_index("shard")
    outer = 2 * lax.axis_index("y") + lax.axis_index("x")
    replica = 2 * outer + core
    clip = block * shards
    hidden_units = feed_up_weight.shape[1]

    holder = {0: 0, 1: 1, 2: 1, 3: 0}
    there = ([], [])
    for c in range(2):
        for s in range(4):
            for turn in range(2):
                slot = turn if s < 2 else 1 - turn
                there[turn].append((c * 4 + s, holder[s] * 4 + 2 * c + slot))
    back = tuple([(b, a) for a, b in pairs] for pairs in there)
    spot = ("core", "shard")
    swap = [(0, 1), (1, 0)]
    even = shard % 2 == 0
    lower = shard < 2
    first_core = core == 0

    def hop(values, distance):
        pairs = [(i, (i + distance) % shards) for i in range(shards)]
        return lax.ppermute(values, "shard", pairs)

    def hops(values):
        return [hop(values, distance) for distance in (1, 2, 3)]

    def line_up(mine, came):
        out = jnp.zeros((shards,) + mine.shape, mine.dtype)
        out = lax.dynamic_update_index_in_dim(out, mine, shard, 0)
        for distance, values in zip((1, 2, 3), came):
            owner = lax.rem(shard + shards - distance, shards)
            out = lax.dynamic_update_index_in_dim(out, values, owner, 0)
        return out

    def to_chip(pair):
        one = lax.ppermute(jnp.where(lower, pair[0], pair[1]), spot, there[0])
        two = lax.ppermute(jnp.where(lower, pair[1], pair[0]), spot, there[1])
        return one, two

    def by_time(one, two):
        return jnp.concatenate([jnp.where(even, one, two), jnp.where(even, two, one)], axis=0)

    def outgoing(values):
        early, late = values[:block], values[block:]
        return jnp.where(even, early, late), jnp.where(even, late, early)

    def from_chip(values):
        one, two = outgoing(values)
        return lax.ppermute(one, spot, back[0]), lax.ppermute(two, spot, back[1])

    def by_slot(one, two):
        return jnp.stack([jnp.where(lower, one, two), jnp.where(lower, two, one)])

    def share_of(weight):
        share = weight.shape[0] // replicas
        return lax.dynamic_slice_in_dim(weight, replica * share, share, 0)

    def from_replicas(line):
        full = lax.all_gather(line, ("y", "x", "core"), axis=1, tiled=True)
        return full.reshape(-1, line.shape[-1])

    qkv_share = jnp.concatenate(
        [share_of(self_query_weight), share_of(self_key_weight), share_of(self_value_weight)],
        axis=1,
    )
    vectors = jnp.concatenate(
        [
            self_norm_gain,
            self_norm_bias,
            cross_norm_gain,
            cross_norm_bias,
            feed_norm_gain,
            feed_norm_bias,
        ]
    )
    vectors = jnp.pad(vectors[None, :], ((0, 15), (0, 3 * width - 6 * block)))
    share = qkv_share.shape[0]
    qkv_mine = jnp.concatenate([qkv_share, vectors], axis=0)
    qkv_came = hops(qkv_mine)
    qkv_matrix = from_replicas(line_up(qkv_share, [values[:share] for values in qkv_came]))
    norms = line_up(vectors[0], [values[share] for values in qkv_came])
    norms = norms[:, : 6 * block].reshape(shards, 6, block).transpose(1, 0, 2)
    norms = norms.reshape(6, width).astype(jnp.float32)
    rest_share = jnp.concatenate(
        [share_of(self_output_weight), share_of(cross_query_weight), share_of(cross_output_weight)],
        axis=1,
    )
    rest_came = hops(after(rest_share, *qkv_came))
    rest = from_replicas(line_up(rest_share, rest_came))
    came = to_chip(after(frames, *rest_came))
    x_low = by_time(*came)
    expand_share = share_of(feed_up_weight)
    expand_came = hops(after(expand_share, *came))

    facts = jnp.concatenate(
        [(clip_lengths // 64)[:, None], (clip_lengths % 64)[:, None], slot_used[:, None], text_mask],
        axis=1,
    ).astype(jnp.bfloat16)
    facts = jnp.pad(facts[:, None, :], ((0, 0), (0, 15), (0, width - facts.shape[1])))
    text_sent = lax.ppermute(jnp.concatenate([text_states, facts], axis=1), "core", swap)
    text_other = text_sent[:, :text_len]
    both = jnp.stack([facts[:, 0], text_sent[:, text_len]])[:, :, : 3 + text_len].astype(jnp.int32)
    lengths = 64 * both[:, :, 0] + both[:, :, 1]
    fact = lax.dynamic_index_in_dim(
        jnp.where(shard // 2 == core, both[0], both[1]), shard % 2, 0, keepdims=False
    )
    length, used = 64 * fact[0] + fact[1], fact[2]
    present = fact[3:].reshape(text_len, 1)
    count = jnp.sum(
        jnp.where(both[:, :, 2] > 0, jnp.minimum(lengths, clip), 0).astype(jnp.float32)
    )
    count = jnp.full((8, 128), count)
    for axis in ("x", "y"):
        count += lax.ppermute(count, axis, swap)
    count = count[0, 0]
    text_all = jnp.concatenate(
        [
            jnp.where(first_core, text_states, text_other),
            jnp.where(first_core, text_other, text_states),
        ],
        axis=0,
    ).reshape(4 * text_len, width)
    text_all = lax.dynamic_slice_in_dim(text_all, shard * block, block, 1)
    text_matrix = jnp.where(first_core, cross_key_weight, cross_value_weight)
    text_part = project(text_all, text_matrix).astype(jnp.bfloat16).reshape(4, text_len, width)
    text_came = [
        hop(
            lax.dynamic_index_in_dim(
                text_part, lax.rem(shard + distance, shards), 0, keepdims=False
            ),
            distance,
        )
        for distance in (1, 2, 3)
    ]

    places = jnp.stack([core, 3 - core, length, 1 - core, 2 + core]).astype(jnp.int32)
    positions = jnp.concatenate(
        [core * block + jnp.arange(block), (3 - core) * block + jnp.arange(block)]
    )
    valid_rows = ((positions < length) & (used > 0)).astype(jnp.float32)[:, None]
    inputs = x_low.astype(jnp.float32)
    parts_one = norm_parts(inputs)
    hidden_one = ((inputs - parts_one[0]) * parts_one[1] * norms[0] + norms[1]).astype(
        jnp.bfloat16
    )
    kv = project(after(hidden_one, count), qkv_matrix[:, width:]).astype(jnp.bfloat16)
    kv_other = lax.ppermute(kv, "core", swap)
    expand_came = held(expand_came, kv)
    text_came = held(text_came, kv)
    queries = project(after(hidden_one, kv, *expand_came), qkv_matrix[:, :width])
    queries = queries.astype(jnp.bfloat16)
    expand_matrix = from_replicas(line_up(expand_share, expand_came))
    reduce_share = share_of(feed_down_weight)
    reduce_came = hops(after(reduce_share, *expand_came))
    output_matrix = rest[:, :width]
    probe_matrix = rest[:, width : 2 * width]
    merge_matrix = rest[:, 2 * width :]
    mixed_self, lse = self_attend(after(places, *expand_came, *text_came), queries, kv, kv_other)
    reduce_came = held(reduce_came, mixed_self)
    reduce_matrix = from_replicas(line_up(reduce_share, reduce_came))
    text_half = lax.dynamic_index_in_dim(text_part, shard, 0, keepdims=False).astype(jnp.float32)
    for values in text_came:
        text_half += values.astype(jnp.float32)
    text_half = text_half.astype(jnp.bfloat16)
    text_swap = lax.ppermute(text_half, "core", swap)
    lookups = jnp.where(first_core, text_half, text_swap)
    contents = jnp.where(first_core, text_swap, text_half)
    after_self = inputs + project(mixed_self, output_matrix)
    parts_two = norm_parts(after_self)
    hidden_two = ((after_self - parts_two[0]) * parts_two[1] * norms[2] + norms[3]).astype(
        jnp.bfloat16
    )
    probes = project(hidden_two, probe_matrix).astype(jnp.bfloat16)
    teacher_came = to_chip(after(teacher, *reduce_came, probes))
    cross_mixed = cross_attend(probes, lookups, contents, present)
    after_cross = after_self + project(cross_mixed, merge_matrix)
    parts_three = norm_parts(after_cross)
    hidden_three = (
        (after_cross - parts_three[0]) * parts_three[1] * norms[4] + norms[5]
    ).astype(jnp.bfloat16)
    upward = project(hidden_three, expand_matrix)
    activated, gelu_pull = jax.vjp(exact_gelu, upward)
    activated_low = activated.astype(jnp.bfloat16)
    teacher_low = by_time(*held(teacher_came, activated_low))
    result = after_cross + project(activated_low, reduce_matrix)
    errors = (result - teacher_low.astype(jnp.float32)) * valid_rows
    squares = jnp.sum(errors * errors)
    grad_result = errors * (4 * outers * clip / count)
    grad_feed_low = grad_result.astype(jnp.bfloat16)

    def theirs_of(right, left):
        columns = right.shape[1] // 2
        part = lax.dynamic_slice_in_dim(right, (1 - core) * columns, columns, 1)
        return outer_sum(part, left).astype(jnp.bfloat16)

    def ours_of(right, left, theirs):
        columns = right.shape[1] // 2
        sent = lax.ppermute(theirs, "core", swap)
        part = lax.dynamic_slice_in_dim(right, core * columns, columns, 1)
        return (outer_sum(part, left) + sent.astype(jnp.float32)).astype(jnp.bfloat16)

    def over_outer(values):
        return lax.psum_scatter(values, ("y", "x"), scatter_dimension=0, tiled=True)

    def shard_hops(values):
        columns = values.shape[1] // shards
        return [
            hop(
                lax.dynamic_slice_in_dim(
                    values, lax.rem(shard + distance, shards) * columns, columns, 1
                ),
                distance,
            )
            for distance in (1, 2, 3)
        ]

    def over_shard(values, came):
        columns = values.shape[1] // shards
        total = lax.dynamic_slice_in_dim(values, shard * columns, columns, 1).astype(jnp.float32)
        for part in came:
            total += part.astype(jnp.float32)
        return total.astype(jnp.bfloat16)

    down_theirs = theirs_of(grad_feed_low, activated_low)
    to_send = outgoing(result.astype(jnp.bfloat16))
    output_one = lax.ppermute(to_send[0], spot, back[0])
    grad_activated = back_project(after(grad_feed_low, down_theirs), reduce_matrix)
    grad_upward = gelu_pull(grad_activated)[0].astype(jnp.bfloat16)
    output_one = after(output_one, grad_upward)
    down_ours = ours_of(
        after(grad_feed_low, grad_upward, output_one), activated_low, down_theirs
    )
    down_sum = over_outer(down_ours)
    up_theirs = theirs_of(after(grad_upward, down_ours), hidden_three)
    grad_hidden_three = back_project(after(grad_upward, up_theirs), expand_matrix)
    output_two = lax.ppermute(after(to_send[1], output_one), spot, back[1])
    output_two = after(output_two, grad_hidden_three)
    output = by_slot(output_one, output_two)
    up_ours = ours_of(after(grad_upward, grad_hidden_three, output_two), hidden_three, up_theirs)
    grad_norm, gain_feed, bias_feed = norm_back(
        after(grad_hidden_three, up_ours), after_cross, parts_three, norms[4]
    )
    grad_after_cross = grad_result + grad_norm
    grad_cross_low = grad_after_cross.astype(jnp.bfloat16)
    merge_theirs = theirs_of(grad_cross_low, cross_mixed)
    grad_cross_mixed = back_project(after(grad_cross_low, merge_theirs), merge_matrix).astype(
        jnp.bfloat16
    )
    probe_grads, lookup_grads, content_grads = cross_attend_back(
        probes, lookups, contents, present, grad_cross_mixed
    )
    up_sum = over_outer(up_ours)
    text_mine = jnp.where(first_core, lookup_grads, content_grads)
    text_sent = lax.ppermute(
        jnp.where(first_core, content_grads, lookup_grads), "core", swap
    )
    text_mine = (text_mine.astype(jnp.float32) + text_sent.astype(jnp.float32)).astype(
        jnp.bfloat16
    )
    merge_ours = ours_of(after(grad_cross_low, probe_grads), cross_mixed, merge_theirs)
    probe_theirs = theirs_of(after(probe_grads, merge_ours), hidden_two)
    grad_hidden_two = back_project(after(probe_grads, probe_theirs), probe_matrix)
    text_four = line_up(text_mine, hops(text_mine)).reshape(4 * text_len, width)
    grad_norm, gain_cross, bias_cross = norm_back(
        grad_hidden_two, after_self, parts_two, norms[2]
    )
    grad_after_self = grad_after_cross + grad_norm
    grad_self_low = grad_after_self.astype(jnp.bfloat16)
    output_theirs = theirs_of(grad_self_low, mixed_self)
    grad_mixed = back_project(after(grad_self_low, output_theirs), output_matrix).astype(
        jnp.bfloat16
    )
    probe_ours = ours_of(after(probe_grads, grad_mixed), hidden_two, probe_theirs)
    text_weights = outer_sum(text_four, text_all).astype(jnp.bfloat16)
    text_back = back_project(text_four, text_matrix).astype(jnp.bfloat16)
    output_ours = ours_of(after(grad_self_low, probe_ours), mixed_self, output_theirs)
    text_rows = width // outers
    middle = jnp.concatenate(
        [
            values.reshape(outers, -1, width)
            for values in (
                output_ours,
                probe_ours,
                merge_ours,
                text_weights.reshape(outers, shards, text_rows // shards, block)
                .transpose(0, 2, 1, 3)
                .reshape(outers, text_rows // shards, width),
            )
        ],
        axis=1,
    )
    middle_rows = middle.shape[1]
    middle = middle.reshape(outers * middle_rows, width)
    middle_sum = over_outer(middle)
    text_split = text_rows // shards
    text_piece = (
        middle_sum[middle_rows - text_split :]
        .reshape(text_split, shards, block)
        .transpose(1, 0, 2)
        .reshape(text_rows, block)
    )
    text_back = text_back.reshape(2, 2, text_len, block)
    text_kept = lax.dynamic_index_in_dim(text_back, core, 0, keepdims=False)
    text_gone = lax.dynamic_index_in_dim(text_back, 1 - core, 0, keepdims=False)
    text_own = text_kept.astype(jnp.float32) + lax.ppermute(text_gone, "core", swap).astype(
        jnp.float32
    )
    text_own = text_own.astype(jnp.bfloat16)
    down_came = shard_hops(down_sum)
    text_came = hops(text_own)
    grad_queries, own_keys, own_values, other_keys, other_values = self_attend_back(
        places, queries, kv, kv_other, mixed_self, after(grad_mixed, middle, text_own), lse
    )
    text_came = held(text_came, grad_queries)
    down_came = held(down_came, grad_queries)
    other_keys, other_values = held([other_keys, other_values], *text_came, *down_came)
    own_keys += lax.ppermute(other_keys, "core", swap)
    own_values += lax.ppermute(other_values, "core", swap)
    down_piece = over_shard(down_sum, down_came)
    up_came = shard_hops(after(up_sum, down_piece))

    qkv_grads = jnp.concatenate([grad_queries, own_keys, own_values], axis=1)
    qkv_theirs = theirs_of(qkv_grads, hidden_one)
    grad_hidden_one = back_project(after(qkv_grads, qkv_theirs), qkv_matrix)
    qkv_ours = ours_of(after(qkv_grads, grad_hidden_one), hidden_one, qkv_theirs)
    up_came = held(up_came, grad_hidden_one)
    up_piece = over_shard(up_sum, up_came)
    text_grad = line_up(text_own, text_came).astype(jnp.float32)
    text_grad = text_grad.transpose(1, 2, 0, 3).reshape(text_states.shape)
    qkv_sum = over_outer(qkv_ours)
    middle_kept = after(middle_sum[: middle_rows - text_split], qkv_ours)
    middle_came = shard_hops(middle_kept)
    middle_piece = over_shard(middle_kept, middle_came)
    early = jnp.concatenate(
        [up_piece]
        + [down_piece[:, i * block : (i + 1) * block] for i in range(4)]
        + [text_piece, middle_piece],
        axis=0,
    )
    grad_norm, gain_self, bias_self = norm_back(
        after(grad_hidden_one, qkv_ours, early), inputs, parts_one, norms[0]
    )
    frames_low = (grad_after_self + grad_norm).astype(jnp.bfloat16)
    late_came = held(shard_hops(after(qkv_sum, *middle_came)), frames_low)
    frames_came = from_chip(after(frames_low, *late_came))
    frames_grad = by_slot(*frames_came).astype(jnp.float32)
    small = jnp.stack(
        [
            gain_self,
            bias_self,
            gain_cross,
            bias_cross,
            gain_feed,
            bias_feed,
            jnp.full((width,), squares),
            jnp.zeros((width,), jnp.float32),
        ]
    )
    small = after(small, *late_came)
    for axis in ("core", "x", "y"):
        small += lax.ppermute(small, axis, swap)
    small_came = shard_hops(small)
    small_own = lax.dynamic_slice_in_dim(small, shard * block, block, 1)
    for part in small_came:
        small_own += part
    loss = small_own[6, 0] / (width * count)
    early = lax.all_gather(after(early, text_grad), REPLICAS, axis=0)
    piece = width // replicas
    square = (block, width)
    up_grad = unpack(early, hidden_units // replicas, 0, (block, hidden_units), 0, 1)
    at = hidden_units // replicas // piece
    down_grad = unpack(early, piece, at, (4 * block, width), 0, 2)
    at += 4
    key_grad = unpack(early, text_rows, at * piece // text_rows, square, 0, 1)
    value_grad = unpack(early, text_rows, at * piece // text_rows, square, 4, 1)
    at += text_rows // piece
    output_grad = unpack(early, piece, at, square, 0, 2)
    probe_grad = unpack(early, piece, at + 1, square, 0, 2)
    merge_grad = unpack(early, piece, at + 2, square, 0, 2)
    late = over_shard(qkv_sum, late_came)
    late = lax.all_gather(
        after(late, early, *frames_came, *small_came), REPLICAS, axis=0, tiled=True
    )
    late = late.reshape(-1, block, block)
    qkv_grad = [unpack(late, block, 0, square, 2 * i, 2) for i in range(3)]
    return (
        output,
        loss,
        frames_grad,
        text_grad,
        small_own[0],
        small_own[1],
        qkv_grad[0],
        qkv_grad[1],
        qkv_grad[2],
        output_grad,
        small_own[2],
        small_own[3],
        probe_grad,
        key_grad,
        value_grad,
        merge_grad,
        small_own[4],
        small_own[5],
        up_grad,
        down_grad,
    )


def solution(mesh):
    by_chip = mesh.shape["shard"] == 4 and mesh.shape["replica"] == 8
    replica = ("y", "x", "core") if by_chip else "replica"
    row = P(replica)
    clip = P(replica, "shard", None)
    text = P(replica, None, None)
    vector = P("shard")
    matrix = P("shard", None)
    weights = (
        [vector, vector] + [matrix] * 4 + [vector, vector] + [matrix] * 4 + [vector, vector]
        + [matrix] * 2
    )
    if by_chip:
        mesh = Mesh(mesh.devices.reshape(2, 2, 2, 4), ("y", "x", "core", "shard"))
    return jax.shard_map(
        clip_body if by_chip else general_body,
        mesh=mesh,
        in_specs=(clip, text, P(replica, None), row, row, clip, *weights),
        out_specs=(clip, P(), clip, text, *weights),
        check_vma=False,
    )
```
